32 devices in a mesh: ep: 8 (over z, x), ws: 4 (over y, core).
Axes of the slice: x: 2, y: 2, z: 4, core: 2. Of those that a mesh axis runs over, the one named last changes fastest.
Arguments:
- hidden_in: bfloat16 [8192, 2048], P(('ep', 'ws')), may hold values from -36 to 36
- attn_gain: bfloat16 [2048], P('ws'), may hold values from 0.5 to 1.5
- w_query: bfloat16 [2048, 4096], P('ws'), may hold values from -0.125 to 0.125
- key_projection: bfloat16 [2048, 512], P('ws'), may hold values from -0.125 to 0.125
- value_projection: bfloat16 [2048, 512], P('ws'), may hold values from -0.125 to 0.125
- query_gain: float32 [128], replicated, may hold values from 0.5 to 1.5
- key_gain: float32 [128], replicated, may hold values from 0.5 to 1.5
- w_output: bfloat16 [4096, 2048], P('ws'), may hold values from -0.375 to 0.375
- ffn_gain: bfloat16 [2048], P('ws'), may hold values from 0.5 to 1.5
- w_router: bfloat16 [2048, 32], P('ws'), may hold values from -0.0625 to 0.0625
- routes: int32 [8192, 8], P(('ep', 'ws')), may hold values from 0 to 31, as said below
- w_gate: bfloat16 [32, 2048, 768], P(('ep', 'ws')), may hold values from -0.125 to 0.125
- w_up: bfloat16 [32, 2048, 768], P(('ep', 'ws')), may hold values from -0.125 to 0.125
- w_down: bfloat16 [32, 768, 2048], P(('ep', 'ws')), may hold values from -1.25 to 1.25
- cotangent: bfloat16 [8192, 2048], P(('ep', 'ws')), may hold values from -36 to 36
Outputs:
- hidden_out: bfloat16 [8192, 2048], P(('ep', 'ws'))
- grad_in: float32 [8192, 2048], P(('ep', 'ws'))
- grad_attn_gain: float32 [2048], P(('ep', 'ws'))
- grad_query: float32 [2048, 4096], P(('ep', 'ws'))
- grad_key: float32 [2048, 512], P(('ep', 'ws'))
- grad_value: float32 [2048, 512], P(('ep', 'ws'))
- grad_query_gain: float32 [128], replicated
- grad_key_gain: float32 [128], replicated
- grad_output: float32 [4096, 2048], P(('ep', 'ws'))
- grad_ffn_gain: float32 [2048], P(('ep', 'ws'))
- grad_router: float32 [2048, 32], P(('ep', 'ws'))
- grad_gate: float32 [32, 2048, 768], P(('ep', 'ws'))
- grad_up: float32 [32, 2048, 768], P(('ep', 'ws'))
- grad_down: float32 [32, 768, 2048], P(('ep', 'ws'))
- root_mean_squares: float32 [4], replicated
The draws below stay inside these ranges and needn't reach their ends.
Inputs may be any that keep to these rules, and one draw needn't show every extreme that they name: `routes`: in each aligned block of 256 rows (the rows of one device) every expert is named by at most 80 rows, and one expert, the same in every block, is named by exactly 80 rows of each block; the 8 experts of a row differ.
All inputs are finite; a program needn't handle non-finite values.
Results may differ from the reference program's by a relative error of at most 0.017.
Values may be sent and summed in bfloat16 or wider, within the bound.
A program may use at most 384 MiB of HBM per device.

```python
from functools import partial
import jax
import jax.numpy as jnp
from jax import lax

MODEL_DIMENSION = 2048
QUERY_HEADS = 32
KEY_VALUE_HEADS = 4
HEAD_DIMENSION = 128
FF = 768
TOP = 8
BLOCK = 256
TOK_DEV = 256
EXPERTS = 32
SEQ = 1024
TOKENS = 8192
CAP = 80
N_EP = 8
N_WS = 4


def rising_field(key):
    column_key, base_key = jax.random.split(key, 2)
    positions = jnp.arange(TOKENS, dtype=jnp.float32)[:, None] / (TOKENS - 1)
    column_scale = jnp.exp(jax.random.uniform(column_key, (1, MODEL_DIMENSION), minval=-1.2, maxval=1.1))
    row_scale = 1.0 + 2.0 * positions
    base = jax.random.truncated_normal(base_key, -4.0, 4.0, (TOKENS, MODEL_DIMENSION))
    return (base * row_scale * column_scale).astype(jnp.float32)


def draw_hidden_in(key, part):
    return rising_field(jax.random.fold_in(key, 3)).astype(jnp.bfloat16)


def draw_cotangent(key, part):
    return rising_field(jax.random.fold_in(key, 5)).astype(jnp.bfloat16)


def shuffle_tokens(subkey):
    return jax.random.permutation(subkey, TOK_DEV)


def draw_routes(key, part):
    block_count = TOKENS // TOK_DEV
    pair_count = TOK_DEV * TOP
    mean_load = pair_count // EXPERTS
    spread = CAP - mean_load
    order_key, spread_key, token_key, roll_key = jax.random.split(jax.random.fold_in(key, 17), 4)
    ordering = jax.random.permutation(order_key, EXPERTS)
    offsets = jax.random.randint(spread_key, (block_count, EXPERTS // 2), 0, spread + 1)
    offsets = offsets.at[:, 0].set(spread)
    loads = jnp.stack([mean_load + offsets, mean_load - offsets], axis=2).reshape(block_count, EXPERTS)
    ends = jnp.cumsum(loads, axis=1)
    tickets = jnp.arange(pair_count)
    owners = jnp.sum((ends[:, None, :] <= tickets[None, :, None]).astype(jnp.int32), axis=2)
    labels = ordering[owners]
    token_order = jax.vmap(shuffle_tokens)(jax.random.split(token_key, block_count))
    rolls = jax.random.randint(roll_key, (block_count, TOK_DEV, 1), 0, TOP)
    slots = jnp.arange(TOP)[None, None, :]
    picks = (slots + rolls) % TOP * TOK_DEV + token_order[:, :, None]
    chosen = jnp.take_along_axis(labels, picks.reshape(block_count, pair_count), axis=1)
    return chosen.reshape(TOKENS, TOP).astype(jnp.int32)


def block_scale(rng, dims, cuts, smallest, high):
    def one(axis_at, shards_of):
        draws = jax.random.uniform(jax.random.fold_in(jax.random.fold_in(rng, 6), axis_at), (shards_of,), jnp.float32, smallest / len(cuts), high / len(cuts))
        return jnp.repeat(jnp.exp(draws), dims[axis_at] // shards_of).reshape((-1,) + (1,) * (len(dims) - axis_at - 1))

    level = one(*cuts[0])
    for cut in cuts[1:]:
        level = level * one(*cut)
    return level


def bell_draw(rng, dims, scale, limit, shards=(), held_as=jnp.bfloat16):
    values = jax.random.normal(rng, dims, jnp.float32) * scale
    if len(shards) > 0:
        values = block_scale(rng, dims, shards, -0.22, 0.18) * values
    return jnp.clip(values, min=-limit, max=limit).astype(held_as)


def setup_inputs(seed: int = 0) -> dict:
    splits = jax.random.split(jax.random.key(seed), 16)
    hidden_in = draw_hidden_in(jax.random.fold_in(splits[15], 71), 0)
    attn_gain = jnp.clip(1.0 + 0.1 * jax.random.normal(splits[1], (MODEL_DIMENSION,), jnp.float32), 0.5, 1.5).astype(jnp.bfloat16)
    w_query = bell_draw(splits[2], (MODEL_DIMENSION, QUERY_HEADS * HEAD_DIMENSION), MODEL_DIMENSION ** -0.5, 0.125, ((0, 4),))
    key_projection = bell_draw(splits[3], (MODEL_DIMENSION, KEY_VALUE_HEADS * HEAD_DIMENSION), MODEL_DIMENSION ** -0.5, 0.125, ((0, 4),))
    value_projection = bell_draw(splits[4], (MODEL_DIMENSION, KEY_VALUE_HEADS * HEAD_DIMENSION), MODEL_DIMENSION ** -0.5, 0.125, ((0, 4),))
    query_gain = jnp.clip(1.0 + 0.1 * jax.random.normal(splits[5], (HEAD_DIMENSION,), jnp.float32), 0.5, 1.5)
    key_gain = jnp.clip(1.0 + 0.1 * jax.random.normal(splits[6], (HEAD_DIMENSION,), jnp.float32), 0.5, 1.5)
    w_output = bell_draw(splits[7], (QUERY_HEADS * HEAD_DIMENSION, MODEL_DIMENSION), (QUERY_HEADS * HEAD_DIMENSION // 16) ** -0.5, 0.375, ((0, 4),))
    ffn_gain = jnp.clip(1.0 + 0.1 * jax.random.normal(splits[8], (MODEL_DIMENSION,), jnp.float32), 0.5, 1.5).astype(jnp.bfloat16)
    w_router = bell_draw(splits[9], (MODEL_DIMENSION, EXPERTS), (MODEL_DIMENSION * 4) ** -0.5, 0.0625, ((0, 4),))
    routes = draw_routes(jax.random.fold_in(splits[15], 71), 0)
    w_gate = bell_draw(splits[11], (EXPERTS, MODEL_DIMENSION, FF), MODEL_DIMENSION ** -0.5, 0.125, ((0, 32),))
    w_up = bell_draw(splits[12], (EXPERTS, MODEL_DIMENSION, FF), MODEL_DIMENSION ** -0.5, 0.125, ((0, 32),))
    w_down = bell_draw(splits[13], (EXPERTS, FF, MODEL_DIMENSION), (FF // 32) ** -0.5, 1.25, ((0, 32),))
    cotangent = draw_cotangent(jax.random.fold_in(splits[15], 71), 0)
    return dict(hidden_in=hidden_in, attn_gain=attn_gain, w_query=w_query, key_projection=key_projection, value_projection=value_projection, query_gain=query_gain, key_gain=key_gain, w_output=w_output, ffn_gain=ffn_gain, w_router=w_router, routes=routes, w_gate=w_gate, w_up=w_up, w_down=w_down, cotangent=cotangent)


@jax.custom_vjp
def reduced_precision(v):
    return lax.optimization_barrier(v.astype(jnp.bfloat16)).astype(jnp.float32)

@jax.custom_vjp
def reduced_backward(v):
    return v

def low_keep(v):
    return (reduced_precision(v), None)

def low_pass(kept, grad):
    return (grad,)

def back_keep(v):
    return (v, None)

def back_low(kept, grad):
    return (reduced_precision(grad),)
reduced_precision.defvjp(low_keep, low_pass)
reduced_backward.defvjp(back_keep, back_low)
epsilon = 1e-06
rope_base = 1000000.0
masked_value = -1e+30
precise = lax.Precision.HIGHEST

def matrix_product(left, right):
    return jnp.dot(left, right, precision=precise, preferred_element_type=jnp.float32)

def normalize(layer_inputs, gain):
    scaling = lax.rsqrt(lax.optimization_barrier(jnp.mean(layer_inputs * layer_inputs, axis=-1, keepdims=True)) + epsilon)
    return layer_inputs * scaling * gain

def rotate(layer_inputs, cosine_table, sine_table):
    halfway = layer_inputs.shape[-1] // 2
    turned = jnp.concatenate([-layer_inputs[..., halfway:], layer_inputs[..., :halfway]], axis=-1)
    return layer_inputs * cosine_table + turned * sine_table

def rope_tables(count):
    positions = jnp.arange(count, dtype=jnp.float32)
    indices = jnp.arange(HEAD_DIMENSION // 2, dtype=jnp.float32)
    frequency = rope_base ** (-2.0 * indices / HEAD_DIMENSION)
    angles = positions[:, None] * frequency[None, :]
    angles = jnp.concatenate([angles, angles], axis=-1)
    return (jnp.cos(angles)[:, None, :], jnp.sin(angles)[:, None, :])

def attend_sequence(weights, tables, layer_inputs):
    w_query, key_projection, value_projection, query_gain, key_gain, w_output = weights
    cosine_table, sine_table, allowed = tables
    sequence_length = layer_inputs.shape[0]
    query_rows_all = reduced_backward(matrix_product(layer_inputs, w_query)).reshape(sequence_length, QUERY_HEADS, HEAD_DIMENSION)
    every_key_row = reduced_backward(matrix_product(layer_inputs, key_projection)).reshape(sequence_length, KEY_VALUE_HEADS, HEAD_DIMENSION)
    every_value_row = reduced_precision(reduced_backward(matrix_product(layer_inputs, value_projection))).reshape(sequence_length, KEY_VALUE_HEADS, HEAD_DIMENSION)
    query_rows_all = reduced_precision(rotate(normalize(query_rows_all, query_gain), cosine_table, sine_table))
    every_key_row = reduced_precision(rotate(normalize(every_key_row, key_gain), cosine_table, sine_table))
    grouped_heads = query_rows_all.reshape(sequence_length, KEY_VALUE_HEADS, QUERY_HEADS // KEY_VALUE_HEADS, HEAD_DIMENSION)
    scores = reduced_backward(jnp.einsum('qhgd,khd->hgqk', grouped_heads, every_key_row, precision=precise) * HEAD_DIMENSION ** (-0.5))
    scores = jnp.where(allowed, scores, masked_value)
    row_peaks = lax.optimization_barrier(jnp.max(scores, axis=-1, keepdims=True))
    exponent = jnp.exp(scores - row_peaks)
    probabilities = exponent / lax.optimization_barrier(jnp.sum(exponent, axis=-1, keepdims=True))
    attended = jnp.einsum('hgqk,khd->qhgd', reduced_precision(probabilities), every_value_row, precision=precise).reshape(sequence_length, QUERY_HEADS * HEAD_DIMENSION)
    return reduced_backward(matrix_product(reduced_precision(reduced_backward(attended)), w_output))

def forward(routes, hidden, attn_gain, w_query, key_projection, value_projection, query_gain, key_gain, w_output, ffn_gain, w_router, w_gate, w_up, w_down):
    cosine_table, sine_table = rope_tables(SEQ)
    blocks = jnp.arange(SEQ) // BLOCK
    allowed = blocks[None, :] <= blocks[:, None]
    first_norm = reduced_precision(normalize(hidden, attn_gain))
    weights = (w_query, key_projection, value_projection, query_gain, key_gain, w_output)
    attend = jax.checkpoint(partial(attend_sequence, weights, (cosine_table, sine_table, allowed)))
    branch = lax.map(attend, first_norm.reshape(TOKENS // SEQ, SEQ, MODEL_DIMENSION)).reshape(TOKENS, MODEL_DIMENSION)
    middle = hidden + branch
    second_norm = reduced_precision(normalize(middle, ffn_gain))
    logits = reduced_backward(matrix_product(second_norm, w_router))
    picked = jnp.take_along_axis(logits, routes, axis=1)
    shifted = jnp.exp(picked - lax.optimization_barrier(jnp.max(picked, axis=1, keepdims=True)))
    shares = shifted / lax.optimization_barrier(jnp.sum(shifted, axis=1, keepdims=True))
    pair_count = TOKENS * TOP
    pair_expert = routes.reshape(pair_count)
    ordering = jnp.argsort(pair_expert, stable=True).astype(jnp.int32)
    counts = jnp.zeros((EXPERTS,), jnp.int32).at[pair_expert].add(1)
    starts = jnp.cumsum(counts) - counts
    sorted_expert = pair_expert[ordering]
    pair_ranks = jnp.arange(pair_count, dtype=jnp.int32) - starts[sorted_expert]
    capacity = N_EP * N_WS * CAP
    pair_table = jnp.full((EXPERTS, capacity), pair_count, jnp.int32).at[sorted_expert, pair_ranks].set(ordering)
    token_table = jnp.where(pair_table < pair_count, pair_table // TOP, TOKENS).astype(jnp.int32)
    padded_rows = jnp.concatenate([second_norm, jnp.zeros((1, MODEL_DIMENSION), jnp.float32)], axis=0)
    padded_shares = jnp.concatenate([shares.reshape(pair_count), jnp.zeros((1,), jnp.float32)])

    def expert_step(summed, operands):
        token_rows, pair_rows, gate_weight, up_weight, down_weight = operands
        layer_inputs = reduced_backward(padded_rows[token_rows])
        gate_values = reduced_backward(matrix_product(layer_inputs, gate_weight))
        up_values = reduced_backward(matrix_product(layer_inputs, up_weight))
        hidden_units = reduced_precision(gate_values / (1.0 + jnp.exp(-gate_values)) * up_values)
        outputs = reduced_precision(reduced_backward(matrix_product(hidden_units, down_weight)))
        return (summed.at[token_rows].add(padded_shares[pair_rows][:, None] * outputs), None)
    start_sum = jnp.zeros((TOKENS + 1, MODEL_DIMENSION), jnp.float32)
    summed, unused = lax.scan(jax.checkpoint(expert_step), start_sum, (token_table, pair_table, w_gate, w_up, w_down))
    expert_sum = summed[:TOKENS]
    return (middle + expert_sum, (branch, expert_sum))

def reference(hidden_in, attn_gain, w_query, key_projection, value_projection, query_gain, key_gain, w_output, ffn_gain, w_router, routes, w_gate, w_up, w_down, cotangent):
    primals = tuple((argument.astype(jnp.float32) for argument in (hidden_in, attn_gain, w_query, key_projection, value_projection, query_gain, key_gain, w_output, ffn_gain, w_router, w_gate, w_up, w_down)))
    result, pullback, extras = jax.vjp(partial(forward, routes), *primals, has_aux=True)
    grads = pullback(cotangent.astype(jnp.float32))
    branch, expert_sum = extras
    grad_in = grads[0]
    source = primals[0]
    squares = jnp.stack([jnp.mean(source * source), jnp.mean(branch * branch), jnp.mean(expert_sum * expert_sum), jnp.mean(grad_in * grad_in)])
    root_mean_squares = jnp.sqrt(squares)
    return (result.astype(jnp.bfloat16), grad_in, grads[1], grads[2], grads[3], grads[4], grads[5], grads[6], grads[7], grads[8], grads[9], grads[10], grads[11], grads[12], root_mean_squares)
```

```python
import functools

import jax
import jax.numpy as jnp
from jax import lax
from jax.experimental import pallas as pl
from jax.experimental.pallas import tpu as pltpu
from jax.sharding import Mesh
from jax.sharding import PartitionSpec as P

BLOCK = 256
EPS = 1e-06
ROPE_BASE = 1000000.0
F32 = jnp.float32
BF16 = jnp.bfloat16
VMEM_LIMIT = 60 * 1024 * 1024


def dot(left, right):
    return jnp.dot(left, right, preferred_element_type=F32)


def dot_tn(left, right):
    return lax.dot_general(left, right, (((0,), (0,)), ((), ())), preferred_element_type=F32)


def dot_nt(left, right):
    return lax.dot_general(left, right, (((1,), (1,)), ((), ())), preferred_element_type=F32)


def rope_tables(seq_length, head_size):
    indices = jnp.arange(head_size // 2, dtype=F32)
    frequency = ROPE_BASE ** (-2.0 * indices / head_size)
    angles = jnp.arange(seq_length, dtype=F32)[:, None] * frequency[None, :]
    cosine, sine = jnp.cos(angles), jnp.sin(angles)
    return jnp.concatenate([cosine, cosine], axis=1), jnp.concatenate([-sine, sine], axis=1)


def norm_forward(values):
    scaling = lax.rsqrt(jnp.mean(values * values, axis=-1, keepdims=True) + EPS)
    return values * scaling, scaling


def norm_backward(grad_normed, normed, scaling):
    return scaling * (grad_normed - normed * jnp.mean(grad_normed * normed, axis=-1, keepdims=True))


def half_turn(values):
    return pltpu.roll(values, values.shape[-1] // 2, 1)


def rotate(values, cosine, signed_sine):
    return values * cosine + half_turn(values) * signed_sine


def unrotate(grads, cosine, signed_sine):
    return grads * cosine - half_turn(grads) * signed_sine


def attention_forward(
    heads_a_step, hidden_ref, gain_ref, wq_ref, wkv_ref, query_gain_ref, key_gain_ref, cosine_ref, sine_ref, wo_ref,
    input_ref, query_raw_ref, key_raw_ref, value_ref, attended_ref, branch_ref, total_ref, key_rot_ref,
):
    step = pl.program_id(0)
    head_size = cosine_ref.shape[1]
    seq_length = cosine_ref.shape[0]
    blocks = seq_length // BLOCK
    factor = head_size ** (-0.5)

    @pl.when(step == 0)
    def _():
        for block in range(blocks):
            rows = pl.ds(block * BLOCK, BLOCK)
            normed, _ = norm_forward(hidden_ref[rows, :].astype(F32))
            first_input = (normed * gain_ref[...]).astype(BF16)
            input_ref[rows, :] = first_input
            key_value = dot(first_input, wkv_ref[...])
            key_raw = key_value[:, :head_size]
            key_raw_ref[rows, :] = key_raw
            value_ref[rows, :] = key_value[:, head_size:].astype(BF16)
            key_normed, _ = norm_forward(key_raw)
            key_rot_ref[rows, :] = rotate(
                key_normed * key_gain_ref[...], cosine_ref[rows, :], sine_ref[rows, :]
            ).astype(BF16)

    for block in range(blocks):
        rows = pl.ds(block * BLOCK, BLOCK)
        seen = pl.ds(0, (block + 1) * BLOCK)
        query_raw = dot(input_ref[rows, :], wq_ref[...])
        query_raw_ref[rows, :] = query_raw
        for head in range(heads_a_step):
            columns = slice(head * head_size, (head + 1) * head_size)
            query_normed, _ = norm_forward(query_raw[:, columns])
            query_rot = rotate(
                query_normed * query_gain_ref[...], cosine_ref[rows, :], sine_ref[rows, :]
            ).astype(BF16)
            scores = dot_nt(query_rot, key_rot_ref[seen, :]) * factor
            exponent = jnp.exp(scores - jnp.max(scores, axis=-1, keepdims=True))
            probs = (exponent / jnp.sum(exponent, axis=-1, keepdims=True)).astype(BF16)
            attended_ref[rows, columns] = dot(probs, value_ref[seen, :]).astype(BF16)
        partial = dot(attended_ref[rows, :], wo_ref[...])

        @pl.when(step == 0)
        def _():
            total_ref[rows, :] = partial

        @pl.when(step > 0)
        def _():
            total_ref[rows, :] += partial

    @pl.when(step == pl.num_programs(0) - 1)
    def _():
        branch_ref[...] = total_ref[...].astype(BF16)


def attention_backward(
    heads_a_step, grad_ref, wo_ref, attended_ref, query_raw_ref, key_raw_ref, value_ref, input_ref, wq_ref, wkv_ref,
    query_gain_ref, key_gain_ref, cosine_ref, sine_ref,
    wo_grad_ref, wq_grad_ref, wkv_grad_ref, first_grad_ref, query_gain_grad_ref, key_gain_grad_ref,
    total_ref, key_rot_ref, key_grad_ref, value_grad_ref, query_grad_ref, turned_ref,
):
    step = pl.program_id(0)
    head_size = cosine_ref.shape[1]
    seq_length = cosine_ref.shape[0]
    blocks = seq_length // BLOCK
    factor = head_size ** (-0.5)

    @pl.when(step == 0)
    def _():
        key_normed, _ = norm_forward(key_raw_ref[...])
        key_rot_ref[...] = rotate(key_normed * key_gain_ref[...], cosine_ref[...], sine_ref[...]).astype(BF16)
        key_grad_ref[...] = jnp.zeros_like(key_grad_ref)
        value_grad_ref[...] = jnp.zeros_like(value_grad_ref)
        query_gain_grad_ref[...] = jnp.zeros_like(query_gain_grad_ref)
        for block in range(blocks):
            rows = pl.ds(block * BLOCK, BLOCK)
            turned_ref[:, rows] = input_ref[rows, :].T

    wo_grad_ref[...] = dot_tn(attended_ref[...], grad_ref[...]).astype(BF16)
    for block in range(blocks):
        rows = pl.ds(block * BLOCK, BLOCK)
        seen = pl.ds(0, (block + 1) * BLOCK)
        attended_grad = dot_nt(grad_ref[rows, :], wo_ref[...]).astype(BF16)
        for head in range(heads_a_step):
            columns = slice(head * head_size, (head + 1) * head_size)
            query_normed, query_scale = norm_forward(query_raw_ref[rows, columns])
            cosine, sine = cosine_ref[rows, :], sine_ref[rows, :]
            query_rot = rotate(query_normed * query_gain_ref[...], cosine, sine).astype(BF16)
            head_grad = attended_grad[:, columns]
            keys, values = key_rot_ref[seen, :], value_ref[seen, :]
            scores = dot_nt(query_rot, keys) * factor
            exponent = jnp.exp(scores - jnp.max(scores, axis=-1, keepdims=True))
            probs = exponent / jnp.sum(exponent, axis=-1, keepdims=True)
            prob_grad = dot_nt(head_grad, values)
            value_grad_ref[seen, :] += dot_tn(probs.astype(BF16), head_grad)
            center = jnp.sum(probs * prob_grad, axis=-1, keepdims=True)
            score_grad = (probs * (prob_grad - center)).astype(BF16)
            key_grad_ref[seen, :] += dot_tn(score_grad, query_rot) * factor
            query_rot_grad = dot(score_grad, keys) * factor
            unrotated = unrotate(query_rot_grad, cosine, sine)
            query_gain_grad_ref[0:1, :] += jnp.sum(unrotated * query_normed, axis=0, keepdims=True)
            query_grad_ref[rows, columns] = norm_backward(
                unrotated * query_gain_ref[...], query_normed, query_scale
            ).astype(BF16)
        partial = dot_nt(query_grad_ref[rows, :], wq_ref[...])

        @pl.when(step == 0)
        def _():
            total_ref[rows, :] = partial

        @pl.when(step > 0)
        def _():
            total_ref[rows, :] += partial

    wq_grad_ref[...] = dot(turned_ref[...], query_grad_ref[...]).astype(BF16)

    @pl.when(step == pl.num_programs(0) - 1)
    def _():
        key_normed, key_scale = norm_forward(key_raw_ref[...])
        unrotated = unrotate(key_grad_ref[...], cosine_ref[...], sine_ref[...])
        key_gain_grad_ref[...] = jnp.zeros_like(key_gain_grad_ref)
        key_gain_grad_ref[0:1, :] = jnp.sum(unrotated * key_normed, axis=0, keepdims=True)
        key_grad = norm_backward(unrotated * key_gain_ref[...], key_normed, key_scale)
        query_grad_ref[:, :head_size] = key_grad.astype(BF16)
        query_grad_ref[:, head_size : 2 * head_size] = value_grad_ref[...].astype(BF16)
        both = query_grad_ref[:, : 2 * head_size]
        wkv_grad_ref[...] = dot(turned_ref[...], both).astype(BF16)
        for block in range(blocks):
            rows = pl.ds(block * BLOCK, BLOCK)
            first_grad_ref[rows, :] = (
                total_ref[rows, :] + dot_nt(query_grad_ref[rows, : 2 * head_size], wkv_ref[...])
            ).astype(BF16)


def whole(shape):
    return pl.BlockSpec(shape, lambda step: (0,) * len(shape), pipeline_mode=pl.Buffered(1))


def run_forward(hidden_all, gain, weights, wo, query_gain, key_gain, cosine, sine):
    seq_length, width = hidden_all.shape
    head_size = query_gain.shape[1]
    heads_here = wo.shape[0] // head_size
    pair = 2
    wide = pair * head_size
    steps = heads_here // pair
    return pl.pallas_call(
        functools.partial(attention_forward, pair),
        grid=(steps,),
        in_specs=[
            whole((seq_length, width)),
            whole((1, width)),
            pl.BlockSpec((width, wide), lambda step: (0, step)),
            pl.BlockSpec((width, wide), lambda step: (0, steps), pipeline_mode=pl.Buffered(1)),
            whole((1, head_size)),
            whole((1, head_size)),
            whole((seq_length, head_size)),
            whole((seq_length, head_size)),
            pl.BlockSpec((wide, width), lambda step: (step, 0)),
        ],
        out_specs=[
            whole((seq_length, width)),
            pl.BlockSpec((seq_length, wide), lambda step: (0, step)),
            whole((seq_length, head_size)),
            whole((seq_length, head_size)),
            pl.BlockSpec((seq_length, wide), lambda step: (0, step)),
            whole((seq_length, width)),
        ],
        out_shape=[
            jax.ShapeDtypeStruct((seq_length, width), BF16),
            jax.ShapeDtypeStruct((seq_length, heads_here * head_size), F32),
            jax.ShapeDtypeStruct((seq_length, head_size), F32),
            jax.ShapeDtypeStruct((seq_length, head_size), BF16),
            jax.ShapeDtypeStruct((seq_length, heads_here * head_size), BF16),
            jax.ShapeDtypeStruct((seq_length, width), BF16),
        ],
        scratch_shapes=[
            pltpu.VMEM((seq_length, width), F32),
            pltpu.VMEM((seq_length, head_size), BF16),
        ],
        compiler_params=pltpu.CompilerParams(vmem_limit_bytes=VMEM_LIMIT),
        cost_estimate=pl.CostEstimate(flops=16 * 10**9, bytes_accessed=40 * 10**6, transcendentals=6 * 10**6),
    )(hidden_all, gain, weights, weights, query_gain, key_gain, cosine, sine, wo)


def run_backward(grad_all, wo, attended, query_raw, key_raw, value, first_input, weights, query_gain, key_gain, cosine, sine):
    seq_length, width = grad_all.shape
    head_size = query_gain.shape[1]
    heads_here = wo.shape[0] // head_size
    pair = 2
    wide = pair * head_size
    steps = heads_here // pair
    return pl.pallas_call(
        functools.partial(attention_backward, pair),
        grid=(steps,),
        in_specs=[
            whole((seq_length, width)),
            pl.BlockSpec((wide, width), lambda step: (step, 0)),
            pl.BlockSpec((seq_length, wide), lambda step: (0, step)),
            pl.BlockSpec((seq_length, wide), lambda step: (0, step)),
            whole((seq_length, head_size)),
            whole((seq_length, head_size)),
            whole((seq_length, width)),
            pl.BlockSpec((width, wide), lambda step: (0, step)),
            pl.BlockSpec((width, wide), lambda step: (0, steps), pipeline_mode=pl.Buffered(1)),
            whole((1, head_size)),
            whole((1, head_size)),
            whole((seq_length, head_size)),
            whole((seq_length, head_size)),
        ],
        out_specs=[
            pl.BlockSpec((wide, width), lambda step: (step, 0)),
            pl.BlockSpec((width, wide), lambda step: (0, step)),
            whole((width, wide)),
            whole((seq_length, width)),
            whole((8, head_size)),
            whole((8, head_size)),
        ],
        out_shape=[
            jax.ShapeDtypeStruct((heads_here * head_size, width), BF16),
            jax.ShapeDtypeStruct((width, heads_here * head_size), BF16),
            jax.ShapeDtypeStruct((width, wide), BF16),
            jax.ShapeDtypeStruct((seq_length, width), BF16),
            jax.ShapeDtypeStruct((8, head_size), F32),
            jax.ShapeDtypeStruct((8, head_size), F32),
        ],
        scratch_shapes=[
            pltpu.VMEM((seq_length, width), F32),
            pltpu.VMEM((seq_length, head_size), BF16),
            pltpu.VMEM((seq_length, head_size), F32),
            pltpu.VMEM((seq_length, head_size), F32),
            pltpu.VMEM((seq_length, wide), BF16),
            pltpu.VMEM((width, seq_length), BF16),
        ],
        compiler_params=pltpu.CompilerParams(vmem_limit_bytes=VMEM_LIMIT),
        cost_estimate=pl.CostEstimate(flops=35 * 10**9, bytes_accessed=60 * 10**6, transcendentals=6 * 10**6),
    )(grad_all, wo, attended, query_raw, key_raw, value, first_input, weights, weights, query_gain, key_gain, cosine, sine)


def local(
    hidden_in, attn_gain, w_query, key_projection, value_projection, query_gain, key_gain, w_output, ffn_gain, w_router,
    routes, w_gate, w_up, w_down, cotangent,
):
    tokens_here, width = hidden_in.shape
    head_size = query_gain.shape[0]
    top_count = routes.shape[1]
    planes, across, shards = lax.axis_size("z"), lax.axis_size("x"), lax.axis_size("w")
    rings = planes * across
    device_count = rings * shards
    in_plane = across * shards
    experts = device_count
    capacity = 5 * tokens_here * top_count // (4 * experts)
    seq_length = tokens_here * shards
    plane, column, shard = lax.axis_index("z"), lax.axis_index("x"), lax.axis_index("w")

    small = jnp.concatenate([w_router, attn_gain[:, None], ffn_gain[:, None]], axis=1)
    depth = w_query.shape[0]
    merged = jnp.concatenate(
        [
            w_query.reshape(depth, shards, -1),
            key_projection.reshape(depth, shards, -1),
            value_projection.reshape(depth, shards, -1),
        ],
        axis=2,
    ).reshape(depth, -1)
    hidden_all = lax.all_gather(hidden_in, "w", axis=0, tiled=True)
    small_all = lax.all_gather(small, "w", axis=0, tiled=True)
    weights = lax.all_to_all(merged, "w", split_axis=1, concat_axis=0, tiled=True)
    router_full = small_all[:, :experts]
    attn_scale = small_all[:, experts].astype(F32)[None, :]
    ffn_scale = small_all[:, experts + 1].astype(F32)[None, :]
    cosine, sine = rope_tables(seq_length, head_size)
    query_gain_row, key_gain_row = query_gain[None, :], key_gain[None, :]

    routes_z = lax.all_gather(routes, "z", axis=0, tiled=False)
    plane_experts = plane * in_plane + jnp.arange(in_plane, dtype=jnp.int32)
    hits = jnp.any(routes_z[:, :, :, None] == plane_experts[None, None, None, :], axis=2)
    lower = (
        jnp.arange(tokens_here)[:, None] > jnp.arange(tokens_here)[None, :]
    ).astype(BF16)
    ranks = jnp.einsum("st,zte->zse", lower, hits.astype(BF16), preferred_element_type=F32).astype(jnp.int32)
    ranks = jnp.where(hits, ranks, -1)
    chosen = (
        ranks.transpose(0, 2, 1)[:, :, None, :] == jnp.arange(capacity, dtype=jnp.int32)[None, None, :, None]
    )
    chosen_flat = chosen.reshape(planes, in_plane * capacity, tokens_here).astype(BF16)

    def send_out(rows_z):
        packed = jnp.einsum("zst,ztd->zsd", chosen_flat, rows_z, preferred_element_type=F32).astype(BF16)
        packed = packed.reshape(planes, in_plane, capacity, width).transpose(1, 0, 2, 3)
        got = lax.all_to_all(
            packed.reshape(in_plane, planes * capacity, width), ("x", "w"), split_axis=0, concat_axis=0, tiled=True
        )
        return got.reshape(in_plane * planes * capacity, width)

    def send_back(rows):
        got = lax.all_to_all(
            rows.reshape(in_plane, planes * capacity, width), ("x", "w"), split_axis=0, concat_axis=0, tiled=True
        )
        got = got.reshape(in_plane, planes, capacity, width).transpose(1, 0, 2, 3)
        got = got.reshape(planes, in_plane * capacity, width)
        summed = jnp.einsum("zst,zsd->ztd", chosen_flat, got, preferred_element_type=F32).astype(BF16)
        return lax.psum_scatter(summed.reshape(planes * tokens_here, width), "z", scatter_dimension=0, tiled=True)

    cotangent_z = lax.all_gather(cotangent, "z", axis=0, tiled=False)
    grads_in = send_out(cotangent_z)

    first_input, query_raw, key_raw, value, attended, branch_part = run_forward(
        hidden_all, attn_scale, weights, w_output, query_gain_row, key_gain_row, cosine, sine
    )
    branch = lax.psum_scatter(branch_part, "w", scatter_dimension=0, tiled=True).astype(F32)
    source = hidden_in.astype(F32)
    first_normed, first_scale = norm_forward(source)
    middle = source + branch
    second_normed, second_scale = norm_forward(middle)
    second_input = (second_normed * ffn_scale).astype(BF16)
    rows_z = lax.all_gather(second_input, "z", axis=0, tiled=False)
    rows_in = send_out(rows_z)

    logits = dot(second_input, router_full)
    expert_ids = jnp.arange(experts, dtype=jnp.int32)
    routed = jnp.any(routes[:, :, None] == expert_ids[None, None, :], axis=1)
    peaks = jnp.max(jnp.where(routed, logits, -jnp.inf), axis=1, keepdims=True)
    shifted = jnp.where(routed, jnp.exp(jnp.where(routed, logits - peaks, 0.0)), 0.0)
    shares = shifted / jnp.sum(shifted, axis=1, keepdims=True)
    shares_z = lax.all_to_all(
        shares.reshape(tokens_here, planes, in_plane).transpose(1, 2, 0), "z", split_axis=0, concat_axis=0, tiled=True
    )
    slot_shares = jnp.sum(jnp.where(chosen, shares_z[:, :, None, :], 0.0), axis=3)
    slot_shares = slot_shares.transpose(1, 0, 2).reshape(in_plane, planes * capacity)
    shares_in = lax.all_to_all(slot_shares, ("x", "w"), split_axis=0, concat_axis=0, tiled=True).reshape(-1, 1)

    gate = dot(rows_in, w_gate[0])
    up = dot(rows_in, w_up[0])
    sigmoid = 1.0 / (1.0 + jnp.exp(-gate))
    hidden_units = (gate * sigmoid * up).astype(BF16)
    pair_out = dot(hidden_units, w_down[0]).astype(BF16)
    top_rows = grads_in.astype(F32)
    pair_values = pair_out.astype(F32)
    share_grad_slots = jnp.sum(pair_values * top_rows, axis=1)
    weighted = (shares_in * pair_values).astype(BF16)
    pair_grad = (shares_in * top_rows).astype(BF16)
    hidden_grad = dot_nt(pair_grad, w_down[0])
    gate_grad = (hidden_grad * up * sigmoid * (1.0 + gate * (1.0 - sigmoid))).astype(BF16)
    up_grad = (hidden_grad * (gate * sigmoid)).astype(BF16)
    row_grad = (dot_nt(gate_grad, w_gate[0]) + dot_nt(up_grad, w_up[0])).astype(BF16)
    grad_down = dot_tn(hidden_units, pair_grad)[None]
    grad_gate = dot_tn(rows_in, gate_grad)[None]
    grad_up = dot_tn(rows_in, up_grad)[None]

    back_shares = lax.all_to_all(
        share_grad_slots.reshape(in_plane, planes * capacity), ("x", "w"), split_axis=0, concat_axis=0, tiled=True
    ).reshape(in_plane, planes, capacity).transpose(1, 0, 2)
    share_grad_z = jnp.sum(jnp.where(chosen, back_shares[:, :, :, None], 0.0), axis=2)
    share_grad = lax.all_to_all(share_grad_z, "z", split_axis=0, concat_axis=0, tiled=True)
    share_grad = share_grad.reshape(experts, tokens_here).T
    row_grad_sum = send_back(row_grad).astype(F32)
    expert_sum = send_back(weighted).astype(F32)
    hidden_out = (middle + expert_sum).astype(BF16)

    grad_top = cotangent.astype(F32)
    share_center = jnp.sum(shares * share_grad, axis=1, keepdims=True)
    logit_grad = (shares * (share_grad - share_center)).astype(BF16)
    router_grad = dot_tn(second_input, logit_grad)
    second_grad = row_grad_sum + dot_nt(logit_grad, router_full)
    ffn_gain_grad = jnp.sum(second_grad * second_normed, axis=0)
    middle_grad = grad_top + norm_backward(second_grad * ffn_scale, second_normed, second_scale)
    grad_all = lax.all_gather(middle_grad.astype(BF16), "w", axis=0, tiled=True)

    wo_grad, wq_grad, wkv_grad, first_part, query_gain_grad, key_gain_grad = run_backward(
        grad_all, w_output, attended, query_raw, key_raw, value, first_input, weights, query_gain_row, key_gain_row, cosine, sine
    )
    first_grad = lax.psum_scatter(first_part, "w", scatter_dimension=0, tiled=True).astype(F32)
    attn_gain_grad = jnp.sum(first_grad * first_normed, axis=0)
    grad_in = middle_grad + norm_backward(first_grad * attn_scale, first_normed, first_scale)

    wo_mine = lax.psum_scatter(wo_grad, ("z", "x"), scatter_dimension=0, tiled=True)
    moves = [(ring * shards + part, part * rings + ring) for ring in range(rings) for part in range(shards)]
    sum_output = lax.ppermute(wo_mine, ("z", "x", "w"), moves).astype(F32)
    wq_mine = lax.psum_scatter(
        jnp.concatenate([wq_grad, wkv_grad], axis=1), ("z", "x"), scatter_dimension=0, tiled=True
    )
    mine = wq_mine.shape[0] // shards
    collected = lax.all_to_all(wq_mine, "w", split_axis=0, concat_axis=0, tiled=True).reshape(shards, mine, -1)
    collected = collected.transpose(1, 0, 2).astype(F32)
    query_columns = w_query.shape[1] // shards
    key_columns = key_projection.shape[1] // shards
    sum_query = collected[:, :, :query_columns].reshape(mine, -1)
    sum_key = collected[:, :, query_columns : query_columns + key_columns].reshape(mine, -1)
    sum_value = collected[:, :, query_columns + key_columns :].reshape(mine, -1)
    small_grads = jnp.concatenate([router_grad, ffn_gain_grad[:, None], attn_gain_grad[:, None]], axis=1)
    small_mine = lax.psum_scatter(small_grads, ("z", "x", "w"), scatter_dimension=0, tiled=True)
    squares = jnp.stack(
        [jnp.sum(source * source), jnp.sum(branch * branch), jnp.sum(expert_sum * expert_sum), jnp.sum(grad_in * grad_in)]
    )
    totals = lax.psum(
        jnp.concatenate([query_gain_grad[0], key_gain_grad[0], squares]), ("z", "x", "w")
    )
    root_mean_squares = jnp.sqrt(totals[2 * head_size :] / (tokens_here * device_count * width))
    return (
        hidden_out,
        grad_in,
        small_mine[:, experts + 1],
        sum_query,
        sum_key,
        sum_value,
        totals[:head_size],
        totals[head_size : 2 * head_size],
        sum_output,
        small_mine[:, experts],
        small_mine[:, :experts],
        grad_gate,
        grad_up,
        grad_down,
        root_mean_squares,
    )


def solution(mesh):
    rings, shards = mesh.shape["ep"], mesh.shape["ws"]
    planes = 4 if rings % 4 == 0 else 1
    fine = Mesh(mesh.devices.reshape(planes, rings // planes, shards), ("z", "x", "w"))
    every = ("z", "x", "w")
    rows, deep = P(every, None), P(every, None, None)
    return jax.shard_map(
        local,
        mesh=fine,
        in_specs=(
            rows, P("w"), P("w", None), P("w", None), P("w", None), P(), P(), P("w", None), P("w"), P("w", None),
            rows, deep, deep, deep, rows,
        ),
        out_specs=(
            rows, rows, P(every), rows, rows, rows, P(), P(), rows, P(every), rows, deep, deep, deep, P(),
        ),
        check_vma=False,
    )
```

```python
import functools

import jax
import jax.numpy as jnp
from jax import lax
from jax.experimental import pallas as pl
from jax.experimental.pallas import tpu as pltpu
from jax.sharding import Mesh
from jax.sharding import PartitionSpec as P

BLOCK = 256
EPS = 1e-06
ROPE_BASE = 1000000.0
F32 = jnp.float32
BF16 = jnp.bfloat16
VMEM_LIMIT = 60 * 1024 * 1024


def dot(left, right):
    return jnp.dot(left, right, preferred_element_type=F32)


def dot_tn(left, right):
    return lax.dot_general(left, right, (((0,), (0,)), ((), ())), preferred_element_type=F32)


def dot_nt(left, right):
    return lax.dot_general(left, right, (((1,), (1,)), ((), ())), preferred_element_type=F32)


def rope_tables(seq_length, head_size):
    indices = jnp.arange(head_size // 2, dtype=F32)
    frequency = ROPE_BASE ** (-2.0 * indices / head_size)
    angles = jnp.arange(seq_length, dtype=F32)[:, None] * frequency[None, :]
    cosine, sine = jnp.cos(angles), jnp.sin(angles)
    return jnp.concatenate([cosine, cosine], axis=1), jnp.concatenate([-sine, sine], axis=1)


def norm_forward(values):
    scaling = lax.rsqrt(jnp.mean(values * values, axis=-1, keepdims=True) + EPS)
    return values * scaling, scaling


def norm_backward(grad_normed, normed, scaling):
    return scaling * (grad_normed - normed * jnp.mean(grad_normed * normed, axis=-1, keepdims=True))


def half_turn(values):
    return pltpu.roll(values, values.shape[-1] // 2, 1)


def rotate(values, cosine, signed_sine):
    return values * cosine + half_turn(values) * signed_sine


def unrotate(grads, cosine, signed_sine):
    return grads * cosine - half_turn(grads) * signed_sine


MESH = pl.DeviceIdType.MESH


def remote(source, target, send, recv, device):
    return pltpu.make_async_remote_copy(
        src_ref=source, dst_ref=target, send_sem=send, recv_sem=recv, device_id=device, device_id_type=MESH
    )


def wait_bytes(ref, sem):
    pltpu.make_async_copy(ref, ref, sem).wait()


def line_order(z, planes, step):
    low = jnp.minimum(z, planes - 1 - z)
    paired = (step <= 2 * low).astype(jnp.int32)
    hop = paired * ((step + 1) // 2) + (1 - paired) * (step - low)
    longer = (z > planes - 1 - z).astype(jnp.int32)
    below = paired * (step % 2) + (1 - paired) * longer
    return z + hop - 2 * below * hop, hop, below


def greet_plane_and_line(planes, across, shards):
    z, x, w = lax.axis_index("z"), lax.axis_index("x"), lax.axis_index("w")
    in_plane = across * shards
    me = x * shards + w
    barrier = pltpu.get_barrier_semaphore()

    @pl.loop(1, in_plane)
    def _(offset):
        index = (me + offset) % in_plane
        pl.semaphore_signal(barrier, inc=1, device_id=(z, index // shards, index % shards), device_id_type=MESH)

    @pl.loop(1, planes)
    def _(offset):
        pl.semaphore_signal(barrier, inc=1, device_id=((z + offset) % planes, x, w), device_id_type=MESH)

    pl.semaphore_wait(barrier, in_plane + planes - 2)


def attention_forward(
    heads_a_step, hidden_ref, gain_ref, wq_ref, wkv_ref, query_gain_ref, key_gain_ref, cosine_ref, sine_ref, wo_ref,
    input_ref, query_raw_ref, key_raw_ref, value_ref, attended_ref, branch_ref, total_ref, key_rot_ref,
):
    step = pl.program_id(0)
    head_size = cosine_ref.shape[1]
    seq_length = cosine_ref.shape[0]
    blocks = seq_length // BLOCK
    factor = head_size ** (-0.5)

    @pl.when(step == 0)
    def _():
        for block in range(blocks):
            rows = pl.ds(block * BLOCK, BLOCK)
            normed, _ = norm_forward(hidden_ref[rows, :].astype(F32))
            first_input = (normed * gain_ref[...]).astype(BF16)
            input_ref[rows, :] = first_input
            key_value = dot(first_input, wkv_ref[...])
            key_raw = key_value[:, :head_size]
            key_raw_ref[rows, :] = key_raw
            value_ref[rows, :] = key_value[:, head_size:].astype(BF16)
            key_normed, _ = norm_forward(key_raw)
            key_rot_ref[rows, :] = rotate(
                key_normed * key_gain_ref[...], cosine_ref[rows, :], sine_ref[rows, :]
            ).astype(BF16)

    for block in range(blocks):
        rows = pl.ds(block * BLOCK, BLOCK)
        seen = pl.ds(0, (block + 1) * BLOCK)
        query_raw = dot(input_ref[rows, :], wq_ref[...])
        query_raw_ref[rows, :] = query_raw
        for head in range(heads_a_step):
            columns = slice(head * head_size, (head + 1) * head_size)
            query_normed, _ = norm_forward(query_raw[:, columns])
            query_rot = rotate(
                query_normed * query_gain_ref[...], cosine_ref[rows, :], sine_ref[rows, :]
            ).astype(BF16)
            scores = dot_nt(query_rot, key_rot_ref[seen, :]) * factor
            exponent = jnp.exp(scores - jnp.max(scores, axis=-1, keepdims=True))
            probs = (exponent / jnp.sum(exponent, axis=-1, keepdims=True)).astype(BF16)
            attended_ref[rows, columns] = dot(probs, value_ref[seen, :]).astype(BF16)
        partial = dot(attended_ref[rows, :], wo_ref[...])

        @pl.when(step == 0)
        def _():
            total_ref[rows, :] = partial

        @pl.when(step > 0)
        def _():
            total_ref[rows, :] += partial

    @pl.when(step == pl.num_programs(0) - 1)
    def _():
        branch_ref[...] = total_ref[...].astype(BF16)


def attention_backward(
    planes, across, shards, capacity, heads_a_step,
    own_grad_ref, wo_ref, attended_ref, query_raw_ref, key_raw_ref, value_ref, input_ref, wq_ref,
    query_gain_ref, key_gain_ref, cosine_ref, sine_ref, slots_ref, weighted_hbm,
    wo_grad_ref, wq_grad_ref, first_grad_ref, query_gain_grad_ref, key_gain_grad_ref, returned_hbm, expert_sum_ref,
    total_ref, key_rot_ref, key_grad_ref, value_grad_ref, query_grad_ref, turned_ref, grad_ref,
    rows, chosen, partial_out, partial_in,
    gather_send, gather_recv, back_send, back_recv, sum_send, sum_recv, load_sem,
):
    step = pl.program_id(0)
    last = pl.num_programs(0) - 1
    head_size = cosine_ref.shape[1]
    seq_length = cosine_ref.shape[0]
    blocks = seq_length // BLOCK
    factor = head_size ** (-0.5)
    z, x, w = lax.axis_index("z"), lax.axis_index("x"), lax.axis_index("w")
    in_plane = across * shards
    me = x * shards + w
    tokens, width = own_grad_ref.shape
    count = in_plane * capacity
    chunk = 512
    pair, core = w // 2, w % 2
    sibling, opposite, other = pair * 2 + 1 - core, (1 - pair) * 2 + core, (1 - pair) * 2 + 1 - core

    def slice_of(index):
        return pl.ds(pl.multiple_of(index * capacity, 16), capacity)

    def tokens_of(index):
        return pl.ds(pl.multiple_of(index * tokens, tokens), tokens)

    def gather_copy(kind, owner, target):
        return remote(
            grad_ref.at[tokens_of(owner)], grad_ref.at[tokens_of(owner)], gather_send.at[kind], gather_recv.at[kind],
            (z, x, target),
        )

    def back_copy(block, index):
        return remote(
            weighted_hbm.at[block, slice_of(index)], returned_hbm.at[block, slice_of(me)],
            back_send.at[block], back_recv.at[block], (z, index // shards, index % shards),
        )

    def start_back(near):
        @pl.loop(0, planes)
        def _(turn):
            block, _, _ = line_order(z, planes, planes - 1 - turn)

            @pl.loop(1, in_plane)
            def _(offset):
                index = (me + offset) % in_plane

                @pl.when((index % shards) // 2 == pair if near else (index % shards) // 2 != pair)
                def _():
                    back_copy(block, index).start()

    def sum_copy(block):
        return remote(partial_out.at[block], partial_in.at[z], sum_send.at[block], sum_recv.at[z], (block, x, w))

    @pl.when(step == 0)
    def _():
        greet_plane_and_line(planes, across, shards)
        grad_ref[tokens_of(w), :] = own_grad_ref[...]
        gather_copy(1, w, opposite).start()
        gather_copy(0, w, sibling).start()
        start_back(True)

        @pl.loop(0, planes)
        def _(block):
            pltpu.make_async_copy(
                weighted_hbm.at[block, slice_of(me)], returned_hbm.at[block, slice_of(me)], back_recv.at[block]
            ).start()

        key_normed, _ = norm_forward(key_raw_ref[...])
        key_rot_ref[...] = rotate(key_normed * key_gain_ref[...], cosine_ref[...], sine_ref[...]).astype(BF16)
        key_grad_ref[...] = jnp.zeros_like(key_grad_ref)
        value_grad_ref[...] = jnp.zeros_like(value_grad_ref)
        query_gain_grad_ref[...] = jnp.zeros_like(query_gain_grad_ref)
        for block in range(blocks):
            rows_here = pl.ds(block * BLOCK, BLOCK)
            turned_ref[:, rows_here] = input_ref[rows_here, :].T
        wait_bytes(grad_ref.at[tokens_of(opposite)], gather_recv.at[1])
        gather_copy(2, opposite, sibling).start()
        start_back(False)
        wait_bytes(grad_ref.at[tokens_of(sibling)], gather_recv.at[0])
        wait_bytes(grad_ref.at[tokens_of(other)], gather_recv.at[2])

    @pl.when(step < last)
    def _():
        wo_grad_ref[...] = dot_tn(attended_ref[...], grad_ref[...]).astype(BF16)
        for block in range(blocks):
            rows_here = pl.ds(block * BLOCK, BLOCK)
            seen = pl.ds(0, (block + 1) * BLOCK)
            attended_grad = dot_nt(grad_ref[rows_here, :], wo_ref[...]).astype(BF16)
            for head in range(heads_a_step):
                columns = slice(head * head_size, (head + 1) * head_size)
                query_normed, query_scale = norm_forward(query_raw_ref[rows_here, columns])
                cosine, sine = cosine_ref[rows_here, :], sine_ref[rows_here, :]
                query_rot = rotate(query_normed * query_gain_ref[...], cosine, sine).astype(BF16)
                head_grad = attended_grad[:, columns]
                keys, values = key_rot_ref[seen, :], value_ref[seen, :]
                scores = dot_nt(query_rot, keys) * factor
                exponent = jnp.exp(scores - jnp.max(scores, axis=-1, keepdims=True))
                probs = exponent / jnp.sum(exponent, axis=-1, keepdims=True)
                prob_grad = dot_nt(head_grad, values)
                value_grad_ref[seen, :] += dot_tn(probs.astype(BF16), head_grad)
                center = jnp.sum(probs * prob_grad, axis=-1, keepdims=True)
                score_grad = (probs * (prob_grad - center)).astype(BF16)
                key_grad_ref[seen, :] += dot_tn(score_grad, query_rot) * factor
                query_rot_grad = dot(score_grad, keys) * factor
                unrotated = unrotate(query_rot_grad, cosine, sine)
                query_gain_grad_ref[0:1, :] += jnp.sum(unrotated * query_normed, axis=0, keepdims=True)
                query_grad_ref[rows_here, columns] = norm_backward(
                    unrotated * query_gain_ref[...], query_normed, query_scale
                ).astype(BF16)
            partial = dot_nt(query_grad_ref[rows_here, :], wq_ref[...])

            @pl.when(step == 0)
            def _():
                total_ref[rows_here, :] = partial

            @pl.when(step > 0)
            def _():
                total_ref[rows_here, :] += partial

    @pl.when(step == last)
    def _():
        key_normed, key_scale = norm_forward(key_raw_ref[...])
        unrotated = unrotate(key_grad_ref[...], cosine_ref[...], sine_ref[...])
        key_gain_grad_ref[...] = jnp.zeros_like(key_gain_grad_ref)
        key_gain_grad_ref[0:1, :] = jnp.sum(unrotated * key_normed, axis=0, keepdims=True)
        key_grad = norm_backward(unrotated * key_gain_ref[...], key_normed, key_scale)
        query_grad_ref[:, :head_size] = key_grad.astype(BF16)
        query_grad_ref[:, head_size : 2 * head_size] = value_grad_ref[...].astype(BF16)
        for block in range(blocks):
            rows_here = pl.ds(block * BLOCK, BLOCK)
            first_grad_ref[rows_here, :] = (
                total_ref[rows_here, :] + dot_nt(query_grad_ref[rows_here, :], wq_ref[...])
            ).astype(BF16)

    wq_grad_ref[...] = dot(turned_ref[...], query_grad_ref[...]).astype(BF16)

    @pl.when(step >= last - planes + 1)
    def _():
        place = last - step
        block, _, _ = line_order(z, planes, place)
        wait_bytes(returned_hbm.at[block], back_recv.at[block])
        load = pltpu.make_async_copy(returned_hbm.at[block], rows, load_sem)
        load.start()
        slot_ids = lax.broadcasted_iota(jnp.int32, (capacity, tokens), 0)

        @pl.loop(0, in_plane)
        def _(index):
            slots = slots_ref[block * in_plane + index]
            chosen[slice_of(index), :] = (slot_ids == slots).astype(F32).astype(BF16)

        load.wait()

        @pl.loop(0, width // chunk)
        def _(part):
            wide = pl.ds(pl.multiple_of(part * chunk, chunk), chunk)
            summed = dot_tn(chosen[...], rows[:, wide])
            partial_out[block, :, wide] = summed.astype(BF16)

            @pl.when(place == 0)
            def _():
                expert_sum_ref[:, wide] = summed

        @pl.when(place > 0)
        def _():
            sum_copy(block).start()

    @pl.when(step == last)
    def _():
        @pl.loop(1, planes)
        def _(offset):
            source = (z + offset) % planes
            wait_bytes(partial_in.at[source], sum_recv.at[source])

            @pl.loop(0, width // chunk)
            def _(part):
                wide = pl.ds(pl.multiple_of(part * chunk, chunk), chunk)
                expert_sum_ref[:, wide] += partial_in[source, :, wide].astype(F32)

            wait_bytes(partial_out.at[source], sum_send.at[source])

        @pl.loop(0, planes)
        def _(block):
            wait_bytes(weighted_hbm.at[block, pl.ds(0, count - capacity)], back_send.at[block])

        wait_bytes(grad_ref.at[tokens_of(w)], gather_send.at[0])
        wait_bytes(grad_ref.at[tokens_of(w)], gather_send.at[1])
        wait_bytes(grad_ref.at[tokens_of(w)], gather_send.at[2])


def whole(shape):
    return pl.BlockSpec(shape, lambda step: (0,) * len(shape), pipeline_mode=pl.Buffered(1))


def run_forward(hidden_all, gain, weights, wo, query_gain, key_gain, cosine, sine):
    seq_length, width = hidden_all.shape
    head_size = query_gain.shape[1]
    heads_here = wo.shape[0] // head_size
    pair = 2
    wide = pair * head_size
    steps = heads_here // pair
    return pl.pallas_call(
        functools.partial(attention_forward, pair),
        grid=(steps,),
        in_specs=[
            whole((seq_length, width)),
            whole((1, width)),
            pl.BlockSpec((width, wide), lambda step: (0, step)),
            pl.BlockSpec((width, wide), lambda step: (0, steps), pipeline_mode=pl.Buffered(1)),
            whole((1, head_size)),
            whole((1, head_size)),
            whole((seq_length, head_size)),
            whole((seq_length, head_size)),
            pl.BlockSpec((wide, width), lambda step: (step, 0)),
        ],
        out_specs=[
            whole((seq_length, width)),
            pl.BlockSpec((seq_length, wide), lambda step: (0, step)),
            whole((seq_length, head_size)),
            whole((seq_length, head_size)),
            pl.BlockSpec((seq_length, wide), lambda step: (0, step)),
            whole((seq_length, width)),
        ],
        out_shape=[
            jax.ShapeDtypeStruct((seq_length, width), BF16),
            jax.ShapeDtypeStruct((seq_length, heads_here * head_size), F32),
            jax.ShapeDtypeStruct((seq_length, head_size), F32),
            jax.ShapeDtypeStruct((seq_length, head_size), BF16),
            jax.ShapeDtypeStruct((seq_length, heads_here * head_size), BF16),
            jax.ShapeDtypeStruct((seq_length, width), BF16),
        ],
        scratch_shapes=[
            pltpu.VMEM((seq_length, width), F32),
            pltpu.VMEM((seq_length, head_size), BF16),
        ],
        compiler_params=pltpu.CompilerParams(vmem_limit_bytes=VMEM_LIMIT),
        cost_estimate=pl.CostEstimate(flops=16 * 10**9, bytes_accessed=40 * 10**6, transcendentals=6 * 10**6),
    )(hidden_all, gain, weights, weights, query_gain, key_gain, cosine, sine, wo)


def run_backward(
    planes, across, shards, capacity, own_grad, wo, attended, query_raw, key_raw, value, first_input, weights, query_gain,
    key_gain, cosine, sine, slots, weighted,
):
    tokens, width = own_grad.shape
    seq_length = attended.shape[0]
    head_size = query_gain.shape[1]
    heads_here = wo.shape[0] // head_size
    pair = 2
    wide = pair * head_size
    steps = heads_here // pair
    count = across * shards * capacity
    hbm = pl.BlockSpec(memory_space=pl.ANY)
    dma = pltpu.SemaphoreType.DMA

    def held(step):
        return jnp.minimum(step, steps - 1)

    return pl.pallas_call(
        functools.partial(attention_backward, planes, across, shards, capacity, pair),
        grid=(steps + 1,),
        in_specs=[
            whole((tokens, width)),
            pl.BlockSpec((wide, width), lambda step: (held(step), 0)),
            pl.BlockSpec((seq_length, wide), lambda step: (0, held(step))),
            pl.BlockSpec((seq_length, wide), lambda step: (0, held(step))),
            whole((seq_length, head_size)),
            whole((seq_length, head_size)),
            whole((seq_length, width)),
            pl.BlockSpec((width, wide), lambda step: (0, step)),
            whole((1, head_size)),
            whole((1, head_size)),
            whole((seq_length, head_size)),
            whole((seq_length, head_size)),
            whole(slots.shape),
            hbm,
        ],
        out_specs=[
            pl.BlockSpec((wide, width), lambda step: (held(step), 0)),
            pl.BlockSpec((width, wide), lambda step: (0, step)),
            whole((seq_length, width)),
            whole((8, head_size)),
            whole((8, head_size)),
            hbm,
            whole((tokens, width)),
        ],
        out_shape=[
            jax.ShapeDtypeStruct((heads_here * head_size, width), BF16),
            jax.ShapeDtypeStruct((width, (steps + 1) * wide), BF16),
            jax.ShapeDtypeStruct((seq_length, width), BF16),
            jax.ShapeDtypeStruct((8, head_size), F32),
            jax.ShapeDtypeStruct((8, head_size), F32),
            jax.ShapeDtypeStruct(weighted.shape, BF16),
            jax.ShapeDtypeStruct((tokens, width), F32),
        ],
        scratch_shapes=[
            pltpu.VMEM((seq_length, width), F32),
            pltpu.VMEM((seq_length, head_size), BF16),
            pltpu.VMEM((seq_length, head_size), F32),
            pltpu.VMEM((seq_length, head_size), F32),
            pltpu.VMEM((seq_length, wide), BF16),
            pltpu.VMEM((width, seq_length), BF16),
            pltpu.VMEM((seq_length, width), BF16),
            pltpu.VMEM((count, width), BF16),
            pltpu.VMEM((count, tokens), BF16),
            pltpu.VMEM((planes, tokens, width), BF16),
            pltpu.VMEM((planes, tokens, width), BF16),
            dma((3,)), dma((3,)), dma((planes,)), dma((planes,)), dma((planes,)), dma((planes,)), dma,
        ],
        compiler_params=pltpu.CompilerParams(vmem_limit_bytes=VMEM_LIMIT, collective_id=2, has_side_effects=True),
        cost_estimate=pl.CostEstimate(flops=70 * 10**9, bytes_accessed=60 * 10**6, transcendentals=6 * 10**6),
    )(
        own_grad, wo, attended, query_raw, key_raw, value, first_input, weights, query_gain, key_gain, cosine, sine, slots,
        weighted,
    )


def reduce_kernel(
    planes, across, shards,
    wq_hbm, wo_hbm, first_hbm,
    query_ref, key_ref, value_ref, output_ref, first_ref,
    wq_parts, wo_parts, wq_out, wo_out, wq_in, wo_in, wq_total, wo_total, wq_final, wo_final, wq_home, wo_home, first_in,
    across_send, across_recv, line_send, line_recv, home_send, home_recv, swap_send, swap_recv, first_send, first_recv,
):
    z, x, w = lax.axis_index("z"), lax.axis_index("x"), lax.axis_index("w")
    rings = planes * across
    ring = z * across + x
    everyone = rings * shards
    wq_rows, wo_rows = wq_total.shape[0], wo_total.shape[0]
    mine = wq_rows // shards
    tokens = first_ref.shape[0]
    query_columns = query_ref.shape[1] // shards
    key_columns = key_ref.shape[1] // shards
    linear = ring * shards + w
    barrier = pltpu.get_barrier_semaphore()

    @pl.loop(1, everyone)
    def _(offset):
        other = (linear + offset) % everyone
        pl.semaphore_signal(
            barrier, inc=1, device_id=(other // shards // across, other // shards % across, other % shards),
            device_id_type=MESH,
        )

    pl.semaphore_wait(barrier, everyone - 1)

    def rows_of(index, size):
        return pl.ds(pl.multiple_of(index * size, 16), size)

    def across_copies(plane, column):
        target = plane * across + column
        return [
            remote(
                wq_hbm.at[rows_of(target, wq_rows)], wq_parts.at[plane, x],
                across_send.at[0, plane], across_recv.at[0, plane], (z, column, w),
            ),
            remote(
                wo_hbm.at[rows_of(target, wo_rows)], wo_parts.at[plane, x],
                across_send.at[1, plane], across_recv.at[1, plane], (z, column, w),
            ),
        ]

    def first_copy(offset):
        target = (w + offset) % shards
        return remote(
            first_hbm.at[rows_of(target, tokens)], first_in.at[offset], first_send.at[offset], first_recv.at[offset],
            (z, x, target),
        )

    @pl.loop(1, shards)
    def _(offset):
        first_copy(offset).start()

    pltpu.make_async_copy(first_hbm.at[rows_of(w, tokens)], first_in.at[0], first_recv.at[0]).start()

    @pl.loop(0, planes)
    def _(turn):
        plane, _, _ = line_order(z, planes, planes - 1 - turn)

        @pl.loop(1, across)
        def _(offset):
            for copy in across_copies(plane, (x + offset) % across):
                copy.start()

        target = plane * across + x
        pltpu.make_async_copy(
            wq_hbm.at[rows_of(target, wq_rows)], wq_parts.at[plane, x], across_recv.at[0, plane]
        ).start()
        pltpu.make_async_copy(
            wo_hbm.at[rows_of(target, wo_rows)], wo_parts.at[plane, x], across_recv.at[1, plane]
        ).start()

    def wq_line_copy(plane):
        return remote(wq_out.at[plane], wq_in.at[z], line_send.at[0, plane], line_recv.at[0, z], (plane, x, w))

    def wo_line_copy(plane):
        return remote(wo_out.at[plane], wo_in.at[z], line_send.at[1, plane], line_recv.at[1, z], (plane, x, w))

    @pl.loop(0, shards)
    def _(offset):
        wait_bytes(first_in.at[offset], first_recv.at[offset])

    first_ref[...] = first_in[0].astype(F32)

    @pl.loop(1, shards)
    def _(offset):
        first_ref[...] += first_in[offset].astype(F32)

    @pl.loop(0, planes)
    def _(turn):
        plane, _, _ = line_order(z, planes, planes - 1 - turn)
        wait_bytes(wq_parts.at[plane], across_recv.at[0, plane])
        wq_total[...] = wq_parts[plane, 0].astype(F32)

        @pl.loop(1, across)
        def _(column):
            wq_total[...] += wq_parts[plane, column].astype(F32)

        @pl.when(turn < planes - 1)
        def _():
            wq_out[plane] = wq_total[...].astype(BF16)
            wq_line_copy(plane).start()

        wait_bytes(wo_parts.at[plane], across_recv.at[1, plane])
        wo_total[...] = wo_parts[plane, 0].astype(F32)

        @pl.loop(1, across)
        def _(column):
            wo_total[...] += wo_parts[plane, column].astype(F32)

        @pl.when(turn < planes - 1)
        def _():
            wo_out[plane] = wo_total[...].astype(BF16)
            wo_line_copy(plane).start()

    @pl.loop(1, planes)
    def _(turn):
        plane, _, _ = line_order(z, planes, turn)
        wait_bytes(wq_in.at[plane], line_recv.at[0, plane])
        wq_total[...] += wq_in[plane].astype(F32)

    wq_final[...] = wq_total[...].astype(BF16)

    def home_copy(offset):
        target = (w + offset) % shards
        return remote(
            wq_final.at[rows_of(target, mine)], wq_home.at[w], home_send.at[offset], home_recv.at[w], (z, x, target)
        )

    @pl.loop(1, shards)
    def _(offset):
        home_copy(offset).start()

    pltpu.make_async_copy(wq_final.at[rows_of(w, mine)], wq_home.at[w], home_recv.at[w]).start()

    @pl.loop(1, planes)
    def _(turn):
        plane, _, _ = line_order(z, planes, turn)
        wait_bytes(wo_in.at[plane], line_recv.at[1, plane])
        wo_total[...] += wo_in[plane].astype(F32)

    wo_final[...] = wo_total[...].astype(BF16)
    goal = w * rings + ring
    stays = goal == linear
    swap = remote(
        wo_final, wo_home, swap_send, swap_recv, (goal // shards // across, goal // shards % across, goal % shards)
    )

    @pl.when(jnp.logical_not(stays))
    def _():
        swap.start()

    @pl.when(stays)
    def _():
        pltpu.make_async_copy(wo_final, wo_home, swap_recv).start()

    for part in range(shards):
        wait_bytes(wq_home.at[part], home_recv.at[part])
        rows = wq_home[part].astype(F32)
        query_ref[:, part * query_columns : (part + 1) * query_columns] = rows[:, :query_columns]
        key_ref[:, part * key_columns : (part + 1) * key_columns] = rows[:, query_columns : query_columns + key_columns]
        value_ref[:, part * key_columns : (part + 1) * key_columns] = rows[:, query_columns + key_columns :]

    wait_bytes(wo_home, swap_recv)
    output_ref[...] = wo_home[...].astype(F32)

    @pl.when(jnp.logical_not(stays))
    def _():
        wait_bytes(wo_final, swap_send)

    @pl.loop(1, shards)
    def _(offset):
        wait_bytes(wq_home.at[0], home_send.at[offset])
        wait_bytes(first_in.at[0], first_send.at[offset])

    if across > 1:

        @pl.loop(0, planes)
        def _(plane):
            wait_bytes(wq_parts.at[plane, pl.ds(0, across - 1)], across_send.at[0, plane])
            wait_bytes(wo_parts.at[plane, pl.ds(0, across - 1)], across_send.at[1, plane])

    @pl.loop(1, planes)
    def _(offset):
        plane = (z + offset) % planes
        wait_bytes(wq_out.at[plane], line_send.at[0, plane])
        wait_bytes(wo_out.at[plane], line_send.at[1, plane])


def run_reduce(planes, across, shards, wq_grad, wo_grad, first_part, query_columns, key_columns):
    rings = planes * across
    everyone = rings * shards
    width = wq_grad.shape[0]
    wq_wide = wq_grad.shape[1]
    wq_rows, wo_rows = width // rings, wo_grad.shape[0] // rings
    tokens = first_part.shape[0] // shards
    mine = wq_rows // shards
    hbm = pl.BlockSpec(memory_space=pl.ANY)
    vmem = pl.BlockSpec(memory_space=pltpu.VMEM)
    dma = pltpu.SemaphoreType.DMA
    return pl.pallas_call(
        functools.partial(reduce_kernel, planes, across, shards),
        in_specs=[hbm] * 3,
        out_specs=[vmem] * 5,
        out_shape=[
            jax.ShapeDtypeStruct((mine, query_columns), F32),
            jax.ShapeDtypeStruct((mine, key_columns), F32),
            jax.ShapeDtypeStruct((mine, key_columns), F32),
            jax.ShapeDtypeStruct((wo_rows, width), F32),
            jax.ShapeDtypeStruct((tokens, width), F32),
        ],
        scratch_shapes=[
            pltpu.VMEM((planes, across, wq_rows, wq_wide), BF16),
            pltpu.VMEM((planes, across, wo_rows, width), BF16),
            pltpu.VMEM((planes, wq_rows, wq_wide), BF16),
            pltpu.VMEM((planes, wo_rows, width), BF16),
            pltpu.VMEM((planes, wq_rows, wq_wide), BF16),
            pltpu.VMEM((planes, wo_rows, width), BF16),
            pltpu.VMEM((wq_rows, wq_wide), F32),
            pltpu.VMEM((wo_rows, width), F32),
            pltpu.VMEM((wq_rows, wq_wide), BF16),
            pltpu.VMEM((wo_rows, width), BF16),
            pltpu.VMEM((shards, mine, wq_wide), BF16),
            pltpu.VMEM((wo_rows, width), BF16),
            pltpu.VMEM((shards, tokens, width), BF16),
            dma((2, planes)), dma((2, planes)), dma((2, planes)), dma((2, planes)), dma((shards,)), dma((shards,)),
            dma, dma, dma((shards,)), dma((shards,)),
        ],
        compiler_params=pltpu.CompilerParams(vmem_limit_bytes=VMEM_LIMIT, collective_id=3, has_side_effects=True),
        cost_estimate=pl.CostEstimate(flops=70 * 10**9, bytes_accessed=40 * 10**6, transcendentals=0),
    )(wq_grad, wo_grad, first_part)


def total_kernel(planes, across, shards, parts_ref, total_ref, parts_in, send, recv):
    z, x, w = lax.axis_index("z"), lax.axis_index("x"), lax.axis_index("w")
    everyone = planes * across * shards
    linear = (z * across + x) * shards + w
    barrier = pltpu.get_barrier_semaphore()

    def place(index):
        return (index // shards // across, index // shards % across, index % shards)

    @pl.loop(1, everyone)
    def _(offset):
        pl.semaphore_signal(barrier, inc=1, device_id=place((linear + offset) % everyone), device_id_type=MESH)

    pl.semaphore_wait(barrier, everyone - 1)

    @pl.loop(1, everyone)
    def _(offset):
        other = (linear + offset) % everyone
        remote(parts_ref.at[other], parts_in.at[linear], send, recv, place(other)).start()

    parts_in[linear] = parts_ref[linear]
    wait_bytes(parts_ref.at[pl.ds(0, everyone - 1)], recv)
    total_ref[...] = jnp.sum(parts_in[...], axis=0)
    wait_bytes(parts_ref.at[pl.ds(0, everyone - 1)], send)


def run_total(planes, across, shards, parts):
    everyone, rows, lanes = parts.shape
    return pl.pallas_call(
        functools.partial(total_kernel, planes, across, shards),
        in_specs=[pl.BlockSpec(memory_space=pltpu.VMEM)],
        out_specs=pl.BlockSpec(memory_space=pltpu.VMEM),
        out_shape=jax.ShapeDtypeStruct((rows, lanes), F32),
        scratch_shapes=[
            pltpu.VMEM((everyone, rows, lanes), F32), pltpu.SemaphoreType.DMA, pltpu.SemaphoreType.DMA,
        ],
        compiler_params=pltpu.CompilerParams(vmem_limit_bytes=VMEM_LIMIT, collective_id=4, has_side_effects=True),
    )(parts)


def expert_kernel(
    planes, across, shards, capacity,
    own_ref, share_ref, slots_ref, my_slots_ref, gate_ref, up_ref, down_ref, top_hbm,
    rows_hbm, back_hbm, weighted_hbm, units_hbm, gate_grad_hbm, up_grad_hbm, pair_grad_hbm, row_grad_ref, share_grad_ref,
    plane_rows, plane_shares, share_in, share_back, share_home, stage, chosen, rows, top, units,
    gate_grad, up_grad, columns, partial_in,
    line_send, line_recv, plane_share_send, plane_share_recv, out_send, out_recv, out_share_send, out_share_recv,
    back_send, back_recv, back_share_send, back_share_recv, sum_send, sum_recv, sum_share_send, sum_share_recv,
    load_sem, top_sem, store_sem,
):
    z, x, w = lax.axis_index("z"), lax.axis_index("x"), lax.axis_index("w")
    in_plane = across * shards
    me = x * shards + w
    tokens, width = own_ref.shape
    count = in_plane * capacity
    half = count // 2
    per_half = in_plane // 2
    chunk = 512

    def place(index):
        return (z, index // shards, index % shards)

    def order(step):
        return line_order(z, planes, step)

    greet_plane_and_line(planes, across, shards)

    def line_up(block, hop):
        return remote(
            plane_rows.at[block], plane_rows.at[block], line_send.at[0, hop], line_recv.at[0, hop], (z + 1, x, w)
        )

    def line_down(block, hop):
        return remote(
            plane_rows.at[block], plane_rows.at[block], line_send.at[1, hop], line_recv.at[1, hop], (z - 1, x, w)
        )

    plane_rows[z] = own_ref[...]

    @pl.when(z + 1 < planes)
    def _():
        line_up(z, 1).start()

    @pl.when(z > 0)
    def _():
        line_down(z, 1).start()

    def plane_share_copy(other):
        return remote(
            share_ref.at[pl.ds(other * in_plane, in_plane)], plane_shares.at[z],
            plane_share_send.at[other], plane_share_recv.at[z], (other, x, w),
        )

    @pl.loop(1, planes)
    def _(offset):
        plane_share_copy((z + offset) % planes).start()

    plane_shares[z] = share_ref[pl.ds(z * in_plane, in_plane)]

    def slice_of(index):
        return pl.ds(pl.multiple_of(index * capacity, 16), capacity)

    def out_copy(step, block, index):
        return remote(
            stage.at[step, slice_of(index)], rows_hbm.at[block, slice_of(me)],
            out_send.at[step], out_recv.at[step], place(index),
        )

    def out_share_copy(step, block, index):
        return remote(
            plane_shares.at[block, index], share_in.at[block, me],
            out_share_send.at[step], out_share_recv.at[step], place(index),
        )

    def back_copy(step, block, index):
        return remote(
            stage.at[step, slice_of(index)], back_hbm.at[block, slice_of(me)],
            back_send.at[step], back_recv.at[step], place(index),
        )

    def back_share_copy(step, block, index):
        return remote(
            share_back.at[block, index], share_home.at[block, me],
            back_share_send.at[step], back_share_recv.at[step], place(index),
        )

    def start_back(step, block):
        @pl.loop(1, in_plane)
        def _(offset):
            index = (me + offset) % in_plane
            back_copy(step, block, index).start()
            back_share_copy(step, block, index).start()

        pltpu.make_async_copy(stage.at[step, slice_of(me)], back_hbm.at[block, slice_of(me)], back_recv.at[step]).start()
        pltpu.make_async_copy(share_back.at[block, me], share_home.at[block, me], back_share_recv.at[step]).start()

    slot_ids = lax.broadcasted_iota(jnp.int32, (capacity, tokens), 0)

    def send_step(step):
        block, hop, below = order(step)

        @pl.when(step > 0)
        def _():
            wait_bytes(plane_rows.at[block], line_recv.at[1 - below, hop])
            wait_bytes(plane_shares.at[block], plane_share_recv.at[block])

            @pl.when((below == 1) & (z + 1 < planes))
            def _():
                line_up(block, hop + 1).start()

            @pl.when((below == 0) & (z > 0))
            def _():
                line_down(block, hop + 1).start()

        @pl.loop(0, in_plane)
        def _(index):
            slots = slots_ref[block * in_plane + index]
            chosen[step, slice_of(index), :] = (slot_ids == slots).astype(F32).astype(BF16)

        @pl.loop(0, width // chunk)
        def _(part):
            wide = pl.ds(pl.multiple_of(part * chunk, chunk), chunk)
            stage[step, :, wide] = dot(chosen[step], plane_rows[block, :, wide]).astype(BF16)

        @pl.loop(1, in_plane)
        def _(offset):
            index = (me + offset) % in_plane
            out_copy(step, block, index).start()
            out_share_copy(step, block, index).start()

        pltpu.make_async_copy(stage.at[step, slice_of(me)], rows_hbm.at[block, slice_of(me)], out_recv.at[step]).start()
        pltpu.make_async_copy(plane_shares.at[block, me], share_in.at[block, me], out_share_recv.at[step]).start()

    def top_copy(block, index):
        return pltpu.make_async_copy(top_hbm.at[index, block], top.at[slice_of(index)], top_sem)

    def expert_step(step):
        block, _, _ = order(step)

        @pl.loop(0, in_plane)
        def _(index):
            top_copy(block, index).start()

        wait_bytes(rows_hbm.at[block], out_recv.at[step])
        load = pltpu.make_async_copy(rows_hbm.at[block], rows, load_sem)
        load.start()
        wait_bytes(share_in.at[block], out_share_recv.at[step])
        wait_bytes(stage.at[step, pl.ds(0, count - capacity)], out_send.at[step])
        wait_bytes(plane_shares.at[block, pl.ds(0, in_plane - 1)], out_share_send.at[step])

        @pl.loop(0, in_plane)
        def _(index):
            mine = slot_ids == my_slots_ref[block * in_plane + index]
            columns[slice_of(index), :] = jnp.broadcast_to(
                jnp.sum(jnp.where(mine, share_in[block, index], 0.0), axis=1, keepdims=True), (capacity, 128)
            )

        load.wait()
        wait_bytes(top, top_sem)

        @pl.loop(0, 2)
        def _(part):
            here = pl.ds(pl.multiple_of(part * half, 16), half)
            gate = dot(rows[here, :], gate_ref[...])
            up = dot(rows[here, :], up_ref[...])
            sigmoid = 1.0 / (1.0 + jnp.exp(-gate))
            active = gate * sigmoid
            hidden = (active * up).astype(BF16)
            units[here, :] = hidden
            share = columns[here, 0:1]
            total = jnp.zeros((half, 1), F32)
            for piece in range(width // chunk):
                wide = pl.ds(piece * chunk, chunk)
                pair_out = dot(hidden, down_ref[:, wide]).astype(BF16).astype(F32)
                top_rows = top[here, wide].astype(F32)
                total += jnp.sum(pair_out * top_rows, axis=1, keepdims=True)
                rows[here, wide] = (share * pair_out).astype(BF16)
                top[here, wide] = (share * top_rows).astype(BF16)
            columns[here, :] = jnp.broadcast_to(total, (half, 128))
            hidden_grad = dot_nt(top[here, :], down_ref[...])
            gate_low = (hidden_grad * up * sigmoid * (1.0 + gate * (1.0 - sigmoid))).astype(BF16)
            up_low = (hidden_grad * active).astype(BF16)
            gate_grad[here, :] = gate_low
            up_grad[here, :] = up_low
            for piece in range(width // chunk):
                wide = pl.ds(piece * chunk, chunk)
                stage[step, here, wide] = (dot_nt(gate_low, gate_ref[wide, :]) + dot_nt(up_low, up_ref[wide, :])).astype(BF16)

        @pl.loop(0, in_plane)
        def _(index):
            mine = slot_ids == my_slots_ref[block * in_plane + index]
            values = columns[slice_of(index), 0:1]
            share_back[block, index] = jnp.sum(jnp.where(mine, values, 0.0), axis=0, keepdims=True)

        @pl.when(step > 0)
        def _():
            start_back(step, block)

        stores = [
            pltpu.make_async_copy(units, units_hbm.at[block], store_sem.at[0]),
            pltpu.make_async_copy(gate_grad, gate_grad_hbm.at[block], store_sem.at[1]),
            pltpu.make_async_copy(up_grad, up_grad_hbm.at[block], store_sem.at[2]),
            pltpu.make_async_copy(top, pair_grad_hbm.at[block], store_sem.at[3]),
            pltpu.make_async_copy(rows, weighted_hbm.at[block], store_sem.at[4]),
        ]
        for store in stores:
            store.start()

        for store in stores:
            store.wait()

    @pl.loop(0, planes + 1)
    def _(step):
        @pl.when(step < planes)
        def _():
            send_step(step)

        @pl.when(step > 0)
        def _():
            expert_step(step - 1)

    start_back(0, z)

    for hop in range(1, planes):

        @pl.when((z - (hop - 1) >= 0) & (z + 1 < planes))
        def _():
            wait_bytes(plane_rows.at[0], line_send.at[0, hop])

        @pl.when((z + (hop - 1) < planes) & (z > 0))
        def _():
            wait_bytes(plane_rows.at[0], line_send.at[1, hop])

    @pl.loop(1, planes)
    def _(offset):
        wait_bytes(plane_shares.at[0], plane_share_send.at[(z + offset) % planes])

    def sum_copy(block):
        return remote(plane_rows.at[block], partial_in.at[z], sum_send.at[block], sum_recv.at[z], (block, x, w))

    def sum_share_copy(block):
        return remote(
            share_home.at[block], share_grad_ref.at[pl.ds(z * in_plane, in_plane)],
            sum_share_send.at[block], sum_share_recv.at[z], (block, x, w),
        )

    @pl.loop(0, planes)
    def _(turn):
        step = (turn + 1) % planes
        block, _, _ = order(step)
        wait_bytes(back_hbm.at[block], back_recv.at[step])
        load = pltpu.make_async_copy(back_hbm.at[block], rows, load_sem)
        load.start()
        wait_bytes(share_home.at[block], back_share_recv.at[step])
        load.wait()

        @pl.when(step > 0)
        def _():
            sum_share_copy(block).start()

            @pl.loop(0, width // chunk)
            def _(part):
                wide = pl.ds(pl.multiple_of(part * chunk, chunk), chunk)
                plane_rows[block, :, wide] = dot_tn(chosen[step], rows[:, wide]).astype(BF16)

            sum_copy(block).start()

        @pl.when(step == 0)
        def _():
            share_grad_ref[pl.ds(z * in_plane, in_plane)] = share_home[z]

            @pl.loop(0, width // chunk)
            def _(part):
                wide = pl.ds(pl.multiple_of(part * chunk, chunk), chunk)
                row_grad_ref[:, wide] = dot_tn(chosen[0], rows[:, wide])

    @pl.loop(1, planes)
    def _(offset):
        other = (z + offset) % planes
        wait_bytes(partial_in.at[other], sum_recv.at[other])
        wait_bytes(share_home.at[other], sum_share_recv.at[other])

        @pl.loop(0, width // chunk)
        def _(part):
            wide = pl.ds(pl.multiple_of(part * chunk, chunk), chunk)
            row_grad_ref[:, wide] += partial_in[other, :, wide].astype(F32)

    @pl.loop(1, planes)
    def _(offset):
        other = (z + offset) % planes
        wait_bytes(plane_rows.at[other], sum_send.at[other])
        wait_bytes(share_home.at[other], sum_share_send.at[other])

    @pl.loop(0, planes)
    def _(step):
        wait_bytes(stage.at[step, pl.ds(0, count - capacity)], back_send.at[step])
        wait_bytes(share_back.at[step, pl.ds(0, in_plane - 1)], back_share_send.at[step])


def run_experts(planes, across, shards, capacity, own, shares, slots, my_slots, w_gate, w_up, w_down, top_rows):
    tokens, width = own.shape
    in_plane = across * shards
    count = in_plane * capacity
    units = w_gate.shape[1]
    experts = planes * in_plane
    hbm = pl.BlockSpec(memory_space=pl.ANY)
    vmem = pl.BlockSpec(memory_space=pltpu.VMEM)
    dma = pltpu.SemaphoreType.DMA
    flops = 12 * planes * count * width * units
    return pl.pallas_call(
        functools.partial(expert_kernel, planes, across, shards, capacity),
        in_specs=[vmem] * 7 + [hbm],
        out_specs=[hbm] * 7 + [vmem] * 2,
        out_shape=[
            jax.ShapeDtypeStruct((planes, count, width), BF16),
            jax.ShapeDtypeStruct((planes, count, width), BF16),
            jax.ShapeDtypeStruct((planes, count, width), BF16),
            jax.ShapeDtypeStruct((planes, count, units), BF16),
            jax.ShapeDtypeStruct((planes, count, units), BF16),
            jax.ShapeDtypeStruct((planes, count, units), BF16),
            jax.ShapeDtypeStruct((planes, count, width), BF16),
            jax.ShapeDtypeStruct((tokens, width), F32),
            jax.ShapeDtypeStruct((experts, 1, tokens), F32),
        ],
        scratch_shapes=[
            pltpu.VMEM((planes, tokens, width), BF16),
            pltpu.VMEM((planes, in_plane, 1, tokens), F32),
            pltpu.VMEM((planes, in_plane, 1, tokens), F32),
            pltpu.VMEM((planes, in_plane, 1, tokens), F32),
            pltpu.VMEM((planes, in_plane, 1, tokens), F32),
            pltpu.VMEM((planes, count, width), BF16),
            pltpu.VMEM((planes, count, tokens), BF16),
            pltpu.VMEM((count, width), BF16),
            pltpu.VMEM((count, width), BF16),
            pltpu.VMEM((count, units), BF16),
            pltpu.VMEM((count, units), BF16),
            pltpu.VMEM((count, units), BF16),
            pltpu.VMEM((count, 128), F32),
            pltpu.VMEM((planes, tokens, width), BF16),
            dma((2, planes + 1)), dma((2, planes + 1)), dma((planes,)), dma((planes,)),
            dma((planes,)), dma((planes,)), dma((planes,)), dma((planes,)),
            dma((planes,)), dma((planes,)), dma((planes,)), dma((planes,)),
            dma((planes,)), dma((planes,)), dma((planes,)), dma((planes,)),
            dma, dma, dma((5,)),
        ],
        compiler_params=pltpu.CompilerParams(vmem_limit_bytes=VMEM_LIMIT, collective_id=1, has_side_effects=True),
        cost_estimate=pl.CostEstimate(flops=4 * flops, bytes_accessed=100 * 10**6, transcendentals=2 * 10**6),
    )(own, shares, slots, my_slots, w_gate, w_up, w_down, top_rows)


def local(
    hidden_in, attn_gain, w_query, key_projection, value_projection, query_gain, key_gain, w_output, ffn_gain, w_router,
    routes, w_gate, w_up, w_down, cotangent,
):
    tokens_here, width = hidden_in.shape
    head_size = query_gain.shape[0]
    top_count = routes.shape[1]
    planes, across, shards = lax.axis_size("z"), lax.axis_size("x"), lax.axis_size("w")
    rings = planes * across
    device_count = rings * shards
    in_plane = across * shards
    experts = device_count
    capacity = 5 * tokens_here * top_count // (4 * experts)
    seq_length = tokens_here * shards
    plane, column, shard = lax.axis_index("z"), lax.axis_index("x"), lax.axis_index("w")

    small = jnp.concatenate([w_router, attn_gain[:, None], ffn_gain[:, None]], axis=1)
    depth = w_query.shape[0]
    merged = jnp.concatenate(
        [
            w_query.reshape(depth, shards, -1),
            key_projection.reshape(depth, shards, -1),
            value_projection.reshape(depth, shards, -1),
        ],
        axis=2,
    ).reshape(depth, -1)
    hidden_all = lax.all_gather(hidden_in, "w", axis=0, tiled=True)
    small_all = lax.all_gather(small, "w", axis=0, tiled=True)
    weights = lax.all_to_all(merged, "w", split_axis=1, concat_axis=0, tiled=True)
    router_full = small_all[:, :experts]
    attn_scale = small_all[:, experts].astype(F32)[None, :]
    ffn_scale = small_all[:, experts + 1].astype(F32)[None, :]
    cosine, sine = rope_tables(seq_length, head_size)
    query_gain_row, key_gain_row = query_gain[None, :], key_gain[None, :]

    capacity = -(-capacity // 16) * 16
    routes_all = lax.all_gather(routes, ("z", "x", "w"), axis=0, tiled=True)
    routes_all = routes_all.reshape(planes, in_plane, tokens_here, top_count)
    me = column * shards + shard
    earlier = (
        jnp.arange(tokens_here)[:, None] < jnp.arange(tokens_here)[None, :]
    ).astype(BF16)

    def slots_of(hits):
        ranks = jnp.einsum("zps,st->zpt", hits.astype(BF16), earlier, preferred_element_type=F32).astype(jnp.int32)
        return jnp.where(hits, ranks, -1)

    routes_z = lax.dynamic_index_in_dim(routes_all, me, 1, keepdims=True)
    plane_experts = plane * in_plane + jnp.arange(in_plane, dtype=jnp.int32)
    slots = slots_of(jnp.any(routes_z == plane_experts[None, :, None, None], axis=3))
    my_slots = slots_of(jnp.any(routes_all == plane * in_plane + me, axis=3))
    slots_flat = slots.reshape(-1, 1, tokens_here)
    chosen = slots[:, :, None, :] == jnp.arange(capacity, dtype=jnp.int32)[None, None, :, None]
    chosen_flat = chosen.reshape(planes, in_plane * capacity, tokens_here).astype(BF16)

    def send_out(rows_z):
        packed = jnp.einsum("zst,ztd->zsd", chosen_flat, rows_z, preferred_element_type=F32).astype(BF16)
        packed = packed.reshape(planes, in_plane, capacity, width).transpose(1, 0, 2, 3)
        got = lax.all_to_all(
            packed.reshape(in_plane, planes * capacity, width), ("x", "w"), split_axis=0, concat_axis=0, tiled=True
        )
        return got.reshape(in_plane * planes * capacity, width)

    cotangent_z = lax.all_gather(cotangent, "z", axis=0, tiled=False)
    grads_in = send_out(cotangent_z)

    first_input, query_raw, key_raw, value, attended, branch_part = run_forward(
        hidden_all, attn_scale, weights, w_output, query_gain_row, key_gain_row, cosine, sine
    )
    branch = lax.psum_scatter(branch_part, "w", scatter_dimension=0, tiled=True).astype(F32)
    source = hidden_in.astype(F32)
    first_normed, first_scale = norm_forward(source)
    middle = source + branch
    second_normed, second_scale = norm_forward(middle)
    second_input = (second_normed * ffn_scale).astype(BF16)
    logits = lax.dot_general(router_full, second_input, (((0,), (1,)), ((), ())), preferred_element_type=F32)
    expert_ids = jnp.arange(experts, dtype=jnp.int32)
    routed = jnp.any(routes.T[None, :, :] == expert_ids[:, None, None], axis=1)
    peaks = jnp.max(jnp.where(routed, logits, -jnp.inf), axis=0, keepdims=True)
    shifted = jnp.where(routed, jnp.exp(jnp.where(routed, logits - peaks, 0.0)), 0.0)
    shares = shifted / jnp.sum(shifted, axis=0, keepdims=True)

    rows_in, _, weighted, hidden_units, gate_grad, up_grad, pair_grad, row_grad_sum, share_grad = run_experts(
        planes, across, shards, capacity, second_input, shares[:, None, :], slots_flat,
        my_slots.reshape(-1, 1, tokens_here), w_gate[0], w_up[0], w_down[0],
        grads_in.reshape(in_plane, planes, capacity, width),
    )
    share_grad = share_grad[:, 0, :]
    rows_in, pair_grad = rows_in.reshape(-1, width), pair_grad.reshape(-1, width)
    units = w_gate.shape[2]
    grad_down = dot_tn(hidden_units.reshape(-1, units), pair_grad)[None]
    grad_gate = dot_tn(rows_in, gate_grad.reshape(-1, units))[None]
    grad_up = dot_tn(rows_in, up_grad.reshape(-1, units))[None]
    grad_top = cotangent.astype(F32)
    share_center = jnp.sum(shares * share_grad, axis=0, keepdims=True)
    logit_grad = (shares * (share_grad - share_center)).astype(BF16)
    router_grad = dot_tn(second_input, logit_grad.T)
    second_grad = row_grad_sum + dot_nt(logit_grad.T, router_full)
    ffn_gain_grad = jnp.sum(second_grad * second_normed, axis=0)
    middle_grad = grad_top + norm_backward(second_grad * ffn_scale, second_normed, second_scale)
    wo_grad, wq_grad, first_part, query_gain_grad, key_gain_grad, _, expert_sum = run_backward(
        planes, across, shards, capacity, middle_grad.astype(BF16), w_output, attended, query_raw, key_raw, value,
        first_input, weights, query_gain_row, key_gain_row, cosine, sine, slots_flat, weighted,
    )
    hidden_out = (middle + expert_sum).astype(BF16)
    sum_query, sum_key, sum_value, sum_output, first_grad = run_reduce(
        planes, across, shards, wq_grad, wo_grad, first_part, w_query.shape[1], key_projection.shape[1]
    )
    attn_gain_grad = jnp.sum(first_grad * first_normed, axis=0)
    grad_in = middle_grad + norm_backward(first_grad * attn_scale, first_normed, first_scale)

    squares = jnp.stack(
        [jnp.sum(source * source), jnp.sum(branch * branch), jnp.sum(expert_sum * expert_sum), jnp.sum(grad_in * grad_in)]
    )
    mine = width // device_count
    shared = jnp.concatenate([query_gain_grad[0], key_gain_grad[0], squares])
    parts = jnp.concatenate(
        [
            router_grad.reshape(device_count, mine * experts),
            ffn_gain_grad.reshape(device_count, mine),
            attn_gain_grad.reshape(device_count, mine),
            jnp.broadcast_to(shared[None, :], (device_count, shared.shape[0])),
        ],
        axis=1,
    )
    length = parts.shape[1]
    padded = -(-length // 1024) * 1024
    parts = jnp.pad(parts, ((0, 0), (0, padded - length))).reshape(device_count, padded // 128, 128)
    summed = run_total(planes, across, shards, parts).reshape(-1)
    sum_router = summed[: mine * experts].reshape(mine, experts)
    sum_ffn = summed[mine * experts : mine * (experts + 1)]
    sum_attn = summed[mine * (experts + 1) : mine * (experts + 2)]
    totals = summed[mine * (experts + 2) : length]
    root_mean_squares = jnp.sqrt(totals[2 * head_size :] / (tokens_here * device_count * width))
    return (
        hidden_out,
        grad_in,
        sum_attn,
        sum_query,
        sum_key,
        sum_value,
        totals[:head_size],
        totals[head_size : 2 * head_size],
        sum_output,
        sum_ffn,
        sum_router,
        grad_gate,
        grad_up,
        grad_down,
        root_mean_squares,
    )


def solution(mesh):
    rings, shards = mesh.shape["ep"], mesh.shape["ws"]
    planes = 4 if rings % 4 == 0 else 1
    fine = Mesh(mesh.devices.reshape(planes, rings // planes, shards), ("z", "x", "w"))
    every = ("z", "x", "w")
    rows, deep = P(every, None), P(every, None, None)
    return jax.shard_map(
        local,
        mesh=fine,
        in_specs=(
            rows, P("w"), P("w", None), P("w", None), P("w", None), P(), P(), P("w", None), P("w"), P("w", None),
            rows, deep, deep, deep, rows,
        ),
        out_specs=(
            rows, rows, P(every), rows, rows, rows, P(), P(), rows, P(every), rows, deep, deep, deep, P(),
        ),
        check_vma=False,
    )
```

```python
import functools

import jax
import jax.numpy as jnp
from jax import lax
from jax.experimental import pallas as pl
from jax.experimental.pallas import tpu as pltpu
from jax.sharding import Mesh
from jax.sharding import PartitionSpec as P

BLOCK = 256
EPS = 1e-06
ROPE_BASE = 1000000.0
F32 = jnp.float32
BF16 = jnp.bfloat16
VMEM_LIMIT = 62 * 1024 * 1024


def dot(left, right):
    return jnp.dot(left, right, preferred_element_type=F32)


def dot_tn(left, right):
    return lax.dot_general(left, right, (((0,), (0,)), ((), ())), preferred_element_type=F32)


def dot_nt(left, right):
    return lax.dot_general(left, right, (((1,), (1,)), ((), ())), preferred_element_type=F32)


def rope_tables(seq_length, head_size):
    indices = jnp.arange(head_size // 2, dtype=F32)
    frequency = ROPE_BASE ** (-2.0 * indices / head_size)
    angles = jnp.arange(seq_length, dtype=F32)[:, None] * frequency[None, :]
    cosine, sine = jnp.cos(angles), jnp.sin(angles)
    return jnp.concatenate([cosine, cosine], axis=1), jnp.concatenate([-sine, sine], axis=1)


def norm_forward(values):
    scaling = lax.rsqrt(jnp.mean(values * values, axis=-1, keepdims=True) + EPS)
    return values * scaling, scaling


def norm_backward(grad_normed, normed, scaling):
    return scaling * (grad_normed - normed * jnp.mean(grad_normed * normed, axis=-1, keepdims=True))


def half_turn(values):
    return pltpu.roll(values, values.shape[-1] // 2, 1)


def rotate(values, cosine, signed_sine):
    return values * cosine + half_turn(values) * signed_sine


def unrotate(grads, cosine, signed_sine):
    return grads * cosine - half_turn(grads) * signed_sine


MESH = pl.DeviceIdType.MESH


def remote(source, target, send, recv, device):
    return pltpu.make_async_remote_copy(
        src_ref=source, dst_ref=target, send_sem=send, recv_sem=recv, device_id=device, device_id_type=MESH
    )


def wait_bytes(ref, sem):
    pltpu.make_async_copy(ref, ref, sem).wait()


def line_order(z, planes, step):
    low = jnp.minimum(z, planes - 1 - z)
    paired = (step <= 2 * low).astype(jnp.int32)
    hop = paired * ((step + 1) // 2) + (1 - paired) * (step - low)
    longer = (z > planes - 1 - z).astype(jnp.int32)
    below = paired * (step % 2) + (1 - paired) * longer
    return z + hop - 2 * below * hop, hop, below


def greet_plane_and_line(planes, across, shards):
    z, x, w = lax.axis_index("z"), lax.axis_index("x"), lax.axis_index("w")
    in_plane = across * shards
    me = x * shards + w
    barrier = pltpu.get_barrier_semaphore()

    @pl.loop(1, in_plane)
    def _(offset):
        index = (me + offset) % in_plane
        pl.semaphore_signal(barrier, inc=1, device_id=(z, index // shards, index % shards), device_id_type=MESH)

    @pl.loop(1, planes)
    def _(offset):
        pl.semaphore_signal(barrier, inc=1, device_id=((z + offset) % planes, x, w), device_id_type=MESH)

    pl.semaphore_wait(barrier, in_plane + planes - 2)


def attention_forward(
    planes, across, shards, capacity, heads_a_step,
    own_ref, small_ref, routes_ref, top_ref, wq_hbm, wk_hbm, wv_hbm, query_gain_ref, key_gain_ref, cosine_ref, sine_ref, wo_ref,
    input_ref, query_raw_ref, key_raw_ref, value_ref, attended_ref, branch_ref, slots_ref, my_slots_ref, small_hbm,
    weights_hbm, top_rows_hbm,
    hidden, small_in, weights, key_rot_ref, routes_in, far_slots, plane_rows, stage, chosen, pair_out, far_out,
    gather_send, gather_recv, gain_send, gain_recv, weight_send, weight_recv, route_send, route_recv, plane_route_send,
    plane_route_recv, far_send, far_recv,
    line_send, line_recv, top_send, top_recv, pair_send, pair_recv, store_sem, small_sem,
):
    step = pl.program_id(0)
    head_size = cosine_ref.shape[1]
    last = wo_ref.shape[0] // (heads_a_step * head_size)
    seq_length = cosine_ref.shape[0]
    blocks = seq_length // BLOCK
    factor = head_size ** (-0.5)
    z, x, w = lax.axis_index("z"), lax.axis_index("x"), lax.axis_index("w")
    in_plane = across * shards
    tokens, width = own_ref.shape
    me = x * shards + w
    depth = width // shards
    experts = planes * in_plane
    wide = heads_a_step * head_size
    chunk = 512
    targets = in_plane // 2
    pair, core = w // 2, w % 2
    sibling, opposite, other = pair * 2 + 1 - core, (1 - pair) * 2 + core, (1 - pair) * 2 + 1 - core

    def slice_of(index):
        return pl.ds(pl.multiple_of(index * capacity, 16), capacity)

    def tokens_of(index):
        return pl.ds(pl.multiple_of(index * tokens, tokens), tokens)

    def gather_copy(kind, owner, target):
        return remote(
            hidden.at[tokens_of(owner)], hidden.at[tokens_of(owner)], gather_send.at[kind], gather_recv.at[kind],
            (z, x, target),
        )

    def gain_copy(offset):
        return remote(small_ref, small_in.at[w], gain_send.at[offset], gain_recv.at[w], (z, x, (w + offset) % shards))

    def columns_at(start, size):
        return pl.ds(pl.multiple_of(start, 128), size)

    my_depth = pl.ds(pl.multiple_of(w * depth, 16), depth)
    query_wide = last * wide

    def weight_pieces(piece, target):
        if piece is None:
            key_at, value_at = columns_at(target * head_size, head_size), columns_at(target * head_size, head_size)
            return [
                (wk_hbm.at[:, key_at], weights.at[my_depth, columns_at(last * wide, head_size)], last),
                (wv_hbm.at[:, value_at], weights.at[my_depth, columns_at(last * wide + head_size, head_size)], last),
            ]
        return [
            (
                wq_hbm.at[:, columns_at(target * query_wide + piece * wide, wide)],
                weights.at[my_depth, columns_at(piece * wide, wide)], piece,
            )
        ]

    def start_weights(piece):
        @pl.loop(1, shards)
        def _(offset):
            for source, goal, sem in weight_pieces(piece, (w + offset) % shards):
                remote(source, goal, weight_send.at[sem], weight_recv.at[sem], (z, x, (w + offset) % shards)).start()

        for source, goal, sem in weight_pieces(piece, w):
            pltpu.make_async_copy(source, goal, weight_recv.at[sem]).start()

    def wait_weights(piece):
        whole_piece = weights.at[:, columns_at(piece * wide, wide)]
        wait_bytes(whole_piece, weight_recv.at[piece])

    def line_copy(column, block, hop, direction):
        rows = plane_rows.at[column, block]
        return remote(
            rows, rows, line_send.at[column, direction, hop], line_recv.at[column, direction, hop],
            (z + 1 - 2 * direction, x, w),
        )

    def start_line(column, block, hop, upward, downward):
        @pl.when(upward & (z + 1 < planes))
        def _():
            line_copy(column, block, hop, 0).start()

        @pl.when(downward & (z > 0))
        def _():
            line_copy(column, block, hop, 1).start()

    def relay(column, turn):
        block, hop, below = line_order(z, planes, turn)
        wait_bytes(plane_rows.at[column, block], line_recv.at[column, 1 - below, hop])
        start_line(column, block, hop + 1, below == 1, below == 0)

    expert_of = z * in_plane + lax.broadcasted_iota(jnp.int32, (in_plane, tokens), 0)
    earlier = (
        lax.broadcasted_iota(jnp.int32, (tokens, tokens), 0) < lax.broadcasted_iota(jnp.int32, (tokens, tokens), 1)
    ).astype(F32).astype(BF16)
    slot_ids = lax.broadcasted_iota(jnp.int32, (capacity, tokens), 0)

    def fill_slots(column, table):
        @pl.loop(0, planes)
        def _(block):
            hits = jnp.zeros((in_plane, tokens), F32)
            for k in range(routes_ref.shape[0]):
                hits += (routes_in[column, block, k : k + 1, :] == expert_of).astype(F32)
            ranks = dot(hits.astype(BF16), earlier).astype(jnp.int32)
            slots = jnp.where(hits > 0.0, ranks, -1)
            for index in range(in_plane):
                table[block * in_plane + index] = slots[index : index + 1, :]

    def pack(column, turn, table):
        block, _, _ = line_order(z, planes, turn)

        def index_of(target):
            return (target // 2) * shards + pair * 2 + target % 2

        for target in range(targets):
            slots = table[block * in_plane + index_of(target)]
            chosen[target * capacity : (target + 1) * capacity, :] = (slot_ids == slots).astype(F32).astype(BF16)

        @pl.loop(0, width // chunk)
        def _(part):
            here = pl.ds(pl.multiple_of(part * chunk, chunk), chunk)
            stage[column, turn, :, here] = dot(chosen[...], plane_rows[column, block, :, here]).astype(BF16)

        source = x * shards + (w if column == 0 else opposite)
        mine = x * 2 + core

        @pl.loop(1, targets)
        def _(offset):
            target = (mine + offset) % targets
            remote(
                stage.at[column, turn, slice_of(target)], top_rows_hbm.at[block, slice_of(source)],
                top_send.at[column, turn], top_recv.at[block], (z, target // 2, pair * 2 + target % 2),
            ).start()

        pltpu.make_async_copy(
            stage.at[column, turn, slice_of(mine)], top_rows_hbm.at[block, slice_of(source)], top_recv.at[block]
        ).start()

    def route_copy(offset):
        return remote(
            routes_ref, routes_in.at[me, z], route_send.at[offset], route_recv.at[z], ((z + offset) % planes, x, w)
        )

    far_top = remote(top_ref, plane_rows.at[1, z], far_send, far_recv, (z, x, opposite))
    opposite_me = x * shards + opposite

    def plane_route_copy(index):
        return remote(
            routes_in.at[me], routes_in.at[me], plane_route_send, plane_route_recv.at[me],
            (z, index // shards, index % shards),
        )

    def fill_my_slots():
        my_expert = z * in_plane + me

        @pl.loop(0, planes)
        def _(block):
            hits = jnp.concatenate(
                [
                    jnp.max((routes_in[index, block] == my_expert).astype(F32), axis=0, keepdims=True)
                    for index in range(in_plane)
                ],
                axis=0,
            )
            ranks = dot(hits.astype(BF16), earlier).astype(jnp.int32)
            slots = jnp.where(hits > 0.0, ranks, -1)
            for index in range(in_plane):
                my_slots_ref[block * in_plane + index] = slots[index : index + 1, :]

    @pl.when(step == 0)
    def _():
        greet_plane_and_line(planes, across, shards)
        hidden[tokens_of(w), :] = own_ref[...]
        gather_copy(1, w, opposite).start()

        @pl.loop(1, shards)
        def _(offset):
            gain_copy(offset).start()

        @pl.loop(1, planes)
        def _(offset):
            route_copy(offset).start()

        plane_rows[0, z] = top_ref[...]
        start_line(0, z, 1, True, True)
        gather_copy(0, w, sibling).start()
        start_weights(None)
        start_weights(0)
        small_in[w] = small_ref[...]
        routes_in[me, z] = routes_ref[...]

        @pl.loop(1, planes)
        def _(offset):
            source = (z + offset) % planes
            wait_bytes(routes_in.at[me, source], route_recv.at[source])

        @pl.loop(1, in_plane)
        def _(offset):
            plane_route_copy((me + offset) % in_plane).start()

        fill_slots(me, slots_ref)
        pack(0, 0, slots_ref)
        wait_bytes(hidden.at[tokens_of(opposite)], gather_recv.at[1])
        gather_copy(2, opposite, sibling).start()
        far_top.start()
        start_weights(1)
        relay(0, 1)
        wait_bytes(hidden.at[tokens_of(sibling)], gather_recv.at[0])
        wait_bytes(hidden.at[tokens_of(other)], gather_recv.at[2])

        @pl.loop(1, shards)
        def _(offset):
            source = (w + offset) % shards
            wait_bytes(small_in.at[source], gain_recv.at[source])

        for block in range(blocks):
            rows = pl.ds(block * BLOCK, BLOCK)
            normed, _ = norm_forward(hidden[rows, :].astype(F32))
            for part in range(shards):
                here = slice(part * depth, (part + 1) * depth)
                input_ref[rows, here] = (normed[:, here] * small_in[part, experts + 1 : experts + 2, :]).astype(BF16)
        pack(0, 1, slots_ref)
        wait_weights(last)
        for block in range(blocks):
            rows = pl.ds(block * BLOCK, BLOCK)
            key_value = dot(input_ref[rows, :], weights[:, columns_at(last * wide, wide)])
            key_raw = key_value[:, :head_size]
            key_raw_ref[rows, :] = key_raw
            value_ref[rows, :] = key_value[:, head_size:].astype(BF16)
            key_normed, _ = norm_forward(key_raw)
            key_rot_ref[rows, :] = rotate(
                key_normed * key_gain_ref[...], cosine_ref[rows, :], sine_ref[rows, :]
            ).astype(BF16)
        relay(0, 2)

    for piece in range(2, last):

        @pl.when(step == piece - 2)
        def _():
            wait_weights(piece - 2)
            if piece == last - 1:
                for kind in range(3):
                    wait_bytes(hidden.at[tokens_of(w)], gather_send.at[kind])
            start_weights(piece)

    @pl.when((step >= last - 2) & (step < last))
    def _():
        wait_weights(step)

    @pl.when(step < last)
    def _():
        here = columns_at(step * wide, wide)
        for block in range(blocks):
            rows = pl.ds(block * BLOCK, BLOCK)
            seen = pl.ds(0, (block + 1) * BLOCK)
            query_raw = dot(input_ref[rows, :], weights[:, here])
            query_raw_ref[rows, :] = query_raw
            parts = []
            for head in range(heads_a_step):
                columns = slice(head * head_size, (head + 1) * head_size)
                query_normed, _ = norm_forward(query_raw[:, columns])
                query_rot = rotate(
                    query_normed * query_gain_ref[...], cosine_ref[rows, :], sine_ref[rows, :]
                ).astype(BF16)
                scores = dot_nt(query_rot, key_rot_ref[seen, :]) * factor
                exponent = jnp.exp(scores - jnp.max(scores, axis=-1, keepdims=True))
                probs = (exponent / jnp.sum(exponent, axis=-1, keepdims=True)).astype(BF16)
                parts.append(dot(probs, value_ref[seen, :]).astype(BF16))
            attended_ref[rows, here] = jnp.concatenate(parts, axis=1)

    @pl.when(step == 0)
    def _():
        pack(0, 2, slots_ref)
        wait_bytes(routes_in.at[opposite_me], plane_route_recv.at[opposite_me])
        fill_slots(opposite_me, far_slots)
        wait_bytes(plane_rows.at[1, z], far_recv)
        start_line(1, z, 1, True, True)
        relay(0, 3)
        pack(1, 0, far_slots)

    @pl.when(step == 1)
    def _():
        pack(0, 3, slots_ref)
        relay(1, 1)

    @pl.when(step == 2)
    def _():
        pack(1, 1, far_slots)

    @pl.when(step == 3)
    def _():
        relay(1, 2)

    def project(owner, goal, added):
        rows = tokens_of(owner)

        @pl.loop(0, width // chunk)
        def _(part):
            here = pl.ds(pl.multiple_of(part * chunk, chunk), chunk)
            value = dot(attended_ref[rows, :], wo_ref[:, here])
            if added is not None:
                value += hidden[added, here].astype(F32)
            goal[:, here] = value.astype(goal.dtype)

    def pair_copy(kind):
        at = pl.ds(kind * tokens, tokens)
        return remote(pair_out.at[kind], hidden.at[at], pair_send.at[kind], pair_recv.at[kind], (z, x, sibling))

    far_at = pl.ds(2 * tokens, tokens)
    far_copy = remote(far_out, hidden.at[far_at], pair_send.at[2], pair_recv.at[2], (z, x, opposite))

    @pl.when(step == last)
    def _():
        store = pltpu.make_async_copy(weights, weights_hbm, store_sem)
        store.start()
        small_store = pltpu.make_async_copy(small_in, small_hbm, small_sem)
        small_store.start()
        project(other, pair_out.at[0], None)
        pair_copy(0).start()
        project(sibling, pair_out.at[1], None)
        pair_copy(1).start()
        wait_bytes(hidden.at[pl.ds(0, tokens)], pair_recv.at[0])
        project(opposite, far_out, pl.ds(0, tokens))
        far_copy.start()
        wait_bytes(hidden.at[pl.ds(tokens, tokens)], pair_recv.at[1])
        project(w, branch_ref, pl.ds(tokens, tokens))
        pack(1, 2, far_slots)

        @pl.loop(1, in_plane)
        def _(offset):
            index = (me + offset) % in_plane

            @pl.when(index != opposite_me)
            def _():
                wait_bytes(routes_in.at[index], plane_route_recv.at[index])

        fill_my_slots()
        relay(1, 3)
        pack(1, 3, far_slots)
        wait_bytes(hidden.at[far_at], pair_recv.at[2])
        branch_ref[...] += hidden[far_at, :].astype(F32)

        @pl.loop(0, planes)
        def _(block):
            wait_bytes(top_rows_hbm.at[block], top_recv.at[block])
            if targets > 1:
                for column in range(2):
                    wait_bytes(stage.at[column, 0, pl.ds(0, (targets - 1) * capacity)], top_send.at[column, block])

        for kind in range(3):
            wait_bytes(far_out, pair_send.at[kind])

        @pl.loop(1, shards)
        def _(offset):
            wait_bytes(small_in.at[w], gain_send.at[offset])

        @pl.loop(1, planes)
        def _(offset):
            wait_bytes(routes_in.at[0, 0], route_send.at[offset])

        wait_bytes(routes_in.at[pl.ds(0, in_plane - 1)], plane_route_send)
        wait_bytes(plane_rows.at[1, 0], far_send)

        @pl.loop(0, last + 1)
        def _(piece):
            wait_bytes(weights.at[pl.ds(0, (shards - 1) * depth), pl.ds(0, wide)], weight_send.at[piece])

        for column in range(2):
            for hop in range(1, planes):

                @pl.when((z - (hop - 1) >= 0) & (z + 1 < planes))
                def _():
                    wait_bytes(plane_rows.at[0, 0], line_send.at[column, 0, hop])

                @pl.when((z + (hop - 1) < planes) & (z > 0))
                def _():
                    wait_bytes(plane_rows.at[0, 0], line_send.at[column, 1, hop])

        store.wait()
        small_store.wait()


def attention_backward(
    planes, across, shards, capacity, heads_a_step,
    own_grad_ref, wo_ref, attended_ref, query_raw_ref, key_raw_ref, value_ref, input_ref, wq_ref,
    query_gain_ref, key_gain_ref, cosine_ref, sine_ref, slots_ref, weighted_hbm,
    wo_grad_ref, wq_grad_ref, first_grad_ref, query_gain_grad_ref, key_gain_grad_ref, returned_hbm, expert_sum_ref,
    total_ref, key_rot_ref, key_grad_ref, value_grad_ref, query_grad_ref, turned_ref, grad_ref,
    rows, chosen, partial_out, partial_in,
    gather_send, gather_recv, back_send, back_recv, sum_send, sum_recv, load_sem,
):
    step = pl.program_id(0)
    last = pl.num_programs(0) - 1
    head_size = cosine_ref.shape[1]
    seq_length = cosine_ref.shape[0]
    blocks = seq_length // BLOCK
    factor = head_size ** (-0.5)
    z, x, w = lax.axis_index("z"), lax.axis_index("x"), lax.axis_index("w")
    in_plane = across * shards
    me = x * shards + w
    tokens, width = own_grad_ref.shape
    count = in_plane * capacity
    chunk = 512
    pair, core = w // 2, w % 2
    sibling, opposite, other = pair * 2 + 1 - core, (1 - pair) * 2 + core, (1 - pair) * 2 + 1 - core

    def slice_of(index):
        return pl.ds(pl.multiple_of(index * capacity, 16), capacity)

    def tokens_of(index):
        return pl.ds(pl.multiple_of(index * tokens, tokens), tokens)

    def gather_copy(kind, owner, target):
        return remote(
            grad_ref.at[tokens_of(owner)], grad_ref.at[tokens_of(owner)], gather_send.at[kind], gather_recv.at[kind],
            (z, x, target),
        )

    def back_copy(block, index):
        return remote(
            weighted_hbm.at[block, slice_of(index)], returned_hbm.at[block, slice_of(me)],
            back_send.at[block], back_recv.at[block], (z, index // shards, index % shards),
        )

    def start_back(turn, near, far):
        block, _, _ = line_order(z, planes, planes - 1 - turn)

        @pl.loop(1, in_plane)
        def _(offset):
            index = (me + offset) % in_plane
            beside = (index % shards) // 2 == pair

            @pl.when((beside & near) | (jnp.logical_not(beside) & far))
            def _():
                back_copy(block, index).start()

        @pl.when(near)
        def _():
            pltpu.make_async_copy(
                weighted_hbm.at[block, slice_of(me)], returned_hbm.at[block, slice_of(me)], back_recv.at[block]
            ).start()

    def sum_copy(block):
        return remote(partial_out.at[block], partial_in.at[z], sum_send.at[block], sum_recv.at[z], (block, x, w))

    @pl.when(step == 0)
    def _():
        greet_plane_and_line(planes, across, shards)
        grad_ref[tokens_of(w), :] = own_grad_ref[...]
        gather_copy(1, w, opposite).start()
        gather_copy(0, w, sibling).start()
        start_back(0, step == 0, step != 0)
        key_normed, _ = norm_forward(key_raw_ref[...])
        key_rot_ref[...] = rotate(key_normed * key_gain_ref[...], cosine_ref[...], sine_ref[...]).astype(BF16)
        key_grad_ref[...] = jnp.zeros_like(key_grad_ref)
        value_grad_ref[...] = jnp.zeros_like(value_grad_ref)
        query_gain_grad_ref[...] = jnp.zeros_like(query_gain_grad_ref)
        for block in range(blocks):
            rows_here = pl.ds(block * BLOCK, BLOCK)
            turned_ref[:, rows_here] = input_ref[rows_here, :].T
        wait_bytes(grad_ref.at[tokens_of(opposite)], gather_recv.at[1])
        gather_copy(2, opposite, sibling).start()
        start_back(0, step != 0, step == 0)
        wait_bytes(grad_ref.at[tokens_of(sibling)], gather_recv.at[0])
        wait_bytes(grad_ref.at[tokens_of(other)], gather_recv.at[2])

    @pl.when((step > 0) & (step < planes))
    def _():
        start_back(step, step > 0, step > 0)

    @pl.when(step < last)
    def _():
        wo_grad_ref[...] = dot_tn(attended_ref[...], grad_ref[...]).astype(BF16)
        for block in range(blocks):
            rows_here = pl.ds(block * BLOCK, BLOCK)
            seen = pl.ds(0, (block + 1) * BLOCK)
            attended_grad = dot_nt(grad_ref[rows_here, :], wo_ref[...]).astype(BF16)
            for head in range(heads_a_step):
                columns = slice(head * head_size, (head + 1) * head_size)
                query_normed, query_scale = norm_forward(query_raw_ref[rows_here, columns])
                cosine, sine = cosine_ref[rows_here, :], sine_ref[rows_here, :]
                query_rot = rotate(query_normed * query_gain_ref[...], cosine, sine).astype(BF16)
                head_grad = attended_grad[:, columns]
                keys, values = key_rot_ref[seen, :], value_ref[seen, :]
                scores = dot_nt(query_rot, keys) * factor
                exponent = jnp.exp(scores - jnp.max(scores, axis=-1, keepdims=True))
                probs = exponent / jnp.sum(exponent, axis=-1, keepdims=True)
                prob_grad = dot_nt(head_grad, values)
                value_grad_ref[seen, :] += dot_tn(probs.astype(BF16), head_grad)
                center = jnp.sum(probs * prob_grad, axis=-1, keepdims=True)
                score_grad = (probs * (prob_grad - center)).astype(BF16)
                key_grad_ref[seen, :] += dot_tn(score_grad, query_rot) * factor
                query_rot_grad = dot(score_grad, keys) * factor
                unrotated = unrotate(query_rot_grad, cosine, sine)
                query_gain_grad_ref[0:1, :] += jnp.sum(unrotated * query_normed, axis=0, keepdims=True)
                query_grad_ref[rows_here, columns] = norm_backward(
                    unrotated * query_gain_ref[...], query_normed, query_scale
                ).astype(BF16)
            partial = dot_nt(query_grad_ref[rows_here, :], wq_ref[...])

            @pl.when(step == 0)
            def _():
                total_ref[rows_here, :] = partial

            @pl.when(step > 0)
            def _():
                total_ref[rows_here, :] += partial

    @pl.when(step == last)
    def _():
        key_normed, key_scale = norm_forward(key_raw_ref[...])
        unrotated = unrotate(key_grad_ref[...], cosine_ref[...], sine_ref[...])
        key_gain_grad_ref[...] = jnp.zeros_like(key_gain_grad_ref)
        key_gain_grad_ref[0:1, :] = jnp.sum(unrotated * key_normed, axis=0, keepdims=True)
        key_grad = norm_backward(unrotated * key_gain_ref[...], key_normed, key_scale)
        query_grad_ref[:, :head_size] = key_grad.astype(BF16)
        query_grad_ref[:, head_size : 2 * head_size] = value_grad_ref[...].astype(BF16)
        for block in range(blocks):
            rows_here = pl.ds(block * BLOCK, BLOCK)
            first_grad_ref[rows_here, :] = (
                total_ref[rows_here, :] + dot_nt(query_grad_ref[rows_here, :], wq_ref[...])
            ).astype(BF16)

    wq_grad_ref[...] = dot(turned_ref[...], query_grad_ref[...]).astype(BF16)

    @pl.when(step >= last - planes + 1)
    def _():
        place = last - step
        block, _, _ = line_order(z, planes, place)
        wait_bytes(returned_hbm.at[block], back_recv.at[block])
        load = pltpu.make_async_copy(returned_hbm.at[block], rows, load_sem)
        load.start()
        slot_ids = lax.broadcasted_iota(jnp.int32, (capacity, tokens), 0)

        @pl.loop(0, in_plane)
        def _(index):
            slots = slots_ref[block * in_plane + index]
            chosen[slice_of(index), :] = (slot_ids == slots).astype(F32).astype(BF16)

        load.wait()

        @pl.loop(0, width // chunk)
        def _(part):
            wide = pl.ds(pl.multiple_of(part * chunk, chunk), chunk)
            summed = dot_tn(chosen[...], rows[:, wide])
            partial_out[block, :, wide] = summed.astype(BF16)

            @pl.when(place == 0)
            def _():
                expert_sum_ref[:, wide] = summed

        @pl.when(place > 0)
        def _():
            sum_copy(block).start()

    @pl.when(step == last)
    def _():
        @pl.loop(1, planes)
        def _(offset):
            source = (z + offset) % planes
            wait_bytes(partial_in.at[source], sum_recv.at[source])

            @pl.loop(0, width // chunk)
            def _(part):
                wide = pl.ds(pl.multiple_of(part * chunk, chunk), chunk)
                expert_sum_ref[:, wide] += partial_in[source, :, wide].astype(F32)

            wait_bytes(partial_out.at[source], sum_send.at[source])

        @pl.loop(0, planes)
        def _(block):
            wait_bytes(weighted_hbm.at[block, pl.ds(0, count - capacity)], back_send.at[block])

        wait_bytes(grad_ref.at[tokens_of(w)], gather_send.at[0])
        wait_bytes(grad_ref.at[tokens_of(w)], gather_send.at[1])
        wait_bytes(grad_ref.at[tokens_of(w)], gather_send.at[2])


def whole(shape):
    return pl.BlockSpec(shape, lambda step: (0,) * len(shape), pipeline_mode=pl.Buffered(1))


def run_forward(
    planes, across, shards, capacity, own, small, routes, top, w_query, w_key, w_value, query_gain, key_gain, cosine, sine, wo
):
    tokens, width = own.shape
    seq_length = tokens * shards
    head_size = query_gain.shape[1]
    heads_here = wo.shape[0] // head_size
    pair = 2
    wide = pair * head_size
    steps = heads_here // pair
    in_plane = across * shards
    count = in_plane * capacity
    hbm = pl.BlockSpec(memory_space=pl.ANY)
    dma = pltpu.SemaphoreType.DMA
    slots_shape = (planes * in_plane, 1, tokens)
    return pl.pallas_call(
        functools.partial(attention_forward, planes, across, shards, capacity, pair),
        grid=(steps + 1,),
        in_specs=[
            whole((tokens, width)),
            whole(small.shape),
            whole(routes.shape),
            whole((tokens, width)),
            hbm,
            hbm,
            hbm,
            whole((1, head_size)),
            whole((1, head_size)),
            whole((seq_length, head_size)),
            whole((seq_length, head_size)),
            whole(wo.shape),
        ],
        out_specs=[
            whole((seq_length, width)),
            pl.BlockSpec((seq_length, wide), lambda step: (0, jnp.minimum(step, steps - 1))),
            whole((seq_length, head_size)),
            whole((seq_length, head_size)),
            whole((seq_length, heads_here * head_size)),
            whole((tokens, width)),
            whole(slots_shape),
            whole(slots_shape),
            hbm,
            hbm,
            hbm,
        ],
        out_shape=[
            jax.ShapeDtypeStruct((seq_length, width), BF16),
            jax.ShapeDtypeStruct((seq_length, heads_here * head_size), F32),
            jax.ShapeDtypeStruct((seq_length, head_size), F32),
            jax.ShapeDtypeStruct((seq_length, head_size), BF16),
            jax.ShapeDtypeStruct((seq_length, heads_here * head_size), BF16),
            jax.ShapeDtypeStruct((tokens, width), F32),
            jax.ShapeDtypeStruct(slots_shape, jnp.int32),
            jax.ShapeDtypeStruct(slots_shape, jnp.int32),
            jax.ShapeDtypeStruct((shards,) + small.shape, F32),
            jax.ShapeDtypeStruct((width, (steps + 1) * wide), BF16),
            jax.ShapeDtypeStruct((planes, count, width), BF16),
        ],
        scratch_shapes=[
            pltpu.VMEM((seq_length, width), BF16),
            pltpu.VMEM((shards,) + small.shape, F32),
            pltpu.VMEM((width, (steps + 1) * wide), BF16),
            pltpu.VMEM((seq_length, head_size), BF16),
            pltpu.VMEM((in_plane, planes) + routes.shape, jnp.int32),
            pltpu.VMEM(slots_shape, jnp.int32),
            pltpu.VMEM((2, planes, tokens, width), BF16),
            pltpu.VMEM((2, planes, count // 2, width), BF16),
            pltpu.VMEM((count // 2, tokens), BF16),
            pltpu.VMEM((2, tokens, width), BF16),
            pltpu.VMEM((tokens, width), BF16),
            dma((3,)), dma((3,)), dma((shards,)), dma((shards,)), dma((steps + 1,)), dma((steps + 1,)),
            dma((planes,)), dma((planes,)), dma, dma((in_plane,)), dma, dma,
            dma((2, 2, planes + 1)), dma((2, 2, planes + 1)), dma((2, planes)), dma((planes,)), dma((3,)), dma((3,)), dma, dma,
        ],
        compiler_params=pltpu.CompilerParams(vmem_limit_bytes=VMEM_LIMIT, collective_id=5, has_side_effects=True),
        cost_estimate=pl.CostEstimate(flops=70 * 10**9, bytes_accessed=40 * 10**6, transcendentals=6 * 10**6),
    )(own, small, routes, top, w_query, w_key, w_value, query_gain, key_gain, cosine, sine, wo)


def run_backward(
    planes, across, shards, capacity, own_grad, wo, attended, query_raw, key_raw, value, first_input, weights, query_gain,
    key_gain, cosine, sine, slots, weighted,
):
    tokens, width = own_grad.shape
    seq_length = attended.shape[0]
    head_size = query_gain.shape[1]
    heads_here = wo.shape[0] // head_size
    pair = 2
    wide = pair * head_size
    steps = heads_here // pair
    count = across * shards * capacity
    hbm = pl.BlockSpec(memory_space=pl.ANY)
    dma = pltpu.SemaphoreType.DMA

    def held(step):
        return jnp.minimum(step, steps - 1)

    return pl.pallas_call(
        functools.partial(attention_backward, planes, across, shards, capacity, pair),
        grid=(steps + 1,),
        in_specs=[
            whole((tokens, width)),
            pl.BlockSpec((wide, width), lambda step: (held(step), 0)),
            pl.BlockSpec((seq_length, wide), lambda step: (0, held(step))),
            pl.BlockSpec((seq_length, wide), lambda step: (0, held(step))),
            whole((seq_length, head_size)),
            whole((seq_length, head_size)),
            whole((seq_length, width)),
            pl.BlockSpec((width, wide), lambda step: (0, step)),
            whole((1, head_size)),
            whole((1, head_size)),
            whole((seq_length, head_size)),
            whole((seq_length, head_size)),
            whole(slots.shape),
            hbm,
        ],
        out_specs=[
            pl.BlockSpec((wide, width), lambda step: (held(step), 0)),
            pl.BlockSpec((width, wide), lambda step: (0, step)),
            whole((seq_length, width)),
            whole((8, head_size)),
            whole((8, head_size)),
            hbm,
            whole((tokens, width)),
        ],
        out_shape=[
            jax.ShapeDtypeStruct((heads_here * head_size, width), BF16),
            jax.ShapeDtypeStruct((width, (steps + 1) * wide), BF16),
            jax.ShapeDtypeStruct((seq_length, width), BF16),
            jax.ShapeDtypeStruct((8, head_size), F32),
            jax.ShapeDtypeStruct((8, head_size), F32),
            jax.ShapeDtypeStruct(weighted.shape, BF16),
            jax.ShapeDtypeStruct((tokens, width), F32),
        ],
        scratch_shapes=[
            pltpu.VMEM((seq_length, width), F32),
            pltpu.VMEM((seq_length, head_size), BF16),
            pltpu.VMEM((seq_length, head_size), F32),
            pltpu.VMEM((seq_length, head_size), F32),
            pltpu.VMEM((seq_length, wide), BF16),
            pltpu.VMEM((width, seq_length), BF16),
            pltpu.VMEM((seq_length, width), BF16),
            pltpu.VMEM((count, width), BF16),
            pltpu.VMEM((count, tokens), BF16),
            pltpu.VMEM((planes, tokens, width), BF16),
            pltpu.VMEM((planes, tokens, width), BF16),
            dma((3,)), dma((3,)), dma((planes,)), dma((planes,)), dma((planes,)), dma((planes,)), dma,
        ],
        compiler_params=pltpu.CompilerParams(vmem_limit_bytes=VMEM_LIMIT, collective_id=2, has_side_effects=True),
        cost_estimate=pl.CostEstimate(flops=70 * 10**9, bytes_accessed=60 * 10**6, transcendentals=6 * 10**6),
    )(
        own_grad, wo, attended, query_raw, key_raw, value, first_input, weights, query_gain, key_gain, cosine, sine, slots,
        weighted,
    )


def reduce_kernel(
    planes, across, shards,
    wq_hbm, wo_hbm, first_hbm,
    query_ref, key_ref, value_ref, output_ref, first_ref,
    wq_parts, wo_parts, wq_out, wo_out, wq_in, wo_in, wq_total, wo_total, wq_final, wo_final, wq_home, wo_home, first_in,
    across_send, across_recv, line_send, line_recv, home_send, home_recv, swap_send, swap_recv, first_send, first_recv,
):
    z, x, w = lax.axis_index("z"), lax.axis_index("x"), lax.axis_index("w")
    rings = planes * across
    ring = z * across + x
    everyone = rings * shards
    wq_rows, wo_rows = wq_total.shape[0], wo_total.shape[0]
    mine = wq_rows // shards
    tokens = first_ref.shape[0]
    query_columns = query_ref.shape[1] // shards
    key_columns = key_ref.shape[1] // shards
    linear = ring * shards + w
    barrier = pltpu.get_barrier_semaphore()

    @pl.loop(1, everyone)
    def _(offset):
        other = (linear + offset) % everyone
        pl.semaphore_signal(
            barrier, inc=1, device_id=(other // shards // across, other // shards % across, other % shards),
            device_id_type=MESH,
        )

    pl.semaphore_wait(barrier, everyone - 1)

    def rows_of(index, size):
        return pl.ds(pl.multiple_of(index * size, 16), size)

    sources = [(wq_hbm, wq_rows, wq_parts), (wo_hbm, wo_rows, wo_parts)]

    def across_copy(kind, plane, column):
        source, rows, goal = sources[kind]
        return remote(
            source.at[rows_of(plane * across + column, rows)], goal.at[plane, x],
            across_send.at[kind, plane], across_recv.at[kind, plane], (z, column, w),
        )

    def first_copy(offset):
        target = (w + offset) % shards
        return remote(
            first_hbm.at[rows_of(target, tokens)], first_in.at[offset], first_send.at[offset], first_recv.at[offset],
            (z, x, target),
        )

    @pl.loop(1, shards)
    def _(offset):
        first_copy(offset).start()

    pltpu.make_async_copy(first_hbm.at[rows_of(w, tokens)], first_in.at[0], first_recv.at[0]).start()

    def start_across(kind, turn):
        plane, _, _ = line_order(z, planes, planes - 1 - turn)

        @pl.loop(1, across)
        def _(offset):
            across_copy(kind, plane, (x + offset) % across).start()

        source, rows, goal = sources[kind]
        pltpu.make_async_copy(
            source.at[rows_of(plane * across + x, rows)], goal.at[plane, x], across_recv.at[kind, plane]
        ).start()

    start_across(0, 0)
    start_across(1, 0)

    def wq_line_copy(plane):
        return remote(wq_out.at[plane], wq_in.at[z], line_send.at[0, plane], line_recv.at[0, z], (plane, x, w))

    def wo_line_copy(plane):
        return remote(wo_out.at[plane], wo_in.at[z], line_send.at[1, plane], line_recv.at[1, z], (plane, x, w))

    @pl.loop(0, planes)
    def _(turn):
        plane, _, _ = line_order(z, planes, planes - 1 - turn)
        wait_bytes(wq_parts.at[plane], across_recv.at[0, plane])

        @pl.when(turn < planes - 1)
        def _():
            start_across(0, turn + 1)

        wq_total[...] = wq_parts[plane, 0].astype(F32)

        @pl.loop(1, across)
        def _(column):
            wq_total[...] += wq_parts[plane, column].astype(F32)

        @pl.when(turn < planes - 1)
        def _():
            wq_out[plane] = wq_total[...].astype(BF16)
            wq_line_copy(plane).start()

        wait_bytes(wo_parts.at[plane], across_recv.at[1, plane])

        @pl.when(turn < planes - 1)
        def _():
            start_across(1, turn + 1)

        wo_total[...] = wo_parts[plane, 0].astype(F32)

        @pl.loop(1, across)
        def _(column):
            wo_total[...] += wo_parts[plane, column].astype(F32)

        @pl.when(turn < planes - 1)
        def _():
            wo_out[plane] = wo_total[...].astype(BF16)
            wo_line_copy(plane).start()

    @pl.loop(0, shards)
    def _(offset):
        wait_bytes(first_in.at[offset], first_recv.at[offset])

    first_ref[...] = first_in[0].astype(F32)

    @pl.loop(1, shards)
    def _(offset):
        first_ref[...] += first_in[offset].astype(F32)

    @pl.loop(1, planes)
    def _(turn):
        plane, _, _ = line_order(z, planes, turn)
        wait_bytes(wq_in.at[plane], line_recv.at[0, plane])
        wq_total[...] += wq_in[plane].astype(F32)

    wq_final[...] = wq_total[...].astype(BF16)

    def home_copy(offset):
        target = (w + offset) % shards
        return remote(
            wq_final.at[rows_of(target, mine)], wq_home.at[w], home_send.at[offset], home_recv.at[w], (z, x, target)
        )

    @pl.loop(1, shards)
    def _(offset):
        home_copy(offset).start()

    pltpu.make_async_copy(wq_final.at[rows_of(w, mine)], wq_home.at[w], home_recv.at[w]).start()

    @pl.loop(1, planes)
    def _(turn):
        plane, _, _ = line_order(z, planes, turn)
        wait_bytes(wo_in.at[plane], line_recv.at[1, plane])
        wo_total[...] += wo_in[plane].astype(F32)

    wo_final[...] = wo_total[...].astype(BF16)
    goal = w * rings + ring
    stays = goal == linear
    swap = remote(
        wo_final, wo_home, swap_send, swap_recv, (goal // shards // across, goal // shards % across, goal % shards)
    )

    @pl.when(jnp.logical_not(stays))
    def _():
        swap.start()

    @pl.when(stays)
    def _():
        pltpu.make_async_copy(wo_final, wo_home, swap_recv).start()

    for part in range(shards):
        wait_bytes(wq_home.at[part], home_recv.at[part])
        rows = wq_home[part].astype(F32)
        query_ref[:, part * query_columns : (part + 1) * query_columns] = rows[:, :query_columns]
        key_ref[:, part * key_columns : (part + 1) * key_columns] = rows[:, query_columns : query_columns + key_columns]
        value_ref[:, part * key_columns : (part + 1) * key_columns] = rows[:, query_columns + key_columns :]

    wait_bytes(wo_home, swap_recv)
    output_ref[...] = wo_home[...].astype(F32)

    @pl.when(jnp.logical_not(stays))
    def _():
        wait_bytes(wo_final, swap_send)

    @pl.loop(1, shards)
    def _(offset):
        wait_bytes(wq_home.at[0], home_send.at[offset])
        wait_bytes(first_in.at[0], first_send.at[offset])

    if across > 1:

        @pl.loop(0, planes)
        def _(plane):
            wait_bytes(wq_parts.at[plane, pl.ds(0, across - 1)], across_send.at[0, plane])
            wait_bytes(wo_parts.at[plane, pl.ds(0, across - 1)], across_send.at[1, plane])

    @pl.loop(1, planes)
    def _(offset):
        plane = (z + offset) % planes
        wait_bytes(wq_out.at[plane], line_send.at[0, plane])
        wait_bytes(wo_out.at[plane], line_send.at[1, plane])


def run_reduce(planes, across, shards, wq_grad, wo_grad, first_part, query_columns, key_columns):
    rings = planes * across
    everyone = rings * shards
    width = wq_grad.shape[0]
    wq_wide = wq_grad.shape[1]
    wq_rows, wo_rows = width // rings, wo_grad.shape[0] // rings
    tokens = first_part.shape[0] // shards
    mine = wq_rows // shards
    hbm = pl.BlockSpec(memory_space=pl.ANY)
    vmem = pl.BlockSpec(memory_space=pltpu.VMEM)
    dma = pltpu.SemaphoreType.DMA
    return pl.pallas_call(
        functools.partial(reduce_kernel, planes, across, shards),
        in_specs=[hbm] * 3,
        out_specs=[vmem] * 5,
        out_shape=[
            jax.ShapeDtypeStruct((mine, query_columns), F32),
            jax.ShapeDtypeStruct((mine, key_columns), F32),
            jax.ShapeDtypeStruct((mine, key_columns), F32),
            jax.ShapeDtypeStruct((wo_rows, width), F32),
            jax.ShapeDtypeStruct((tokens, width), F32),
        ],
        scratch_shapes=[
            pltpu.VMEM((planes, across, wq_rows, wq_wide), BF16),
            pltpu.VMEM((planes, across, wo_rows, width), BF16),
            pltpu.VMEM((planes, wq_rows, wq_wide), BF16),
            pltpu.VMEM((planes, wo_rows, width), BF16),
            pltpu.VMEM((planes, wq_rows, wq_wide), BF16),
            pltpu.VMEM((planes, wo_rows, width), BF16),
            pltpu.VMEM((wq_rows, wq_wide), F32),
            pltpu.VMEM((wo_rows, width), F32),
            pltpu.VMEM((wq_rows, wq_wide), BF16),
            pltpu.VMEM((wo_rows, width), BF16),
            pltpu.VMEM((shards, mine, wq_wide), BF16),
            pltpu.VMEM((wo_rows, width), BF16),
            pltpu.VMEM((shards, tokens, width), BF16),
            dma((2, planes)), dma((2, planes)), dma((2, planes)), dma((2, planes)), dma((shards,)), dma((shards,)),
            dma, dma, dma((shards,)), dma((shards,)),
        ],
        compiler_params=pltpu.CompilerParams(vmem_limit_bytes=VMEM_LIMIT, collective_id=3, has_side_effects=True),
        cost_estimate=pl.CostEstimate(flops=70 * 10**9, bytes_accessed=40 * 10**6, transcendentals=0),
    )(wq_grad, wo_grad, first_part)


def total_kernel(planes, across, shards, parts_ref, total_ref, parts_in, send, recv):
    z, x, w = lax.axis_index("z"), lax.axis_index("x"), lax.axis_index("w")
    everyone = planes * across * shards
    linear = (z * across + x) * shards + w
    barrier = pltpu.get_barrier_semaphore()

    def place(index):
        return (index // shards // across, index // shards % across, index % shards)

    @pl.loop(1, everyone)
    def _(offset):
        pl.semaphore_signal(barrier, inc=1, device_id=place((linear + offset) % everyone), device_id_type=MESH)

    pl.semaphore_wait(barrier, everyone - 1)

    @pl.loop(1, everyone)
    def _(offset):
        other = (linear + offset) % everyone
        remote(parts_ref.at[other], parts_in.at[linear], send, recv, place(other)).start()

    parts_in[linear] = parts_ref[linear]
    wait_bytes(parts_ref.at[pl.ds(0, everyone - 1)], recv)
    total_ref[...] = jnp.sum(parts_in[...], axis=0)
    wait_bytes(parts_ref.at[pl.ds(0, everyone - 1)], send)


def run_total(planes, across, shards, parts):
    everyone, rows, lanes = parts.shape
    return pl.pallas_call(
        functools.partial(total_kernel, planes, across, shards),
        in_specs=[pl.BlockSpec(memory_space=pltpu.VMEM)],
        out_specs=pl.BlockSpec(memory_space=pltpu.VMEM),
        out_shape=jax.ShapeDtypeStruct((rows, lanes), F32),
        scratch_shapes=[
            pltpu.VMEM((everyone, rows, lanes), F32), pltpu.SemaphoreType.DMA, pltpu.SemaphoreType.DMA,
        ],
        compiler_params=pltpu.CompilerParams(vmem_limit_bytes=VMEM_LIMIT, collective_id=4, has_side_effects=True),
    )(parts)


def expert_kernel(
    planes, across, shards, capacity,
    own_ref, share_ref, slots_ref, my_slots_ref, gate_ref, up_ref, down_ref, top_hbm,
    rows_hbm, back_hbm, weighted_hbm, units_hbm, gate_grad_hbm, up_grad_hbm, pair_grad_hbm, row_grad_ref, share_grad_ref,
    plane_rows, plane_shares, share_in, share_back, share_home, stage, chosen, rows, top, units,
    gate_grad, up_grad, columns, partial_in,
    line_send, line_recv, plane_share_send, plane_share_recv, out_send, out_recv, out_share_send, out_share_recv,
    back_send, back_recv, back_share_send, back_share_recv, sum_send, sum_recv, sum_share_send, sum_share_recv,
    load_sem, top_sem, store_sem,
):
    z, x, w = lax.axis_index("z"), lax.axis_index("x"), lax.axis_index("w")
    in_plane = across * shards
    me = x * shards + w
    tokens, width = own_ref.shape
    count = in_plane * capacity
    half = count // 2
    per_half = in_plane // 2
    chunk = 512

    def place(index):
        return (z, index // shards, index % shards)

    def order(step):
        return line_order(z, planes, step)

    greet_plane_and_line(planes, across, shards)

    def line_up(block, hop):
        return remote(
            plane_rows.at[block], plane_rows.at[block], line_send.at[0, hop], line_recv.at[0, hop], (z + 1, x, w)
        )

    def line_down(block, hop):
        return remote(
            plane_rows.at[block], plane_rows.at[block], line_send.at[1, hop], line_recv.at[1, hop], (z - 1, x, w)
        )

    plane_rows[z] = own_ref[...]

    @pl.when(z + 1 < planes)
    def _():
        line_up(z, 1).start()

    @pl.when(z > 0)
    def _():
        line_down(z, 1).start()

    def plane_share_copy(other):
        return remote(
            share_ref.at[pl.ds(other * in_plane, in_plane)], plane_shares.at[z],
            plane_share_send.at[other], plane_share_recv.at[z], (other, x, w),
        )

    @pl.loop(1, planes)
    def _(offset):
        plane_share_copy((z + offset) % planes).start()

    plane_shares[z] = share_ref[pl.ds(z * in_plane, in_plane)]

    def slice_of(index):
        return pl.ds(pl.multiple_of(index * capacity, 16), capacity)

    def out_copy(step, block, index):
        return remote(
            stage.at[step, slice_of(index)], rows_hbm.at[block, slice_of(me)],
            out_send.at[step], out_recv.at[step], place(index),
        )

    def out_share_copy(step, block, index):
        return remote(
            plane_shares.at[block, index], share_in.at[block, me],
            out_share_send.at[step], out_share_recv.at[step], place(index),
        )

    def back_copy(step, block, index):
        return remote(
            stage.at[step, slice_of(index)], back_hbm.at[block, slice_of(me)],
            back_send.at[step], back_recv.at[step], place(index),
        )

    def back_share_copy(step, block, index):
        return remote(
            share_back.at[block, index], share_home.at[block, me],
            back_share_send.at[step], back_share_recv.at[step], place(index),
        )

    def start_back(step, block):
        @pl.loop(1, in_plane)
        def _(offset):
            index = (me + offset) % in_plane
            back_copy(step, block, index).start()
            back_share_copy(step, block, index).start()

        pltpu.make_async_copy(stage.at[step, slice_of(me)], back_hbm.at[block, slice_of(me)], back_recv.at[step]).start()
        pltpu.make_async_copy(share_back.at[block, me], share_home.at[block, me], back_share_recv.at[step]).start()

    slot_ids = lax.broadcasted_iota(jnp.int32, (capacity, tokens), 0)

    def send_step(step):
        block, hop, below = order(step)

        @pl.when(step > 0)
        def _():
            wait_bytes(plane_rows.at[block], line_recv.at[1 - below, hop])
            wait_bytes(plane_shares.at[block], plane_share_recv.at[block])

            @pl.when((below == 1) & (z + 1 < planes))
            def _():
                line_up(block, hop + 1).start()

            @pl.when((below == 0) & (z > 0))
            def _():
                line_down(block, hop + 1).start()

        @pl.loop(0, in_plane)
        def _(index):
            slots = slots_ref[block * in_plane + index]
            chosen[step, slice_of(index), :] = (slot_ids == slots).astype(F32).astype(BF16)

        @pl.loop(0, width // chunk)
        def _(part):
            wide = pl.ds(pl.multiple_of(part * chunk, chunk), chunk)
            stage[step, :, wide] = dot(chosen[step], plane_rows[block, :, wide]).astype(BF16)

        @pl.loop(1, in_plane)
        def _(offset):
            index = (me + offset) % in_plane
            out_copy(step, block, index).start()
            out_share_copy(step, block, index).start()

        pltpu.make_async_copy(stage.at[step, slice_of(me)], rows_hbm.at[block, slice_of(me)], out_recv.at[step]).start()
        pltpu.make_async_copy(plane_shares.at[block, me], share_in.at[block, me], out_share_recv.at[step]).start()

    def expert_step(step):
        block, _, _ = order(step)

        pltpu.make_async_copy(top_hbm.at[block], top, top_sem).start()
        wait_bytes(rows_hbm.at[block], out_recv.at[step])
        load = pltpu.make_async_copy(rows_hbm.at[block], rows, load_sem)
        load.start()
        wait_bytes(share_in.at[block], out_share_recv.at[step])
        wait_bytes(stage.at[step, pl.ds(0, count - capacity)], out_send.at[step])
        wait_bytes(plane_shares.at[block, pl.ds(0, in_plane - 1)], out_share_send.at[step])

        @pl.loop(0, in_plane)
        def _(index):
            mine = slot_ids == my_slots_ref[block * in_plane + index]
            columns[slice_of(index), :] = jnp.broadcast_to(
                jnp.sum(jnp.where(mine, share_in[block, index], 0.0), axis=1, keepdims=True), (capacity, 128)
            )

        load.wait()
        wait_bytes(top, top_sem)

        @pl.loop(0, 2)
        def _(part):
            here = pl.ds(pl.multiple_of(part * half, 16), half)
            gate = dot(rows[here, :], gate_ref[...])
            up = dot(rows[here, :], up_ref[...])
            sigmoid = 1.0 / (1.0 + jnp.exp(-gate))
            active = gate * sigmoid
            hidden = (active * up).astype(BF16)
            units[here, :] = hidden
            share = columns[here, 0:1]
            total = jnp.zeros((half, 1), F32)
            for piece in range(width // chunk):
                wide = pl.ds(piece * chunk, chunk)
                pair_out = dot(hidden, down_ref[:, wide]).astype(BF16).astype(F32)
                top_rows = top[here, wide].astype(F32)
                total += jnp.sum(pair_out * top_rows, axis=1, keepdims=True)
                rows[here, wide] = (share * pair_out).astype(BF16)
                top[here, wide] = (share * top_rows).astype(BF16)
            columns[here, :] = jnp.broadcast_to(total, (half, 128))
            hidden_grad = dot_nt(top[here, :], down_ref[...])
            gate_low = (hidden_grad * up * sigmoid * (1.0 + gate * (1.0 - sigmoid))).astype(BF16)
            up_low = (hidden_grad * active).astype(BF16)
            gate_grad[here, :] = gate_low
            up_grad[here, :] = up_low
            for piece in range(width // chunk):
                wide = pl.ds(piece * chunk, chunk)
                stage[step, here, wide] = (dot_nt(gate_low, gate_ref[wide, :]) + dot_nt(up_low, up_ref[wide, :])).astype(BF16)

        @pl.loop(0, in_plane)
        def _(index):
            mine = slot_ids == my_slots_ref[block * in_plane + index]
            values = columns[slice_of(index), 0:1]
            share_back[block, index] = jnp.sum(jnp.where(mine, values, 0.0), axis=0, keepdims=True)

        @pl.when(step > 0)
        def _():
            start_back(step, block)

        stores = [
            pltpu.make_async_copy(units, units_hbm.at[block], store_sem.at[0]),
            pltpu.make_async_copy(gate_grad, gate_grad_hbm.at[block], store_sem.at[1]),
            pltpu.make_async_copy(up_grad, up_grad_hbm.at[block], store_sem.at[2]),
            pltpu.make_async_copy(top, pair_grad_hbm.at[block], store_sem.at[3]),
            pltpu.make_async_copy(rows, weighted_hbm.at[block], store_sem.at[4]),
        ]
        for store in stores:
            store.start()

        for store in stores:
            store.wait()

    @pl.loop(0, planes + 1)
    def _(step):
        @pl.when(step < planes)
        def _():
            send_step(step)

        @pl.when(step > 0)
        def _():
            expert_step(step - 1)

    start_back(0, z)

    for hop in range(1, planes):

        @pl.when((z - (hop - 1) >= 0) & (z + 1 < planes))
        def _():
            wait_bytes(plane_rows.at[0], line_send.at[0, hop])

        @pl.when((z + (hop - 1) < planes) & (z > 0))
        def _():
            wait_bytes(plane_rows.at[0], line_send.at[1, hop])

    @pl.loop(1, planes)
    def _(offset):
        wait_bytes(plane_shares.at[0], plane_share_send.at[(z + offset) % planes])

    def sum_copy(block):
        return remote(plane_rows.at[block], partial_in.at[z], sum_send.at[block], sum_recv.at[z], (block, x, w))

    def sum_share_copy(block):
        return remote(
            share_home.at[block], share_grad_ref.at[pl.ds(z * in_plane, in_plane)],
            sum_share_send.at[block], sum_share_recv.at[z], (block, x, w),
        )

    @pl.loop(0, planes)
    def _(turn):
        step = (turn + 1) % planes
        block, _, _ = order(step)
        wait_bytes(back_hbm.at[block], back_recv.at[step])
        load = pltpu.make_async_copy(back_hbm.at[block], rows, load_sem)
        load.start()
        wait_bytes(share_home.at[block], back_share_recv.at[step])
        load.wait()

        @pl.when(step > 0)
        def _():
            sum_share_copy(block).start()

            @pl.loop(0, width // chunk)
            def _(part):
                wide = pl.ds(pl.multiple_of(part * chunk, chunk), chunk)
                plane_rows[block, :, wide] = dot_tn(chosen[step], rows[:, wide]).astype(BF16)

            sum_copy(block).start()

        @pl.when(step == 0)
        def _():
            share_grad_ref[pl.ds(z * in_plane, in_plane)] = share_home[z]

            @pl.loop(0, width // chunk)
            def _(part):
                wide = pl.ds(pl.multiple_of(part * chunk, chunk), chunk)
                row_grad_ref[:, wide] = dot_tn(chosen[0], rows[:, wide])

    @pl.loop(1, planes)
    def _(offset):
        other = (z + offset) % planes
        wait_bytes(partial_in.at[other], sum_recv.at[other])
        wait_bytes(share_home.at[other], sum_share_recv.at[other])

        @pl.loop(0, width // chunk)
        def _(part):
            wide = pl.ds(pl.multiple_of(part * chunk, chunk), chunk)
            row_grad_ref[:, wide] += partial_in[other, :, wide].astype(F32)

    @pl.loop(1, planes)
    def _(offset):
        other = (z + offset) % planes
        wait_bytes(plane_rows.at[other], sum_send.at[other])
        wait_bytes(share_home.at[other], sum_share_send.at[other])

    @pl.loop(0, planes)
    def _(step):
        wait_bytes(stage.at[step, pl.ds(0, count - capacity)], back_send.at[step])
        wait_bytes(share_back.at[step, pl.ds(0, in_plane - 1)], back_share_send.at[step])


def run_experts(planes, across, shards, capacity, own, shares, slots, my_slots, w_gate, w_up, w_down, top_rows):
    tokens, width = own.shape
    in_plane = across * shards
    count = in_plane * capacity
    units = w_gate.shape[1]
    experts = planes * in_plane
    hbm = pl.BlockSpec(memory_space=pl.ANY)
    vmem = pl.BlockSpec(memory_space=pltpu.VMEM)
    dma = pltpu.SemaphoreType.DMA
    flops = 12 * planes * count * width * units
    return pl.pallas_call(
        functools.partial(expert_kernel, planes, across, shards, capacity),
        in_specs=[vmem] * 7 + [hbm],
        out_specs=[hbm] * 7 + [vmem] * 2,
        out_shape=[
            jax.ShapeDtypeStruct((planes, count, width), BF16),
            jax.ShapeDtypeStruct((planes, count, width), BF16),
            jax.ShapeDtypeStruct((planes, count, width), BF16),
            jax.ShapeDtypeStruct((planes, count, units), BF16),
            jax.ShapeDtypeStruct((planes, count, units), BF16),
            jax.ShapeDtypeStruct((planes, count, units), BF16),
            jax.ShapeDtypeStruct((planes, count, width), BF16),
            jax.ShapeDtypeStruct((tokens, width), F32),
            jax.ShapeDtypeStruct((experts, 1, tokens), F32),
        ],
        scratch_shapes=[
            pltpu.VMEM((planes, tokens, width), BF16),
            pltpu.VMEM((planes, in_plane, 1, tokens), F32),
            pltpu.VMEM((planes, in_plane, 1, tokens), F32),
            pltpu.VMEM((planes, in_plane, 1, tokens), F32),
            pltpu.VMEM((planes, in_plane, 1, tokens), F32),
            pltpu.VMEM((planes, count, width), BF16),
            pltpu.VMEM((planes, count, tokens), BF16),
            pltpu.VMEM((count, width), BF16),
            pltpu.VMEM((count, width), BF16),
            pltpu.VMEM((count, units), BF16),
            pltpu.VMEM((count, units), BF16),
            pltpu.VMEM((count, units), BF16),
            pltpu.VMEM((count, 128), F32),
            pltpu.VMEM((planes, tokens, width), BF16),
            dma((2, planes + 1)), dma((2, planes + 1)), dma((planes,)), dma((planes,)),
            dma((planes,)), dma((planes,)), dma((planes,)), dma((planes,)),
            dma((planes,)), dma((planes,)), dma((planes,)), dma((planes,)),
            dma((planes,)), dma((planes,)), dma((planes,)), dma((planes,)),
            dma, dma, dma((5,)),
        ],
        compiler_params=pltpu.CompilerParams(vmem_limit_bytes=VMEM_LIMIT, collective_id=1, has_side_effects=True),
        cost_estimate=pl.CostEstimate(flops=4 * flops, bytes_accessed=100 * 10**6, transcendentals=2 * 10**6),
    )(own, shares, slots, my_slots, w_gate, w_up, w_down, top_rows)


def local(
    hidden_in, attn_gain, w_query, key_projection, value_projection, query_gain, key_gain, w_output, ffn_gain, w_router,
    routes, w_gate, w_up, w_down, cotangent,
):
    tokens_here, width = hidden_in.shape
    head_size = query_gain.shape[0]
    top_count = routes.shape[1]
    planes, across, shards = lax.axis_size("z"), lax.axis_size("x"), lax.axis_size("w")
    rings = planes * across
    device_count = rings * shards
    in_plane = across * shards
    experts = device_count
    capacity = 5 * tokens_here * top_count // (4 * experts)
    seq_length = tokens_here * shards

    cosine, sine = rope_tables(seq_length, head_size)
    query_gain_row, key_gain_row = query_gain[None, :], key_gain[None, :]

    capacity = -(-capacity // 16) * 16
    small = jnp.concatenate([w_router.T, ffn_gain[None, :], attn_gain[None, :]], axis=0).astype(F32)
    small = jnp.pad(small, ((0, -small.shape[0] % 8), (0, 0)))
    first_input, query_raw, key_raw, value, attended, branch, slots_flat, my_slots, small_all, weights, top_rows = (
        run_forward(
        planes, across, shards, capacity, hidden_in, small, routes.T, cotangent, w_query,
        key_projection, value_projection, query_gain_row, key_gain_row, cosine, sine, w_output,
        )
    )
    small_all = small_all.transpose(1, 0, 2).reshape(small.shape[0], width)
    router_full = small_all[:experts].astype(BF16)
    ffn_scale, attn_scale = small_all[experts : experts + 1], small_all[experts + 1 : experts + 2]
    source = hidden_in.astype(F32)
    first_normed, first_scale = norm_forward(source)
    middle = source + branch
    second_normed, second_scale = norm_forward(middle)
    second_input = (second_normed * ffn_scale).astype(BF16)
    logits = dot_nt(router_full, second_input)
    expert_ids = jnp.arange(experts, dtype=jnp.int32)
    routed = jnp.any(routes.T[None, :, :] == expert_ids[:, None, None], axis=1)
    peaks = jnp.max(jnp.where(routed, logits, -jnp.inf), axis=0, keepdims=True)
    shifted = jnp.where(routed, jnp.exp(jnp.where(routed, logits - peaks, 0.0)), 0.0)
    shares = shifted / jnp.sum(shifted, axis=0, keepdims=True)

    rows_in, _, weighted, hidden_units, gate_grad, up_grad, pair_grad, row_grad_sum, share_grad = run_experts(
        planes, across, shards, capacity, second_input, shares[:, None, :], slots_flat,
        my_slots, w_gate[0], w_up[0], w_down[0],
        top_rows,
    )
    share_grad = share_grad[:, 0, :]
    rows_in, pair_grad = rows_in.reshape(-1, width), pair_grad.reshape(-1, width)
    units = w_gate.shape[2]
    grad_down = dot_tn(hidden_units.reshape(-1, units), pair_grad)[None]
    grad_gate = dot_tn(rows_in, gate_grad.reshape(-1, units))[None]
    grad_up = dot_tn(rows_in, up_grad.reshape(-1, units))[None]
    grad_top = cotangent.astype(F32)
    share_center = jnp.sum(shares * share_grad, axis=0, keepdims=True)
    logit_grad = (shares * (share_grad - share_center)).astype(BF16)
    router_grad = dot_tn(second_input, logit_grad.T)
    second_grad = row_grad_sum + dot(logit_grad.T, router_full)
    ffn_gain_grad = jnp.sum(second_grad * second_normed, axis=0)
    middle_grad = grad_top + norm_backward(second_grad * ffn_scale, second_normed, second_scale)
    wo_grad, wq_grad, first_part, query_gain_grad, key_gain_grad, _, expert_sum = run_backward(
        planes, across, shards, capacity, middle_grad.astype(BF16), w_output, attended, query_raw, key_raw, value,
        first_input, weights, query_gain_row, key_gain_row, cosine, sine, slots_flat, weighted,
    )
    hidden_out = (middle + expert_sum).astype(BF16)
    sum_query, sum_key, sum_value, sum_output, first_grad = run_reduce(
        planes, across, shards, wq_grad, wo_grad, first_part, w_query.shape[1], key_projection.shape[1]
    )
    attn_gain_grad = jnp.sum(first_grad * first_normed, axis=0)
    grad_in = middle_grad + norm_backward(first_grad * attn_scale, first_normed, first_scale)

    squares = jnp.stack(
        [jnp.sum(source * source), jnp.sum(branch * branch), jnp.sum(expert_sum * expert_sum), jnp.sum(grad_in * grad_in)]
    )
    mine = width // device_count
    shared = jnp.concatenate([query_gain_grad[0], key_gain_grad[0], squares])
    parts = jnp.concatenate(
        [
            router_grad.reshape(device_count, mine * experts),
            ffn_gain_grad.reshape(device_count, mine),
            attn_gain_grad.reshape(device_count, mine),
            jnp.broadcast_to(shared[None, :], (device_count, shared.shape[0])),
        ],
        axis=1,
    )
    length = parts.shape[1]
    padded = -(-length // 1024) * 1024
    parts = jnp.pad(parts, ((0, 0), (0, padded - length))).reshape(device_count, padded // 128, 128)
    summed = run_total(planes, across, shards, parts).reshape(-1)
    sum_router = summed[: mine * experts].reshape(mine, experts)
    sum_ffn = summed[mine * experts : mine * (experts + 1)]
    sum_attn = summed[mine * (experts + 1) : mine * (experts + 2)]
    totals = summed[mine * (experts + 2) : length]
    root_mean_squares = jnp.sqrt(totals[2 * head_size :] / (tokens_here * device_count * width))
    return (
        hidden_out,
        grad_in,
        sum_attn,
        sum_query,
        sum_key,
        sum_value,
        totals[:head_size],
        totals[head_size : 2 * head_size],
        sum_output,
        sum_ffn,
        sum_router,
        grad_gate,
        grad_up,
        grad_down,
        root_mean_squares,
    )


def solution(mesh):
    rings, shards = mesh.shape["ep"], mesh.shape["ws"]
    planes = 4 if rings % 4 == 0 else 1
    fine = Mesh(mesh.devices.reshape(planes, rings // planes, shards), ("z", "x", "w"))
    every = ("z", "x", "w")
    rows, deep = P(every, None), P(every, None, None)
    return jax.shard_map(
        local,
        mesh=fine,
        in_specs=(
            rows, P("w"), P("w", None), P("w", None), P("w", None), P(), P(), P("w", None), P("w"), P("w", None),
            rows, deep, deep, deep, rows,
        ),
        out_specs=(
            rows, rows, P(every), rows, rows, rows, P(), P(), rows, P(every), rows, deep, deep, deep, P(),
        ),
        check_vma=False,
    )
```

```python
import functools

import jax
import jax.numpy as jnp
from jax import lax
from jax.experimental import pallas as pl
from jax.experimental.pallas import tpu as pltpu
from jax.sharding import Mesh
from jax.sharding import PartitionSpec as P

BLOCK = 256
EPS = 1e-06
ROPE_BASE = 1000000.0
F32 = jnp.float32
BF16 = jnp.bfloat16
VMEM_LIMIT = 62 * 1024 * 1024


def dot(left, right):
    return jnp.dot(left, right, preferred_element_type=F32)


def dot_tn(left, right):
    return lax.dot_general(left, right, (((0,), (0,)), ((), ())), preferred_element_type=F32)


def dot_nt(left, right):
    return lax.dot_general(left, right, (((1,), (1,)), ((), ())), preferred_element_type=F32)


def rope_tables(seq_length, head_size):
    indices = jnp.arange(head_size // 2, dtype=F32)
    frequency = ROPE_BASE ** (-2.0 * indices / head_size)
    angles = jnp.arange(seq_length, dtype=F32)[:, None] * frequency[None, :]
    cosine, sine = jnp.cos(angles), jnp.sin(angles)
    return jnp.concatenate([cosine, cosine], axis=1), jnp.concatenate([-sine, sine], axis=1)


def norm_forward(values):
    scaling = lax.rsqrt(jnp.mean(values * values, axis=-1, keepdims=True) + EPS)
    return values * scaling, scaling


def norm_backward(grad_normed, normed, scaling):
    return scaling * (grad_normed - normed * jnp.mean(grad_normed * normed, axis=-1, keepdims=True))


def half_turn(values):
    return pltpu.roll(values, values.shape[-1] // 2, 1)


def rotate(values, cosine, signed_sine):
    return values * cosine + half_turn(values) * signed_sine


def unrotate(grads, cosine, signed_sine):
    return grads * cosine - half_turn(grads) * signed_sine


MESH = pl.DeviceIdType.MESH


def remote(source, target, send, recv, device):
    return pltpu.make_async_remote_copy(
        src_ref=source, dst_ref=target, send_sem=send, recv_sem=recv, device_id=device, device_id_type=MESH
    )


def wait_bytes(ref, sem):
    pltpu.make_async_copy(ref, ref, sem).wait()


def line_order(z, planes, step):
    low = jnp.minimum(z, planes - 1 - z)
    paired = (step <= 2 * low).astype(jnp.int32)
    hop = paired * ((step + 1) // 2) + (1 - paired) * (step - low)
    longer = (z > planes - 1 - z).astype(jnp.int32)
    below = paired * (step % 2) + (1 - paired) * longer
    return z + hop - 2 * below * hop, hop, below


def greet_plane_and_line(planes, across, shards):
    z, x, w = lax.axis_index("z"), lax.axis_index("x"), lax.axis_index("w")
    in_plane = across * shards
    me = x * shards + w
    barrier = pltpu.get_barrier_semaphore()

    @pl.loop(1, in_plane)
    def _(offset):
        index = (me + offset) % in_plane
        pl.semaphore_signal(barrier, inc=1, device_id=(z, index // shards, index % shards), device_id_type=MESH)

    @pl.loop(1, planes)
    def _(offset):
        pl.semaphore_signal(barrier, inc=1, device_id=((z + offset) % planes, x, w), device_id_type=MESH)

    pl.semaphore_wait(barrier, in_plane + planes - 2)


def attention_forward(
    planes, across, shards, capacity, heads_a_step,
    own_ref, small_ref, routes_ref, top_ref, wq_hbm, wk_hbm, wv_hbm, query_gain_ref, key_gain_ref, cosine_ref, sine_ref, wo_ref,
    input_ref, query_raw_ref, key_raw_ref, value_ref, attended_ref, branch_ref, slots_ref, my_slots_ref, small_hbm,
    weights_hbm, top_rows_hbm,
    hidden, small_in, weights, key_rot_ref, routes_in, far_slots, plane_rows, stage, chosen, pair_out, far_out,
    gather_send, gather_recv, small_send, small_recv, weight_send, weight_recv, route_send, route_recv, plane_route_send,
    plane_route_recv, far_send, far_recv,
    line_send, line_recv, top_send, top_recv, pair_send, pair_recv, store_sem, small_sem,
):
    step = pl.program_id(0)
    head_size = cosine_ref.shape[1]
    last = wo_ref.shape[0] // (heads_a_step * head_size)
    seq_length = cosine_ref.shape[0]
    blocks = seq_length // BLOCK
    factor = head_size ** (-0.5)
    z, x, w = lax.axis_index("z"), lax.axis_index("x"), lax.axis_index("w")
    in_plane = across * shards
    tokens, width = own_ref.shape
    me = x * shards + w
    depth = width // shards
    experts = planes * in_plane
    wide = heads_a_step * head_size
    chunk = 512
    targets = in_plane // 2
    pair, core = w // 2, w % 2
    sibling, opposite, other = pair * 2 + 1 - core, (1 - pair) * 2 + core, (1 - pair) * 2 + 1 - core

    def slice_of(index):
        return pl.ds(pl.multiple_of(index * capacity, 16), capacity)

    def tokens_of(index):
        return pl.ds(pl.multiple_of(index * tokens, tokens), tokens)

    def gather_copy(kind, owner, target):
        return remote(
            hidden.at[tokens_of(owner)], hidden.at[tokens_of(owner)], gather_send.at[kind], gather_recv.at[kind],
            (z, x, target),
        )

    def small_copy(offset):
        return remote(small_ref, small_in.at[w], small_send.at[offset], small_recv.at[w], (z, x, (w + offset) % shards))

    def columns_at(start, size):
        return pl.ds(pl.multiple_of(start, 128), size)

    my_depth = pl.ds(pl.multiple_of(w * depth, 16), depth)
    query_wide = last * wide

    def weight_pieces(piece, target):
        if piece is None:
            key_at, value_at = columns_at(target * head_size, head_size), columns_at(target * head_size, head_size)
            return [
                (wk_hbm.at[:, key_at], weights.at[my_depth, columns_at(last * wide, head_size)], last),
                (wv_hbm.at[:, value_at], weights.at[my_depth, columns_at(last * wide + head_size, head_size)], last),
            ]
        return [
            (
                wq_hbm.at[:, columns_at(target * query_wide + piece * wide, wide)],
                weights.at[my_depth, columns_at(piece * wide, wide)], piece,
            )
        ]

    def start_weights(piece):
        @pl.loop(1, shards)
        def _(offset):
            for source, goal, sem in weight_pieces(piece, (w + offset) % shards):
                remote(source, goal, weight_send.at[sem], weight_recv.at[sem], (z, x, (w + offset) % shards)).start()

        for source, goal, sem in weight_pieces(piece, w):
            pltpu.make_async_copy(source, goal, weight_recv.at[sem]).start()

    def wait_weights(piece):
        whole_piece = weights.at[:, columns_at(piece * wide, wide)]
        wait_bytes(whole_piece, weight_recv.at[piece])

    def line_copy(column, block, hop, direction):
        rows = plane_rows.at[column, block]
        return remote(
            rows, rows, line_send.at[column, direction, hop], line_recv.at[column, direction, hop],
            (z + 1 - 2 * direction, x, w),
        )

    def start_line(column, block, hop, upward, downward):
        @pl.when(upward & (z + 1 < planes))
        def _():
            line_copy(column, block, hop, 0).start()

        @pl.when(downward & (z > 0))
        def _():
            line_copy(column, block, hop, 1).start()

    def relay(column, hop):
        @pl.when(z - hop >= 0)
        def _():
            wait_bytes(plane_rows.at[column, 0], line_recv.at[column, 0, hop])

            @pl.when(z + 1 < planes)
            def _():
                line_copy(column, z - hop, hop + 1, 0).start()

        @pl.when(z + hop < planes)
        def _():
            wait_bytes(plane_rows.at[column, 0], line_recv.at[column, 1, hop])

            @pl.when(z > 0)
            def _():
                line_copy(column, z + hop, hop + 1, 1).start()

    expert_of = z * in_plane + lax.broadcasted_iota(jnp.int32, (in_plane, tokens), 0)
    earlier = (
        lax.broadcasted_iota(jnp.int32, (tokens, tokens), 0) < lax.broadcasted_iota(jnp.int32, (tokens, tokens), 1)
    ).astype(F32).astype(BF16)
    slot_ids = lax.broadcasted_iota(jnp.int32, (capacity, tokens), 0)

    def fill_slots(column, table):
        @pl.loop(0, planes)
        def _(block):
            hits = jnp.zeros((in_plane, tokens), F32)
            for k in range(routes_ref.shape[0]):
                hits += (routes_in[column, block, k : k + 1, :] == expert_of).astype(F32)
            ranks = dot(hits.astype(BF16), earlier).astype(jnp.int32)
            slots = jnp.where(hits > 0.0, ranks, -1)
            for index in range(in_plane):
                table[block * in_plane + index] = slots[index : index + 1, :]

    def pack(column, turn, table):
        block, _, _ = line_order(z, planes, turn)

        def index_of(target):
            return (target // 2) * shards + pair * 2 + target % 2

        for target in range(targets):
            slots = table[block * in_plane + index_of(target)]
            chosen[target * capacity : (target + 1) * capacity, :] = (slot_ids == slots).astype(F32).astype(BF16)

        @pl.loop(0, width // chunk)
        def _(part):
            here = pl.ds(pl.multiple_of(part * chunk, chunk), chunk)
            stage[column, turn, :, here] = dot(chosen[...], plane_rows[column, block, :, here]).astype(BF16)

        source = x * shards + (w if column == 0 else opposite)
        mine = x * 2 + core

        @pl.loop(1, targets)
        def _(offset):
            target = (mine + offset) % targets
            remote(
                stage.at[column, turn, slice_of(target)], top_rows_hbm.at[block, slice_of(source)],
                top_send.at[column, turn], top_recv.at[block], (z, target // 2, pair * 2 + target % 2),
            ).start()

        pltpu.make_async_copy(
            stage.at[column, turn, slice_of(mine)], top_rows_hbm.at[block, slice_of(source)], top_recv.at[block]
        ).start()

    def route_copy(offset):
        return remote(
            routes_ref, routes_in.at[me, z], route_send.at[offset], route_recv.at[z], ((z + offset) % planes, x, w)
        )

    far_top = remote(top_ref, plane_rows.at[1, z], far_send, far_recv, (z, x, opposite))
    opposite_me = x * shards + opposite

    def plane_route_copy(index):
        return remote(
            routes_in.at[me], routes_in.at[me], plane_route_send, plane_route_recv.at[me],
            (z, index // shards, index % shards),
        )

    def fill_my_slots():
        my_expert = z * in_plane + me

        @pl.loop(0, planes)
        def _(block):
            hits = jnp.concatenate(
                [
                    jnp.max((routes_in[index, block] == my_expert).astype(F32), axis=0, keepdims=True)
                    for index in range(in_plane)
                ],
                axis=0,
            )
            ranks = dot(hits.astype(BF16), earlier).astype(jnp.int32)
            slots = jnp.where(hits > 0.0, ranks, -1)
            for index in range(in_plane):
                my_slots_ref[block * in_plane + index] = slots[index : index + 1, :]

    @pl.when(step == 0)
    def _():
        greet_plane_and_line(planes, across, shards)
        far_top.start()

        @pl.loop(1, planes)
        def _(offset):
            route_copy(offset).start()

        @pl.loop(1, shards)
        def _(offset):
            small_copy(offset).start()

        plane_rows[0, z] = top_ref[...]
        start_line(0, z, 1, True, True)
        hidden[tokens_of(w), :] = own_ref[...]
        gather_copy(0, w, sibling).start()
        small_in[w] = small_ref[...]
        routes_in[me, z] = routes_ref[...]

        @pl.loop(1, planes)
        def _(offset):
            source = (z + offset) % planes
            wait_bytes(routes_in.at[me, source], route_recv.at[source])

        @pl.loop(1, in_plane)
        def _(offset):
            plane_route_copy((me + offset) % in_plane).start()

        fill_slots(me, slots_ref)
        pack(0, 0, slots_ref)
        gather_copy(1, w, opposite).start()
        relay(0, 1)
        wait_bytes(plane_rows.at[1, z], far_recv)
        start_line(1, z, 1, True, True)
        start_weights(None)
        wait_bytes(routes_in.at[opposite_me], plane_route_recv.at[opposite_me])
        fill_slots(opposite_me, far_slots)
        pack(1, 0, far_slots)
        wait_bytes(hidden.at[tokens_of(opposite)], gather_recv.at[1])
        gather_copy(2, opposite, sibling).start()
        start_weights(0)
        pack(0, 1, slots_ref)

        @pl.loop(1, shards)
        def _(offset):
            source = (w + offset) % shards
            wait_bytes(small_in.at[source], small_recv.at[source])

        wait_bytes(hidden.at[tokens_of(sibling)], gather_recv.at[0])
        wait_bytes(hidden.at[tokens_of(other)], gather_recv.at[2])
        for block in range(blocks):
            rows = pl.ds(block * BLOCK, BLOCK)
            normed, _ = norm_forward(hidden[rows, :].astype(F32))
            for part in range(shards):
                here = slice(part * depth, (part + 1) * depth)
                input_ref[rows, here] = (normed[:, here] * small_in[part, experts + 1 : experts + 2, :]).astype(BF16)
        relay(0, 2)
        start_weights(1)
        pack(0, 2, slots_ref)
        wait_weights(last)
        for block in range(blocks):
            rows = pl.ds(block * BLOCK, BLOCK)
            key_value = dot(input_ref[rows, :], weights[:, columns_at(last * wide, wide)])
            key_raw = key_value[:, :head_size]
            key_raw_ref[rows, :] = key_raw
            value_ref[rows, :] = key_value[:, head_size:].astype(BF16)
            key_normed, _ = norm_forward(key_raw)
            key_rot_ref[rows, :] = rotate(
                key_normed * key_gain_ref[...], cosine_ref[rows, :], sine_ref[rows, :]
            ).astype(BF16)
        relay(1, 1)
        pack(1, 1, far_slots)

    for piece in range(2, last):

        @pl.when(step == piece - 2)
        def _():
            wait_weights(piece - 2)
            if piece == last - 1:
                for kind in range(3):
                    wait_bytes(hidden.at[tokens_of(w)], gather_send.at[kind])
            start_weights(piece)

    @pl.when((step >= last - 2) & (step < last))
    def _():
        wait_weights(step)

    @pl.when(step < last)
    def _():
        here = columns_at(step * wide, wide)
        for block in range(blocks):
            rows = pl.ds(block * BLOCK, BLOCK)
            seen = pl.ds(0, (block + 1) * BLOCK)
            query_raw = dot(input_ref[rows, :], weights[:, here])
            query_raw_ref[rows, :] = query_raw
            parts = []
            for head in range(heads_a_step):
                columns = slice(head * head_size, (head + 1) * head_size)
                query_normed, _ = norm_forward(query_raw[:, columns])
                query_rot = rotate(
                    query_normed * query_gain_ref[...], cosine_ref[rows, :], sine_ref[rows, :]
                ).astype(BF16)
                scores = dot_nt(query_rot, key_rot_ref[seen, :]) * factor
                exponent = jnp.exp(scores - jnp.max(scores, axis=-1, keepdims=True))
                probs = (exponent / jnp.sum(exponent, axis=-1, keepdims=True)).astype(BF16)
                parts.append(dot(probs, value_ref[seen, :]).astype(BF16))
            attended_ref[rows, here] = jnp.concatenate(parts, axis=1)

    @pl.when(step == 1)
    def _():
        relay(0, 3)
        pack(0, 3, slots_ref)

    @pl.when(step == 2)
    def _():
        relay(1, 2)
        pack(1, 2, far_slots)

    def project(owner, goal, added):
        rows = tokens_of(owner)

        @pl.loop(0, width // chunk)
        def _(part):
            here = pl.ds(pl.multiple_of(part * chunk, chunk), chunk)
            value = dot(attended_ref[rows, :], wo_ref[:, here])
            if added is not None:
                value += hidden[added, here].astype(F32)
            goal[:, here] = value.astype(goal.dtype)

    def pair_copy(kind):
        at = pl.ds(kind * tokens, tokens)
        return remote(pair_out.at[kind], hidden.at[at], pair_send.at[kind], pair_recv.at[kind], (z, x, sibling))

    far_at = pl.ds(2 * tokens, tokens)
    far_copy = remote(far_out, hidden.at[far_at], pair_send.at[2], pair_recv.at[2], (z, x, opposite))

    @pl.when(step == last)
    def _():
        store = pltpu.make_async_copy(weights, weights_hbm, store_sem)
        store.start()
        small_store = pltpu.make_async_copy(small_in, small_hbm, small_sem)
        small_store.start()
        project(other, pair_out.at[0], None)
        pair_copy(0).start()
        project(sibling, pair_out.at[1], None)
        pair_copy(1).start()
        wait_bytes(hidden.at[pl.ds(0, tokens)], pair_recv.at[0])
        project(opposite, far_out, pl.ds(0, tokens))
        far_copy.start()
        wait_bytes(hidden.at[pl.ds(tokens, tokens)], pair_recv.at[1])
        project(w, branch_ref, pl.ds(tokens, tokens))
        @pl.loop(1, in_plane)
        def _(offset):
            index = (me + offset) % in_plane

            @pl.when(index != opposite_me)
            def _():
                wait_bytes(routes_in.at[index], plane_route_recv.at[index])

        fill_my_slots()
        relay(1, 3)
        pack(1, 3, far_slots)
        wait_bytes(hidden.at[far_at], pair_recv.at[2])
        branch_ref[...] += hidden[far_at, :].astype(F32)

        @pl.loop(0, planes)
        def _(block):
            wait_bytes(top_rows_hbm.at[block], top_recv.at[block])
            if targets > 1:
                for column in range(2):
                    wait_bytes(stage.at[column, 0, pl.ds(0, (targets - 1) * capacity)], top_send.at[column, block])

        for kind in range(3):
            wait_bytes(far_out, pair_send.at[kind])

        @pl.loop(1, shards)
        def _(offset):
            wait_bytes(small_in.at[w], small_send.at[offset])

        @pl.loop(1, planes)
        def _(offset):
            wait_bytes(routes_in.at[0, 0], route_send.at[offset])

        wait_bytes(routes_in.at[pl.ds(0, in_plane - 1)], plane_route_send)
        wait_bytes(plane_rows.at[1, 0], far_send)

        @pl.loop(0, last + 1)
        def _(piece):
            wait_bytes(weights.at[pl.ds(0, (shards - 1) * depth), pl.ds(0, wide)], weight_send.at[piece])

        for column in range(2):
            for hop in range(1, planes):

                @pl.when((z - (hop - 1) >= 0) & (z + 1 < planes))
                def _():
                    wait_bytes(plane_rows.at[0, 0], line_send.at[column, 0, hop])

                @pl.when((z + (hop - 1) < planes) & (z > 0))
                def _():
                    wait_bytes(plane_rows.at[0, 0], line_send.at[column, 1, hop])

        store.wait()
        small_store.wait()


def attention_backward(
    planes, across, shards, capacity, heads_a_step,
    own_grad_ref, wo_ref, attended_ref, query_raw_ref, key_raw_ref, value_ref, input_ref, wq_ref,
    query_gain_ref, key_gain_ref, cosine_ref, sine_ref, slots_ref, weighted_hbm,
    wo_grad_ref, wq_grad_ref, first_grad_ref, query_gain_grad_ref, key_gain_grad_ref, returned_hbm, expert_sum_ref,
    total_ref, key_rot_ref, key_grad_ref, value_grad_ref, query_grad_ref, turned_ref, grad_ref,
    rows, chosen, partial_out, partial_in,
    gather_send, gather_recv, back_send, back_recv, sum_send, sum_recv, load_sem,
):
    step = pl.program_id(0)
    last = pl.num_programs(0) - 1
    head_size = cosine_ref.shape[1]
    seq_length = cosine_ref.shape[0]
    blocks = seq_length // BLOCK
    factor = head_size ** (-0.5)
    z, x, w = lax.axis_index("z"), lax.axis_index("x"), lax.axis_index("w")
    in_plane = across * shards
    me = x * shards + w
    tokens, width = own_grad_ref.shape
    count = in_plane * capacity
    chunk = 512
    pair, core = w // 2, w % 2
    sibling, opposite, other = pair * 2 + 1 - core, (1 - pair) * 2 + core, (1 - pair) * 2 + 1 - core

    def slice_of(index):
        return pl.ds(pl.multiple_of(index * capacity, 16), capacity)

    def tokens_of(index):
        return pl.ds(pl.multiple_of(index * tokens, tokens), tokens)

    def gather_copy(kind, owner, target):
        return remote(
            grad_ref.at[tokens_of(owner)], grad_ref.at[tokens_of(owner)], gather_send.at[kind], gather_recv.at[kind],
            (z, x, target),
        )

    def back_copy(block, index):
        return remote(
            weighted_hbm.at[block, slice_of(index)], returned_hbm.at[block, slice_of(me)],
            back_send.at[block], back_recv.at[block], (z, index // shards, index % shards),
        )

    pace = [(1, 1), (2, 2), (3, 3)]

    def start_back(turn, near, far):
        block, _, _ = line_order(z, planes, planes - 1 - turn)

        @pl.loop(1, in_plane)
        def _(offset):
            index = (me + offset) % in_plane
            beside = (index % shards) // 2 == pair

            @pl.when((beside & near) | (jnp.logical_not(beside) & far))
            def _():
                back_copy(block, index).start()

        @pl.when(near)
        def _():
            pltpu.make_async_copy(
                weighted_hbm.at[block, slice_of(me)], returned_hbm.at[block, slice_of(me)], back_recv.at[block]
            ).start()

    def sum_copy(block):
        return remote(partial_out.at[block], partial_in.at[z], sum_send.at[block], sum_recv.at[z], (block, x, w))

    def combine(turn):
        place = planes - 1 - turn
        block, _, _ = line_order(z, planes, place)
        wait_bytes(returned_hbm.at[block], back_recv.at[block])
        load = pltpu.make_async_copy(returned_hbm.at[block], rows, load_sem)
        load.start()
        if place > 0:
            start_back(turn + 1, step >= 0, step >= 0)
        slot_ids = lax.broadcasted_iota(jnp.int32, (capacity, tokens), 0)

        @pl.loop(0, in_plane)
        def _(index):
            slots = slots_ref[block * in_plane + index]
            chosen[slice_of(index), :] = (slot_ids == slots).astype(F32).astype(BF16)

        load.wait()

        @pl.loop(0, width // chunk)
        def _(part):
            wide = pl.ds(pl.multiple_of(part * chunk, chunk), chunk)
            summed = dot_tn(chosen[...], rows[:, wide])
            if place > 0:
                partial_out[block, :, wide] = summed.astype(BF16)
            else:
                expert_sum_ref[:, wide] = summed

        if place > 0:
            sum_copy(block).start()

    @pl.when(step == 0)
    def _():
        greet_plane_and_line(planes, across, shards)
        grad_ref[tokens_of(w), :] = own_grad_ref[...]
        gather_copy(1, w, opposite).start()
        gather_copy(0, w, sibling).start()
        start_back(0, step == 0, step != 0)
        key_normed, _ = norm_forward(key_raw_ref[...])
        key_rot_ref[...] = rotate(key_normed * key_gain_ref[...], cosine_ref[...], sine_ref[...]).astype(BF16)
        key_grad_ref[...] = jnp.zeros_like(key_grad_ref)
        value_grad_ref[...] = jnp.zeros_like(value_grad_ref)
        query_gain_grad_ref[...] = jnp.zeros_like(query_gain_grad_ref)
        for block in range(blocks):
            rows_here = pl.ds(block * BLOCK, BLOCK)
            turned_ref[:, rows_here] = input_ref[rows_here, :].T
        wait_bytes(grad_ref.at[tokens_of(opposite)], gather_recv.at[1])
        gather_copy(2, opposite, sibling).start()
        start_back(0, step != 0, step == 0)
        wait_bytes(grad_ref.at[tokens_of(sibling)], gather_recv.at[0])
        wait_bytes(grad_ref.at[tokens_of(other)], gather_recv.at[2])

    @pl.when(step < last)
    def _():
        wo_grad_ref[...] = dot_tn(attended_ref[...], grad_ref[...]).astype(BF16)
        for block in range(blocks):
            rows_here = pl.ds(block * BLOCK, BLOCK)
            seen = pl.ds(0, (block + 1) * BLOCK)
            attended_grad = dot_nt(grad_ref[rows_here, :], wo_ref[...]).astype(BF16)
            for head in range(heads_a_step):
                columns = slice(head * head_size, (head + 1) * head_size)
                query_normed, query_scale = norm_forward(query_raw_ref[rows_here, columns])
                cosine, sine = cosine_ref[rows_here, :], sine_ref[rows_here, :]
                query_rot = rotate(query_normed * query_gain_ref[...], cosine, sine).astype(BF16)
                head_grad = attended_grad[:, columns]
                keys, values = key_rot_ref[seen, :], value_ref[seen, :]
                scores = dot_nt(query_rot, keys) * factor
                exponent = jnp.exp(scores - jnp.max(scores, axis=-1, keepdims=True))
                probs = exponent / jnp.sum(exponent, axis=-1, keepdims=True)
                prob_grad = dot_nt(head_grad, values)
                value_grad_ref[seen, :] += dot_tn(probs.astype(BF16), head_grad)
                center = jnp.sum(probs * prob_grad, axis=-1, keepdims=True)
                score_grad = (probs * (prob_grad - center)).astype(BF16)
                key_grad_ref[seen, :] += dot_tn(score_grad, query_rot) * factor
                query_rot_grad = dot(score_grad, keys) * factor
                unrotated = unrotate(query_rot_grad, cosine, sine)
                query_gain_grad_ref[0:1, :] += jnp.sum(unrotated * query_normed, axis=0, keepdims=True)
                query_grad_ref[rows_here, columns] = norm_backward(
                    unrotated * query_gain_ref[...], query_normed, query_scale
                ).astype(BF16)
            partial = dot_nt(query_grad_ref[rows_here, :], wq_ref[...])

            @pl.when(step == 0)
            def _():
                total_ref[rows_here, :] = partial

            @pl.when(step > 0)
            def _():
                total_ref[rows_here, :] += partial

            for turn, place in enumerate(pace):
                if place[1] == block:

                    @pl.when(step == place[0])
                    def _():
                        combine(turn)

    @pl.when(step == last)
    def _():
        key_normed, key_scale = norm_forward(key_raw_ref[...])
        unrotated = unrotate(key_grad_ref[...], cosine_ref[...], sine_ref[...])
        key_gain_grad_ref[...] = jnp.zeros_like(key_gain_grad_ref)
        key_gain_grad_ref[0:1, :] = jnp.sum(unrotated * key_normed, axis=0, keepdims=True)
        key_grad = norm_backward(unrotated * key_gain_ref[...], key_normed, key_scale)
        query_grad_ref[:, :head_size] = key_grad.astype(BF16)
        query_grad_ref[:, head_size : 2 * head_size] = value_grad_ref[...].astype(BF16)
        for block in range(blocks):
            rows_here = pl.ds(block * BLOCK, BLOCK)
            first_grad_ref[rows_here, :] = (
                total_ref[rows_here, :] + dot_nt(query_grad_ref[rows_here, :], wq_ref[...])
            ).astype(BF16)

    wq_grad_ref[...] = dot(turned_ref[...], query_grad_ref[...]).astype(BF16)

    @pl.when(step == last)
    def _():
        for turn in range(len(pace), planes):
            combine(turn)

        @pl.loop(1, planes)
        def _(offset):
            source = (z + offset) % planes
            wait_bytes(partial_in.at[source], sum_recv.at[source])

            @pl.loop(0, width // chunk)
            def _(part):
                wide = pl.ds(pl.multiple_of(part * chunk, chunk), chunk)
                expert_sum_ref[:, wide] += partial_in[source, :, wide].astype(F32)

            wait_bytes(partial_out.at[source], sum_send.at[source])

        @pl.loop(0, planes)
        def _(block):
            wait_bytes(weighted_hbm.at[block, pl.ds(0, count - capacity)], back_send.at[block])

        wait_bytes(grad_ref.at[tokens_of(w)], gather_send.at[0])
        wait_bytes(grad_ref.at[tokens_of(w)], gather_send.at[1])
        wait_bytes(grad_ref.at[tokens_of(w)], gather_send.at[2])


def whole(shape):
    return pl.BlockSpec(shape, lambda step: (0,) * len(shape), pipeline_mode=pl.Buffered(1))


def run_forward(
    planes, across, shards, capacity, own, small, routes, top, w_query, w_key, w_value, query_gain, key_gain, cosine, sine, wo
):
    tokens, width = own.shape
    seq_length = tokens * shards
    head_size = query_gain.shape[1]
    heads_here = wo.shape[0] // head_size
    pair = 2
    wide = pair * head_size
    steps = heads_here // pair
    in_plane = across * shards
    count = in_plane * capacity
    hbm = pl.BlockSpec(memory_space=pl.ANY)
    dma = pltpu.SemaphoreType.DMA
    slots_shape = (planes * in_plane, 1, tokens)
    return pl.pallas_call(
        functools.partial(attention_forward, planes, across, shards, capacity, pair),
        grid=(steps + 1,),
        in_specs=[
            whole((tokens, width)),
            whole(small.shape),
            whole(routes.shape),
            whole((tokens, width)),
            hbm,
            hbm,
            hbm,
            whole((1, head_size)),
            whole((1, head_size)),
            whole((seq_length, head_size)),
            whole((seq_length, head_size)),
            whole(wo.shape),
        ],
        out_specs=[
            whole((seq_length, width)),
            pl.BlockSpec((seq_length, wide), lambda step: (0, jnp.minimum(step, steps - 1))),
            whole((seq_length, head_size)),
            whole((seq_length, head_size)),
            whole((seq_length, heads_here * head_size)),
            whole((tokens, width)),
            whole(slots_shape),
            whole(slots_shape),
            hbm,
            hbm,
            hbm,
        ],
        out_shape=[
            jax.ShapeDtypeStruct((seq_length, width), BF16),
            jax.ShapeDtypeStruct((seq_length, heads_here * head_size), F32),
            jax.ShapeDtypeStruct((seq_length, head_size), F32),
            jax.ShapeDtypeStruct((seq_length, head_size), BF16),
            jax.ShapeDtypeStruct((seq_length, heads_here * head_size), BF16),
            jax.ShapeDtypeStruct((tokens, width), F32),
            jax.ShapeDtypeStruct(slots_shape, jnp.int32),
            jax.ShapeDtypeStruct(slots_shape, jnp.int32),
            jax.ShapeDtypeStruct((shards,) + small.shape, F32),
            jax.ShapeDtypeStruct((width, (steps + 1) * wide), BF16),
            jax.ShapeDtypeStruct((planes, count, width), BF16),
        ],
        scratch_shapes=[
            pltpu.VMEM((seq_length, width), BF16),
            pltpu.VMEM((shards,) + small.shape, F32),
            pltpu.VMEM((width, (steps + 1) * wide), BF16),
            pltpu.VMEM((seq_length, head_size), BF16),
            pltpu.VMEM((in_plane, planes) + routes.shape, jnp.int32),
            pltpu.VMEM(slots_shape, jnp.int32),
            pltpu.VMEM((2, planes, tokens, width), BF16),
            pltpu.VMEM((2, planes, count // 2, width), BF16),
            pltpu.VMEM((count // 2, tokens), BF16),
            pltpu.VMEM((2, tokens, width), BF16),
            pltpu.VMEM((tokens, width), BF16),
            dma((3,)), dma((3,)), dma((shards,)), dma((shards,)), dma((steps + 1,)), dma((steps + 1,)),
            dma((planes,)), dma((planes,)), dma, dma((in_plane,)), dma, dma,
            dma((2, 2, planes + 1)), dma((2, 2, planes + 1)), dma((2, planes)), dma((planes,)), dma((3,)), dma((3,)), dma, dma,
        ],
        compiler_params=pltpu.CompilerParams(vmem_limit_bytes=VMEM_LIMIT, collective_id=5, has_side_effects=True),
        cost_estimate=pl.CostEstimate(flops=70 * 10**9, bytes_accessed=40 * 10**6, transcendentals=6 * 10**6),
    )(own, small, routes, top, w_query, w_key, w_value, query_gain, key_gain, cosine, sine, wo)


def run_backward(
    planes, across, shards, capacity, own_grad, wo, attended, query_raw, key_raw, value, first_input, weights, query_gain,
    key_gain, cosine, sine, slots, weighted,
):
    tokens, width = own_grad.shape
    seq_length = attended.shape[0]
    head_size = query_gain.shape[1]
    heads_here = wo.shape[0] // head_size
    pair = 2
    wide = pair * head_size
    steps = heads_here // pair
    count = across * shards * capacity
    hbm = pl.BlockSpec(memory_space=pl.ANY)
    dma = pltpu.SemaphoreType.DMA

    def held(step):
        return jnp.minimum(step, steps - 1)

    return pl.pallas_call(
        functools.partial(attention_backward, planes, across, shards, capacity, pair),
        grid=(steps + 1,),
        in_specs=[
            whole((tokens, width)),
            pl.BlockSpec((wide, width), lambda step: (held(step), 0)),
            pl.BlockSpec((seq_length, wide), lambda step: (0, held(step))),
            pl.BlockSpec((seq_length, wide), lambda step: (0, held(step))),
            whole((seq_length, head_size)),
            whole((seq_length, head_size)),
            whole((seq_length, width)),
            pl.BlockSpec((width, wide), lambda step: (0, step)),
            whole((1, head_size)),
            whole((1, head_size)),
            whole((seq_length, head_size)),
            whole((seq_length, head_size)),
            whole(slots.shape),
            hbm,
        ],
        out_specs=[
            pl.BlockSpec((wide, width), lambda step: (held(step), 0)),
            pl.BlockSpec((width, wide), lambda step: (0, step)),
            whole((seq_length, width)),
            whole((8, head_size)),
            whole((8, head_size)),
            hbm,
            whole((tokens, width)),
        ],
        out_shape=[
            jax.ShapeDtypeStruct((heads_here * head_size, width), BF16),
            jax.ShapeDtypeStruct((width, (steps + 1) * wide), BF16),
            jax.ShapeDtypeStruct((seq_length, width), BF16),
            jax.ShapeDtypeStruct((8, head_size), F32),
            jax.ShapeDtypeStruct((8, head_size), F32),
            jax.ShapeDtypeStruct(weighted.shape, BF16),
            jax.ShapeDtypeStruct((tokens, width), F32),
        ],
        scratch_shapes=[
            pltpu.VMEM((seq_length, width), F32),
            pltpu.VMEM((seq_length, head_size), BF16),
            pltpu.VMEM((seq_length, head_size), F32),
            pltpu.VMEM((seq_length, head_size), F32),
            pltpu.VMEM((seq_length, wide), BF16),
            pltpu.VMEM((width, seq_length), BF16),
            pltpu.VMEM((seq_length, width), BF16),
            pltpu.VMEM((count, width), BF16),
            pltpu.VMEM((count, tokens), BF16),
            pltpu.VMEM((planes, tokens, width), BF16),
            pltpu.VMEM((planes, tokens, width), BF16),
            dma((3,)), dma((3,)), dma((planes,)), dma((planes,)), dma((planes,)), dma((planes,)), dma,
        ],
        compiler_params=pltpu.CompilerParams(vmem_limit_bytes=VMEM_LIMIT, collective_id=2, has_side_effects=True),
        cost_estimate=pl.CostEstimate(flops=70 * 10**9, bytes_accessed=60 * 10**6, transcendentals=6 * 10**6),
    )(
        own_grad, wo, attended, query_raw, key_raw, value, first_input, weights, query_gain, key_gain, cosine, sine, slots,
        weighted,
    )


def reduce_kernel(
    planes, across, shards,
    wq_hbm, wo_hbm, first_hbm,
    query_ref, key_ref, value_ref, output_ref, first_ref,
    wq_parts, wo_parts, wq_out, wo_out, wq_in, wo_in, wq_total, wo_total, wq_final, wo_final, wq_home, wo_home, first_in,
    across_send, across_recv, line_send, line_recv, home_send, home_recv, swap_send, swap_recv, first_send, first_recv,
):
    z, x, w = lax.axis_index("z"), lax.axis_index("x"), lax.axis_index("w")
    rings = planes * across
    ring = z * across + x
    everyone = rings * shards
    wq_rows, wo_rows = wq_total.shape[0], wo_total.shape[0]
    mine = wq_rows // shards
    tokens = first_ref.shape[0]
    query_columns = query_ref.shape[1] // shards
    key_columns = key_ref.shape[1] // shards
    linear = ring * shards + w
    barrier = pltpu.get_barrier_semaphore()

    @pl.loop(1, everyone)
    def _(offset):
        other = (linear + offset) % everyone
        pl.semaphore_signal(
            barrier, inc=1, device_id=(other // shards // across, other // shards % across, other % shards),
            device_id_type=MESH,
        )

    pl.semaphore_wait(barrier, everyone - 1)

    def rows_of(index, size):
        return pl.ds(pl.multiple_of(index * size, 16), size)

    sources = [(wq_hbm, wq_rows, wq_parts), (wo_hbm, wo_rows, wo_parts)]

    def across_copy(kind, plane, column):
        source, rows, goal = sources[kind]
        return remote(
            source.at[rows_of(plane * across + column, rows)], goal.at[plane, x],
            across_send.at[kind, plane], across_recv.at[kind, plane], (z, column, w),
        )

    def first_copy(offset):
        target = (w + offset) % shards
        return remote(
            first_hbm.at[rows_of(target, tokens)], first_in.at[offset], first_send.at[offset], first_recv.at[offset],
            (z, x, target),
        )

    @pl.loop(1, shards)
    def _(offset):
        first_copy(offset).start()

    pltpu.make_async_copy(first_hbm.at[rows_of(w, tokens)], first_in.at[0], first_recv.at[0]).start()

    def start_across(kind, turn):
        plane, _, _ = line_order(z, planes, planes - 1 - turn)

        @pl.loop(1, across)
        def _(offset):
            across_copy(kind, plane, (x + offset) % across).start()

        source, rows, goal = sources[kind]
        pltpu.make_async_copy(
            source.at[rows_of(plane * across + x, rows)], goal.at[plane, x], across_recv.at[kind, plane]
        ).start()

    start_across(0, 0)
    start_across(1, 0)

    outs, ins = [wq_out, wo_out], [wq_in, wo_in]
    totals, parts = [wq_total, wo_total], [wq_parts, wo_parts]

    def line_copy(kind, plane):
        up = (plane > z).astype(jnp.int32)
        ends = (plane == z + 2 * up - 1).astype(jnp.int32)
        slot = plane + ends * (1 - up) * (planes - plane)
        return remote(
            outs[kind].at[plane], ins[kind].at[slot], line_send.at[kind, plane], line_recv.at[kind, slot],
            (z + 2 * up - 1, x, w),
        )

    def take(kind, slot):
        wait_bytes(ins[kind].at[slot], line_recv.at[kind, slot])
        totals[kind][...] += ins[kind][slot].astype(F32)

    @pl.loop(0, planes)
    def _(turn):
        plane, _, _ = line_order(z, planes, planes - 1 - turn)
        for kind in range(2):
            wait_bytes(parts[kind].at[plane], across_recv.at[kind, plane])

            @pl.when(turn < planes - 1)
            def _():
                start_across(kind, turn + 1)

            totals[kind][...] = parts[kind][plane, 0].astype(F32)

            @pl.loop(1, across)
            def _(column):
                totals[kind][...] += parts[kind][plane, column].astype(F32)

            @pl.when(((plane > z) & (z > 0)) | ((plane < z) & (z < planes - 1)))
            def _():
                take(kind, plane)

            @pl.when(plane != z)
            def _():
                outs[kind][plane] = totals[kind][...].astype(BF16)
                line_copy(kind, plane).start()

    @pl.loop(0, shards)
    def _(offset):
        wait_bytes(first_in.at[offset], first_recv.at[offset])

    first_ref[...] = first_in[0].astype(F32)

    @pl.loop(1, shards)
    def _(offset):
        first_ref[...] += first_in[offset].astype(F32)

    def finish(kind):
        @pl.when(z > 0)
        def _():
            take(kind, z)

        @pl.when(z < planes - 1)
        def _():
            take(kind, planes)

    finish(0)
    wq_final[...] = wq_total[...].astype(BF16)

    def home_copy(offset):
        target = (w + offset) % shards
        return remote(
            wq_final.at[rows_of(target, mine)], wq_home.at[w], home_send.at[offset], home_recv.at[w], (z, x, target)
        )

    @pl.loop(1, shards)
    def _(offset):
        home_copy(offset).start()

    pltpu.make_async_copy(wq_final.at[rows_of(w, mine)], wq_home.at[w], home_recv.at[w]).start()

    finish(1)
    wo_final[...] = wo_total[...].astype(BF16)
    goal = w * rings + ring
    stays = goal == linear
    swap = remote(
        wo_final, wo_home, swap_send, swap_recv, (goal // shards // across, goal // shards % across, goal % shards)
    )

    @pl.when(jnp.logical_not(stays))
    def _():
        swap.start()

    @pl.when(stays)
    def _():
        pltpu.make_async_copy(wo_final, wo_home, swap_recv).start()

    for part in range(shards):
        wait_bytes(wq_home.at[part], home_recv.at[part])
        rows = wq_home[part].astype(F32)
        query_ref[:, part * query_columns : (part + 1) * query_columns] = rows[:, :query_columns]
        key_ref[:, part * key_columns : (part + 1) * key_columns] = rows[:, query_columns : query_columns + key_columns]
        value_ref[:, part * key_columns : (part + 1) * key_columns] = rows[:, query_columns + key_columns :]

    wait_bytes(wo_home, swap_recv)
    output_ref[...] = wo_home[...].astype(F32)

    @pl.when(jnp.logical_not(stays))
    def _():
        wait_bytes(wo_final, swap_send)

    @pl.loop(1, shards)
    def _(offset):
        wait_bytes(wq_home.at[0], home_send.at[offset])
        wait_bytes(first_in.at[0], first_send.at[offset])

    if across > 1:

        @pl.loop(0, planes)
        def _(plane):
            wait_bytes(wq_parts.at[plane, pl.ds(0, across - 1)], across_send.at[0, plane])
            wait_bytes(wo_parts.at[plane, pl.ds(0, across - 1)], across_send.at[1, plane])

    @pl.loop(1, planes)
    def _(offset):
        plane = (z + offset) % planes
        wait_bytes(wq_out.at[plane], line_send.at[0, plane])
        wait_bytes(wo_out.at[plane], line_send.at[1, plane])


def run_reduce(planes, across, shards, wq_grad, wo_grad, first_part, query_columns, key_columns):
    rings = planes * across
    everyone = rings * shards
    width = wq_grad.shape[0]
    wq_wide = wq_grad.shape[1]
    wq_rows, wo_rows = width // rings, wo_grad.shape[0] // rings
    tokens = first_part.shape[0] // shards
    mine = wq_rows // shards
    hbm = pl.BlockSpec(memory_space=pl.ANY)
    vmem = pl.BlockSpec(memory_space=pltpu.VMEM)
    dma = pltpu.SemaphoreType.DMA
    return pl.pallas_call(
        functools.partial(reduce_kernel, planes, across, shards),
        in_specs=[hbm] * 3,
        out_specs=[vmem] * 5,
        out_shape=[
            jax.ShapeDtypeStruct((mine, query_columns), F32),
            jax.ShapeDtypeStruct((mine, key_columns), F32),
            jax.ShapeDtypeStruct((mine, key_columns), F32),
            jax.ShapeDtypeStruct((wo_rows, width), F32),
            jax.ShapeDtypeStruct((tokens, width), F32),
        ],
        scratch_shapes=[
            pltpu.VMEM((planes, across, wq_rows, wq_wide), BF16),
            pltpu.VMEM((planes, across, wo_rows, width), BF16),
            pltpu.VMEM((planes, wq_rows, wq_wide), BF16),
            pltpu.VMEM((planes, wo_rows, width), BF16),
            pltpu.VMEM((planes + 1, wq_rows, wq_wide), BF16),
            pltpu.VMEM((planes + 1, wo_rows, width), BF16),
            pltpu.VMEM((wq_rows, wq_wide), F32),
            pltpu.VMEM((wo_rows, width), F32),
            pltpu.VMEM((wq_rows, wq_wide), BF16),
            pltpu.VMEM((wo_rows, width), BF16),
            pltpu.VMEM((shards, mine, wq_wide), BF16),
            pltpu.VMEM((wo_rows, width), BF16),
            pltpu.VMEM((shards, tokens, width), BF16),
            dma((2, planes)), dma((2, planes)), dma((2, planes)), dma((2, planes + 1)), dma((shards,)), dma((shards,)),
            dma, dma, dma((shards,)), dma((shards,)),
        ],
        compiler_params=pltpu.CompilerParams(vmem_limit_bytes=VMEM_LIMIT, collective_id=3, has_side_effects=True),
        cost_estimate=pl.CostEstimate(flops=70 * 10**9, bytes_accessed=40 * 10**6, transcendentals=0),
    )(wq_grad, wo_grad, first_part)


def total_kernel(planes, across, shards, parts_ref, total_ref, parts_in, send, recv):
    z, x, w = lax.axis_index("z"), lax.axis_index("x"), lax.axis_index("w")
    everyone = planes * across * shards
    linear = (z * across + x) * shards + w
    barrier = pltpu.get_barrier_semaphore()

    def place(index):
        return (index // shards // across, index // shards % across, index % shards)

    @pl.loop(1, everyone)
    def _(offset):
        pl.semaphore_signal(barrier, inc=1, device_id=place((linear + offset) % everyone), device_id_type=MESH)

    pl.semaphore_wait(barrier, everyone - 1)

    @pl.loop(1, everyone)
    def _(offset):
        other = (linear + offset) % everyone
        remote(parts_ref.at[other], parts_in.at[linear], send, recv, place(other)).start()

    parts_in[linear] = parts_ref[linear]
    wait_bytes(parts_ref.at[pl.ds(0, everyone - 1)], recv)
    total_ref[...] = jnp.sum(parts_in[...], axis=0)
    wait_bytes(parts_ref.at[pl.ds(0, everyone - 1)], send)


def run_total(planes, across, shards, parts):
    everyone, rows, lanes = parts.shape
    return pl.pallas_call(
        functools.partial(total_kernel, planes, across, shards),
        in_specs=[pl.BlockSpec(memory_space=pltpu.VMEM)],
        out_specs=pl.BlockSpec(memory_space=pltpu.VMEM),
        out_shape=jax.ShapeDtypeStruct((rows, lanes), F32),
        scratch_shapes=[
            pltpu.VMEM((everyone, rows, lanes), F32), pltpu.SemaphoreType.DMA, pltpu.SemaphoreType.DMA,
        ],
        compiler_params=pltpu.CompilerParams(vmem_limit_bytes=VMEM_LIMIT, collective_id=4, has_side_effects=True),
    )(parts)


def expert_kernel(
    planes, across, shards, capacity,
    own_ref, share_ref, slots_ref, my_slots_ref, gate_ref, up_ref, down_ref, top_hbm,
    rows_hbm, back_hbm, weighted_hbm, units_hbm, gate_grad_hbm, up_grad_hbm, pair_grad_hbm, row_grad_ref, share_grad_ref,
    plane_rows, plane_shares, share_in, share_back, share_home, stage, chosen, rows, top, units,
    gate_grad, up_grad, columns, partial_in,
    line_send, line_recv, plane_share_send, plane_share_recv, out_send, out_recv, out_share_send, out_share_recv,
    back_send, back_recv, back_share_send, back_share_recv, sum_send, sum_recv, sum_share_send, sum_share_recv,
    load_sem, top_sem, store_sem,
):
    z, x, w = lax.axis_index("z"), lax.axis_index("x"), lax.axis_index("w")
    in_plane = across * shards
    me = x * shards + w
    tokens, width = own_ref.shape
    count = in_plane * capacity
    half = count // 2
    per_half = in_plane // 2
    chunk = 512

    def place(index):
        return (z, index // shards, index % shards)

    def order(step):
        return line_order(z, planes, step)

    greet_plane_and_line(planes, across, shards)

    def line_up(block, hop):
        return remote(
            plane_rows.at[block], plane_rows.at[block], line_send.at[0, hop], line_recv.at[0, hop], (z + 1, x, w)
        )

    def line_down(block, hop):
        return remote(
            plane_rows.at[block], plane_rows.at[block], line_send.at[1, hop], line_recv.at[1, hop], (z - 1, x, w)
        )

    plane_rows[z] = own_ref[...]

    @pl.when(z + 1 < planes)
    def _():
        line_up(z, 1).start()

    @pl.when(z > 0)
    def _():
        line_down(z, 1).start()

    def plane_share_copy(other):
        return remote(
            share_ref.at[pl.ds(other * in_plane, in_plane)], plane_shares.at[z],
            plane_share_send.at[other], plane_share_recv.at[z], (other, x, w),
        )

    @pl.loop(1, planes)
    def _(offset):
        plane_share_copy((z + offset) % planes).start()

    plane_shares[z] = share_ref[pl.ds(z * in_plane, in_plane)]

    def slice_of(index):
        return pl.ds(pl.multiple_of(index * capacity, 16), capacity)

    def out_copy(step, block, index):
        return remote(
            stage.at[step, slice_of(index)], rows_hbm.at[block, slice_of(me)],
            out_send.at[step], out_recv.at[step], place(index),
        )

    def out_share_copy(step, block, index):
        return remote(
            plane_shares.at[block, index], share_in.at[block, me],
            out_share_send.at[step], out_share_recv.at[step], place(index),
        )

    def back_copy(step, block, index):
        return remote(
            stage.at[step, slice_of(index)], back_hbm.at[block, slice_of(me)],
            back_send.at[step], back_recv.at[step], place(index),
        )

    def back_share_copy(step, block, index):
        return remote(
            share_back.at[block, index], share_home.at[block, me],
            back_share_send.at[step], back_share_recv.at[step], place(index),
        )

    def start_back(step, block):
        @pl.loop(1, in_plane)
        def _(offset):
            index = (me + offset) % in_plane
            back_copy(step, block, index).start()
            back_share_copy(step, block, index).start()

        pltpu.make_async_copy(stage.at[step, slice_of(me)], back_hbm.at[block, slice_of(me)], back_recv.at[step]).start()
        pltpu.make_async_copy(share_back.at[block, me], share_home.at[block, me], back_share_recv.at[step]).start()

    slot_ids = lax.broadcasted_iota(jnp.int32, (capacity, tokens), 0)

    def pack_step(step):
        block, _, _ = order(step)

        @pl.when(step > 0)
        def _():
            @pl.when(z - step >= 0)
            def _():
                wait_bytes(plane_rows.at[0], line_recv.at[0, step])

                @pl.when(z + 1 < planes)
                def _():
                    line_up(z - step, step + 1).start()

            @pl.when(z + step < planes)
            def _():
                wait_bytes(plane_rows.at[0], line_recv.at[1, step])

                @pl.when(z > 0)
                def _():
                    line_down(z + step, step + 1).start()

            wait_bytes(plane_shares.at[block], plane_share_recv.at[block])

        @pl.loop(0, in_plane)
        def _(index):
            slots = slots_ref[block * in_plane + index]
            chosen[step, slice_of(index), :] = (slot_ids == slots).astype(F32).astype(BF16)

        @pl.loop(0, width // chunk)
        def _(part):
            wide = pl.ds(pl.multiple_of(part * chunk, chunk), chunk)
            stage[step, :, wide] = dot(chosen[step], plane_rows[block, :, wide]).astype(BF16)

    def send_step(step):
        block, _, _ = order(step)

        @pl.loop(1, in_plane)
        def _(offset):
            index = (me + offset) % in_plane
            out_copy(step, block, index).start()
            out_share_copy(step, block, index).start()

        pltpu.make_async_copy(stage.at[step, slice_of(me)], rows_hbm.at[block, slice_of(me)], out_recv.at[step]).start()
        pltpu.make_async_copy(plane_shares.at[block, me], share_in.at[block, me], out_share_recv.at[step]).start()

    def expert_step(step):
        block, _, _ = order(step)

        pltpu.make_async_copy(top_hbm.at[block], top, top_sem).start()
        wait_bytes(rows_hbm.at[block], out_recv.at[step])
        load = pltpu.make_async_copy(rows_hbm.at[block], rows, load_sem)
        load.start()

        @pl.when(step + 1 < planes)
        def _():
            send_step(step + 1)

        wait_bytes(share_in.at[block], out_share_recv.at[step])
        wait_bytes(stage.at[step, pl.ds(0, count - capacity)], out_send.at[step])
        wait_bytes(plane_shares.at[block, pl.ds(0, in_plane - 1)], out_share_send.at[step])

        @pl.loop(0, in_plane)
        def _(index):
            mine = slot_ids == my_slots_ref[block * in_plane + index]
            columns[slice_of(index), :] = jnp.broadcast_to(
                jnp.sum(jnp.where(mine, share_in[block, index], 0.0), axis=1, keepdims=True), (capacity, 128)
            )

        load.wait()
        wait_bytes(top, top_sem)

        @pl.loop(0, 2)
        def _(part):
            here = pl.ds(pl.multiple_of(part * half, 16), half)
            gate = dot(rows[here, :], gate_ref[...])
            up = dot(rows[here, :], up_ref[...])
            sigmoid = 1.0 / (1.0 + jnp.exp(-gate))
            active = gate * sigmoid
            hidden = (active * up).astype(BF16)
            units[here, :] = hidden
            share = columns[here, 0:1]
            total = jnp.zeros((half, 1), F32)
            for piece in range(width // chunk):
                wide = pl.ds(piece * chunk, chunk)
                pair_out = dot(hidden, down_ref[:, wide]).astype(BF16).astype(F32)
                top_rows = top[here, wide].astype(F32)
                total += jnp.sum(pair_out * top_rows, axis=1, keepdims=True)
                rows[here, wide] = (share * pair_out).astype(BF16)
                top[here, wide] = (share * top_rows).astype(BF16)
            columns[here, :] = jnp.broadcast_to(total, (half, 128))
            hidden_grad = dot_nt(top[here, :], down_ref[...])
            gate_low = (hidden_grad * up * sigmoid * (1.0 + gate * (1.0 - sigmoid))).astype(BF16)
            up_low = (hidden_grad * active).astype(BF16)
            gate_grad[here, :] = gate_low
            up_grad[here, :] = up_low
            for piece in range(width // chunk):
                wide = pl.ds(piece * chunk, chunk)
                stage[step, here, wide] = (dot_nt(gate_low, gate_ref[wide, :]) + dot_nt(up_low, up_ref[wide, :])).astype(BF16)

        @pl.loop(0, in_plane)
        def _(index):
            mine = slot_ids == my_slots_ref[block * in_plane + index]
            values = columns[slice_of(index), 0:1]
            share_back[block, index] = jnp.sum(jnp.where(mine, values, 0.0), axis=0, keepdims=True)

        @pl.when(step > 1)
        def _():
            start_back(step, block)

        stores = [
            pltpu.make_async_copy(units, units_hbm.at[block], store_sem.at[0]),
            pltpu.make_async_copy(gate_grad, gate_grad_hbm.at[block], store_sem.at[1]),
            pltpu.make_async_copy(up_grad, up_grad_hbm.at[block], store_sem.at[2]),
            pltpu.make_async_copy(top, pair_grad_hbm.at[block], store_sem.at[3]),
            pltpu.make_async_copy(rows, weighted_hbm.at[block], store_sem.at[4]),
        ]
        for store in stores:
            store.start()

        for store in stores:
            store.wait()

    @pl.loop(0, planes + 1)
    def _(step):
        @pl.when(step < planes)
        def _():
            pack_step(step)

        @pl.when(step == 0)
        def _():
            send_step(step)

        @pl.when(step > 0)
        def _():
            expert_step(step - 1)

    for hop in range(1, planes):

        @pl.when((z - (hop - 1) >= 0) & (z + 1 < planes))
        def _():
            wait_bytes(plane_rows.at[0], line_send.at[0, hop])

        @pl.when((z + (hop - 1) < planes) & (z > 0))
        def _():
            wait_bytes(plane_rows.at[0], line_send.at[1, hop])

    @pl.loop(1, planes)
    def _(offset):
        wait_bytes(plane_shares.at[0], plane_share_send.at[(z + offset) % planes])

    def wait_back(step):
        wait_bytes(stage.at[step, pl.ds(0, count - capacity)], back_send.at[step])
        wait_bytes(share_back.at[0, pl.ds(0, in_plane - 1)], back_share_send.at[step])

    def sum_copy(block):
        return remote(plane_rows.at[block], partial_in.at[z], sum_send.at[block], sum_recv.at[z], (block, x, w))

    def sum_share_copy(block):
        return remote(
            share_home.at[block], share_grad_ref.at[pl.ds(z * in_plane, in_plane)],
            sum_share_send.at[block], sum_share_recv.at[z], (block, x, w),
        )

    @pl.loop(0, planes)
    def _(turn):
        step = jnp.where(turn < planes - 2, turn + 2, planes - 1 - turn)
        block, _, _ = order(step)
        wait_bytes(back_hbm.at[block], back_recv.at[step])
        load = pltpu.make_async_copy(back_hbm.at[block], rows, load_sem)
        load.start()
        wait_bytes(share_home.at[block], back_share_recv.at[step])
        load.wait()

        @pl.when(step > 0)
        def _():
            sum_share_copy(block).start()

            @pl.loop(0, width // chunk)
            def _(part):
                wide = pl.ds(pl.multiple_of(part * chunk, chunk), chunk)
                plane_rows[block, :, wide] = dot_tn(chosen[step], rows[:, wide]).astype(BF16)

            sum_copy(block).start()

        @pl.when(step == 0)
        def _():
            share_grad_ref[pl.ds(z * in_plane, in_plane)] = share_home[z]

            @pl.loop(0, width // chunk)
            def _(part):
                wide = pl.ds(pl.multiple_of(part * chunk, chunk), chunk)
                row_grad_ref[:, wide] = dot_tn(chosen[0], rows[:, wide])

        @pl.when(turn == planes - 4)
        def _():
            wait_back(planes - 1)
            start_back(1, order(1)[0])

        @pl.when(turn == planes - 3)
        def _():
            wait_back(1)
            start_back(0, z)

    @pl.loop(1, planes)
    def _(offset):
        other = (z + offset) % planes
        wait_bytes(partial_in.at[other], sum_recv.at[other])
        wait_bytes(share_home.at[other], sum_share_recv.at[other])

        @pl.loop(0, width // chunk)
        def _(part):
            wide = pl.ds(pl.multiple_of(part * chunk, chunk), chunk)
            row_grad_ref[:, wide] += partial_in[other, :, wide].astype(F32)

    @pl.loop(1, planes)
    def _(offset):
        other = (z + offset) % planes
        wait_bytes(plane_rows.at[other], sum_send.at[other])
        wait_bytes(share_home.at[other], sum_share_send.at[other])

    wait_back(0)
    for step in range(2, planes - 1):
        wait_back(step)


def run_experts(planes, across, shards, capacity, own, shares, slots, my_slots, w_gate, w_up, w_down, top_rows):
    tokens, width = own.shape
    in_plane = across * shards
    count = in_plane * capacity
    units = w_gate.shape[1]
    experts = planes * in_plane
    hbm = pl.BlockSpec(memory_space=pl.ANY)
    vmem = pl.BlockSpec(memory_space=pltpu.VMEM)
    dma = pltpu.SemaphoreType.DMA
    flops = 12 * planes * count * width * units
    return pl.pallas_call(
        functools.partial(expert_kernel, planes, across, shards, capacity),
        in_specs=[vmem] * 7 + [hbm],
        out_specs=[hbm] * 7 + [vmem] * 2,
        out_shape=[
            jax.ShapeDtypeStruct((planes, count, width), BF16),
            jax.ShapeDtypeStruct((planes, count, width), BF16),
            jax.ShapeDtypeStruct((planes, count, width), BF16),
            jax.ShapeDtypeStruct((planes, count, units), BF16),
            jax.ShapeDtypeStruct((planes, count, units), BF16),
            jax.ShapeDtypeStruct((planes, count, units), BF16),
            jax.ShapeDtypeStruct((planes, count, width), BF16),
            jax.ShapeDtypeStruct((tokens, width), F32),
            jax.ShapeDtypeStruct((experts, 1, tokens), F32),
        ],
        scratch_shapes=[
            pltpu.VMEM((planes, tokens, width), BF16),
            pltpu.VMEM((planes, in_plane, 1, tokens), F32),
            pltpu.VMEM((planes, in_plane, 1, tokens), F32),
            pltpu.VMEM((planes, in_plane, 1, tokens), F32),
            pltpu.VMEM((planes, in_plane, 1, tokens), F32),
            pltpu.VMEM((planes, count, width), BF16),
            pltpu.VMEM((planes, count, tokens), BF16),
            pltpu.VMEM((count, width), BF16),
            pltpu.VMEM((count, width), BF16),
            pltpu.VMEM((count, units), BF16),
            pltpu.VMEM((count, units), BF16),
            pltpu.VMEM((count, units), BF16),
            pltpu.VMEM((count, 128), F32),
            pltpu.VMEM((planes, tokens, width), BF16),
            dma((2, planes + 1)), dma((2, planes + 1)), dma((planes,)), dma((planes,)),
            dma((planes,)), dma((planes,)), dma((planes,)), dma((planes,)),
            dma((planes,)), dma((planes,)), dma((planes,)), dma((planes,)),
            dma((planes,)), dma((planes,)), dma((planes,)), dma((planes,)),
            dma, dma, dma((5,)),
        ],
        compiler_params=pltpu.CompilerParams(vmem_limit_bytes=VMEM_LIMIT, collective_id=1, has_side_effects=True),
        cost_estimate=pl.CostEstimate(flops=4 * flops, bytes_accessed=100 * 10**6, transcendentals=2 * 10**6),
    )(own, shares, slots, my_slots, w_gate, w_up, w_down, top_rows)


def local(
    hidden_in, attn_gain, w_query, key_projection, value_projection, query_gain, key_gain, w_output, ffn_gain, w_router,
    routes, w_gate, w_up, w_down, cotangent,
):
    tokens_here, width = hidden_in.shape
    head_size = query_gain.shape[0]
    top_count = routes.shape[1]
    planes, across, shards = lax.axis_size("z"), lax.axis_size("x"), lax.axis_size("w")
    rings = planes * across
    device_count = rings * shards
    in_plane = across * shards
    experts = device_count
    capacity = 5 * tokens_here * top_count // (4 * experts)
    seq_length = tokens_here * shards

    cosine, sine = rope_tables(seq_length, head_size)
    query_gain_row, key_gain_row = query_gain[None, :], key_gain[None, :]

    capacity = -(-capacity // 16) * 16
    small = jnp.concatenate([w_router.T, ffn_gain[None, :], attn_gain[None, :]], axis=0).astype(F32)
    small = jnp.pad(small, ((0, -small.shape[0] % 8), (0, 0)))
    first_input, query_raw, key_raw, value, attended, branch, slots_flat, my_slots, small_all, weights, top_rows = (
        run_forward(
        planes, across, shards, capacity, hidden_in, small, routes.T, cotangent, w_query,
        key_projection, value_projection, query_gain_row, key_gain_row, cosine, sine, w_output,
        )
    )
    small_all = small_all.transpose(1, 0, 2).reshape(small.shape[0], width)
    router_full = small_all[:experts].astype(BF16)
    ffn_scale, attn_scale = small_all[experts : experts + 1], small_all[experts + 1 : experts + 2]
    source = hidden_in.astype(F32)
    first_normed, first_scale = norm_forward(source)
    middle = source + branch
    second_normed, second_scale = norm_forward(middle)
    second_input = (second_normed * ffn_scale).astype(BF16)
    logits = dot_nt(router_full, second_input)
    expert_ids = jnp.arange(experts, dtype=jnp.int32)
    routed = jnp.any(routes.T[None, :, :] == expert_ids[:, None, None], axis=1)
    peaks = jnp.max(jnp.where(routed, logits, -jnp.inf), axis=0, keepdims=True)
    shifted = jnp.where(routed, jnp.exp(jnp.where(routed, logits - peaks, 0.0)), 0.0)
    shares = shifted / jnp.sum(shifted, axis=0, keepdims=True)

    rows_in, _, weighted, hidden_units, gate_grad, up_grad, pair_grad, row_grad_sum, share_grad = run_experts(
        planes, across, shards, capacity, second_input, shares[:, None, :], slots_flat,
        my_slots, w_gate[0], w_up[0], w_down[0],
        top_rows,
    )
    share_grad = share_grad[:, 0, :]
    rows_in, pair_grad = rows_in.reshape(-1, width), pair_grad.reshape(-1, width)
    units = w_gate.shape[2]
    grad_down = dot_tn(hidden_units.reshape(-1, units), pair_grad)[None]
    grad_gate = dot_tn(rows_in, gate_grad.reshape(-1, units))[None]
    grad_up = dot_tn(rows_in, up_grad.reshape(-1, units))[None]
    grad_top = cotangent.astype(F32)
    share_center = jnp.sum(shares * share_grad, axis=0, keepdims=True)
    logit_grad = (shares * (share_grad - share_center)).astype(BF16)
    router_grad = dot_tn(second_input, logit_grad.T)
    second_grad = row_grad_sum + dot(logit_grad.T, router_full)
    ffn_gain_grad = jnp.sum(second_grad * second_normed, axis=0)
    middle_grad = grad_top + norm_backward(second_grad * ffn_scale, second_normed, second_scale)
    wo_grad, wq_grad, first_part, query_gain_grad, key_gain_grad, _, expert_sum = run_backward(
        planes, across, shards, capacity, middle_grad.astype(BF16), w_output, attended, query_raw, key_raw, value,
        first_input, weights, query_gain_row, key_gain_row, cosine, sine, slots_flat, weighted,
    )
    hidden_out = (middle + expert_sum).astype(BF16)
    sum_query, sum_key, sum_value, sum_output, first_grad = run_reduce(
        planes, across, shards, wq_grad, wo_grad, first_part, w_query.shape[1], key_projection.shape[1]
    )
    attn_gain_grad = jnp.sum(first_grad * first_normed, axis=0)
    grad_in = middle_grad + norm_backward(first_grad * attn_scale, first_normed, first_scale)

    squares = jnp.stack(
        [jnp.sum(source * source), jnp.sum(branch * branch), jnp.sum(expert_sum * expert_sum), jnp.sum(grad_in * grad_in)]
    )
    mine = width // device_count
    shared = jnp.concatenate([query_gain_grad[0], key_gain_grad[0], squares])
    parts = jnp.concatenate(
        [
            router_grad.reshape(device_count, mine * experts),
            ffn_gain_grad.reshape(device_count, mine),
            attn_gain_grad.reshape(device_count, mine),
            jnp.broadcast_to(shared[None, :], (device_count, shared.shape[0])),
        ],
        axis=1,
    )
    length = parts.shape[1]
    padded = -(-length // 1024) * 1024
    parts = jnp.pad(parts, ((0, 0), (0, padded - length))).reshape(device_count, padded // 128, 128)
    summed = run_total(planes, across, shards, parts).reshape(-1)
    sum_router = summed[: mine * experts].reshape(mine, experts)
    sum_ffn = summed[mine * experts : mine * (experts + 1)]
    sum_attn = summed[mine * (experts + 1) : mine * (experts + 2)]
    totals = summed[mine * (experts + 2) : length]
    root_mean_squares = jnp.sqrt(totals[2 * head_size :] / (tokens_here * device_count * width))
    return (
        hidden_out,
        grad_in,
        sum_attn,
        sum_query,
        sum_key,
        sum_value,
        totals[:head_size],
        totals[head_size : 2 * head_size],
        sum_output,
        sum_ffn,
        sum_router,
        grad_gate,
        grad_up,
        grad_down,
        root_mean_squares,
    )


def solution(mesh):
    rings, shards = mesh.shape["ep"], mesh.shape["ws"]
    planes = 4 if rings % 4 == 0 else 1
    fine = Mesh(mesh.devices.reshape(planes, rings // planes, shards), ("z", "x", "w"))
    every = ("z", "x", "w")
    rows, deep = P(every, None), P(every, None, None)
    return jax.shard_map(
        local,
        mesh=fine,
        in_specs=(
            rows, P("w"), P("w", None), P("w", None), P("w", None), P(), P(), P("w", None), P("w"), P("w", None),
            rows, deep, deep, deep, rows,
        ),
        out_specs=(
            rows, rows, P(every), rows, rows, rows, P(), P(), rows, P(every), rows, deep, deep, deep, P(),
        ),
        check_vma=False,
    )
```

```python
import functools

import jax
import jax.numpy as jnp
from jax import lax
from jax.experimental import pallas as pl
from jax.experimental.pallas import tpu as pltpu
from jax.sharding import Mesh
from jax.sharding import PartitionSpec as P

BLOCK = 256
EPS = 1e-06
ROPE_BASE = 1000000.0
F32 = jnp.float32
BF16 = jnp.bfloat16
VMEM_LIMIT = 62 * 1024 * 1024


def dot(left, right):
    return jnp.dot(left, right, preferred_element_type=F32)


def dot_tn(left, right):
    return lax.dot_general(left, right, (((0,), (0,)), ((), ())), preferred_element_type=F32)


def dot_nt(left, right):
    return lax.dot_general(left, right, (((1,), (1,)), ((), ())), preferred_element_type=F32)


def rope_tables(seq_length, head_size):
    indices = jnp.arange(head_size // 2, dtype=F32)
    frequency = ROPE_BASE ** (-2.0 * indices / head_size)
    angles = jnp.arange(seq_length, dtype=F32)[:, None] * frequency[None, :]
    cosine, sine = jnp.cos(angles), jnp.sin(angles)
    return jnp.concatenate([cosine, cosine], axis=1), jnp.concatenate([-sine, sine], axis=1)


def norm_forward(values):
    scaling = lax.rsqrt(jnp.mean(values * values, axis=-1, keepdims=True) + EPS)
    return values * scaling, scaling


def norm_backward(grad_normed, normed, scaling):
    return scaling * (grad_normed - normed * jnp.mean(grad_normed * normed, axis=-1, keepdims=True))


def half_turn(values):
    return pltpu.roll(values, values.shape[-1] // 2, 1)


def rotate(values, cosine, signed_sine):
    return values * cosine + half_turn(values) * signed_sine


def unrotate(grads, cosine, signed_sine):
    return grads * cosine - half_turn(grads) * signed_sine


MESH = pl.DeviceIdType.MESH


def remote(source, target, send, recv, device):
    return pltpu.make_async_remote_copy(
        src_ref=source, dst_ref=target, send_sem=send, recv_sem=recv, device_id=device, device_id_type=MESH
    )


def wait_bytes(ref, sem):
    pltpu.make_async_copy(ref, ref, sem).wait()


def line_order(z, planes, step):
    low = jnp.minimum(z, planes - 1 - z)
    paired = (step <= 2 * low).astype(jnp.int32)
    hop = paired * ((step + 1) // 2) + (1 - paired) * (step - low)
    longer = (z > planes - 1 - z).astype(jnp.int32)
    below = paired * (step % 2) + (1 - paired) * longer
    return z + hop - 2 * below * hop, hop, below


def greet_plane_and_line(planes, across, shards):
    z, x, w = lax.axis_index("z"), lax.axis_index("x"), lax.axis_index("w")
    in_plane = across * shards
    me = x * shards + w
    barrier = pltpu.get_barrier_semaphore()

    @pl.loop(1, in_plane)
    def _(offset):
        index = (me + offset) % in_plane
        pl.semaphore_signal(barrier, inc=1, device_id=(z, index // shards, index % shards), device_id_type=MESH)

    @pl.loop(1, planes)
    def _(offset):
        pl.semaphore_signal(barrier, inc=1, device_id=((z + offset) % planes, x, w), device_id_type=MESH)

    pl.semaphore_wait(barrier, in_plane + planes - 2)


def attention_forward(
    planes, across, shards, capacity, heads_a_step,
    own_ref, small_ref, routes_ref, top_ref, wq_hbm, wk_hbm, wv_hbm, query_gain_ref, key_gain_ref, cosine_ref, sine_ref, wo_ref,
    input_ref, query_raw_ref, key_raw_ref, value_ref, attended_ref, branch_ref, slots_ref, my_slots_ref, small_hbm,
    weights_hbm, top_rows_hbm,
    hidden, small_in, weights, key_rot_ref, routes_in, far_slots, plane_rows, stage, chosen, pair_out, far_out,
    gather_send, gather_recv, small_send, small_recv, weight_send, weight_recv, route_send, route_recv, plane_route_send,
    plane_route_recv, far_send, far_recv,
    line_send, line_recv, top_send, top_recv, pair_send, pair_recv, store_sem, small_sem,
):
    step = pl.program_id(0)
    head_size = cosine_ref.shape[1]
    last = wo_ref.shape[0] // (heads_a_step * head_size)
    seq_length = cosine_ref.shape[0]
    blocks = seq_length // BLOCK
    factor = head_size ** (-0.5)
    z, x, w = lax.axis_index("z"), lax.axis_index("x"), lax.axis_index("w")
    in_plane = across * shards
    tokens, width = own_ref.shape
    me = x * shards + w
    depth = width // shards
    experts = planes * in_plane
    wide = heads_a_step * head_size
    chunk = 512
    targets = in_plane // 2
    pair, core = w // 2, w % 2
    sibling, opposite, other = pair * 2 + 1 - core, (1 - pair) * 2 + core, (1 - pair) * 2 + 1 - core

    def slice_of(index):
        return pl.ds(pl.multiple_of(index * capacity, 16), capacity)

    def tokens_of(index):
        return pl.ds(pl.multiple_of(index * tokens, tokens), tokens)

    def gather_copy(kind, owner, target):
        return remote(
            hidden.at[tokens_of(owner)], hidden.at[tokens_of(owner)], gather_send.at[kind], gather_recv.at[kind],
            (z, x, target),
        )

    def small_copy(offset):
        return remote(small_ref, small_in.at[w], small_send.at[offset], small_recv.at[w], (z, x, (w + offset) % shards))

    def columns_at(start, size):
        return pl.ds(pl.multiple_of(start, 128), size)

    my_depth = pl.ds(pl.multiple_of(w * depth, 16), depth)
    query_wide = last * wide

    def weight_pieces(piece, target):
        if piece is None:
            key_at, value_at = columns_at(target * head_size, head_size), columns_at(target * head_size, head_size)
            return [
                (wk_hbm.at[:, key_at], weights.at[my_depth, columns_at(last * wide, head_size)], last),
                (wv_hbm.at[:, value_at], weights.at[my_depth, columns_at(last * wide + head_size, head_size)], last),
            ]
        return [
            (
                wq_hbm.at[:, columns_at(target * query_wide + piece * wide, wide)],
                weights.at[my_depth, columns_at(piece * wide, wide)], piece,
            )
        ]

    def start_weights(piece):
        @pl.loop(1, shards)
        def _(offset):
            for source, goal, sem in weight_pieces(piece, (w + offset) % shards):
                remote(source, goal, weight_send.at[sem], weight_recv.at[sem], (z, x, (w + offset) % shards)).start()

        for source, goal, sem in weight_pieces(piece, w):
            pltpu.make_async_copy(source, goal, weight_recv.at[sem]).start()

    def wait_weights(piece):
        whole_piece = weights.at[:, columns_at(piece * wide, wide)]
        wait_bytes(whole_piece, weight_recv.at[piece])

    def line_copy(column, block, hop, direction):
        rows = plane_rows.at[column, block]
        return remote(
            rows, rows, line_send.at[column, direction, hop], line_recv.at[column, direction, hop],
            (z + 1 - 2 * direction, x, w),
        )

    def start_line(column, block, hop, upward, downward):
        @pl.when(upward & (z + 1 < planes))
        def _():
            line_copy(column, block, hop, 0).start()

        @pl.when(downward & (z > 0))
        def _():
            line_copy(column, block, hop, 1).start()

    def relay(column, hop):
        @pl.when(z - hop >= 0)
        def _():
            wait_bytes(plane_rows.at[column, 0], line_recv.at[column, 0, hop])

            @pl.when(z + 1 < planes)
            def _():
                line_copy(column, z - hop, hop + 1, 0).start()

        @pl.when(z + hop < planes)
        def _():
            wait_bytes(plane_rows.at[column, 0], line_recv.at[column, 1, hop])

            @pl.when(z > 0)
            def _():
                line_copy(column, z + hop, hop + 1, 1).start()

    expert_of = z * in_plane + lax.broadcasted_iota(jnp.int32, (in_plane, tokens), 0)
    earlier = (
        lax.broadcasted_iota(jnp.int32, (tokens, tokens), 0) < lax.broadcasted_iota(jnp.int32, (tokens, tokens), 1)
    ).astype(F32).astype(BF16)
    slot_ids = lax.broadcasted_iota(jnp.int32, (capacity, tokens), 0)

    def fill_slots(column, table):
        @pl.loop(0, planes)
        def _(block):
            hits = jnp.zeros((in_plane, tokens), F32)
            for k in range(routes_ref.shape[0]):
                hits += (routes_in[column, block, k : k + 1, :] == expert_of).astype(F32)
            ranks = dot(hits.astype(BF16), earlier).astype(jnp.int32)
            slots = jnp.where(hits > 0.0, ranks, -1)
            for index in range(in_plane):
                table[block * in_plane + index] = slots[index : index + 1, :]

    def pack(column, turn, table):
        block, _, _ = line_order(z, planes, turn)

        def index_of(target):
            return (target // 2) * shards + pair * 2 + target % 2

        for target in range(targets):
            slots = table[block * in_plane + index_of(target)]
            chosen[target * capacity : (target + 1) * capacity, :] = (slot_ids == slots).astype(F32).astype(BF16)

        @pl.loop(0, width // chunk)
        def _(part):
            here = pl.ds(pl.multiple_of(part * chunk, chunk), chunk)
            stage[column, turn, :, here] = dot(chosen[...], plane_rows[column, block, :, here]).astype(BF16)

        source = x * shards + (w if column == 0 else opposite)
        mine = x * 2 + core

        @pl.loop(1, targets)
        def _(offset):
            target = (mine + offset) % targets
            remote(
                stage.at[column, turn, slice_of(target)], top_rows_hbm.at[block, slice_of(source)],
                top_send.at[column, turn], top_recv.at[block], (z, target // 2, pair * 2 + target % 2),
            ).start()

        pltpu.make_async_copy(
            stage.at[column, turn, slice_of(mine)], top_rows_hbm.at[block, slice_of(source)], top_recv.at[block]
        ).start()

    def route_copy(offset):
        return remote(
            routes_ref, routes_in.at[me, z], route_send.at[offset], route_recv.at[z], ((z + offset) % planes, x, w)
        )

    far_top = remote(top_ref, plane_rows.at[1, z], far_send, far_recv, (z, x, opposite))
    opposite_me = x * shards + opposite

    def plane_route_copy(index):
        return remote(
            routes_in.at[me], routes_in.at[me], plane_route_send, plane_route_recv.at[me],
            (z, index // shards, index % shards),
        )

    def fill_my_slots():
        my_expert = z * in_plane + me

        @pl.loop(0, planes)
        def _(block):
            hits = jnp.concatenate(
                [
                    jnp.max((routes_in[index, block] == my_expert).astype(F32), axis=0, keepdims=True)
                    for index in range(in_plane)
                ],
                axis=0,
            )
            ranks = dot(hits.astype(BF16), earlier).astype(jnp.int32)
            slots = jnp.where(hits > 0.0, ranks, -1)
            for index in range(in_plane):
                my_slots_ref[block * in_plane + index] = slots[index : index + 1, :]

    @pl.when(step == 0)
    def _():
        greet_plane_and_line(planes, across, shards)
        far_top.start()

        @pl.loop(1, planes)
        def _(offset):
            route_copy(offset).start()

        @pl.loop(1, shards)
        def _(offset):
            small_copy(offset).start()

        plane_rows[0, z] = top_ref[...]
        start_line(0, z, 1, True, True)
        hidden[tokens_of(w), :] = own_ref[...]
        gather_copy(0, w, sibling).start()
        small_in[w] = small_ref[...]
        routes_in[me, z] = routes_ref[...]

        @pl.loop(1, planes)
        def _(offset):
            source = (z + offset) % planes
            wait_bytes(routes_in.at[me, source], route_recv.at[source])

        @pl.loop(1, in_plane)
        def _(offset):
            plane_route_copy((me + offset) % in_plane).start()

        fill_slots(me, slots_ref)
        pack(0, 0, slots_ref)
        gather_copy(1, w, opposite).start()
        relay(0, 1)
        wait_bytes(plane_rows.at[1, z], far_recv)
        start_line(1, z, 1, True, True)
        start_weights(None)
        wait_bytes(routes_in.at[opposite_me], plane_route_recv.at[opposite_me])
        fill_slots(opposite_me, far_slots)
        pack(1, 0, far_slots)
        wait_bytes(hidden.at[tokens_of(opposite)], gather_recv.at[1])
        gather_copy(2, opposite, sibling).start()
        start_weights(0)
        pack(0, 1, slots_ref)

        @pl.loop(1, shards)
        def _(offset):
            source = (w + offset) % shards
            wait_bytes(small_in.at[source], small_recv.at[source])

        wait_bytes(hidden.at[tokens_of(sibling)], gather_recv.at[0])
        wait_bytes(hidden.at[tokens_of(other)], gather_recv.at[2])
        for block in range(blocks):
            rows = pl.ds(block * BLOCK, BLOCK)
            normed, _ = norm_forward(hidden[rows, :].astype(F32))
            for part in range(shards):
                here = slice(part * depth, (part + 1) * depth)
                input_ref[rows, here] = (normed[:, here] * small_in[part, experts + 1 : experts + 2, :]).astype(BF16)
        relay(0, 2)
        start_weights(1)
        pack(0, 2, slots_ref)
        wait_weights(last)
        for block in range(blocks):
            rows = pl.ds(block * BLOCK, BLOCK)
            key_value = dot(input_ref[rows, :], weights[:, columns_at(last * wide, wide)])
            key_raw = key_value[:, :head_size]
            key_raw_ref[rows, :] = key_raw
            value_ref[rows, :] = key_value[:, head_size:].astype(BF16)
            key_normed, _ = norm_forward(key_raw)
            key_rot_ref[rows, :] = rotate(
                key_normed * key_gain_ref[...], cosine_ref[rows, :], sine_ref[rows, :]
            ).astype(BF16)
        relay(1, 1)
        pack(1, 1, far_slots)

    for piece in range(2, last):

        @pl.when(step == piece - 2)
        def _():
            wait_weights(piece - 2)
            if piece == last - 1:
                for kind in range(3):
                    wait_bytes(hidden.at[tokens_of(w)], gather_send.at[kind])
            start_weights(piece)

    @pl.when((step >= last - 2) & (step < last))
    def _():
        wait_weights(step)

    @pl.when(step < last)
    def _():
        here = columns_at(step * wide, wide)
        for block in range(blocks):
            rows = pl.ds(block * BLOCK, BLOCK)
            seen = pl.ds(0, (block + 1) * BLOCK)
            query_raw = dot(input_ref[rows, :], weights[:, here])
            query_raw_ref[rows, :] = query_raw
            parts = []
            for head in range(heads_a_step):
                columns = slice(head * head_size, (head + 1) * head_size)
                query_normed, _ = norm_forward(query_raw[:, columns])
                query_rot = rotate(
                    query_normed * query_gain_ref[...], cosine_ref[rows, :], sine_ref[rows, :]
                ).astype(BF16)
                scores = dot_nt(query_rot, key_rot_ref[seen, :]) * factor
                exponent = jnp.exp(scores - jnp.max(scores, axis=-1, keepdims=True))
                probs = (exponent / jnp.sum(exponent, axis=-1, keepdims=True)).astype(BF16)
                parts.append(dot(probs, value_ref[seen, :]).astype(BF16))
            attended_ref[rows, here] = jnp.concatenate(parts, axis=1)

    @pl.when(step == 1)
    def _():
        relay(0, 3)
        pack(0, 3, slots_ref)

    @pl.when(step == 2)
    def _():
        relay(1, 2)
        pack(1, 2, far_slots)

    def project(owner, goal, added):
        rows = tokens_of(owner)

        @pl.loop(0, width // chunk)
        def _(part):
            here = pl.ds(pl.multiple_of(part * chunk, chunk), chunk)
            value = dot(attended_ref[rows, :], wo_ref[:, here])
            if added is not None:
                value += hidden[added, here].astype(F32)
            goal[:, here] = value.astype(goal.dtype)

    def pair_copy(kind):
        at = pl.ds(kind * tokens, tokens)
        return remote(pair_out.at[kind], hidden.at[at], pair_send.at[kind], pair_recv.at[kind], (z, x, sibling))

    far_at = pl.ds(2 * tokens, tokens)
    far_copy = remote(far_out, hidden.at[far_at], pair_send.at[2], pair_recv.at[2], (z, x, opposite))

    @pl.when(step == last)
    def _():
        store = pltpu.make_async_copy(weights, weights_hbm, store_sem)
        store.start()
        small_store = pltpu.make_async_copy(small_in, small_hbm, small_sem)
        small_store.start()
        project(other, pair_out.at[0], None)
        pair_copy(0).start()
        project(sibling, pair_out.at[1], None)
        pair_copy(1).start()
        wait_bytes(hidden.at[pl.ds(0, tokens)], pair_recv.at[0])
        project(opposite, far_out, pl.ds(0, tokens))
        far_copy.start()
        wait_bytes(hidden.at[pl.ds(tokens, tokens)], pair_recv.at[1])
        project(w, branch_ref, pl.ds(tokens, tokens))
        @pl.loop(1, in_plane)
        def _(offset):
            index = (me + offset) % in_plane

            @pl.when(index != opposite_me)
            def _():
                wait_bytes(routes_in.at[index], plane_route_recv.at[index])

        fill_my_slots()
        relay(1, 3)
        pack(1, 3, far_slots)
        wait_bytes(hidden.at[far_at], pair_recv.at[2])
        branch_ref[...] += hidden[far_at, :].astype(F32)

        @pl.loop(0, planes)
        def _(block):
            wait_bytes(top_rows_hbm.at[block], top_recv.at[block])
            if targets > 1:
                for column in range(2):
                    wait_bytes(stage.at[column, 0, pl.ds(0, (targets - 1) * capacity)], top_send.at[column, block])

        for kind in range(3):
            wait_bytes(far_out, pair_send.at[kind])

        @pl.loop(1, shards)
        def _(offset):
            wait_bytes(small_in.at[w], small_send.at[offset])

        @pl.loop(1, planes)
        def _(offset):
            wait_bytes(routes_in.at[0, 0], route_send.at[offset])

        wait_bytes(routes_in.at[pl.ds(0, in_plane - 1)], plane_route_send)
        wait_bytes(plane_rows.at[1, 0], far_send)

        @pl.loop(0, last + 1)
        def _(piece):
            wait_bytes(weights.at[pl.ds(0, (shards - 1) * depth), pl.ds(0, wide)], weight_send.at[piece])

        for column in range(2):
            for hop in range(1, planes):

                @pl.when((z - (hop - 1) >= 0) & (z + 1 < planes))
                def _():
                    wait_bytes(plane_rows.at[0, 0], line_send.at[column, 0, hop])

                @pl.when((z + (hop - 1) < planes) & (z > 0))
                def _():
                    wait_bytes(plane_rows.at[0, 0], line_send.at[column, 1, hop])

        store.wait()
        small_store.wait()


def attention_backward(
    planes, across, shards, capacity, heads_a_step,
    own_grad_ref, wo_ref, attended_ref, query_raw_ref, key_raw_ref, value_ref, input_ref, wq_ref,
    query_gain_ref, key_gain_ref, cosine_ref, sine_ref, slots_ref, weighted_hbm,
    wo_grad_ref, wq_grad_ref, first_grad_ref, query_gain_grad_ref, key_gain_grad_ref, returned_hbm, expert_sum_ref,
    total_ref, key_rot_ref, key_grad_ref, value_grad_ref, query_grad_ref, turned_ref, grad_ref,
    rows, chosen, partial_out, partial_in,
    gather_send, gather_recv, back_send, back_recv, sum_send, sum_recv, load_sem,
):
    step = pl.program_id(0)
    last = pl.num_programs(0) - 1
    head_size = cosine_ref.shape[1]
    seq_length = cosine_ref.shape[0]
    blocks = seq_length // BLOCK
    factor = head_size ** (-0.5)
    z, x, w = lax.axis_index("z"), lax.axis_index("x"), lax.axis_index("w")
    in_plane = across * shards
    me = x * shards + w
    tokens, width = own_grad_ref.shape
    count = in_plane * capacity
    chunk = 512
    pair, core = w // 2, w % 2
    sibling, opposite, other = pair * 2 + 1 - core, (1 - pair) * 2 + core, (1 - pair) * 2 + 1 - core

    def slice_of(index):
        return pl.ds(pl.multiple_of(index * capacity, 16), capacity)

    def tokens_of(index):
        return pl.ds(pl.multiple_of(index * tokens, tokens), tokens)

    def gather_copy(kind, owner, target):
        return remote(
            grad_ref.at[tokens_of(owner)], grad_ref.at[tokens_of(owner)], gather_send.at[kind], gather_recv.at[kind],
            (z, x, target),
        )

    def back_copy(block, index):
        return remote(
            weighted_hbm.at[block, slice_of(index)], returned_hbm.at[block, slice_of(me)],
            back_send.at[block], back_recv.at[block], (z, index // shards, index % shards),
        )

    pace = [(1, 1), (2, 2), (3, 3)]

    def start_back(turn, near, far):
        block, _, _ = line_order(z, planes, planes - 1 - turn)

        @pl.loop(1, in_plane)
        def _(offset):
            index = (me + offset) % in_plane
            beside = (index % shards) // 2 == pair

            @pl.when((beside & near) | (jnp.logical_not(beside) & far))
            def _():
                back_copy(block, index).start()

        @pl.when(near)
        def _():
            pltpu.make_async_copy(
                weighted_hbm.at[block, slice_of(me)], returned_hbm.at[block, slice_of(me)], back_recv.at[block]
            ).start()

    def sum_copy(block):
        return remote(partial_out.at[block], partial_in.at[z], sum_send.at[block], sum_recv.at[z], (block, x, w))

    def combine(turn):
        place = planes - 1 - turn
        block, _, _ = line_order(z, planes, place)
        wait_bytes(returned_hbm.at[block], back_recv.at[block])
        load = pltpu.make_async_copy(returned_hbm.at[block], rows, load_sem)
        load.start()
        if place > 0:
            start_back(turn + 1, step >= 0, step >= 0)
        slot_ids = lax.broadcasted_iota(jnp.int32, (capacity, tokens), 0)

        @pl.loop(0, in_plane)
        def _(index):
            slots = slots_ref[block * in_plane + index]
            chosen[slice_of(index), :] = (slot_ids == slots).astype(F32).astype(BF16)

        load.wait()

        @pl.loop(0, width // chunk)
        def _(part):
            wide = pl.ds(pl.multiple_of(part * chunk, chunk), chunk)
            summed = dot_tn(chosen[...], rows[:, wide])
            if place > 0:
                partial_out[block, :, wide] = summed.astype(BF16)
            else:
                expert_sum_ref[:, wide] = summed

        if place > 0:
            sum_copy(block).start()

    @pl.when(step == 0)
    def _():
        greet_plane_and_line(planes, across, shards)
        grad_ref[tokens_of(w), :] = own_grad_ref[...]
        gather_copy(1, w, opposite).start()
        gather_copy(0, w, sibling).start()
        start_back(0, step == 0, step != 0)
        key_normed, _ = norm_forward(key_raw_ref[...])
        key_rot_ref[...] = rotate(key_normed * key_gain_ref[...], cosine_ref[...], sine_ref[...]).astype(BF16)
        key_grad_ref[...] = jnp.zeros_like(key_grad_ref)
        value_grad_ref[...] = jnp.zeros_like(value_grad_ref)
        query_gain_grad_ref[...] = jnp.zeros_like(query_gain_grad_ref)
        for block in range(blocks):
            rows_here = pl.ds(block * BLOCK, BLOCK)
            turned_ref[:, rows_here] = input_ref[rows_here, :].T
        wait_bytes(grad_ref.at[tokens_of(opposite)], gather_recv.at[1])
        gather_copy(2, opposite, sibling).start()
        start_back(0, step != 0, step == 0)
        wait_bytes(grad_ref.at[tokens_of(sibling)], gather_recv.at[0])
        wait_bytes(grad_ref.at[tokens_of(other)], gather_recv.at[2])

    @pl.when(step < last)
    def _():
        wo_grad_ref[...] = dot_tn(attended_ref[...], grad_ref[...]).astype(BF16)
        for block in range(blocks):
            rows_here = pl.ds(block * BLOCK, BLOCK)
            seen = pl.ds(0, (block + 1) * BLOCK)
            attended_grad = dot_nt(grad_ref[rows_here, :], wo_ref[...]).astype(BF16)
            for head in range(heads_a_step):
                columns = slice(head * head_size, (head + 1) * head_size)
                query_normed, query_scale = norm_forward(query_raw_ref[rows_here, columns])
                cosine, sine = cosine_ref[rows_here, :], sine_ref[rows_here, :]
                query_rot = rotate(query_normed * query_gain_ref[...], cosine, sine).astype(BF16)
                head_grad = attended_grad[:, columns]
                keys, values = key_rot_ref[seen, :], value_ref[seen, :]
                scores = dot_nt(query_rot, keys) * factor
                exponent = jnp.exp(scores - jnp.max(scores, axis=-1, keepdims=True))
                probs = exponent / jnp.sum(exponent, axis=-1, keepdims=True)
                prob_grad = dot_nt(head_grad, values)
                value_grad_ref[seen, :] += dot_tn(probs.astype(BF16), head_grad)
                center = jnp.sum(probs * prob_grad, axis=-1, keepdims=True)
                score_grad = (probs * (prob_grad - center)).astype(BF16)
                key_grad_ref[seen, :] += dot_tn(score_grad, query_rot) * factor
                query_rot_grad = dot(score_grad, keys) * factor
                unrotated = unrotate(query_rot_grad, cosine, sine)
                query_gain_grad_ref[0:1, :] += jnp.sum(unrotated * query_normed, axis=0, keepdims=True)
                query_grad_ref[rows_here, columns] = norm_backward(
                    unrotated * query_gain_ref[...], query_normed, query_scale
                ).astype(BF16)
            partial = dot_nt(query_grad_ref[rows_here, :], wq_ref[...])

            @pl.when(step == 0)
            def _():
                total_ref[rows_here, :] = partial

            @pl.when(step > 0)
            def _():
                total_ref[rows_here, :] += partial

            for turn, place in enumerate(pace):
                if place[1] == block:

                    @pl.when(step == place[0])
                    def _():
                        combine(turn)

    @pl.when(step == last)
    def _():
        key_normed, key_scale = norm_forward(key_raw_ref[...])
        unrotated = unrotate(key_grad_ref[...], cosine_ref[...], sine_ref[...])
        key_gain_grad_ref[...] = jnp.zeros_like(key_gain_grad_ref)
        key_gain_grad_ref[0:1, :] = jnp.sum(unrotated * key_normed, axis=0, keepdims=True)
        key_grad = norm_backward(unrotated * key_gain_ref[...], key_normed, key_scale)
        query_grad_ref[:, :head_size] = key_grad.astype(BF16)
        query_grad_ref[:, head_size : 2 * head_size] = value_grad_ref[...].astype(BF16)
        for block in range(blocks):
            rows_here = pl.ds(block * BLOCK, BLOCK)
            first_grad_ref[rows_here, :] = (
                total_ref[rows_here, :] + dot_nt(query_grad_ref[rows_here, :], wq_ref[...])
            ).astype(BF16)

    wq_grad_ref[...] = dot(turned_ref[...], query_grad_ref[...]).astype(BF16)

    @pl.when(step == last)
    def _():
        for turn in range(len(pace), planes):
            combine(turn)

        @pl.loop(1, planes)
        def _(offset):
            source = (z + offset) % planes
            wait_bytes(partial_in.at[source], sum_recv.at[source])

            @pl.loop(0, width // chunk)
            def _(part):
                wide = pl.ds(pl.multiple_of(part * chunk, chunk), chunk)
                expert_sum_ref[:, wide] += partial_in[source, :, wide].astype(F32)

            wait_bytes(partial_out.at[source], sum_send.at[source])

        @pl.loop(0, planes)
        def _(block):
            wait_bytes(weighted_hbm.at[block, pl.ds(0, count - capacity)], back_send.at[block])

        wait_bytes(grad_ref.at[tokens_of(w)], gather_send.at[0])
        wait_bytes(grad_ref.at[tokens_of(w)], gather_send.at[1])
        wait_bytes(grad_ref.at[tokens_of(w)], gather_send.at[2])


def whole(shape):
    return pl.BlockSpec(shape, lambda step: (0,) * len(shape), pipeline_mode=pl.Buffered(1))


def run_forward(
    planes, across, shards, capacity, own, small, routes, top, w_query, w_key, w_value, query_gain, key_gain, cosine, sine, wo
):
    tokens, width = own.shape
    seq_length = tokens * shards
    head_size = query_gain.shape[1]
    heads_here = wo.shape[0] // head_size
    pair = 2
    wide = pair * head_size
    steps = heads_here // pair
    in_plane = across * shards
    count = in_plane * capacity
    hbm = pl.BlockSpec(memory_space=pl.ANY)
    dma = pltpu.SemaphoreType.DMA
    slots_shape = (planes * in_plane, 1, tokens)
    return pl.pallas_call(
        functools.partial(attention_forward, planes, across, shards, capacity, pair),
        grid=(steps + 1,),
        in_specs=[
            whole((tokens, width)),
            whole(small.shape),
            whole(routes.shape),
            whole((tokens, width)),
            hbm,
            hbm,
            hbm,
            whole((1, head_size)),
            whole((1, head_size)),
            whole((seq_length, head_size)),
            whole((seq_length, head_size)),
            whole(wo.shape),
        ],
        out_specs=[
            whole((seq_length, width)),
            pl.BlockSpec((seq_length, wide), lambda step: (0, jnp.minimum(step, steps - 1))),
            whole((seq_length, head_size)),
            whole((seq_length, head_size)),
            whole((seq_length, heads_here * head_size)),
            whole((tokens, width)),
            whole(slots_shape),
            whole(slots_shape),
            hbm,
            hbm,
            hbm,
        ],
        out_shape=[
            jax.ShapeDtypeStruct((seq_length, width), BF16),
            jax.ShapeDtypeStruct((seq_length, heads_here * head_size), F32),
            jax.ShapeDtypeStruct((seq_length, head_size), F32),
            jax.ShapeDtypeStruct((seq_length, head_size), BF16),
            jax.ShapeDtypeStruct((seq_length, heads_here * head_size), BF16),
            jax.ShapeDtypeStruct((tokens, width), F32),
            jax.ShapeDtypeStruct(slots_shape, jnp.int32),
            jax.ShapeDtypeStruct(slots_shape, jnp.int32),
            jax.ShapeDtypeStruct((shards,) + small.shape, F32),
            jax.ShapeDtypeStruct((width, (steps + 1) * wide), BF16),
            jax.ShapeDtypeStruct((planes, count, width), BF16),
        ],
        scratch_shapes=[
            pltpu.VMEM((seq_length, width), BF16),
            pltpu.VMEM((shards,) + small.shape, F32),
            pltpu.VMEM((width, (steps + 1) * wide), BF16),
            pltpu.VMEM((seq_length, head_size), BF16),
            pltpu.VMEM((in_plane, planes) + routes.shape, jnp.int32),
            pltpu.VMEM(slots_shape, jnp.int32),
            pltpu.VMEM((2, planes, tokens, width), BF16),
            pltpu.VMEM((2, planes, count // 2, width), BF16),
            pltpu.VMEM((count // 2, tokens), BF16),
            pltpu.VMEM((2, tokens, width), BF16),
            pltpu.VMEM((tokens, width), BF16),
            dma((3,)), dma((3,)), dma((shards,)), dma((shards,)), dma((steps + 1,)), dma((steps + 1,)),
            dma((planes,)), dma((planes,)), dma, dma((in_plane,)), dma, dma,
            dma((2, 2, planes + 1)), dma((2, 2, planes + 1)), dma((2, planes)), dma((planes,)), dma((3,)), dma((3,)), dma, dma,
        ],
        compiler_params=pltpu.CompilerParams(vmem_limit_bytes=VMEM_LIMIT, collective_id=5, has_side_effects=True),
        cost_estimate=pl.CostEstimate(flops=70 * 10**9, bytes_accessed=40 * 10**6, transcendentals=6 * 10**6),
    )(own, small, routes, top, w_query, w_key, w_value, query_gain, key_gain, cosine, sine, wo)


def run_backward(
    planes, across, shards, capacity, own_grad, wo, attended, query_raw, key_raw, value, first_input, weights, query_gain,
    key_gain, cosine, sine, slots, weighted,
):
    tokens, width = own_grad.shape
    seq_length = attended.shape[0]
    head_size = query_gain.shape[1]
    heads_here = wo.shape[0] // head_size
    pair = 2
    wide = pair * head_size
    steps = heads_here // pair
    count = across * shards * capacity
    hbm = pl.BlockSpec(memory_space=pl.ANY)
    dma = pltpu.SemaphoreType.DMA

    def held(step):
        return jnp.minimum(step, steps - 1)

    return pl.pallas_call(
        functools.partial(attention_backward, planes, across, shards, capacity, pair),
        grid=(steps + 1,),
        in_specs=[
            whole((tokens, width)),
            pl.BlockSpec((wide, width), lambda step: (held(step), 0)),
            pl.BlockSpec((seq_length, wide), lambda step: (0, held(step))),
            pl.BlockSpec((seq_length, wide), lambda step: (0, held(step))),
            whole((seq_length, head_size)),
            whole((seq_length, head_size)),
            whole((seq_length, width)),
            pl.BlockSpec((width, wide), lambda step: (0, step)),
            whole((1, head_size)),
            whole((1, head_size)),
            whole((seq_length, head_size)),
            whole((seq_length, head_size)),
            whole(slots.shape),
            hbm,
        ],
        out_specs=[
            pl.BlockSpec((wide, width), lambda step: (held(step), 0)),
            pl.BlockSpec((width, wide), lambda step: (0, step)),
            whole((seq_length, width)),
            whole((8, head_size)),
            whole((8, head_size)),
            hbm,
            whole((tokens, width)),
        ],
        out_shape=[
            jax.ShapeDtypeStruct((heads_here * head_size, width), BF16),
            jax.ShapeDtypeStruct((width, (steps + 1) * wide), BF16),
            jax.ShapeDtypeStruct((seq_length, width), BF16),
            jax.ShapeDtypeStruct((8, head_size), F32),
            jax.ShapeDtypeStruct((8, head_size), F32),
            jax.ShapeDtypeStruct(weighted.shape, BF16),
            jax.ShapeDtypeStruct((tokens, width), F32),
        ],
        scratch_shapes=[
            pltpu.VMEM((seq_length, width), F32),
            pltpu.VMEM((seq_length, head_size), BF16),
            pltpu.VMEM((seq_length, head_size), F32),
            pltpu.VMEM((seq_length, head_size), F32),
            pltpu.VMEM((seq_length, wide), BF16),
            pltpu.VMEM((width, seq_length), BF16),
            pltpu.VMEM((seq_length, width), BF16),
            pltpu.VMEM((count, width), BF16),
            pltpu.VMEM((count, tokens), BF16),
            pltpu.VMEM((planes, tokens, width), BF16),
            pltpu.VMEM((planes, tokens, width), BF16),
            dma((3,)), dma((3,)), dma((planes,)), dma((planes,)), dma((planes,)), dma((planes,)), dma,
        ],
        compiler_params=pltpu.CompilerParams(vmem_limit_bytes=VMEM_LIMIT, collective_id=2, has_side_effects=True),
        cost_estimate=pl.CostEstimate(flops=70 * 10**9, bytes_accessed=60 * 10**6, transcendentals=6 * 10**6),
    )(
        own_grad, wo, attended, query_raw, key_raw, value, first_input, weights, query_gain, key_gain, cosine, sine, slots,
        weighted,
    )


def reduce_kernel(
    planes, across, shards,
    wq_hbm, wo_hbm, first_hbm, hidden_ref, middle_hbm, expert_sum_hbm, middle_grad_hbm, scale_ref, early_ref, shared_ref,
    rows_hbm, gate_grad_hbm, up_grad_hbm, units_hbm, pair_grad_hbm,
    query_ref, key_ref, value_ref, output_ref, hidden_out_ref, grad_in_ref, early_total_ref, late_total_ref,
    gate_out_hbm, up_out_hbm, down_out_hbm,
    wq_parts, wo_parts, wq_out, wo_out, wq_in, wo_in, wq_total, wo_total, wq_final, wo_final, wq_home, wo_home, first_in,
    early_in, late, late_in, held_a, held_b, side, turned, tiles, tall, flat,
    across_send, across_recv, line_send, line_recv, home_send, home_recv, swap_send, swap_recv, first_send, first_recv,
    early_send, early_recv, late_send, late_recv, held_sem, side_sem, tile_sem, result_sem,
):
    z, x, w = lax.axis_index("z"), lax.axis_index("x"), lax.axis_index("w")
    rings = planes * across
    ring = z * across + x
    everyone = rings * shards
    wq_rows, wo_rows = wq_total.shape[0], wo_total.shape[0]
    mine = wq_rows // shards
    tokens, width = grad_in_ref.shape
    query_columns = query_ref.shape[1] // shards
    key_columns = key_ref.shape[1] // shards
    linear = ring * shards + w
    barrier = pltpu.get_barrier_semaphore()

    def place(index):
        return (index // shards // across, index // shards % across, index % shards)

    @pl.loop(1, everyone)
    def _(offset):
        pl.semaphore_signal(barrier, inc=1, device_id=place((linear + offset) % everyone), device_id_type=MESH)

    pl.semaphore_wait(barrier, everyone - 1)

    def rows_of(index, size):
        return pl.ds(pl.multiple_of(index * size, 16), size)

    sources = [(wq_hbm, wq_rows, wq_parts), (wo_hbm, wo_rows, wo_parts)]

    def across_copy(kind, plane, column):
        source, rows, goal = sources[kind]
        return remote(
            source.at[rows_of(plane * across + column, rows)], goal.at[plane, x],
            across_send.at[kind, plane], across_recv.at[kind, plane], (z, column, w),
        )

    def first_copy(offset):
        target = (w + offset) % shards
        return remote(
            first_hbm.at[rows_of(target, tokens)], first_in.at[offset], first_send.at[offset], first_recv.at[offset],
            (z, x, target),
        )

    @pl.loop(1, shards)
    def _(offset):
        first_copy(offset).start()

    pltpu.make_async_copy(first_hbm.at[rows_of(w, tokens)], first_in.at[0], first_recv.at[0]).start()
    hold_a = pltpu.make_async_copy(middle_hbm, held_a, held_sem.at[0])
    hold_b = pltpu.make_async_copy(expert_sum_hbm, held_b, held_sem.at[1])
    hold_a.start()
    hold_b.start()

    def start_across(kind, turn):
        plane, _, _ = line_order(z, planes, planes - 1 - turn)

        @pl.loop(1, across)
        def _(offset):
            across_copy(kind, plane, (x + offset) % across).start()

        source, rows, goal = sources[kind]
        pltpu.make_async_copy(
            source.at[rows_of(plane * across + x, rows)], goal.at[plane, x], across_recv.at[kind, plane]
        ).start()

    start_across(1, 0)
    start_across(1, 1)

    @pl.loop(1, everyone)
    def _(offset):
        other = (linear + offset) % everyone
        remote(early_ref.at[other], early_in.at[linear], early_send, early_recv, place(other)).start()

    early_in[linear] = early_ref[linear]
    lanes = tiles.shape[2]
    per_kind = width // lanes
    depth = side.shape[0]
    late_rows = width // 128
    pick = (lax.broadcasted_iota(jnp.int32, (8, 128), 0) == 2).astype(F32)
    lane = lax.broadcasted_iota(jnp.int32, (8, 128), 1)

    def tile_copy(unit):
        slot = unit % 2
        here = pl.ds(pl.multiple_of((unit % per_kind) * lanes, lanes), lanes)

        @pl.when(unit < 2 * per_kind)
        def _():
            pltpu.make_async_copy(rows_hbm.at[:, here], tiles.at[slot], tile_sem.at[slot]).start()

        @pl.when(unit >= 2 * per_kind)
        def _():
            pltpu.make_async_copy(pair_grad_hbm.at[:, here], tiles.at[slot], tile_sem.at[slot]).start()

    tile_copy(0)

    def multiply(unit):
        slot = unit % 2
        here = pl.ds(pl.multiple_of((unit % per_kind) * lanes, lanes), lanes)
        for kind, source in enumerate([gate_grad_hbm, up_grad_hbm, units_hbm]):

            @pl.when(unit == kind * per_kind)
            def _():
                load = pltpu.make_async_copy(source, side, side_sem)
                load.start()
                load.wait()
                if kind == 2:

                    @pl.loop(0, depth // 128)
                    def _(part):
                        at = pl.ds(pl.multiple_of(part * 128, 128), 128)
                        turned[:, at] = side[at, :].T

        @pl.when(unit + 1 < 3 * per_kind)
        def _():
            tile_copy(unit + 1)

        wait_bytes(tiles.at[slot], tile_sem.at[slot])

        @pl.when(unit >= 2)
        def _():
            wait_bytes(tall.at[slot], result_sem.at[slot])

        @pl.when(unit < 2 * per_kind)
        def _():
            tall[slot] = dot_tn(tiles[slot], side[...])

        @pl.when(unit < per_kind)
        def _():
            pltpu.make_async_copy(tall.at[slot], gate_out_hbm.at[here], result_sem.at[slot]).start()

        @pl.when((unit >= per_kind) & (unit < 2 * per_kind))
        def _():
            pltpu.make_async_copy(tall.at[slot], up_out_hbm.at[here], result_sem.at[slot]).start()

        @pl.when(unit >= 2 * per_kind)
        def _():
            flat[slot] = dot(turned[...], tiles[slot])
            pltpu.make_async_copy(flat.at[slot], down_out_hbm.at[:, here], result_sem.at[slot]).start()

    def late_copy(other):
        return remote(late, late_in.at[linear], late_send, late_recv, place(other))

    def finish_rows():
        hold_a.wait()
        hold_b.wait()
        pieces = tokens // 64

        def add_rows(piece, carry):
            at = pl.ds(pl.multiple_of(piece * 64, 64), 64)
            extra = held_b[at, :]
            hidden_out_ref[at, :] = (held_a[at, :] + extra).astype(BF16)
            return carry + jnp.sum(jnp.sum(extra * extra, axis=1, keepdims=True), axis=0, keepdims=True)

        expert_square = lax.fori_loop(0, pieces, add_rows, jnp.zeros((1, 1), F32))
        load = pltpu.make_async_copy(middle_grad_hbm, held_a, held_sem.at[0])
        load.start()

        @pl.loop(0, shards)
        def _(offset):
            wait_bytes(first_in.at[offset], first_recv.at[offset])

        load.wait()

        def grad_rows(piece, carry):
            square, gain_grad = carry
            at = pl.ds(pl.multiple_of(piece * 64, 64), 64)
            first = first_in[0, at, :].astype(F32)
            for offset in range(1, shards):
                first += first_in[offset, at, :].astype(F32)
            normed, scaling = norm_forward(hidden_ref[at, :].astype(F32))
            grad = held_a[at, :] + norm_backward(first * scale_ref[...], normed, scaling)
            grad_in_ref[at, :] = grad
            return (
                square + jnp.sum(jnp.sum(grad * grad, axis=1, keepdims=True), axis=0, keepdims=True),
                gain_grad + jnp.sum(first * normed, axis=0, keepdims=True),
            )

        square, gain_grad = lax.fori_loop(
            0, pieces, grad_rows, (jnp.zeros((1, 1), F32), jnp.zeros((1, width), F32))
        )
        for row in range(late_rows):
            late[row : row + 1, :] = gain_grad[:, row * 128 : (row + 1) * 128]
        late[late_rows:, :] = shared_ref[...] + pick * (
            jnp.where(lane == 2, expert_square, 0.0) + jnp.where(lane == 3, square, 0.0)
        )

        @pl.loop(1, everyone)
        def _(offset):
            late_copy((linear + offset) % everyone).start()

        late_in[linear] = late[...]

    outs, ins = [wq_out, wo_out], [wq_in, wo_in]
    totals, parts = [wq_total, wo_total], [wq_parts, wo_parts]

    def line_copy(kind, plane):
        up = (plane > z).astype(jnp.int32)
        ends = (plane == z + 2 * up - 1).astype(jnp.int32)
        slot = plane + ends * (1 - up) * (planes - plane)
        return remote(
            outs[kind].at[plane], ins[kind].at[slot], line_send.at[kind, plane], line_recv.at[kind, slot],
            (z + 2 * up - 1, x, w),
        )

    per_turn = 3 * per_kind // (2 * planes)

    def take(kind, slot):
        wait_bytes(ins[kind].at[slot], line_recv.at[kind, slot])
        totals[kind][...] += ins[kind][slot].astype(F32)

    def collect(kind):
        @pl.loop(0, planes)
        def _(turn):
            plane, _, _ = line_order(z, planes, planes - 1 - turn)

            @pl.loop(0, per_turn)
            def _(unit):
                multiply((turn + (1 - kind) * planes) * per_turn + unit)

            wait_bytes(parts[kind].at[plane], across_recv.at[kind, plane])

            @pl.when(turn < planes - 2)
            def _():
                start_across(kind, turn + 2)

            if kind == 1:

                @pl.when(turn >= planes - 2)
                def _():
                    start_across(0, turn + 2 - planes)

            totals[kind][...] = parts[kind][plane, 0].astype(F32)

            @pl.loop(1, across)
            def _(column):
                totals[kind][...] += parts[kind][plane, column].astype(F32)

            @pl.when(((plane > z) & (z > 0)) | ((plane < z) & (z < planes - 1)))
            def _():
                take(kind, plane)

            @pl.when(plane != z)
            def _():
                outs[kind][plane] = totals[kind][...].astype(BF16)
                line_copy(kind, plane).start()

    def finish(kind):
        @pl.when(z > 0)
        def _():
            take(kind, z)

        @pl.when(z < planes - 1)
        def _():
            take(kind, planes)

    collect(1)
    finish(1)
    wo_final[...] = wo_total[...].astype(BF16)
    goal = w * rings + ring
    stays = goal == linear
    swap = remote(
        wo_final, wo_home, swap_send, swap_recv, (goal // shards // across, goal // shards % across, goal % shards)
    )

    @pl.when(jnp.logical_not(stays))
    def _():
        swap.start()

    @pl.when(stays)
    def _():
        pltpu.make_async_copy(wo_final, wo_home, swap_recv).start()

    finish_rows()
    collect(0)
    finish(0)
    wq_final[...] = wq_total[...].astype(BF16)

    def home_copy(offset):
        target = (w + offset) % shards
        return remote(
            wq_final.at[rows_of(target, mine)], wq_home.at[w], home_send.at[offset], home_recv.at[w], (z, x, target)
        )

    @pl.loop(1, shards)
    def _(offset):
        home_copy(offset).start()

    pltpu.make_async_copy(wq_final.at[rows_of(w, mine)], wq_home.at[w], home_recv.at[w]).start()

    for part in range(shards):
        wait_bytes(wq_home.at[part], home_recv.at[part])
        rows = wq_home[part].astype(F32)
        query_ref[:, part * query_columns : (part + 1) * query_columns] = rows[:, :query_columns]
        key_ref[:, part * key_columns : (part + 1) * key_columns] = rows[:, query_columns : query_columns + key_columns]
        value_ref[:, part * key_columns : (part + 1) * key_columns] = rows[:, query_columns + key_columns :]

    wait_bytes(early_ref.at[pl.ds(0, everyone - 1)], early_recv)
    early_total_ref[...] = jnp.sum(early_in[...], axis=0)
    wait_bytes(late_in.at[pl.ds(0, everyone - 1)], late_recv)
    late_total_ref[...] = jnp.sum(late_in[...], axis=0)
    wait_bytes(early_ref.at[pl.ds(0, everyone - 1)], early_send)
    wait_bytes(late_in.at[pl.ds(0, everyone - 1)], late_send)
    for slot in range(2):
        wait_bytes(tall.at[slot], result_sem.at[slot])
    wait_bytes(wo_home, swap_recv)
    output_ref[...] = wo_home[...].astype(F32)

    @pl.when(jnp.logical_not(stays))
    def _():
        wait_bytes(wo_final, swap_send)

    @pl.loop(1, shards)
    def _(offset):
        wait_bytes(wq_home.at[0], home_send.at[offset])
        wait_bytes(first_in.at[0], first_send.at[offset])

    if across > 1:

        @pl.loop(0, planes)
        def _(plane):
            wait_bytes(wq_parts.at[plane, pl.ds(0, across - 1)], across_send.at[0, plane])
            wait_bytes(wo_parts.at[plane, pl.ds(0, across - 1)], across_send.at[1, plane])

    @pl.loop(1, planes)
    def _(offset):
        plane = (z + offset) % planes
        wait_bytes(wq_out.at[plane], line_send.at[0, plane])
        wait_bytes(wo_out.at[plane], line_send.at[1, plane])


def run_reduce(
    planes, across, shards, wq_grad, wo_grad, first_part, hidden, middle, expert_sum, middle_grad, scale, early, shared,
    rows_in, gate_grad, up_grad, units, pair_grad, query_columns, key_columns,
):
    rings = planes * across
    everyone = rings * shards
    width = wq_grad.shape[0]
    wq_wide = wq_grad.shape[1]
    wq_rows, wo_rows = width // rings, wo_grad.shape[0] // rings
    tokens = first_part.shape[0] // shards
    mine = wq_rows // shards
    depth, wide = units.shape
    late_rows = width // 128 + 8
    hbm = pl.BlockSpec(memory_space=pl.ANY)
    vmem = pl.BlockSpec(memory_space=pltpu.VMEM)
    dma = pltpu.SemaphoreType.DMA
    return pl.pallas_call(
        functools.partial(reduce_kernel, planes, across, shards),
        in_specs=[hbm] * 3 + [vmem] + [hbm] * 3 + [vmem] * 3 + [hbm] * 5,
        out_specs=[vmem] * 8 + [hbm] * 3,
        out_shape=[
            jax.ShapeDtypeStruct((mine, query_columns), F32),
            jax.ShapeDtypeStruct((mine, key_columns), F32),
            jax.ShapeDtypeStruct((mine, key_columns), F32),
            jax.ShapeDtypeStruct((wo_rows, width), F32),
            jax.ShapeDtypeStruct((tokens, width), BF16),
            jax.ShapeDtypeStruct((tokens, width), F32),
            jax.ShapeDtypeStruct(early.shape[1:], F32),
            jax.ShapeDtypeStruct((late_rows, 128), F32),
            jax.ShapeDtypeStruct((width, wide), F32),
            jax.ShapeDtypeStruct((width, wide), F32),
            jax.ShapeDtypeStruct((wide, width), F32),
        ],
        scratch_shapes=[
            pltpu.VMEM((planes, across, wq_rows, wq_wide), BF16),
            pltpu.VMEM((planes, across, wo_rows, width), BF16),
            pltpu.VMEM((planes, wq_rows, wq_wide), BF16),
            pltpu.VMEM((planes, wo_rows, width), BF16),
            pltpu.VMEM((planes + 1, wq_rows, wq_wide), BF16),
            pltpu.VMEM((planes + 1, wo_rows, width), BF16),
            pltpu.VMEM((wq_rows, wq_wide), F32),
            pltpu.VMEM((wo_rows, width), F32),
            pltpu.VMEM((wq_rows, wq_wide), BF16),
            pltpu.VMEM((wo_rows, width), BF16),
            pltpu.VMEM((shards, mine, wq_wide), BF16),
            pltpu.VMEM((wo_rows, width), BF16),
            pltpu.VMEM((shards, tokens, width), BF16),
            pltpu.VMEM(early.shape, F32),
            pltpu.VMEM((late_rows, 128), F32),
            pltpu.VMEM((everyone, late_rows, 128), F32),
            pltpu.VMEM((tokens, width), F32),
            pltpu.VMEM((tokens, width), F32),
            pltpu.VMEM((depth, wide), BF16),
            pltpu.VMEM((wide, depth), BF16),
            pltpu.VMEM((2, depth, 256), BF16),
            pltpu.VMEM((2, 256, wide), F32),
            pltpu.VMEM((2, wide, 256), F32),
            dma((2, planes)), dma((2, planes)), dma((2, planes)), dma((2, planes + 1)), dma((shards,)), dma((shards,)),
            dma, dma, dma((shards,)), dma((shards,)), dma, dma, dma, dma, dma((2,)), dma, dma((2,)), dma((2,)),
        ],
        compiler_params=pltpu.CompilerParams(vmem_limit_bytes=VMEM_LIMIT, collective_id=3, has_side_effects=True),
        cost_estimate=pl.CostEstimate(flops=70 * 10**9, bytes_accessed=40 * 10**6, transcendentals=0),
    )(
        wq_grad, wo_grad, first_part, hidden, middle, expert_sum, middle_grad, scale, early, shared, rows_in, gate_grad,
        up_grad, units, pair_grad,
    )


def expert_kernel(
    planes, across, shards, capacity,
    own_ref, share_ref, slots_ref, my_slots_ref, gate_ref, up_ref, down_ref, top_hbm,
    rows_hbm, back_hbm, weighted_hbm, units_hbm, gate_grad_hbm, up_grad_hbm, pair_grad_hbm, row_grad_ref, share_grad_ref,
    plane_rows, plane_shares, share_in, share_back, share_home, stage, chosen, rows, top, units,
    gate_grad, up_grad, columns, partial_in,
    line_send, line_recv, plane_share_send, plane_share_recv, out_send, out_recv, out_share_send, out_share_recv,
    back_send, back_recv, back_share_send, back_share_recv, sum_send, sum_recv, sum_share_send, sum_share_recv,
    load_sem, top_sem, store_sem,
):
    z, x, w = lax.axis_index("z"), lax.axis_index("x"), lax.axis_index("w")
    in_plane = across * shards
    me = x * shards + w
    tokens, width = own_ref.shape
    count = in_plane * capacity
    half = count // 2
    per_half = in_plane // 2
    chunk = 512

    def place(index):
        return (z, index // shards, index % shards)

    def order(step):
        return line_order(z, planes, step)

    inner = ((z > 0) & (z < planes - 1)).astype(jnp.int32)
    first_back = 2 - (z == 1).astype(jnp.int32)
    second_back = 3 - inner * first_back
    third_back = 1 + 2 * inner
    greet_plane_and_line(planes, across, shards)

    def line_up(block, hop):
        return remote(
            plane_rows.at[block], plane_rows.at[block], line_send.at[0, hop], line_recv.at[0, hop], (z + 1, x, w)
        )

    def line_down(block, hop):
        return remote(
            plane_rows.at[block], plane_rows.at[block], line_send.at[1, hop], line_recv.at[1, hop], (z - 1, x, w)
        )

    plane_rows[z] = own_ref[...]

    @pl.when(z + 1 < planes)
    def _():
        line_up(z, 1).start()

    @pl.when(z > 0)
    def _():
        line_down(z, 1).start()

    def plane_share_copy(other):
        return remote(
            share_ref.at[pl.ds(other * in_plane, in_plane)], plane_shares.at[z],
            plane_share_send.at[other], plane_share_recv.at[z], (other, x, w),
        )

    @pl.loop(1, planes)
    def _(offset):
        plane_share_copy((z + offset) % planes).start()

    plane_shares[z] = share_ref[pl.ds(z * in_plane, in_plane)]

    def slice_of(index):
        return pl.ds(pl.multiple_of(index * capacity, 16), capacity)

    def out_copy(step, block, index):
        return remote(
            stage.at[step, slice_of(index)], rows_hbm.at[block, slice_of(me)],
            out_send.at[step], out_recv.at[step], place(index),
        )

    def out_share_copy(step, block, index):
        return remote(
            plane_shares.at[block, index], share_in.at[block, me],
            out_share_send.at[step], out_share_recv.at[step], place(index),
        )

    def back_copy(step, block, index):
        return remote(
            stage.at[step, slice_of(index)], back_hbm.at[block, slice_of(me)],
            back_send.at[step], back_recv.at[step], place(index),
        )

    def back_share_copy(step, block, index):
        return remote(
            share_back.at[block, index], share_home.at[block, me],
            back_share_send.at[step], back_share_recv.at[step], place(index),
        )

    def start_back(step, block):
        @pl.loop(1, in_plane)
        def _(offset):
            index = (me + offset) % in_plane
            back_copy(step, block, index).start()
            back_share_copy(step, block, index).start()

        pltpu.make_async_copy(stage.at[step, slice_of(me)], back_hbm.at[block, slice_of(me)], back_recv.at[step]).start()
        pltpu.make_async_copy(share_back.at[block, me], share_home.at[block, me], back_share_recv.at[step]).start()

    slot_ids = lax.broadcasted_iota(jnp.int32, (capacity, tokens), 0)

    def pack_step(step):
        block, _, _ = order(step)

        @pl.when(step > 0)
        def _():
            @pl.when(z - step >= 0)
            def _():
                wait_bytes(plane_rows.at[0], line_recv.at[0, step])

                @pl.when(z + 1 < planes)
                def _():
                    line_up(z - step, step + 1).start()

            @pl.when(z + step < planes)
            def _():
                wait_bytes(plane_rows.at[0], line_recv.at[1, step])

                @pl.when(z > 0)
                def _():
                    line_down(z + step, step + 1).start()

            wait_bytes(plane_shares.at[block], plane_share_recv.at[block])

        @pl.loop(0, in_plane)
        def _(index):
            slots = slots_ref[block * in_plane + index]
            chosen[step, slice_of(index), :] = (slot_ids == slots).astype(F32).astype(BF16)

        @pl.loop(0, width // chunk)
        def _(part):
            wide = pl.ds(pl.multiple_of(part * chunk, chunk), chunk)
            stage[step, :, wide] = dot(chosen[step], plane_rows[block, :, wide]).astype(BF16)

    def send_step(step):
        block, _, _ = order(step)

        @pl.loop(1, in_plane)
        def _(offset):
            index = (me + offset) % in_plane
            out_copy(step, block, index).start()
            out_share_copy(step, block, index).start()

        pltpu.make_async_copy(stage.at[step, slice_of(me)], rows_hbm.at[block, slice_of(me)], out_recv.at[step]).start()
        pltpu.make_async_copy(plane_shares.at[block, me], share_in.at[block, me], out_share_recv.at[step]).start()

    def expert_step(step):
        block, _, _ = order(step)

        pltpu.make_async_copy(top_hbm.at[block], top, top_sem).start()
        wait_bytes(rows_hbm.at[block], out_recv.at[step])
        load = pltpu.make_async_copy(rows_hbm.at[block], rows, load_sem)
        load.start()

        @pl.when(step + 1 < planes)
        def _():
            send_step(step + 1)

        wait_bytes(share_in.at[block], out_share_recv.at[step])
        wait_bytes(stage.at[step, pl.ds(0, count - capacity)], out_send.at[step])
        wait_bytes(plane_shares.at[block, pl.ds(0, in_plane - 1)], out_share_send.at[step])

        @pl.loop(0, in_plane)
        def _(index):
            mine = slot_ids == my_slots_ref[block * in_plane + index]
            columns[slice_of(index), :] = jnp.broadcast_to(
                jnp.sum(jnp.where(mine, share_in[block, index], 0.0), axis=1, keepdims=True), (capacity, 128)
            )

        load.wait()
        wait_bytes(top, top_sem)

        @pl.loop(0, 2)
        def _(part):
            here = pl.ds(pl.multiple_of(part * half, 16), half)
            gate = dot(rows[here, :], gate_ref[...])
            up = dot(rows[here, :], up_ref[...])
            sigmoid = 1.0 / (1.0 + jnp.exp(-gate))
            active = gate * sigmoid
            hidden = (active * up).astype(BF16)
            units[here, :] = hidden
            share = columns[here, 0:1]
            total = jnp.zeros((half, 1), F32)
            for piece in range(width // chunk):
                wide = pl.ds(piece * chunk, chunk)
                pair_out = dot(hidden, down_ref[:, wide]).astype(BF16).astype(F32)
                top_rows = top[here, wide].astype(F32)
                total += jnp.sum(pair_out * top_rows, axis=1, keepdims=True)
                rows[here, wide] = (share * pair_out).astype(BF16)
                top[here, wide] = (share * top_rows).astype(BF16)
            columns[here, :] = jnp.broadcast_to(total, (half, 128))
            hidden_grad = dot_nt(top[here, :], down_ref[...])
            gate_low = (hidden_grad * up * sigmoid * (1.0 + gate * (1.0 - sigmoid))).astype(BF16)
            up_low = (hidden_grad * active).astype(BF16)
            gate_grad[here, :] = gate_low
            up_grad[here, :] = up_low
            for piece in range(width // chunk):
                wide = pl.ds(piece * chunk, chunk)
                stage[step, here, wide] = (dot_nt(gate_low, gate_ref[wide, :]) + dot_nt(up_low, up_ref[wide, :])).astype(BF16)

        @pl.loop(0, in_plane)
        def _(index):
            mine = slot_ids == my_slots_ref[block * in_plane + index]
            values = columns[slice_of(index), 0:1]
            share_back[block, index] = jnp.sum(jnp.where(mine, values, 0.0), axis=0, keepdims=True)

        @pl.when((step == first_back) | (step == second_back))
        def _():
            start_back(step, block)

        stores = [
            pltpu.make_async_copy(units, units_hbm.at[block], store_sem.at[0]),
            pltpu.make_async_copy(gate_grad, gate_grad_hbm.at[block], store_sem.at[1]),
            pltpu.make_async_copy(up_grad, up_grad_hbm.at[block], store_sem.at[2]),
            pltpu.make_async_copy(top, pair_grad_hbm.at[block], store_sem.at[3]),
            pltpu.make_async_copy(rows, weighted_hbm.at[block], store_sem.at[4]),
        ]
        for store in stores:
            store.start()

        for store in stores:
            store.wait()

    @pl.loop(0, planes + 1)
    def _(step):
        @pl.when(step < planes)
        def _():
            pack_step(step)

        @pl.when(step == 0)
        def _():
            send_step(step)

        @pl.when(step > 0)
        def _():
            expert_step(step - 1)

    for hop in range(1, planes):

        @pl.when((z - (hop - 1) >= 0) & (z + 1 < planes))
        def _():
            wait_bytes(plane_rows.at[0], line_send.at[0, hop])

        @pl.when((z + (hop - 1) < planes) & (z > 0))
        def _():
            wait_bytes(plane_rows.at[0], line_send.at[1, hop])

    @pl.loop(1, planes)
    def _(offset):
        wait_bytes(plane_shares.at[0], plane_share_send.at[(z + offset) % planes])

    def wait_back(step):
        wait_bytes(stage.at[step, pl.ds(0, count - capacity)], back_send.at[step])
        wait_bytes(share_back.at[0, pl.ds(0, in_plane - 1)], back_share_send.at[step])

    def sum_copy(block):
        up = (block > z).astype(jnp.int32)
        relayed = (jnp.abs(block - z) == planes - 1).astype(jnp.int32)
        slot = z + relayed * (planes - z)
        goal = block + relayed * (1 - 2 * up) * (planes - 2)
        return remote(plane_rows.at[block], partial_in.at[slot], sum_send.at[block], sum_recv.at[slot], (goal, x, w))

    def sum_share_copy(block):
        return remote(
            share_home.at[block], share_grad_ref.at[pl.ds(z * in_plane, in_plane)],
            sum_share_send.at[block], sum_share_recv.at[z], (block, x, w),
        )

    @pl.loop(0, planes)
    def _(turn):
        step = jnp.where(turn == 0, first_back, jnp.where(turn == 1, second_back, jnp.where(turn == 2, third_back, 0)))
        block, _, _ = order(step)
        wait_bytes(back_hbm.at[block], back_recv.at[step])
        load = pltpu.make_async_copy(back_hbm.at[block], rows, load_sem)
        load.start()
        wait_bytes(share_home.at[block], back_share_recv.at[step])
        load.wait()

        @pl.when(step > 0)
        def _():
            sum_share_copy(block).start()

            merges = (inner == 1) & (jnp.abs(block - z) == 2)

            @pl.when(merges)
            def _():
                wait_bytes(partial_in.at[planes], sum_recv.at[planes])

            @pl.loop(0, width // chunk)
            def _(part):
                wide = pl.ds(pl.multiple_of(part * chunk, chunk), chunk)
                summed = dot_tn(chosen[step], rows[:, wide])

                @pl.when(merges)
                def _():
                    plane_rows[block, :, wide] = (summed + partial_in[planes, :, wide].astype(F32)).astype(BF16)

                @pl.when(jnp.logical_not(merges))
                def _():
                    plane_rows[block, :, wide] = summed.astype(BF16)

            sum_copy(block).start()

        @pl.when(step == 0)
        def _():
            share_grad_ref[pl.ds(z * in_plane, in_plane)] = share_home[z]

            @pl.loop(0, width // chunk)
            def _(part):
                wide = pl.ds(pl.multiple_of(part * chunk, chunk), chunk)
                row_grad_ref[:, wide] = dot_tn(chosen[0], rows[:, wide])

        @pl.when(turn == 0)
        def _():
            wait_back(second_back)
            start_back(third_back, order(third_back)[0])

        @pl.when(turn == 1)
        def _():
            wait_back(third_back)
            start_back(0, z)

    @pl.loop(1, planes)
    def _(offset):
        other = (z + offset) % planes
        wait_bytes(share_home.at[other], sum_share_recv.at[other])

        @pl.when(jnp.abs(other - z) < planes - 1)
        def _():
            wait_bytes(partial_in.at[other], sum_recv.at[other])

            @pl.loop(0, width // chunk)
            def _(part):
                wide = pl.ds(pl.multiple_of(part * chunk, chunk), chunk)
                row_grad_ref[:, wide] += partial_in[other, :, wide].astype(F32)

    @pl.loop(1, planes)
    def _(offset):
        other = (z + offset) % planes
        wait_bytes(plane_rows.at[other], sum_send.at[other])
        wait_bytes(share_home.at[other], sum_share_send.at[other])

    wait_back(0)
    wait_back(first_back)


def run_experts(planes, across, shards, capacity, own, shares, slots, my_slots, w_gate, w_up, w_down, top_rows):
    tokens, width = own.shape
    in_plane = across * shards
    count = in_plane * capacity
    units = w_gate.shape[1]
    experts = planes * in_plane
    hbm = pl.BlockSpec(memory_space=pl.ANY)
    vmem = pl.BlockSpec(memory_space=pltpu.VMEM)
    dma = pltpu.SemaphoreType.DMA
    flops = 12 * planes * count * width * units
    return pl.pallas_call(
        functools.partial(expert_kernel, planes, across, shards, capacity),
        in_specs=[vmem] * 7 + [hbm],
        out_specs=[hbm] * 7 + [vmem] * 2,
        out_shape=[
            jax.ShapeDtypeStruct((planes, count, width), BF16),
            jax.ShapeDtypeStruct((planes, count, width), BF16),
            jax.ShapeDtypeStruct((planes, count, width), BF16),
            jax.ShapeDtypeStruct((planes, count, units), BF16),
            jax.ShapeDtypeStruct((planes, count, units), BF16),
            jax.ShapeDtypeStruct((planes, count, units), BF16),
            jax.ShapeDtypeStruct((planes, count, width), BF16),
            jax.ShapeDtypeStruct((tokens, width), F32),
            jax.ShapeDtypeStruct((experts, 1, tokens), F32),
        ],
        scratch_shapes=[
            pltpu.VMEM((planes, tokens, width), BF16),
            pltpu.VMEM((planes, in_plane, 1, tokens), F32),
            pltpu.VMEM((planes, in_plane, 1, tokens), F32),
            pltpu.VMEM((planes, in_plane, 1, tokens), F32),
            pltpu.VMEM((planes, in_plane, 1, tokens), F32),
            pltpu.VMEM((planes, count, width), BF16),
            pltpu.VMEM((planes, count, tokens), BF16),
            pltpu.VMEM((count, width), BF16),
            pltpu.VMEM((count, width), BF16),
            pltpu.VMEM((count, units), BF16),
            pltpu.VMEM((count, units), BF16),
            pltpu.VMEM((count, units), BF16),
            pltpu.VMEM((count, 128), F32),
            pltpu.VMEM((planes + 1, tokens, width), BF16),
            dma((2, planes + 1)), dma((2, planes + 1)), dma((planes,)), dma((planes,)),
            dma((planes,)), dma((planes,)), dma((planes,)), dma((planes,)),
            dma((planes,)), dma((planes,)), dma((planes,)), dma((planes,)),
            dma((planes,)), dma((planes + 1,)), dma((planes,)), dma((planes,)),
            dma, dma, dma((5,)),
        ],
        compiler_params=pltpu.CompilerParams(vmem_limit_bytes=VMEM_LIMIT, collective_id=1, has_side_effects=True),
        cost_estimate=pl.CostEstimate(flops=4 * flops, bytes_accessed=100 * 10**6, transcendentals=2 * 10**6),
    )(own, shares, slots, my_slots, w_gate, w_up, w_down, top_rows)


def local(
    hidden_in, attn_gain, w_query, key_projection, value_projection, query_gain, key_gain, w_output, ffn_gain, w_router,
    routes, w_gate, w_up, w_down, cotangent,
):
    tokens_here, width = hidden_in.shape
    head_size = query_gain.shape[0]
    top_count = routes.shape[1]
    planes, across, shards = lax.axis_size("z"), lax.axis_size("x"), lax.axis_size("w")
    rings = planes * across
    device_count = rings * shards
    in_plane = across * shards
    experts = device_count
    capacity = 5 * tokens_here * top_count // (4 * experts)
    seq_length = tokens_here * shards

    cosine, sine = rope_tables(seq_length, head_size)
    query_gain_row, key_gain_row = query_gain[None, :], key_gain[None, :]

    capacity = -(-capacity // 16) * 16
    small = jnp.concatenate([w_router.T, ffn_gain[None, :], attn_gain[None, :]], axis=0).astype(F32)
    small = jnp.pad(small, ((0, -small.shape[0] % 8), (0, 0)))
    first_input, query_raw, key_raw, value, attended, branch, slots_flat, my_slots, small_all, weights, top_rows = (
        run_forward(
        planes, across, shards, capacity, hidden_in, small, routes.T, cotangent, w_query,
        key_projection, value_projection, query_gain_row, key_gain_row, cosine, sine, w_output,
        )
    )
    small_all = small_all.transpose(1, 0, 2).reshape(small.shape[0], width)
    router_full = small_all[:experts].astype(BF16)
    ffn_scale, attn_scale = small_all[experts : experts + 1], small_all[experts + 1 : experts + 2]
    source = hidden_in.astype(F32)
    middle = source + branch
    second_normed, second_scale = norm_forward(middle)
    second_input = (second_normed * ffn_scale).astype(BF16)
    logits = dot_nt(router_full, second_input)
    expert_ids = jnp.arange(experts, dtype=jnp.int32)
    routed = jnp.any(routes.T[None, :, :] == expert_ids[:, None, None], axis=1)
    peaks = jnp.max(jnp.where(routed, logits, -jnp.inf), axis=0, keepdims=True)
    shifted = jnp.where(routed, jnp.exp(jnp.where(routed, logits - peaks, 0.0)), 0.0)
    shares = shifted / jnp.sum(shifted, axis=0, keepdims=True)

    rows_in, _, weighted, hidden_units, gate_grad, up_grad, pair_grad, row_grad_sum, share_grad = run_experts(
        planes, across, shards, capacity, second_input, shares[:, None, :], slots_flat,
        my_slots, w_gate[0], w_up[0], w_down[0],
        top_rows,
    )
    share_grad = share_grad[:, 0, :]
    units = w_gate.shape[2]
    grad_top = cotangent.astype(F32)
    share_center = jnp.sum(shares * share_grad, axis=0, keepdims=True)
    logit_grad = (shares * (share_grad - share_center)).astype(BF16)
    router_grad = dot_tn(second_input, logit_grad.T)
    second_grad = row_grad_sum + dot(logit_grad.T, router_full)
    ffn_gain_grad = jnp.sum(second_grad * second_normed, axis=0)
    middle_grad = grad_top + norm_backward(second_grad * ffn_scale, second_normed, second_scale)
    wo_grad, wq_grad, first_part, query_gain_grad, key_gain_grad, _, expert_sum = run_backward(
        planes, across, shards, capacity, middle_grad.astype(BF16), w_output, attended, query_raw, key_raw, value,
        first_input, weights, query_gain_row, key_gain_row, cosine, sine, slots_flat, weighted,
    )
    mine = width // device_count
    early = jnp.concatenate(
        [router_grad.reshape(device_count, mine * experts), ffn_gain_grad.reshape(device_count, mine)], axis=1
    )
    early = jnp.pad(early, ((0, 0), (0, -early.shape[1] % 1024))).reshape(device_count, -1, 128)
    squares = jnp.stack([jnp.sum(source * source), jnp.sum(branch * branch)])
    shared = jnp.concatenate(
        [
            query_gain_grad[0:1],
            key_gain_grad[0:1],
            jnp.pad(squares, (0, head_size - 2))[None, :],
            jnp.zeros((5, head_size), F32),
        ],
        axis=0,
    )
    (
        sum_query, sum_key, sum_value, sum_output, hidden_out, grad_in, early_total, late_total, grad_gate, grad_up, grad_down,
    ) = run_reduce(
        planes, across, shards, wq_grad, wo_grad, first_part, hidden_in, middle, expert_sum, middle_grad, attn_scale, early,
        shared, rows_in.reshape(-1, width), gate_grad.reshape(-1, units), up_grad.reshape(-1, units),
        hidden_units.reshape(-1, units), pair_grad.reshape(-1, width), w_query.shape[1], key_projection.shape[1],
    )
    early_total = early_total.reshape(-1)
    sum_router = early_total[: mine * experts].reshape(mine, experts)
    sum_ffn = early_total[mine * experts : mine * (experts + 1)]
    linear = (lax.axis_index("z") * across + lax.axis_index("x")) * shards + lax.axis_index("w")
    sum_attn = lax.dynamic_slice_in_dim(late_total[: width // 128].reshape(-1), linear * mine, mine)
    late_total = late_total[width // 128 :]
    totals = jnp.concatenate([late_total[0], late_total[1], late_total[2, :4]])
    root_mean_squares = jnp.sqrt(totals[2 * head_size :] / (tokens_here * device_count * width))
    return (
        hidden_out,
        grad_in,
        sum_attn,
        sum_query,
        sum_key,
        sum_value,
        totals[:head_size],
        totals[head_size : 2 * head_size],
        sum_output,
        sum_ffn,
        sum_router,
        grad_gate[None],
        grad_up[None],
        grad_down[None],
        root_mean_squares,
    )


def solution(mesh):
    rings, shards = mesh.shape["ep"], mesh.shape["ws"]
    planes = 4 if rings % 4 == 0 else 1
    fine = Mesh(mesh.devices.reshape(planes, rings // planes, shards), ("z", "x", "w"))
    every = ("z", "x", "w")
    rows, deep = P(every, None), P(every, None, None)
    return jax.shard_map(
        local,
        mesh=fine,
        in_specs=(
            rows, P("w"), P("w", None), P("w", None), P("w", None), P(), P(), P("w", None), P("w"), P("w", None),
            rows, deep, deep, deep, rows,
        ),
        out_specs=(
            rows, rows, P(every), rows, rows, rows, P(), P(), rows, P(every), rows, deep, deep, deep, P(),
        ),
        check_vma=False,
    )
```

```python
import functools

import jax
import jax.numpy as jnp
import numpy as np
from jax import lax
from jax.experimental import pallas as pl
from jax.experimental.pallas import tpu as pltpu
from jax.sharding import Mesh
from jax.sharding import PartitionSpec as P

BLOCK = 256
EPS = 1e-06
ROPE_BASE = 1000000.0
F32 = jnp.float32
BF16 = jnp.bfloat16
VMEM_LIMIT = 65024 * 1024


def dot(left, right):
    return jnp.dot(left, right, preferred_element_type=F32)


def dot_tn(left, right):
    return lax.dot_general(left, right, (((0,), (0,)), ((), ())), preferred_element_type=F32)


def dot_nt(left, right):
    return lax.dot_general(left, right, (((1,), (1,)), ((), ())), preferred_element_type=F32)


def rope_tables(seq_length, head_size):
    indices = np.arange(head_size // 2, dtype=np.float32)
    frequency = (np.float32(ROPE_BASE) ** (np.float32(-2.0) * indices / np.float32(head_size))).astype(np.float32)
    angles = np.arange(seq_length, dtype=np.float32)[:, None] * frequency[None, :]
    cosine, sine = np.cos(angles), np.sin(angles)
    return np.concatenate([cosine, cosine], axis=1), np.concatenate([-sine, sine], axis=1)


def norm_forward(values):
    scaling = lax.rsqrt(jnp.mean(values * values, axis=-1, keepdims=True) + EPS)
    return values * scaling, scaling


def norm_backward(grad_normed, normed, scaling):
    return scaling * (grad_normed - normed * jnp.mean(grad_normed * normed, axis=-1, keepdims=True))


def half_turn(values):
    return pltpu.roll(values, values.shape[-1] // 2, 1)


def rotate(values, cosine, signed_sine):
    return values * cosine + half_turn(values) * signed_sine


def unrotate(grads, cosine, signed_sine):
    return grads * cosine - half_turn(grads) * signed_sine


MESH = pl.DeviceIdType.MESH


def remote(source, target, send, recv, device):
    return pltpu.make_async_remote_copy(
        src_ref=source, dst_ref=target, send_sem=send, recv_sem=recv, device_id=device, device_id_type=MESH
    )


def wait_bytes(ref, sem):
    pltpu.make_async_copy(ref, ref, sem).wait()


def line_order(z, planes, step):
    low = jnp.minimum(z, planes - 1 - z)
    paired = (step <= 2 * low).astype(jnp.int32)
    hop = paired * ((step + 1) // 2) + (1 - paired) * (step - low)
    longer = (z > planes - 1 - z).astype(jnp.int32)
    below = paired * (step % 2) + (1 - paired) * longer
    return z + hop - 2 * below * hop, hop, below


def greet_plane_and_line(planes, across, shards):
    z, x, w = lax.axis_index("z"), lax.axis_index("x"), lax.axis_index("w")
    in_plane = across * shards
    me = x * shards + w
    barrier = pltpu.get_barrier_semaphore()

    @pl.loop(1, in_plane)
    def _(offset):
        index = (me + offset) % in_plane
        pl.semaphore_signal(barrier, inc=1, device_id=(z, index // shards, index % shards), device_id_type=MESH)

    @pl.loop(1, planes)
    def _(offset):
        pl.semaphore_signal(barrier, inc=1, device_id=((z + offset) % planes, x, w), device_id_type=MESH)

    pl.semaphore_wait(barrier, in_plane + planes - 2)


def attention_forward(
    planes, across, shards, capacity, heads_a_step,
    own_ref, small_ref, routes_ref, top_ref, wq_hbm, wk_hbm, wv_hbm, query_gain_ref, key_gain_ref, cosine_ref, sine_ref, wo_ref,
    input_ref, query_raw_ref, key_raw_ref, value_ref, attended_ref, middle_ref, slots_ref, my_slots_ref, shares_ref, squares_ref,
    second_hbm, small_hbm,
    weights_hbm, top_rows_hbm,
    hidden, small_in, weights, key_rot_ref, routes_in, far_slots, plane_rows, stage, chosen, pair_out, far_out,
    gather_send, gather_recv, small_send, small_recv, weight_send, weight_recv, route_send, route_recv, plane_route_send,
    plane_route_recv, far_send, far_recv,
    line_send, line_recv, top_send, top_recv, pair_send, pair_recv, store_sem, small_sem, second_sem,
):
    step = pl.program_id(0)
    head_size = cosine_ref.shape[1]
    last = wo_ref.shape[0] // (heads_a_step * head_size)
    seq_length = cosine_ref.shape[0]
    blocks = seq_length // BLOCK
    factor = head_size ** (-0.5)
    z, x, w = lax.axis_index("z"), lax.axis_index("x"), lax.axis_index("w")
    in_plane = across * shards
    tokens, width = own_ref.shape
    me = x * shards + w
    depth = width // shards
    experts = planes * in_plane
    wide = heads_a_step * head_size
    chunk = 512
    targets = in_plane // 2
    pair, core = w // 2, w % 2
    sibling, opposite, other = pair * 2 + 1 - core, (1 - pair) * 2 + core, (1 - pair) * 2 + 1 - core

    def slice_of(index):
        return pl.ds(pl.multiple_of(index * capacity, 16), capacity)

    def tokens_of(index):
        return pl.ds(pl.multiple_of(index * tokens, tokens), tokens)

    def gather_copy(kind, owner, target):
        return remote(
            hidden.at[tokens_of(owner)], hidden.at[tokens_of(owner)], gather_send.at[kind], gather_recv.at[kind],
            (z, x, target),
        )

    def small_copy(offset):
        return remote(small_ref, small_in.at[w], small_send.at[offset], small_recv.at[w], (z, x, (w + offset) % shards))

    def columns_at(start, size):
        return pl.ds(pl.multiple_of(start, 128), size)

    my_depth = pl.ds(pl.multiple_of(w * depth, 16), depth)
    query_wide = last * wide

    def weight_pieces(piece, target):
        if piece is None:
            key_at, value_at = columns_at(target * head_size, head_size), columns_at(target * head_size, head_size)
            return [
                (wk_hbm.at[:, key_at], weights.at[my_depth, columns_at(last * wide, head_size)], last),
                (wv_hbm.at[:, value_at], weights.at[my_depth, columns_at(last * wide + head_size, head_size)], last),
            ]
        return [
            (
                wq_hbm.at[:, columns_at(target * query_wide + piece * wide, wide)],
                weights.at[my_depth, columns_at(piece * wide, wide)], piece,
            )
        ]

    def start_weights(piece):
        @pl.loop(1, shards)
        def _(offset):
            for source, goal, sem in weight_pieces(piece, (w + offset) % shards):
                remote(source, goal, weight_send.at[sem], weight_recv.at[sem], (z, x, (w + offset) % shards)).start()

        for source, goal, sem in weight_pieces(piece, w):
            pltpu.make_async_copy(source, goal, weight_recv.at[sem]).start()

    def wait_weights(piece):
        whole_piece = weights.at[:, columns_at(piece * wide, wide)]
        wait_bytes(whole_piece, weight_recv.at[piece])

    def line_copy(column, block, hop, direction):
        rows = plane_rows.at[column, block]
        return remote(
            rows, rows, line_send.at[column, direction, hop], line_recv.at[column, direction, hop],
            (z + 1 - 2 * direction, x, w),
        )

    def start_line(column, block, hop, upward, downward):
        @pl.when(upward & (z + 1 < planes))
        def _():
            line_copy(column, block, hop, 0).start()

        @pl.when(downward & (z > 0))
        def _():
            line_copy(column, block, hop, 1).start()

    def relay(column, hop):
        @pl.when(z - hop >= 0)
        def _():
            wait_bytes(plane_rows.at[column, 0], line_recv.at[column, 0, hop])

            @pl.when(z + 1 < planes)
            def _():
                line_copy(column, z - hop, hop + 1, 0).start()

        @pl.when(z + hop < planes)
        def _():
            wait_bytes(plane_rows.at[column, 0], line_recv.at[column, 1, hop])

            @pl.when(z > 0)
            def _():
                line_copy(column, z + hop, hop + 1, 1).start()

    expert_of = z * in_plane + lax.broadcasted_iota(jnp.int32, (in_plane, tokens), 0)
    earlier = (
        lax.broadcasted_iota(jnp.int32, (tokens, tokens), 0) < lax.broadcasted_iota(jnp.int32, (tokens, tokens), 1)
    ).astype(F32).astype(BF16)
    slot_ids = lax.broadcasted_iota(jnp.int32, (capacity, tokens), 0)

    def fill_slots(column, table):
        @pl.loop(0, planes)
        def _(block):
            hits = jnp.zeros((in_plane, tokens), F32)
            for k in range(routes_ref.shape[0]):
                hits += (routes_in[column, block, k : k + 1, :] == expert_of).astype(F32)
            ranks = dot(hits.astype(BF16), earlier).astype(jnp.int32)
            slots = jnp.where(hits > 0.0, ranks, -1)
            for index in range(in_plane):
                table[block * in_plane + index] = slots[index : index + 1, :]

    def pack(column, turn, table):
        block, _, _ = line_order(z, planes, turn)

        def index_of(target):
            return (target // 2) * shards + pair * 2 + target % 2

        for target in range(targets):
            slots = table[block * in_plane + index_of(target)]
            chosen[target * capacity : (target + 1) * capacity, :] = (slot_ids == slots).astype(F32).astype(BF16)

        @pl.loop(0, width // chunk)
        def _(part):
            here = pl.ds(pl.multiple_of(part * chunk, chunk), chunk)
            stage[column, turn, :, here] = dot(chosen[...], plane_rows[column, block, :, here]).astype(BF16)

        source = x * shards + (w if column == 0 else opposite)
        mine = x * 2 + core

        @pl.loop(1, targets)
        def _(offset):
            target = (mine + offset) % targets
            remote(
                stage.at[column, turn, slice_of(target)], top_rows_hbm.at[block, slice_of(source)],
                top_send.at[column, turn], top_recv.at[block], (z, target // 2, pair * 2 + target % 2),
            ).start()

        pltpu.make_async_copy(
            stage.at[column, turn, slice_of(mine)], top_rows_hbm.at[block, slice_of(source)], top_recv.at[block]
        ).start()

    def route_copy(offset):
        return remote(
            routes_ref, routes_in.at[me, z], route_send.at[offset], route_recv.at[z], ((z + offset) % planes, x, w)
        )

    far_top = remote(top_ref, plane_rows.at[1, z], far_send, far_recv, (z, x, opposite))
    opposite_me = x * shards + opposite

    def plane_route_copy(index):
        return remote(
            routes_in.at[me], routes_in.at[me], plane_route_send, plane_route_recv.at[me],
            (z, index // shards, index % shards),
        )

    def fill_my_slots():
        my_expert = z * in_plane + me

        @pl.loop(0, planes)
        def _(block):
            hits = jnp.concatenate(
                [
                    jnp.max((routes_in[index, block] == my_expert).astype(F32), axis=0, keepdims=True)
                    for index in range(in_plane)
                ],
                axis=0,
            )
            ranks = dot(hits.astype(BF16), earlier).astype(jnp.int32)
            slots = jnp.where(hits > 0.0, ranks, -1)
            for index in range(in_plane):
                my_slots_ref[block * in_plane + index] = slots[index : index + 1, :]

    @pl.when(step == 0)
    def _():
        greet_plane_and_line(planes, across, shards)
        far_top.start()

        @pl.loop(1, planes)
        def _(offset):
            route_copy(offset).start()

        @pl.loop(1, shards)
        def _(offset):
            small_copy(offset).start()

        plane_rows[0, z] = top_ref[...]
        start_line(0, z, 1, True, True)
        hidden[tokens_of(w), :] = own_ref[...]
        gather_copy(0, w, sibling).start()
        small_in[w] = small_ref[...]
        routes_in[me, z] = routes_ref[...]

        @pl.loop(1, planes)
        def _(offset):
            source = (z + offset) % planes
            wait_bytes(routes_in.at[me, source], route_recv.at[source])

        @pl.loop(1, in_plane)
        def _(offset):
            plane_route_copy((me + offset) % in_plane).start()

        fill_slots(me, slots_ref)
        pack(0, 0, slots_ref)
        gather_copy(1, w, opposite).start()
        relay(0, 1)
        wait_bytes(plane_rows.at[1, z], far_recv)
        start_line(1, z, 1, True, True)
        start_weights(None)
        wait_bytes(routes_in.at[opposite_me], plane_route_recv.at[opposite_me])
        fill_slots(opposite_me, far_slots)
        pack(1, 0, far_slots)
        wait_bytes(hidden.at[tokens_of(opposite)], gather_recv.at[1])
        gather_copy(2, opposite, sibling).start()
        start_weights(0)
        pack(0, 1, slots_ref)

        @pl.loop(1, shards)
        def _(offset):
            source = (w + offset) % shards
            wait_bytes(small_in.at[source], small_recv.at[source])

        wait_bytes(hidden.at[tokens_of(sibling)], gather_recv.at[0])
        wait_bytes(hidden.at[tokens_of(other)], gather_recv.at[2])
        for block in range(blocks):
            rows = pl.ds(block * BLOCK, BLOCK)
            normed, _ = norm_forward(hidden[rows, :].astype(F32))
            for part in range(shards):
                here = slice(part * depth, (part + 1) * depth)
                input_ref[rows, here] = (normed[:, here] * small_in[part, experts + 1 : experts + 2, :]).astype(BF16)
        relay(0, 2)
        start_weights(1)
        pack(0, 2, slots_ref)
        wait_weights(last)
        for block in range(blocks):
            rows = pl.ds(block * BLOCK, BLOCK)
            key_value = dot(input_ref[rows, :], weights[:, columns_at(last * wide, wide)])
            key_raw = key_value[:, :head_size]
            key_raw_ref[rows, :] = key_raw
            value_ref[rows, :] = key_value[:, head_size:].astype(BF16)
            key_normed, _ = norm_forward(key_raw)
            key_rot_ref[rows, :] = rotate(
                key_normed * key_gain_ref[...], cosine_ref[rows, :], sine_ref[rows, :]
            ).astype(BF16)
        relay(1, 1)
        pack(1, 1, far_slots)

    for piece in range(2, last):

        @pl.when(step == piece - 2)
        def _():
            wait_weights(piece - 2)
            if piece == last - 1:
                for kind in range(3):
                    wait_bytes(hidden.at[tokens_of(w)], gather_send.at[kind])
            start_weights(piece)

    @pl.when((step >= last - 2) & (step < last))
    def _():
        wait_weights(step)

    @pl.when(step < last)
    def _():
        here = columns_at(step * wide, wide)
        for block in range(blocks):
            rows = pl.ds(block * BLOCK, BLOCK)
            seen = pl.ds(0, (block + 1) * BLOCK)
            query_raw = dot(input_ref[rows, :], weights[:, here])
            query_raw_ref[rows, :] = query_raw
            parts = []
            for head in range(heads_a_step):
                columns = slice(head * head_size, (head + 1) * head_size)
                query_normed, _ = norm_forward(query_raw[:, columns])
                query_rot = rotate(
                    query_normed * query_gain_ref[...], cosine_ref[rows, :], sine_ref[rows, :]
                ).astype(BF16)
                scores = dot_nt(query_rot, key_rot_ref[seen, :]) * factor
                exponent = jnp.exp(scores - jnp.max(scores, axis=-1, keepdims=True))
                probs = (exponent / jnp.sum(exponent, axis=-1, keepdims=True)).astype(BF16)
                parts.append(dot(probs, value_ref[seen, :]).astype(BF16))
            attended_ref[rows, here] = jnp.concatenate(parts, axis=1)

    @pl.when(step == 1)
    def _():
        relay(0, 3)
        pack(0, 3, slots_ref)

    @pl.when(step == 2)
    def _():
        relay(1, 2)
        pack(1, 2, far_slots)

    def project(owner, goal, added):
        rows = tokens_of(owner)

        @pl.loop(0, width // chunk)
        def _(part):
            here = pl.ds(pl.multiple_of(part * chunk, chunk), chunk)
            value = dot(attended_ref[rows, :], wo_ref[:, here])
            if added is not None:
                value += hidden[added, here].astype(F32)
            goal[:, here] = value.astype(goal.dtype)

    def pair_copy(kind):
        at = pl.ds(kind * tokens, tokens)
        return remote(pair_out.at[kind], hidden.at[at], pair_send.at[kind], pair_recv.at[kind], (z, x, sibling))

    far_at = pl.ds(2 * tokens, tokens)
    far_copy = remote(far_out, hidden.at[far_at], pair_send.at[2], pair_recv.at[2], (z, x, opposite))

    @pl.when(step == last)
    def _():
        store = pltpu.make_async_copy(weights, weights_hbm, store_sem)
        store.start()
        small_store = pltpu.make_async_copy(small_in, small_hbm, small_sem)
        small_store.start()
        project(other, pair_out.at[0], None)
        pair_copy(0).start()
        project(sibling, pair_out.at[1], None)
        pair_copy(1).start()
        wait_bytes(hidden.at[pl.ds(0, tokens)], pair_recv.at[0])
        project(opposite, far_out, pl.ds(0, tokens))
        far_copy.start()
        wait_bytes(hidden.at[pl.ds(tokens, tokens)], pair_recv.at[1])
        project(w, middle_ref, pl.ds(tokens, tokens))
        @pl.loop(1, in_plane)
        def _(offset):
            index = (me + offset) % in_plane

            @pl.when(index != opposite_me)
            def _():
                wait_bytes(routes_in.at[index], plane_route_recv.at[index])

        fill_my_slots()
        relay(1, 3)
        pack(1, 3, far_slots)
        wait_bytes(hidden.at[far_at], pair_recv.at[2])
        wait_bytes(far_out, pair_send.at[2])
        ffn_row = jnp.concatenate([small_in[part, experts : experts + 1, :] for part in range(shards)], axis=1)

        def finish_rows(piece, carry):
            at = pl.ds(pl.multiple_of(piece * 64, 64), 64)
            far = pl.ds(pl.multiple_of(2 * tokens + piece * 64, 64), 64)
            branch = middle_ref[at, :] + hidden[far, :].astype(F32)
            source = own_ref[at, :].astype(F32)
            middle = source + branch
            middle_ref[at, :] = middle
            normed, _ = norm_forward(middle)
            far_out[at, :] = (normed * ffn_row).astype(BF16)
            return (
                carry[0] + jnp.sum(jnp.sum(source * source, axis=1, keepdims=True), axis=0, keepdims=True),
                carry[1] + jnp.sum(jnp.sum(branch * branch, axis=1, keepdims=True), axis=0, keepdims=True),
            )

        zero = jnp.zeros((1, 1), F32)
        source_square, branch_square = lax.fori_loop(0, tokens // 64, finish_rows, (zero, zero))
        second_store = pltpu.make_async_copy(far_out, second_hbm, second_sem)
        second_store.start()
        lane = lax.broadcasted_iota(jnp.int32, (8, 128), 1)
        row = lax.broadcasted_iota(jnp.int32, (8, 128), 0)
        values = jnp.where(lane == 0, source_square, 0.0) + jnp.where(lane == 1, branch_square, 0.0)
        squares_ref[...] = jnp.where(row == 2, values, 0.0)
        logits = jnp.zeros((experts, tokens), F32)
        for part in range(shards):
            logits += dot_nt(small_in[part, :experts, :].astype(BF16), far_out[:, part * depth : (part + 1) * depth])
        expert_ids = lax.broadcasted_iota(jnp.int32, (experts, tokens), 0)
        hits = jnp.zeros((experts, tokens), F32)
        for k in range(routes_ref.shape[0]):
            hits += (routes_ref[k : k + 1, :] == expert_ids).astype(F32)
        routed = hits > 0.0
        peaks = jnp.max(jnp.where(routed, logits, -jnp.inf), axis=0, keepdims=True)
        shifted = jnp.where(routed, jnp.exp(jnp.where(routed, logits - peaks, 0.0)), 0.0)
        shares = shifted / jnp.sum(shifted, axis=0, keepdims=True)
        for expert in range(experts):
            shares_ref[expert] = shares[expert : expert + 1, :]

        @pl.loop(0, planes)
        def _(block):
            wait_bytes(top_rows_hbm.at[block], top_recv.at[block])
            if targets > 1:
                for column in range(2):
                    wait_bytes(stage.at[column, 0, pl.ds(0, (targets - 1) * capacity)], top_send.at[column, block])

        for kind in range(2):
            wait_bytes(far_out, pair_send.at[kind])

        @pl.loop(1, shards)
        def _(offset):
            wait_bytes(small_in.at[w], small_send.at[offset])

        @pl.loop(1, planes)
        def _(offset):
            wait_bytes(routes_in.at[0, 0], route_send.at[offset])

        wait_bytes(routes_in.at[pl.ds(0, in_plane - 1)], plane_route_send)
        wait_bytes(plane_rows.at[1, 0], far_send)

        @pl.loop(0, last + 1)
        def _(piece):
            wait_bytes(weights.at[pl.ds(0, (shards - 1) * depth), pl.ds(0, wide)], weight_send.at[piece])

        for column in range(2):
            for hop in range(1, planes):

                @pl.when((z - (hop - 1) >= 0) & (z + 1 < planes))
                def _():
                    wait_bytes(plane_rows.at[0, 0], line_send.at[column, 0, hop])

                @pl.when((z + (hop - 1) < planes) & (z > 0))
                def _():
                    wait_bytes(plane_rows.at[0, 0], line_send.at[column, 1, hop])

        store.wait()
        small_store.wait()
        second_store.wait()


def attention_backward(
    planes, across, shards, capacity, heads_a_step,
    own_grad_ref, wo_ref, attended_ref, query_raw_ref, key_raw_ref, value_ref, input_ref, wq_ref,
    query_gain_ref, key_gain_ref, cosine_ref, sine_ref, slots_ref, weighted_hbm,
    wo_grad_ref, wq_grad_ref, first_grad_ref, query_gain_grad_ref, key_gain_grad_ref, returned_hbm, expert_sum_ref,
    total_ref, key_rot_ref, key_grad_ref, value_grad_ref, query_grad_ref, turned_ref, grad_ref,
    rows, chosen, partial_out, partial_in,
    gather_send, gather_recv, back_send, back_recv, sum_send, sum_recv, load_sem,
):
    step = pl.program_id(0)
    last = pl.num_programs(0) - 1
    head_size = cosine_ref.shape[1]
    seq_length = cosine_ref.shape[0]
    blocks = seq_length // BLOCK
    factor = head_size ** (-0.5)
    z, x, w = lax.axis_index("z"), lax.axis_index("x"), lax.axis_index("w")
    in_plane = across * shards
    me = x * shards + w
    tokens, width = own_grad_ref.shape
    count = in_plane * capacity
    chunk = 512
    pair, core = w // 2, w % 2
    sibling, opposite, other = pair * 2 + 1 - core, (1 - pair) * 2 + core, (1 - pair) * 2 + 1 - core

    def slice_of(index):
        return pl.ds(pl.multiple_of(index * capacity, 16), capacity)

    def tokens_of(index):
        return pl.ds(pl.multiple_of(index * tokens, tokens), tokens)

    def gather_copy(kind, owner, target):
        return remote(
            grad_ref.at[tokens_of(owner)], grad_ref.at[tokens_of(owner)], gather_send.at[kind], gather_recv.at[kind],
            (z, x, target),
        )

    def back_copy(block, index):
        return remote(
            weighted_hbm.at[block, slice_of(index)], returned_hbm.at[block, slice_of(me)],
            back_send.at[block], back_recv.at[block], (z, index // shards, index % shards),
        )

    pace = [(1, 1), (2, 2), (3, 3)]

    def start_back(turn, near, far):
        block, _, _ = line_order(z, planes, planes - 1 - turn)

        @pl.loop(1, in_plane)
        def _(offset):
            index = (me + offset) % in_plane
            beside = (index % shards) // 2 == pair

            @pl.when((beside & near) | (jnp.logical_not(beside) & far))
            def _():
                back_copy(block, index).start()

        @pl.when(near)
        def _():
            pltpu.make_async_copy(
                weighted_hbm.at[block, slice_of(me)], returned_hbm.at[block, slice_of(me)], back_recv.at[block]
            ).start()

    def sum_copy(block):
        return remote(partial_out.at[block], partial_in.at[z], sum_send.at[block], sum_recv.at[z], (block, x, w))

    def combine(turn):
        place = planes - 1 - turn
        block, _, _ = line_order(z, planes, place)
        wait_bytes(returned_hbm.at[block], back_recv.at[block])
        load = pltpu.make_async_copy(returned_hbm.at[block], rows, load_sem)
        load.start()
        if place > 0:
            start_back(turn + 1, step >= 0, step >= 0)
        slot_ids = lax.broadcasted_iota(jnp.int32, (capacity, tokens), 0)

        @pl.loop(0, in_plane)
        def _(index):
            slots = slots_ref[block * in_plane + index]
            chosen[slice_of(index), :] = (slot_ids == slots).astype(F32).astype(BF16)

        load.wait()

        @pl.loop(0, width // chunk)
        def _(part):
            wide = pl.ds(pl.multiple_of(part * chunk, chunk), chunk)
            summed = dot_tn(chosen[...], rows[:, wide])
            if place > 0:
                partial_out[block, :, wide] = summed.astype(BF16)
            else:
                expert_sum_ref[:, wide] = summed

        if place > 0:
            sum_copy(block).start()

    @pl.when(step == 0)
    def _():
        greet_plane_and_line(planes, across, shards)
        grad_ref[tokens_of(w), :] = own_grad_ref[...]
        gather_copy(1, w, opposite).start()
        gather_copy(0, w, sibling).start()
        start_back(0, step == 0, step != 0)
        key_normed, _ = norm_forward(key_raw_ref[...])
        key_rot_ref[...] = rotate(key_normed * key_gain_ref[...], cosine_ref[...], sine_ref[...]).astype(BF16)
        key_grad_ref[...] = jnp.zeros_like(key_grad_ref)
        value_grad_ref[...] = jnp.zeros_like(value_grad_ref)
        query_gain_grad_ref[...] = jnp.zeros_like(query_gain_grad_ref)
        for block in range(blocks):
            rows_here = pl.ds(block * BLOCK, BLOCK)
            turned_ref[:, rows_here] = input_ref[rows_here, :].T
        wait_bytes(grad_ref.at[tokens_of(opposite)], gather_recv.at[1])
        gather_copy(2, opposite, sibling).start()
        start_back(0, step != 0, step == 0)
        wait_bytes(grad_ref.at[tokens_of(sibling)], gather_recv.at[0])
        wait_bytes(grad_ref.at[tokens_of(other)], gather_recv.at[2])

    @pl.when(step < last)
    def _():
        wo_grad_ref[...] = dot_tn(attended_ref[...], grad_ref[...]).astype(BF16)
        for block in range(blocks):
            rows_here = pl.ds(block * BLOCK, BLOCK)
            seen = pl.ds(0, (block + 1) * BLOCK)
            attended_grad = dot_nt(grad_ref[rows_here, :], wo_ref[...]).astype(BF16)
            for head in range(heads_a_step):
                columns = slice(head * head_size, (head + 1) * head_size)
                query_normed, query_scale = norm_forward(query_raw_ref[rows_here, columns])
                cosine, sine = cosine_ref[rows_here, :], sine_ref[rows_here, :]
                query_rot = rotate(query_normed * query_gain_ref[...], cosine, sine).astype(BF16)
                head_grad = attended_grad[:, columns]
                keys, values = key_rot_ref[seen, :], value_ref[seen, :]
                scores = dot_nt(query_rot, keys) * factor
                exponent = jnp.exp(scores - jnp.max(scores, axis=-1, keepdims=True))
                probs = exponent / jnp.sum(exponent, axis=-1, keepdims=True)
                prob_grad = dot_nt(head_grad, values)
                value_grad_ref[seen, :] += dot_tn(probs.astype(BF16), head_grad)
                center = jnp.sum(probs * prob_grad, axis=-1, keepdims=True)
                score_grad = (probs * (prob_grad - center)).astype(BF16)
                key_grad_ref[seen, :] += dot_tn(score_grad, query_rot) * factor
                query_rot_grad = dot(score_grad, keys) * factor
                unrotated = unrotate(query_rot_grad, cosine, sine)
                query_gain_grad_ref[0:1, :] += jnp.sum(unrotated * query_normed, axis=0, keepdims=True)
                query_grad_ref[rows_here, columns] = norm_backward(
                    unrotated * query_gain_ref[...], query_normed, query_scale
                ).astype(BF16)
            partial = dot_nt(query_grad_ref[rows_here, :], wq_ref[...])

            @pl.when(step == 0)
            def _():
                total_ref[rows_here, :] = partial

            @pl.when(step > 0)
            def _():
                total_ref[rows_here, :] += partial

            for turn, place in enumerate(pace):
                if place[1] == block:

                    @pl.when(step == place[0])
                    def _():
                        combine(turn)

    @pl.when(step == last)
    def _():
        key_normed, key_scale = norm_forward(key_raw_ref[...])
        unrotated = unrotate(key_grad_ref[...], cosine_ref[...], sine_ref[...])
        key_gain_grad_ref[...] = jnp.zeros_like(key_gain_grad_ref)
        key_gain_grad_ref[0:1, :] = jnp.sum(unrotated * key_normed, axis=0, keepdims=True)
        key_grad = norm_backward(unrotated * key_gain_ref[...], key_normed, key_scale)
        query_grad_ref[:, :head_size] = key_grad.astype(BF16)
        query_grad_ref[:, head_size : 2 * head_size] = value_grad_ref[...].astype(BF16)
        for block in range(blocks):
            rows_here = pl.ds(block * BLOCK, BLOCK)
            first_grad_ref[rows_here, :] = (
                total_ref[rows_here, :] + dot_nt(query_grad_ref[rows_here, :], wq_ref[...])
            ).astype(BF16)

    wq_grad_ref[...] = dot(turned_ref[...], query_grad_ref[...]).astype(BF16)

    @pl.when(step == last)
    def _():
        for turn in range(len(pace), planes):
            combine(turn)

        @pl.loop(1, planes)
        def _(offset):
            source = (z + offset) % planes
            wait_bytes(partial_in.at[source], sum_recv.at[source])

            @pl.loop(0, width // chunk)
            def _(part):
                wide = pl.ds(pl.multiple_of(part * chunk, chunk), chunk)
                expert_sum_ref[:, wide] += partial_in[source, :, wide].astype(F32)

            wait_bytes(partial_out.at[source], sum_send.at[source])

        @pl.loop(0, planes)
        def _(block):
            wait_bytes(weighted_hbm.at[block, pl.ds(0, count - capacity)], back_send.at[block])

        wait_bytes(grad_ref.at[tokens_of(w)], gather_send.at[0])
        wait_bytes(grad_ref.at[tokens_of(w)], gather_send.at[1])
        wait_bytes(grad_ref.at[tokens_of(w)], gather_send.at[2])


def whole(shape):
    return pl.BlockSpec(shape, lambda step: (0,) * len(shape), pipeline_mode=pl.Buffered(1))


def run_forward(
    planes, across, shards, capacity, own, small, routes, top, w_query, w_key, w_value, query_gain, key_gain, cosine, sine, wo
):
    tokens, width = own.shape
    seq_length = tokens * shards
    head_size = query_gain.shape[1]
    heads_here = wo.shape[0] // head_size
    pair = 2
    wide = pair * head_size
    steps = heads_here // pair
    in_plane = across * shards
    count = in_plane * capacity
    hbm = pl.BlockSpec(memory_space=pl.ANY)
    dma = pltpu.SemaphoreType.DMA
    slots_shape = (planes * in_plane, 1, tokens)
    return pl.pallas_call(
        functools.partial(attention_forward, planes, across, shards, capacity, pair),
        grid=(steps + 1,),
        in_specs=[
            whole((tokens, width)),
            whole(small.shape),
            whole(routes.shape),
            whole((tokens, width)),
            hbm,
            hbm,
            hbm,
            whole((1, head_size)),
            whole((1, head_size)),
            whole((seq_length, head_size)),
            whole((seq_length, head_size)),
            whole(wo.shape),
        ],
        out_specs=[
            whole((seq_length, width)),
            pl.BlockSpec((seq_length, wide), lambda step: (0, jnp.minimum(step, steps - 1))),
            whole((seq_length, head_size)),
            whole((seq_length, head_size)),
            whole((seq_length, heads_here * head_size)),
            whole((tokens, width)),
            whole(slots_shape),
            whole(slots_shape),
            whole(slots_shape),
            whole((8, 128)),
            hbm,
            hbm,
            hbm,
            hbm,
        ],
        out_shape=[
            jax.ShapeDtypeStruct((seq_length, width), BF16),
            jax.ShapeDtypeStruct((seq_length, heads_here * head_size), F32),
            jax.ShapeDtypeStruct((seq_length, head_size), F32),
            jax.ShapeDtypeStruct((seq_length, head_size), BF16),
            jax.ShapeDtypeStruct((seq_length, heads_here * head_size), BF16),
            jax.ShapeDtypeStruct((tokens, width), F32),
            jax.ShapeDtypeStruct(slots_shape, jnp.int32),
            jax.ShapeDtypeStruct(slots_shape, jnp.int32),
            jax.ShapeDtypeStruct(slots_shape, F32),
            jax.ShapeDtypeStruct((8, 128), F32),
            jax.ShapeDtypeStruct((tokens, width), BF16),
            jax.ShapeDtypeStruct((shards,) + small.shape, F32),
            jax.ShapeDtypeStruct((width, (steps + 1) * wide), BF16),
            jax.ShapeDtypeStruct((planes, count, width), BF16),
        ],
        scratch_shapes=[
            pltpu.VMEM((seq_length, width), BF16),
            pltpu.VMEM((shards,) + small.shape, F32),
            pltpu.VMEM((width, (steps + 1) * wide), BF16),
            pltpu.VMEM((seq_length, head_size), BF16),
            pltpu.VMEM((in_plane, planes) + routes.shape, jnp.int32),
            pltpu.VMEM(slots_shape, jnp.int32),
            pltpu.VMEM((2, planes, tokens, width), BF16),
            pltpu.VMEM((2, planes, count // 2, width), BF16),
            pltpu.VMEM((count // 2, tokens), BF16),
            pltpu.VMEM((2, tokens, width), BF16),
            pltpu.VMEM((tokens, width), BF16),
            dma((3,)), dma((3,)), dma((shards,)), dma((shards,)), dma((steps + 1,)), dma((steps + 1,)),
            dma((planes,)), dma((planes,)), dma, dma((in_plane,)), dma, dma,
            dma((2, 2, planes + 1)), dma((2, 2, planes + 1)), dma((2, planes)), dma((planes,)), dma((3,)), dma((3,)), dma, dma, dma,
        ],
        compiler_params=pltpu.CompilerParams(vmem_limit_bytes=VMEM_LIMIT, collective_id=5, has_side_effects=True),
        cost_estimate=pl.CostEstimate(flops=70 * 10**9, bytes_accessed=40 * 10**6, transcendentals=6 * 10**6),
    )(own, small, routes, top, w_query, w_key, w_value, query_gain, key_gain, cosine, sine, wo)


def run_backward(
    planes, across, shards, capacity, own_grad, wo, attended, query_raw, key_raw, value, first_input, weights, query_gain,
    key_gain, cosine, sine, slots, weighted,
):
    tokens, width = own_grad.shape
    seq_length = attended.shape[0]
    head_size = query_gain.shape[1]
    heads_here = wo.shape[0] // head_size
    pair = 2
    wide = pair * head_size
    steps = heads_here // pair
    count = across * shards * capacity
    hbm = pl.BlockSpec(memory_space=pl.ANY)
    dma = pltpu.SemaphoreType.DMA

    def held(step):
        return jnp.minimum(step, steps - 1)

    return pl.pallas_call(
        functools.partial(attention_backward, planes, across, shards, capacity, pair),
        grid=(steps + 1,),
        in_specs=[
            whole((tokens, width)),
            pl.BlockSpec((wide, width), lambda step: (held(step), 0)),
            pl.BlockSpec((seq_length, wide), lambda step: (0, held(step))),
            pl.BlockSpec((seq_length, wide), lambda step: (0, held(step))),
            whole((seq_length, head_size)),
            whole((seq_length, head_size)),
            whole((seq_length, width)),
            pl.BlockSpec((width, wide), lambda step: (0, step)),
            whole((1, head_size)),
            whole((1, head_size)),
            whole((seq_length, head_size)),
            whole((seq_length, head_size)),
            whole(slots.shape),
            hbm,
        ],
        out_specs=[
            pl.BlockSpec((wide, width), lambda step: (held(step), 0)),
            pl.BlockSpec((width, wide), lambda step: (0, step)),
            whole((seq_length, width)),
            whole((8, head_size)),
            whole((8, head_size)),
            hbm,
            whole((tokens, width)),
        ],
        out_shape=[
            jax.ShapeDtypeStruct((heads_here * head_size, width), BF16),
            jax.ShapeDtypeStruct((width, (steps + 1) * wide), BF16),
            jax.ShapeDtypeStruct((seq_length, width), BF16),
            jax.ShapeDtypeStruct((8, head_size), F32),
            jax.ShapeDtypeStruct((8, head_size), F32),
            jax.ShapeDtypeStruct(weighted.shape, BF16),
            jax.ShapeDtypeStruct((tokens, width), F32),
        ],
        scratch_shapes=[
            pltpu.VMEM((seq_length, width), F32),
            pltpu.VMEM((seq_length, head_size), BF16),
            pltpu.VMEM((seq_length, head_size), F32),
            pltpu.VMEM((seq_length, head_size), F32),
            pltpu.VMEM((seq_length, wide), BF16),
            pltpu.VMEM((width, seq_length), BF16),
            pltpu.VMEM((seq_length, width), BF16),
            pltpu.VMEM((count, width), BF16),
            pltpu.VMEM((count, tokens), BF16),
            pltpu.VMEM((planes, tokens, width), BF16),
            pltpu.VMEM((planes, tokens, width), BF16),
            dma((3,)), dma((3,)), dma((planes,)), dma((planes,)), dma((planes,)), dma((planes,)), dma,
        ],
        compiler_params=pltpu.CompilerParams(vmem_limit_bytes=VMEM_LIMIT, collective_id=2, has_side_effects=True),
        cost_estimate=pl.CostEstimate(flops=70 * 10**9, bytes_accessed=60 * 10**6, transcendentals=6 * 10**6),
    )(
        own_grad, wo, attended, query_raw, key_raw, value, first_input, weights, query_gain, key_gain, cosine, sine, slots,
        weighted,
    )


def reduce_kernel(
    planes, across, shards,
    wq_hbm, wo_hbm, first_hbm, hidden_ref, middle_hbm, expert_sum_hbm, middle_grad_hbm, scale_ref, early_ref, shared_ref,
    rows_hbm, gate_grad_hbm, up_grad_hbm, units_hbm, pair_grad_hbm,
    query_ref, key_ref, value_ref, output_ref, hidden_out_ref, grad_in_ref, early_total_ref, late_total_ref,
    gate_out_hbm, up_out_hbm, down_out_hbm,
    wq_parts, wo_parts, wq_out, wo_out, wq_in, wo_in, wq_total, wo_total, wq_final, wo_final, wq_home, wo_home, first_in,
    early_in, late, late_in, held_a, held_b, side, turned, tiles, tall, flat,
    across_send, across_recv, line_send, line_recv, home_send, home_recv, swap_send, swap_recv, first_send, first_recv,
    early_send, early_recv, late_send, late_recv, held_sem, side_sem, tile_sem, result_sem,
):
    z, x, w = lax.axis_index("z"), lax.axis_index("x"), lax.axis_index("w")
    rings = planes * across
    ring = z * across + x
    everyone = rings * shards
    wq_rows, wo_rows = wq_total.shape[0], wo_total.shape[0]
    mine = wq_rows // shards
    tokens, width = grad_in_ref.shape
    query_columns = query_ref.shape[1] // shards
    key_columns = key_ref.shape[1] // shards
    linear = ring * shards + w
    barrier = pltpu.get_barrier_semaphore()

    def place(index):
        return (index // shards // across, index // shards % across, index % shards)

    @pl.loop(1, everyone)
    def _(offset):
        pl.semaphore_signal(barrier, inc=1, device_id=place((linear + offset) % everyone), device_id_type=MESH)

    pl.semaphore_wait(barrier, everyone - 1)

    def rows_of(index, size):
        return pl.ds(pl.multiple_of(index * size, 16), size)

    sources = [(wq_hbm, wq_rows, wq_parts), (wo_hbm, wo_rows, wo_parts)]

    def across_copy(kind, plane, column):
        source, rows, goal = sources[kind]
        return remote(
            source.at[rows_of(plane * across + column, rows)], goal.at[plane, x],
            across_send.at[kind, plane], across_recv.at[kind, plane], (z, column, w),
        )

    def first_copy(offset):
        target = (w + offset) % shards
        return remote(
            first_hbm.at[rows_of(target, tokens)], first_in.at[offset], first_send.at[offset], first_recv.at[offset],
            (z, x, target),
        )

    @pl.loop(1, shards)
    def _(offset):
        first_copy(offset).start()

    pltpu.make_async_copy(first_hbm.at[rows_of(w, tokens)], first_in.at[0], first_recv.at[0]).start()
    hold_a = pltpu.make_async_copy(middle_hbm, held_a, held_sem.at[0])
    hold_b = pltpu.make_async_copy(expert_sum_hbm, held_b, held_sem.at[1])
    hold_a.start()
    hold_b.start()

    def start_across(kind, turn):
        plane, _, _ = line_order(z, planes, planes - 1 - turn)

        @pl.loop(1, across)
        def _(offset):
            across_copy(kind, plane, (x + offset) % across).start()

        source, rows, goal = sources[kind]
        pltpu.make_async_copy(
            source.at[rows_of(plane * across + x, rows)], goal.at[plane, x], across_recv.at[kind, plane]
        ).start()

    start_across(1, 0)
    start_across(1, 1)

    @pl.loop(1, everyone)
    def _(offset):
        other = (linear + offset) % everyone
        remote(early_ref.at[other], early_in.at[linear], early_send, early_recv, place(other)).start()

    early_in[linear] = early_ref[linear]
    lanes = tiles.shape[2]
    per_kind = width // lanes
    depth = side.shape[0]
    late_rows = width // 128
    pick = (lax.broadcasted_iota(jnp.int32, (8, 128), 0) == 2).astype(F32)
    lane = lax.broadcasted_iota(jnp.int32, (8, 128), 1)

    def tile_copy(unit):
        slot = unit % 2
        here = pl.ds(pl.multiple_of((unit % per_kind) * lanes, lanes), lanes)

        @pl.when(unit < 2 * per_kind)
        def _():
            pltpu.make_async_copy(rows_hbm.at[:, here], tiles.at[slot], tile_sem.at[slot]).start()

        @pl.when(unit >= 2 * per_kind)
        def _():
            pltpu.make_async_copy(pair_grad_hbm.at[:, here], tiles.at[slot], tile_sem.at[slot]).start()

    tile_copy(0)

    def multiply(unit):
        slot = unit % 2
        here = pl.ds(pl.multiple_of((unit % per_kind) * lanes, lanes), lanes)
        for kind, source in enumerate([gate_grad_hbm, up_grad_hbm, units_hbm]):

            @pl.when(unit == kind * per_kind)
            def _():
                load = pltpu.make_async_copy(source, side, side_sem)
                load.start()
                load.wait()
                if kind == 2:

                    @pl.loop(0, depth // 128)
                    def _(part):
                        at = pl.ds(pl.multiple_of(part * 128, 128), 128)
                        turned[:, at] = side[at, :].T

        @pl.when(unit + 1 < 3 * per_kind)
        def _():
            tile_copy(unit + 1)

        wait_bytes(tiles.at[slot], tile_sem.at[slot])

        @pl.when(unit >= 2)
        def _():
            wait_bytes(tall.at[slot], result_sem.at[slot])

        @pl.when(unit < 2 * per_kind)
        def _():
            tall[slot] = dot_tn(tiles[slot], side[...])

        @pl.when(unit < per_kind)
        def _():
            pltpu.make_async_copy(tall.at[slot], gate_out_hbm.at[here], result_sem.at[slot]).start()

        @pl.when((unit >= per_kind) & (unit < 2 * per_kind))
        def _():
            pltpu.make_async_copy(tall.at[slot], up_out_hbm.at[here], result_sem.at[slot]).start()

        @pl.when(unit >= 2 * per_kind)
        def _():
            flat[slot] = dot(turned[...], tiles[slot])
            pltpu.make_async_copy(flat.at[slot], down_out_hbm.at[:, here], result_sem.at[slot]).start()

    def late_copy(other):
        return remote(late, late_in.at[linear], late_send, late_recv, place(other))

    def finish_rows():
        hold_a.wait()
        hold_b.wait()
        pieces = tokens // 64

        def add_rows(piece, carry):
            at = pl.ds(pl.multiple_of(piece * 64, 64), 64)
            extra = held_b[at, :]
            hidden_out_ref[at, :] = (held_a[at, :] + extra).astype(BF16)
            return carry + jnp.sum(jnp.sum(extra * extra, axis=1, keepdims=True), axis=0, keepdims=True)

        expert_square = lax.fori_loop(0, pieces, add_rows, jnp.zeros((1, 1), F32))
        load = pltpu.make_async_copy(middle_grad_hbm, held_a, held_sem.at[0])
        load.start()

        @pl.loop(0, shards)
        def _(offset):
            wait_bytes(first_in.at[offset], first_recv.at[offset])

        load.wait()

        def grad_rows(piece, carry):
            square, gain_grad = carry
            at = pl.ds(pl.multiple_of(piece * 64, 64), 64)
            first = first_in[0, at, :].astype(F32)
            for offset in range(1, shards):
                first += first_in[offset, at, :].astype(F32)
            normed, scaling = norm_forward(hidden_ref[at, :].astype(F32))
            grad = held_a[at, :] + norm_backward(first * scale_ref[...], normed, scaling)
            grad_in_ref[at, :] = grad
            return (
                square + jnp.sum(jnp.sum(grad * grad, axis=1, keepdims=True), axis=0, keepdims=True),
                gain_grad + jnp.sum(first * normed, axis=0, keepdims=True),
            )

        square, gain_grad = lax.fori_loop(
            0, pieces, grad_rows, (jnp.zeros((1, 1), F32), jnp.zeros((1, width), F32))
        )
        for row in range(late_rows):
            late[row : row + 1, :] = gain_grad[:, row * 128 : (row + 1) * 128]
        late[late_rows:, :] = shared_ref[...] + pick * (
            jnp.where(lane == 2, expert_square, 0.0) + jnp.where(lane == 3, square, 0.0)
        )

        @pl.loop(1, everyone)
        def _(offset):
            late_copy((linear + offset) % everyone).start()

        late_in[linear] = late[...]

    outs, ins = [wq_out, wo_out], [wq_in, wo_in]
    totals, parts = [wq_total, wo_total], [wq_parts, wo_parts]

    def line_copy(kind, plane):
        up = (plane > z).astype(jnp.int32)
        ends = (plane == z + 2 * up - 1).astype(jnp.int32)
        slot = plane + ends * (1 - up) * (planes - plane)
        return remote(
            outs[kind].at[plane], ins[kind].at[slot], line_send.at[kind, plane], line_recv.at[kind, slot],
            (z + 2 * up - 1, x, w),
        )

    per_turn = 3 * per_kind // (2 * planes)

    def take(kind, slot):
        wait_bytes(ins[kind].at[slot], line_recv.at[kind, slot])
        totals[kind][...] += ins[kind][slot].astype(F32)

    def collect(kind):
        @pl.loop(0, planes)
        def _(turn):
            plane, _, _ = line_order(z, planes, planes - 1 - turn)

            @pl.loop(0, per_turn)
            def _(unit):
                multiply((turn + (1 - kind) * planes) * per_turn + unit)

            wait_bytes(parts[kind].at[plane], across_recv.at[kind, plane])

            @pl.when(turn < planes - 2)
            def _():
                start_across(kind, turn + 2)

            if kind == 1:

                @pl.when(turn >= planes - 2)
                def _():
                    start_across(0, turn + 2 - planes)

            totals[kind][...] = parts[kind][plane, 0].astype(F32)

            @pl.loop(1, across)
            def _(column):
                totals[kind][...] += parts[kind][plane, column].astype(F32)

            @pl.when(((plane > z) & (z > 0)) | ((plane < z) & (z < planes - 1)))
            def _():
                take(kind, plane)

            @pl.when(plane != z)
            def _():
                outs[kind][plane] = totals[kind][...].astype(BF16)
                line_copy(kind, plane).start()

    def finish(kind):
        @pl.when(z > 0)
        def _():
            take(kind, z)

        @pl.when(z < planes - 1)
        def _():
            take(kind, planes)

    collect(1)
    finish(1)
    wo_final[...] = wo_total[...].astype(BF16)
    goal = w * rings + ring
    stays = goal == linear
    swap = remote(
        wo_final, wo_home, swap_send, swap_recv, (goal // shards // across, goal // shards % across, goal % shards)
    )

    @pl.when(jnp.logical_not(stays))
    def _():
        swap.start()

    @pl.when(stays)
    def _():
        pltpu.make_async_copy(wo_final, wo_home, swap_recv).start()

    finish_rows()
    collect(0)
    finish(0)
    wq_final[...] = wq_total[...].astype(BF16)

    def home_copy(offset):
        target = (w + offset) % shards
        return remote(
            wq_final.at[rows_of(target, mine)], wq_home.at[w], home_send.at[offset], home_recv.at[w], (z, x, target)
        )

    @pl.loop(1, shards)
    def _(offset):
        home_copy(offset).start()

    pltpu.make_async_copy(wq_final.at[rows_of(w, mine)], wq_home.at[w], home_recv.at[w]).start()

    for part in range(shards):
        wait_bytes(wq_home.at[part], home_recv.at[part])
        rows = wq_home[part].astype(F32)
        query_ref[:, part * query_columns : (part + 1) * query_columns] = rows[:, :query_columns]
        key_ref[:, part * key_columns : (part + 1) * key_columns] = rows[:, query_columns : query_columns + key_columns]
        value_ref[:, part * key_columns : (part + 1) * key_columns] = rows[:, query_columns + key_columns :]

    wait_bytes(early_ref.at[pl.ds(0, everyone - 1)], early_recv)
    early_total_ref[...] = jnp.sum(early_in[...], axis=0)
    wait_bytes(late_in.at[pl.ds(0, everyone - 1)], late_recv)
    late_total_ref[...] = jnp.sum(late_in[...], axis=0)
    wait_bytes(early_ref.at[pl.ds(0, everyone - 1)], early_send)
    wait_bytes(late_in.at[pl.ds(0, everyone - 1)], late_send)
    for slot in range(2):
        wait_bytes(tall.at[slot], result_sem.at[slot])
    wait_bytes(wo_home, swap_recv)
    output_ref[...] = wo_home[...].astype(F32)

    @pl.when(jnp.logical_not(stays))
    def _():
        wait_bytes(wo_final, swap_send)

    @pl.loop(1, shards)
    def _(offset):
        wait_bytes(wq_home.at[0], home_send.at[offset])
        wait_bytes(first_in.at[0], first_send.at[offset])

    if across > 1:

        @pl.loop(0, planes)
        def _(plane):
            wait_bytes(wq_parts.at[plane, pl.ds(0, across - 1)], across_send.at[0, plane])
            wait_bytes(wo_parts.at[plane, pl.ds(0, across - 1)], across_send.at[1, plane])

    @pl.loop(1, planes)
    def _(offset):
        plane = (z + offset) % planes
        wait_bytes(wq_out.at[plane], line_send.at[0, plane])
        wait_bytes(wo_out.at[plane], line_send.at[1, plane])


def run_reduce(
    planes, across, shards, wq_grad, wo_grad, first_part, hidden, middle, expert_sum, middle_grad, scale, early, shared,
    rows_in, gate_grad, up_grad, units, pair_grad, query_columns, key_columns,
):
    rings = planes * across
    everyone = rings * shards
    width = wq_grad.shape[0]
    wq_wide = wq_grad.shape[1]
    wq_rows, wo_rows = width // rings, wo_grad.shape[0] // rings
    tokens = first_part.shape[0] // shards
    mine = wq_rows // shards
    depth, wide = units.shape
    late_rows = width // 128 + 8
    hbm = pl.BlockSpec(memory_space=pl.ANY)
    vmem = pl.BlockSpec(memory_space=pltpu.VMEM)
    dma = pltpu.SemaphoreType.DMA
    return pl.pallas_call(
        functools.partial(reduce_kernel, planes, across, shards),
        in_specs=[hbm] * 3 + [vmem] + [hbm] * 3 + [vmem] * 3 + [hbm] * 5,
        out_specs=[vmem] * 8 + [hbm] * 3,
        out_shape=[
            jax.ShapeDtypeStruct((mine, query_columns), F32),
            jax.ShapeDtypeStruct((mine, key_columns), F32),
            jax.ShapeDtypeStruct((mine, key_columns), F32),
            jax.ShapeDtypeStruct((wo_rows, width), F32),
            jax.ShapeDtypeStruct((tokens, width), BF16),
            jax.ShapeDtypeStruct((tokens, width), F32),
            jax.ShapeDtypeStruct(early.shape[1:], F32),
            jax.ShapeDtypeStruct((late_rows, 128), F32),
            jax.ShapeDtypeStruct((width, wide), F32),
            jax.ShapeDtypeStruct((width, wide), F32),
            jax.ShapeDtypeStruct((wide, width), F32),
        ],
        scratch_shapes=[
            pltpu.VMEM((planes, across, wq_rows, wq_wide), BF16),
            pltpu.VMEM((planes, across, wo_rows, width), BF16),
            pltpu.VMEM((planes, wq_rows, wq_wide), BF16),
            pltpu.VMEM((planes, wo_rows, width), BF16),
            pltpu.VMEM((planes + 1, wq_rows, wq_wide), BF16),
            pltpu.VMEM((planes + 1, wo_rows, width), BF16),
            pltpu.VMEM((wq_rows, wq_wide), F32),
            pltpu.VMEM((wo_rows, width), F32),
            pltpu.VMEM((wq_rows, wq_wide), BF16),
            pltpu.VMEM((wo_rows, width), BF16),
            pltpu.VMEM((shards, mine, wq_wide), BF16),
            pltpu.VMEM((wo_rows, width), BF16),
            pltpu.VMEM((shards, tokens, width), BF16),
            pltpu.VMEM(early.shape, F32),
            pltpu.VMEM((late_rows, 128), F32),
            pltpu.VMEM((everyone, late_rows, 128), F32),
            pltpu.VMEM((tokens, width), F32),
            pltpu.VMEM((tokens, width), F32),
            pltpu.VMEM((depth, wide), BF16),
            pltpu.VMEM((wide, depth), BF16),
            pltpu.VMEM((2, depth, 256), BF16),
            pltpu.VMEM((2, 256, wide), F32),
            pltpu.VMEM((2, wide, 256), F32),
            dma((2, planes)), dma((2, planes)), dma((2, planes)), dma((2, planes + 1)), dma((shards,)), dma((shards,)),
            dma, dma, dma((shards,)), dma((shards,)), dma, dma, dma, dma, dma((2,)), dma, dma((2,)), dma((2,)),
        ],
        compiler_params=pltpu.CompilerParams(vmem_limit_bytes=VMEM_LIMIT, collective_id=3, has_side_effects=True),
        cost_estimate=pl.CostEstimate(flops=70 * 10**9, bytes_accessed=40 * 10**6, transcendentals=0),
    )(
        wq_grad, wo_grad, first_part, hidden, middle, expert_sum, middle_grad, scale, early, shared, rows_in, gate_grad,
        up_grad, units, pair_grad,
    )


def expert_kernel(
    planes, across, shards, capacity,
    own_ref, share_ref, slots_ref, my_slots_ref, gate_ref, up_ref, down_ref, small_ref, top_hbm,
    middle_hbm, cotangent_hbm, rows_hbm, back_hbm, weighted_hbm, units_hbm, gate_grad_hbm, up_grad_hbm, pair_grad_hbm, row_grad_ref, low_grad_hbm, logit_grad_ref, gain_grad_ref,
    share_grad_ref, middle, plane_rows, plane_shares, share_in, share_back, share_home, stage, chosen, rows, top, units,
    gate_grad, up_grad, columns, partial_in,
    line_send, line_recv, plane_share_send, plane_share_recv, out_send, out_recv, out_share_send, out_share_recv,
    back_send, back_recv, back_share_send, back_share_recv, sum_send, sum_recv, sum_share_send, sum_share_recv,
    load_sem, top_sem, store_sem, middle_sem,
):
    z, x, w = lax.axis_index("z"), lax.axis_index("x"), lax.axis_index("w")
    in_plane = across * shards
    experts = planes * in_plane
    me = x * shards + w
    tokens, width = own_ref.shape
    count = in_plane * capacity
    half = count // 2
    per_half = in_plane // 2
    chunk = 512

    def place(index):
        return (z, index // shards, index % shards)

    def order(step):
        return line_order(z, planes, step)

    inner = ((z > 0) & (z < planes - 1)).astype(jnp.int32)
    first_back = 2 - (z == 1).astype(jnp.int32)
    second_back = 3 - inner * first_back
    third_back = 1 + 2 * inner
    greet_plane_and_line(planes, across, shards)

    def line_up(block, hop):
        return remote(
            plane_rows.at[block], plane_rows.at[block], line_send.at[0, hop], line_recv.at[0, hop], (z + 1, x, w)
        )

    def line_down(block, hop):
        return remote(
            plane_rows.at[block], plane_rows.at[block], line_send.at[1, hop], line_recv.at[1, hop], (z - 1, x, w)
        )

    middle_load = pltpu.make_async_copy(middle_hbm, middle, middle_sem)
    middle_load.start()
    plane_rows[z] = own_ref[...]

    @pl.when(z + 1 < planes)
    def _():
        line_up(z, 1).start()

    @pl.when(z > 0)
    def _():
        line_down(z, 1).start()

    def plane_share_copy(other):
        return remote(
            share_ref.at[pl.ds(other * in_plane, in_plane)], plane_shares.at[z],
            plane_share_send.at[other], plane_share_recv.at[z], (other, x, w),
        )

    @pl.loop(1, planes)
    def _(offset):
        plane_share_copy((z + offset) % planes).start()

    plane_shares[z] = share_ref[pl.ds(z * in_plane, in_plane)]

    def slice_of(index):
        return pl.ds(pl.multiple_of(index * capacity, 16), capacity)

    def out_copy(step, block, index):
        return remote(
            stage.at[step, slice_of(index)], rows_hbm.at[block, slice_of(me)],
            out_send.at[step], out_recv.at[step], place(index),
        )

    def out_share_copy(step, block, index):
        return remote(
            plane_shares.at[block, index], share_in.at[block, me],
            out_share_send.at[step], out_share_recv.at[step], place(index),
        )

    def back_copy(step, block, index):
        return remote(
            stage.at[step, slice_of(index)], back_hbm.at[block, slice_of(me)],
            back_send.at[step], back_recv.at[step], place(index),
        )

    def back_share_copy(step, block, index):
        return remote(
            share_back.at[block, index], share_home.at[block, me],
            back_share_send.at[step], back_share_recv.at[step], place(index),
        )

    def start_back(step, block):
        @pl.loop(1, in_plane)
        def _(offset):
            index = (me + offset) % in_plane
            back_copy(step, block, index).start()
            back_share_copy(step, block, index).start()

        pltpu.make_async_copy(stage.at[step, slice_of(me)], back_hbm.at[block, slice_of(me)], back_recv.at[step]).start()
        pltpu.make_async_copy(share_back.at[block, me], share_home.at[block, me], back_share_recv.at[step]).start()

    slot_ids = lax.broadcasted_iota(jnp.int32, (capacity, tokens), 0)

    def pack_step(step):
        block, _, _ = order(step)

        @pl.when(step > 0)
        def _():
            @pl.when(z - step >= 0)
            def _():
                wait_bytes(plane_rows.at[0], line_recv.at[0, step])

                @pl.when(z + 1 < planes)
                def _():
                    line_up(z - step, step + 1).start()

            @pl.when(z + step < planes)
            def _():
                wait_bytes(plane_rows.at[0], line_recv.at[1, step])

                @pl.when(z > 0)
                def _():
                    line_down(z + step, step + 1).start()

            wait_bytes(plane_shares.at[block], plane_share_recv.at[block])

        @pl.loop(0, in_plane)
        def _(index):
            slots = slots_ref[block * in_plane + index]
            chosen[step, slice_of(index), :] = (slot_ids == slots).astype(F32).astype(BF16)

        @pl.loop(0, width // chunk)
        def _(part):
            wide = pl.ds(pl.multiple_of(part * chunk, chunk), chunk)
            stage[step, :, wide] = dot(chosen[step], plane_rows[block, :, wide]).astype(BF16)

    def send_step(step):
        block, _, _ = order(step)

        @pl.loop(1, in_plane)
        def _(offset):
            index = (me + offset) % in_plane
            out_copy(step, block, index).start()
            out_share_copy(step, block, index).start()

        pltpu.make_async_copy(stage.at[step, slice_of(me)], rows_hbm.at[block, slice_of(me)], out_recv.at[step]).start()
        pltpu.make_async_copy(plane_shares.at[block, me], share_in.at[block, me], out_share_recv.at[step]).start()

    def expert_step(step):
        block, _, _ = order(step)

        pltpu.make_async_copy(top_hbm.at[block], top, top_sem).start()
        wait_bytes(rows_hbm.at[block], out_recv.at[step])
        load = pltpu.make_async_copy(rows_hbm.at[block], rows, load_sem)
        load.start()

        @pl.when(step + 1 < planes)
        def _():
            send_step(step + 1)

        wait_bytes(share_in.at[block], out_share_recv.at[step])
        wait_bytes(stage.at[step, pl.ds(0, count - capacity)], out_send.at[step])
        wait_bytes(plane_shares.at[block, pl.ds(0, in_plane - 1)], out_share_send.at[step])

        @pl.loop(0, in_plane)
        def _(index):
            mine = slot_ids == my_slots_ref[block * in_plane + index]
            columns[slice_of(index), :] = jnp.broadcast_to(
                jnp.sum(jnp.where(mine, share_in[block, index], 0.0), axis=1, keepdims=True), (capacity, 128)
            )

        load.wait()
        wait_bytes(top, top_sem)

        @pl.loop(0, 2)
        def _(part):
            here = pl.ds(pl.multiple_of(part * half, 16), half)
            gate = dot(rows[here, :], gate_ref[...])
            up = dot(rows[here, :], up_ref[...])
            sigmoid = 1.0 / (1.0 + jnp.exp(-gate))
            active = gate * sigmoid
            hidden = (active * up).astype(BF16)
            units[here, :] = hidden
            share = columns[here, 0:1]
            total = jnp.zeros((half, 1), F32)
            for piece in range(width // chunk):
                wide = pl.ds(piece * chunk, chunk)
                pair_out = dot(hidden, down_ref[:, wide]).astype(BF16).astype(F32)
                top_rows = top[here, wide].astype(F32)
                total += jnp.sum(pair_out * top_rows, axis=1, keepdims=True)
                rows[here, wide] = (share * pair_out).astype(BF16)
                top[here, wide] = (share * top_rows).astype(BF16)
            columns[here, :] = jnp.broadcast_to(total, (half, 128))
            hidden_grad = dot_nt(top[here, :], down_ref[...])
            gate_low = (hidden_grad * up * sigmoid * (1.0 + gate * (1.0 - sigmoid))).astype(BF16)
            up_low = (hidden_grad * active).astype(BF16)
            gate_grad[here, :] = gate_low
            up_grad[here, :] = up_low
            for piece in range(width // chunk):
                wide = pl.ds(piece * chunk, chunk)
                stage[step, here, wide] = (dot_nt(gate_low, gate_ref[wide, :]) + dot_nt(up_low, up_ref[wide, :])).astype(BF16)

        @pl.loop(0, in_plane)
        def _(index):
            mine = slot_ids == my_slots_ref[block * in_plane + index]
            values = columns[slice_of(index), 0:1]
            share_back[block, index] = jnp.sum(jnp.where(mine, values, 0.0), axis=0, keepdims=True)

        @pl.when((step == first_back) | (step == second_back))
        def _():
            start_back(step, block)

        stores = [
            pltpu.make_async_copy(units, units_hbm.at[block], store_sem.at[0]),
            pltpu.make_async_copy(gate_grad, gate_grad_hbm.at[block], store_sem.at[1]),
            pltpu.make_async_copy(up_grad, up_grad_hbm.at[block], store_sem.at[2]),
            pltpu.make_async_copy(top, pair_grad_hbm.at[block], store_sem.at[3]),
            pltpu.make_async_copy(rows, weighted_hbm.at[block], store_sem.at[4]),
        ]
        for store in stores:
            store.start()

        for store in stores:
            store.wait()

    @pl.loop(0, planes + 1)
    def _(step):
        @pl.when(step < planes)
        def _():
            pack_step(step)

        @pl.when(step == 0)
        def _():
            send_step(step)

        @pl.when(step > 0)
        def _():
            expert_step(step - 1)

    for hop in range(1, planes):

        @pl.when((z - (hop - 1) >= 0) & (z + 1 < planes))
        def _():
            wait_bytes(plane_rows.at[0], line_send.at[0, hop])

        @pl.when((z + (hop - 1) < planes) & (z > 0))
        def _():
            wait_bytes(plane_rows.at[0], line_send.at[1, hop])

    @pl.loop(1, planes)
    def _(offset):
        wait_bytes(plane_shares.at[0], plane_share_send.at[(z + offset) % planes])

    def wait_back(step):
        wait_bytes(stage.at[step, pl.ds(0, count - capacity)], back_send.at[step])
        wait_bytes(share_back.at[0, pl.ds(0, in_plane - 1)], back_share_send.at[step])

    def sum_copy(block):
        up = (block > z).astype(jnp.int32)
        relayed = (jnp.abs(block - z) == planes - 1).astype(jnp.int32)
        goal = block + relayed * (1 - 2 * up) * (planes - 2)
        slot = z + relayed * (goal - z)
        return remote(plane_rows.at[block], partial_in.at[slot], sum_send.at[block], sum_recv.at[slot], (goal, x, w))

    def sum_share_copy(block):
        return remote(
            share_home.at[block], share_grad_ref.at[pl.ds(z * in_plane, in_plane)],
            sum_share_send.at[block], sum_share_recv.at[z], (block, x, w),
        )

    @pl.loop(0, planes)
    def _(turn):
        step = jnp.where(turn == 0, first_back, jnp.where(turn == 1, second_back, jnp.where(turn == 2, third_back, 0)))
        block, _, _ = order(step)
        wait_bytes(back_hbm.at[block], back_recv.at[step])
        load = pltpu.make_async_copy(back_hbm.at[block], rows, load_sem)
        load.start()
        wait_bytes(share_home.at[block], back_share_recv.at[step])
        load.wait()

        @pl.when(step > 0)
        def _():
            sum_share_copy(block).start()

            merges = (inner == 1) & (jnp.abs(block - z) == 2)

            @pl.when(merges)
            def _():
                wait_bytes(partial_in.at[z], sum_recv.at[z])

            @pl.loop(0, width // chunk)
            def _(part):
                wide = pl.ds(pl.multiple_of(part * chunk, chunk), chunk)
                summed = dot_tn(chosen[step], rows[:, wide])

                @pl.when(merges)
                def _():
                    plane_rows[block, :, wide] = (summed + partial_in[z, :, wide].astype(F32)).astype(BF16)

                @pl.when(jnp.logical_not(merges))
                def _():
                    plane_rows[block, :, wide] = summed.astype(BF16)

            sum_copy(block).start()

        @pl.when(step == 0)
        def _():
            share_grad_ref[pl.ds(z * in_plane, in_plane)] = share_home[z]

            @pl.loop(0, width // chunk)
            def _(part):
                wide = pl.ds(pl.multiple_of(part * chunk, chunk), chunk)
                row_grad_ref[:, wide] = dot_tn(chosen[0], rows[:, wide])

        @pl.when(turn == 0)
        def _():
            wait_back(second_back)
            start_back(third_back, order(third_back)[0])

        @pl.when(turn == 1)
        def _():
            wait_back(third_back)
            start_back(0, z)

    cotangent_load = pltpu.make_async_copy(cotangent_hbm, rows.at[pl.ds(0, tokens)], load_sem)
    cotangent_load.start()

    @pl.loop(1, planes)
    def _(offset):
        other = (z + offset) % planes
        wait_bytes(share_home.at[other], sum_share_recv.at[other])

        @pl.when(jnp.abs(other - z) < planes - 1)
        def _():
            wait_bytes(partial_in.at[other], sum_recv.at[other])

            @pl.loop(0, width // chunk)
            def _(part):
                wide = pl.ds(pl.multiple_of(part * chunk, chunk), chunk)
                row_grad_ref[:, wide] += partial_in[other, :, wide].astype(F32)

    @pl.loop(1, planes)
    def _(offset):
        other = (z + offset) % planes
        wait_bytes(plane_rows.at[other], sum_send.at[other])
        wait_bytes(share_home.at[other], sum_share_send.at[other])

    cotangent_load.wait()
    middle_load.wait()
    depth = width // shards
    share_grad = jnp.concatenate([share_grad_ref[index] for index in range(experts)], axis=0)
    shares = jnp.concatenate([share_ref[index] for index in range(experts)], axis=0)
    center = jnp.sum(shares * share_grad, axis=0, keepdims=True)
    logit_grad_ref[...] = (shares * (share_grad - center)).astype(BF16)
    for part in range(shards):
        wide = slice(part * depth, (part + 1) * depth)
        row_grad_ref[:, wide] += dot_tn(logit_grad_ref[...], small_ref[part, :experts, :].astype(BF16))
    ffn_row = jnp.concatenate([small_ref[part, experts : experts + 1, :] for part in range(shards)], axis=1)

    def finish_rows(piece, gain_grad):
        at = pl.ds(pl.multiple_of(piece * 64, 64), 64)
        normed, scaling = norm_forward(middle[at, :])
        second_grad = row_grad_ref[at, :]
        grad = rows[at, :].astype(F32) + norm_backward(second_grad * ffn_row, normed, scaling)
        row_grad_ref[at, :] = grad
        rows[pl.ds(pl.multiple_of(tokens + piece * 64, 64), 64), :] = grad.astype(BF16)
        return gain_grad + jnp.sum(second_grad * normed, axis=0, keepdims=True)

    gain_grad_ref[...] = lax.fori_loop(0, tokens // 64, finish_rows, jnp.zeros((1, width), F32))
    low_store = pltpu.make_async_copy(rows.at[pl.ds(tokens, tokens)], low_grad_hbm, middle_sem)
    low_store.start()
    wait_back(0)
    wait_back(first_back)
    low_store.wait()


def run_experts(planes, across, shards, capacity, own, shares, slots, my_slots, w_gate, w_up, w_down, small_all, top_rows, middle, cotangent):
    tokens, width = own.shape
    in_plane = across * shards
    count = in_plane * capacity
    units = w_gate.shape[1]
    experts = planes * in_plane
    hbm = pl.BlockSpec(memory_space=pl.ANY)
    vmem = pl.BlockSpec(memory_space=pltpu.VMEM)
    dma = pltpu.SemaphoreType.DMA
    flops = 12 * planes * count * width * units
    return pl.pallas_call(
        functools.partial(expert_kernel, planes, across, shards, capacity),
        in_specs=[vmem] * 8 + [hbm] * 3,
        out_specs=[hbm] * 7 + [vmem, hbm, vmem, vmem],
        out_shape=[
            jax.ShapeDtypeStruct((planes, count, width), BF16),
            jax.ShapeDtypeStruct((planes, count, width), BF16),
            jax.ShapeDtypeStruct((planes, count, width), BF16),
            jax.ShapeDtypeStruct((planes, count, units), BF16),
            jax.ShapeDtypeStruct((planes, count, units), BF16),
            jax.ShapeDtypeStruct((planes, count, units), BF16),
            jax.ShapeDtypeStruct((planes, count, width), BF16),
            jax.ShapeDtypeStruct((tokens, width), F32),
            jax.ShapeDtypeStruct((tokens, width), BF16),
            jax.ShapeDtypeStruct((experts, tokens), BF16),
            jax.ShapeDtypeStruct((1, width), F32),
        ],
        scratch_shapes=[
            pltpu.VMEM((experts, 1, tokens), F32),
            pltpu.VMEM((tokens, width), F32),
            pltpu.VMEM((planes, tokens, width), BF16),
            pltpu.VMEM((planes, in_plane, 1, tokens), F32),
            pltpu.VMEM((planes, in_plane, 1, tokens), F32),
            pltpu.VMEM((planes, in_plane, 1, tokens), F32),
            pltpu.VMEM((planes, in_plane, 1, tokens), F32),
            pltpu.VMEM((planes, count, width), BF16),
            pltpu.VMEM((planes, count, tokens), BF16),
            pltpu.VMEM((count, width), BF16),
            pltpu.VMEM((count, width), BF16),
            pltpu.VMEM((count, units), BF16),
            pltpu.VMEM((count, units), BF16),
            pltpu.VMEM((count, units), BF16),
            pltpu.VMEM((count, 128), F32),
            pltpu.VMEM((planes, tokens, width), BF16),
            dma((2, planes + 1)), dma((2, planes + 1)), dma((planes,)), dma((planes,)),
            dma((planes,)), dma((planes,)), dma((planes,)), dma((planes,)),
            dma((planes,)), dma((planes,)), dma((planes,)), dma((planes,)),
            dma((planes,)), dma((planes,)), dma((planes,)), dma((planes,)),
            dma, dma, dma((5,)), dma,
        ],
        compiler_params=pltpu.CompilerParams(vmem_limit_bytes=VMEM_LIMIT, collective_id=1, has_side_effects=True),
        cost_estimate=pl.CostEstimate(flops=4 * flops, bytes_accessed=100 * 10**6, transcendentals=2 * 10**6),
    )(own, shares, slots, my_slots, w_gate, w_up, w_down, small_all, top_rows, middle, cotangent)


def local(
    hidden_in, attn_gain, w_query, key_projection, value_projection, query_gain, key_gain, w_output, ffn_gain, w_router,
    routes, w_gate, w_up, w_down, cotangent,
):
    tokens_here, width = hidden_in.shape
    head_size = query_gain.shape[0]
    top_count = routes.shape[1]
    planes, across, shards = lax.axis_size("z"), lax.axis_size("x"), lax.axis_size("w")
    rings = planes * across
    device_count = rings * shards
    in_plane = across * shards
    experts = device_count
    capacity = 5 * tokens_here * top_count // (4 * experts)
    seq_length = tokens_here * shards

    cosine, sine = rope_tables(seq_length, head_size)
    query_gain_row, key_gain_row = query_gain[None, :], key_gain[None, :]

    capacity = -(-capacity // 16) * 16
    small = jnp.concatenate([w_router.T, ffn_gain[None, :], attn_gain[None, :]], axis=0).astype(F32)
    small = jnp.pad(small, ((0, -small.shape[0] % 8), (0, 0)))
    (
        first_input, query_raw, key_raw, value, attended, middle, slots_flat, my_slots, shares, squares, second_input,
        small_all, weights, top_rows,
    ) = run_forward(
        planes, across, shards, capacity, hidden_in, small, routes.T, cotangent, w_query, key_projection,
        value_projection, query_gain_row, key_gain_row, cosine, sine, w_output,
    )
    (
        rows_in, _, weighted, hidden_units, gate_grad, up_grad, pair_grad, middle_grad, low_grad, logit_grad, ffn_gain_grad,
    ) = run_experts(
        planes, across, shards, capacity, second_input, shares, slots_flat, my_slots, w_gate[0], w_up[0], w_down[0],
        small_all, top_rows, middle, cotangent,
    )
    units = w_gate.shape[2]
    router_grad = dot_tn(second_input, logit_grad.T)
    attn_scale = small_all[:, experts + 1, :].reshape(1, width)
    wo_grad, wq_grad, first_part, query_gain_grad, key_gain_grad, _, expert_sum = run_backward(
        planes, across, shards, capacity, low_grad, w_output, attended, query_raw, key_raw, value,
        first_input, weights, query_gain_row, key_gain_row, cosine, sine, slots_flat, weighted,
    )
    mine = width // device_count
    early = jnp.concatenate(
        [router_grad.reshape(device_count, mine * experts), ffn_gain_grad.reshape(device_count, mine)], axis=1
    )
    early = jnp.pad(early, ((0, 0), (0, -early.shape[1] % 1024))).reshape(device_count, -1, 128)
    shared = squares + jnp.concatenate(
        [query_gain_grad[0:1], key_gain_grad[0:1], jnp.zeros((6, head_size), F32)], axis=0
    )
    (
        sum_query, sum_key, sum_value, sum_output, hidden_out, grad_in, early_total, late_total, grad_gate, grad_up, grad_down,
    ) = run_reduce(
        planes, across, shards, wq_grad, wo_grad, first_part, hidden_in, middle, expert_sum, middle_grad, attn_scale, early,
        shared, rows_in.reshape(-1, width), gate_grad.reshape(-1, units), up_grad.reshape(-1, units),
        hidden_units.reshape(-1, units), pair_grad.reshape(-1, width), w_query.shape[1], key_projection.shape[1],
    )
    early_total = early_total.reshape(-1)
    sum_router = early_total[: mine * experts].reshape(mine, experts)
    sum_ffn = early_total[mine * experts : mine * (experts + 1)]
    linear = (lax.axis_index("z") * across + lax.axis_index("x")) * shards + lax.axis_index("w")
    sum_attn = lax.dynamic_slice_in_dim(late_total[: width // 128].reshape(-1), linear * mine, mine)
    late_total = late_total[width // 128 :]
    totals = jnp.concatenate([late_total[0], late_total[1], late_total[2, :4]])
    root_mean_squares = jnp.sqrt(totals[2 * head_size :] / (tokens_here * device_count * width))
    return (
        hidden_out,
        grad_in,
        sum_attn,
        sum_query,
        sum_key,
        sum_value,
        totals[:head_size],
        totals[head_size : 2 * head_size],
        sum_output,
        sum_ffn,
        sum_router,
        grad_gate[None],
        grad_up[None],
        grad_down[None],
        root_mean_squares,
    )


def solution(mesh):
    rings, shards = mesh.shape["ep"], mesh.shape["ws"]
    planes = 4 if rings % 4 == 0 else 1
    fine = Mesh(mesh.devices.reshape(planes, rings // planes, shards), ("z", "x", "w"))
    every = ("z", "x", "w")
    rows, deep = P(every, None), P(every, None, None)
    return jax.shard_map(
        local,
        mesh=fine,
        in_specs=(
            rows, P("w"), P("w", None), P("w", None), P("w", None), P(), P(), P("w", None), P("w"), P("w", None),
            rows, deep, deep, deep, rows,
        ),
        out_specs=(
            rows, rows, P(every), rows, rows, rows, P(), P(), rows, P(every), rows, deep, deep, deep, P(),
        ),
        check_vma=False,
    )
```

```python
import functools

import jax
import jax.numpy as jnp
import numpy as np
from jax import lax
from jax.experimental import pallas as pl
from jax.experimental.pallas import tpu as pltpu
from jax.sharding import Mesh
from jax.sharding import PartitionSpec as P

BLOCK = 256
EPS = 1e-06
ROPE_BASE = 1000000.0
F32 = jnp.float32
BF16 = jnp.bfloat16
VMEM_LIMIT = 65024 * 1024


def dot(left, right):
    return jnp.dot(left, right, preferred_element_type=F32)


def dot_tn(left, right):
    return lax.dot_general(left, right, (((0,), (0,)), ((), ())), preferred_element_type=F32)


def dot_nt(left, right):
    return lax.dot_general(left, right, (((1,), (1,)), ((), ())), preferred_element_type=F32)


def rope_tables(seq_length, head_size):
    indices = np.arange(head_size // 2, dtype=np.float32)
    frequency = (np.float32(ROPE_BASE) ** (np.float32(-2.0) * indices / np.float32(head_size))).astype(np.float32)
    angles = np.arange(seq_length, dtype=np.float32)[:, None] * frequency[None, :]
    cosine, sine = np.cos(angles), np.sin(angles)
    return np.concatenate([cosine, cosine], axis=1), np.concatenate([-sine, sine], axis=1)


def norm_forward(values):
    scaling = lax.rsqrt(jnp.mean(values * values, axis=-1, keepdims=True) + EPS)
    return values * scaling, scaling


def norm_backward(grad_normed, normed, scaling):
    return scaling * (grad_normed - normed * jnp.mean(grad_normed * normed, axis=-1, keepdims=True))


def half_turn(values):
    return pltpu.roll(values, values.shape[-1] // 2, 1)


def rotate(values, cosine, signed_sine):
    return values * cosine + half_turn(values) * signed_sine


def unrotate(grads, cosine, signed_sine):
    return grads * cosine - half_turn(grads) * signed_sine


MESH = pl.DeviceIdType.MESH


def remote(source, target, send, recv, device):
    return pltpu.make_async_remote_copy(
        src_ref=source, dst_ref=target, send_sem=send, recv_sem=recv, device_id=device, device_id_type=MESH
    )


def wait_bytes(ref, sem):
    pltpu.make_async_copy(ref, ref, sem).wait()


def line_order(z, planes, step):
    low = jnp.minimum(z, planes - 1 - z)
    paired = (step <= 2 * low).astype(jnp.int32)
    hop = paired * ((step + 1) // 2) + (1 - paired) * (step - low)
    longer = (z > planes - 1 - z).astype(jnp.int32)
    below = paired * (step % 2) + (1 - paired) * longer
    return z + hop - 2 * below * hop, hop, below


def greet_plane_and_line(planes, across, shards):
    z, x, w = lax.axis_index("z"), lax.axis_index("x"), lax.axis_index("w")
    in_plane = across * shards
    me = x * shards + w
    barrier = pltpu.get_barrier_semaphore()

    @pl.loop(1, in_plane)
    def _(offset):
        index = (me + offset) % in_plane
        pl.semaphore_signal(barrier, inc=1, device_id=(z, index // shards, index % shards), device_id_type=MESH)

    @pl.loop(1, planes)
    def _(offset):
        pl.semaphore_signal(barrier, inc=1, device_id=((z + offset) % planes, x, w), device_id_type=MESH)

    pl.semaphore_wait(barrier, in_plane + planes - 2)


def attention_forward(
    planes, across, shards, capacity, heads_a_step,
    own_ref, small_ref, routes_ref, top_ref, wq_hbm, wk_hbm, wv_hbm, query_gain_ref, key_gain_ref, cosine_ref, sine_ref, wo_ref,
    input_ref, query_raw_ref, key_raw_ref, value_ref, attended_ref, middle_ref, slots_ref, my_slots_ref, shares_ref, squares_ref,
    second_hbm, small_hbm,
    weights_hbm, top_rows_hbm,
    hidden, small_in, weights, key_rot_ref, routes_in, far_slots, plane_rows, stage, chosen, pair_out, far_out,
    gather_send, gather_recv, small_send, small_recv, weight_send, weight_recv, route_send, route_recv, plane_route_send,
    plane_route_recv, far_send, far_recv,
    line_send, line_recv, top_send, top_recv, pair_send, pair_recv, store_sem, small_sem, second_sem,
):
    step = pl.program_id(0)
    head_size = cosine_ref.shape[1]
    last = wo_ref.shape[0] // (heads_a_step * head_size)
    seq_length = cosine_ref.shape[0]
    blocks = seq_length // BLOCK
    factor = head_size ** (-0.5)
    z, x, w = lax.axis_index("z"), lax.axis_index("x"), lax.axis_index("w")
    in_plane = across * shards
    tokens, width = own_ref.shape
    me = x * shards + w
    depth = width // shards
    experts = planes * in_plane
    wide = heads_a_step * head_size
    chunk = 512
    targets = in_plane // 2
    pair, core = w // 2, w % 2
    sibling, opposite, other = pair * 2 + 1 - core, (1 - pair) * 2 + core, (1 - pair) * 2 + 1 - core

    def slice_of(index):
        return pl.ds(pl.multiple_of(index * capacity, 16), capacity)

    def tokens_of(index):
        return pl.ds(pl.multiple_of(index * tokens, tokens), tokens)

    def gather_copy(kind, owner, target):
        return remote(
            hidden.at[tokens_of(owner)], hidden.at[tokens_of(owner)], gather_send.at[kind], gather_recv.at[kind],
            (z, x, target),
        )

    def small_copy(offset):
        return remote(small_ref, small_in.at[w], small_send.at[offset], small_recv.at[w], (z, x, (w + offset) % shards))

    def columns_at(start, size):
        return pl.ds(pl.multiple_of(start, 128), size)

    my_depth = pl.ds(pl.multiple_of(w * depth, 16), depth)
    query_wide = last * wide

    def weight_pieces(piece, target):
        if piece is None:
            key_at, value_at = columns_at(target * head_size, head_size), columns_at(target * head_size, head_size)
            return [
                (wk_hbm.at[:, key_at], weights.at[my_depth, columns_at(last * wide, head_size)], last),
                (wv_hbm.at[:, value_at], weights.at[my_depth, columns_at(last * wide + head_size, head_size)], last),
            ]
        return [
            (
                wq_hbm.at[:, columns_at(target * query_wide + piece * wide, wide)],
                weights.at[my_depth, columns_at(piece * wide, wide)], piece,
            )
        ]

    def start_weights(piece):
        @pl.loop(1, shards)
        def _(offset):
            for source, goal, sem in weight_pieces(piece, (w + offset) % shards):
                remote(source, goal, weight_send.at[sem], weight_recv.at[sem], (z, x, (w + offset) % shards)).start()

        for source, goal, sem in weight_pieces(piece, w):
            pltpu.make_async_copy(source, goal, weight_recv.at[sem]).start()

    def wait_weights(piece):
        whole_piece = weights.at[:, columns_at(piece * wide, wide)]
        wait_bytes(whole_piece, weight_recv.at[piece])

    def line_copy(column, block, hop, direction):
        rows = plane_rows.at[column, block]
        return remote(
            rows, rows, line_send.at[column, direction, hop], line_recv.at[column, direction, hop],
            (z + 1 - 2 * direction, x, w),
        )

    def start_line(column, block, hop, upward, downward):
        @pl.when(upward & (z + 1 < planes))
        def _():
            line_copy(column, block, hop, 0).start()

        @pl.when(downward & (z > 0))
        def _():
            line_copy(column, block, hop, 1).start()

    def relay(column, hop):
        @pl.when(z - hop >= 0)
        def _():
            wait_bytes(plane_rows.at[column, 0], line_recv.at[column, 0, hop])

            @pl.when(z + 1 < planes)
            def _():
                line_copy(column, z - hop, hop + 1, 0).start()

        @pl.when(z + hop < planes)
        def _():
            wait_bytes(plane_rows.at[column, 0], line_recv.at[column, 1, hop])

            @pl.when(z > 0)
            def _():
                line_copy(column, z + hop, hop + 1, 1).start()

    expert_of = z * in_plane + lax.broadcasted_iota(jnp.int32, (in_plane, tokens), 0)
    earlier = (
        lax.broadcasted_iota(jnp.int32, (tokens, tokens), 0) < lax.broadcasted_iota(jnp.int32, (tokens, tokens), 1)
    ).astype(F32).astype(BF16)
    slot_ids = lax.broadcasted_iota(jnp.int32, (capacity, tokens), 0)

    def fill_slots(column, table):
        @pl.loop(0, planes)
        def _(block):
            hits = jnp.zeros((in_plane, tokens), F32)
            for k in range(routes_ref.shape[0]):
                hits += (routes_in[column, block, k : k + 1, :] == expert_of).astype(F32)
            ranks = dot(hits.astype(BF16), earlier).astype(jnp.int32)
            slots = jnp.where(hits > 0.0, ranks, -1)
            for index in range(in_plane):
                table[block * in_plane + index] = slots[index : index + 1, :]

    def pack(column, turn, table):
        block, _, _ = line_order(z, planes, turn)

        def index_of(target):
            return (target // 2) * shards + pair * 2 + target % 2

        for target in range(targets):
            slots = table[block * in_plane + index_of(target)]
            chosen[target * capacity : (target + 1) * capacity, :] = (slot_ids == slots).astype(F32).astype(BF16)

        @pl.loop(0, width // chunk)
        def _(part):
            here = pl.ds(pl.multiple_of(part * chunk, chunk), chunk)
            stage[column, turn, :, here] = dot(chosen[...], plane_rows[column, block, :, here]).astype(BF16)

        source = x * shards + (w if column == 0 else opposite)
        mine = x * 2 + core

        @pl.loop(1, targets)
        def _(offset):
            target = (mine + offset) % targets
            remote(
                stage.at[column, turn, slice_of(target)], top_rows_hbm.at[block, slice_of(source)],
                top_send.at[column, turn], top_recv.at[block], (z, target // 2, pair * 2 + target % 2),
            ).start()

        pltpu.make_async_copy(
            stage.at[column, turn, slice_of(mine)], top_rows_hbm.at[block, slice_of(source)], top_recv.at[block]
        ).start()

    def route_copy(offset):
        return remote(
            routes_ref, routes_in.at[me, z], route_send.at[offset], route_recv.at[z], ((z + offset) % planes, x, w)
        )

    far_top = remote(top_ref, plane_rows.at[1, z], far_send, far_recv, (z, x, opposite))
    opposite_me = x * shards + opposite

    def plane_route_copy(index):
        return remote(
            routes_in.at[me], routes_in.at[me], plane_route_send, plane_route_recv.at[me],
            (z, index // shards, index % shards),
        )

    def fill_my_slots():
        my_expert = z * in_plane + me

        @pl.loop(0, planes)
        def _(block):
            hits = jnp.concatenate(
                [
                    jnp.max((routes_in[index, block] == my_expert).astype(F32), axis=0, keepdims=True)
                    for index in range(in_plane)
                ],
                axis=0,
            )
            ranks = dot(hits.astype(BF16), earlier).astype(jnp.int32)
            slots = jnp.where(hits > 0.0, ranks, -1)
            for index in range(in_plane):
                my_slots_ref[block * in_plane + index] = slots[index : index + 1, :]

    @pl.when(step == 0)
    def _():
        greet_plane_and_line(planes, across, shards)
        far_top.start()

        @pl.loop(1, planes)
        def _(offset):
            route_copy(offset).start()

        @pl.loop(1, shards)
        def _(offset):
            small_copy(offset).start()

        plane_rows[0, z] = top_ref[...]
        start_line(0, z, 1, True, True)
        hidden[tokens_of(w), :] = own_ref[...]
        gather_copy(0, w, sibling).start()
        small_in[w] = small_ref[...]
        routes_in[me, z] = routes_ref[...]

        @pl.loop(1, planes)
        def _(offset):
            source = (z + offset) % planes
            wait_bytes(routes_in.at[me, source], route_recv.at[source])

        @pl.loop(1, in_plane)
        def _(offset):
            plane_route_copy((me + offset) % in_plane).start()

        fill_slots(me, slots_ref)
        pack(0, 0, slots_ref)
        gather_copy(1, w, opposite).start()
        relay(0, 1)
        wait_bytes(plane_rows.at[1, z], far_recv)
        start_line(1, z, 1, True, True)
        start_weights(None)
        wait_bytes(routes_in.at[opposite_me], plane_route_recv.at[opposite_me])
        fill_slots(opposite_me, far_slots)
        pack(1, 0, far_slots)
        wait_bytes(hidden.at[tokens_of(opposite)], gather_recv.at[1])
        gather_copy(2, opposite, sibling).start()
        start_weights(0)
        pack(0, 1, slots_ref)

        @pl.loop(1, shards)
        def _(offset):
            source = (w + offset) % shards
            wait_bytes(small_in.at[source], small_recv.at[source])

        wait_bytes(hidden.at[tokens_of(sibling)], gather_recv.at[0])
        wait_bytes(hidden.at[tokens_of(other)], gather_recv.at[2])
        for block in range(blocks):
            rows = pl.ds(block * BLOCK, BLOCK)
            normed, _ = norm_forward(hidden[rows, :].astype(F32))
            for part in range(shards):
                here = slice(part * depth, (part + 1) * depth)
                input_ref[rows, here] = (normed[:, here] * small_in[part, experts + 1 : experts + 2, :]).astype(BF16)
        relay(0, 2)
        start_weights(1)
        pack(0, 2, slots_ref)
        wait_weights(last)
        for block in range(blocks):
            rows = pl.ds(block * BLOCK, BLOCK)
            key_value = dot(input_ref[rows, :], weights[:, columns_at(last * wide, wide)])
            key_raw = key_value[:, :head_size]
            key_raw_ref[rows, :] = key_raw
            value_ref[rows, :] = key_value[:, head_size:].astype(BF16)
            key_normed, _ = norm_forward(key_raw)
            key_rot_ref[rows, :] = rotate(
                key_normed * key_gain_ref[...], cosine_ref[rows, :], sine_ref[rows, :]
            ).astype(BF16)
        relay(1, 1)
        pack(1, 1, far_slots)

    for piece in range(2, last):

        @pl.when(step == piece - 2)
        def _():
            wait_weights(piece - 2)
            if piece == last - 1:
                for kind in range(3):
                    wait_bytes(hidden.at[tokens_of(w)], gather_send.at[kind])
            start_weights(piece)

    @pl.when((step >= last - 2) & (step < last))
    def _():
        wait_weights(step)

    @pl.when(step < last)
    def _():
        here = columns_at(step * wide, wide)
        for block in range(blocks):
            rows = pl.ds(block * BLOCK, BLOCK)
            seen = pl.ds(0, (block + 1) * BLOCK)
            query_raw = dot(input_ref[rows, :], weights[:, here])
            query_raw_ref[rows, :] = query_raw

            @pl.loop(0, heads_a_step)
            def _(head):
                query_normed, _ = norm_forward(query_raw_ref[rows, columns_at(head * head_size, head_size)])
                query_rot = rotate(
                    query_normed * query_gain_ref[...], cosine_ref[rows, :], sine_ref[rows, :]
                ).astype(BF16)
                scores = dot_nt(query_rot, key_rot_ref[seen, :]) * factor
                exponent = jnp.exp(scores - jnp.max(scores, axis=-1, keepdims=True))
                probs = (exponent / jnp.sum(exponent, axis=-1, keepdims=True)).astype(BF16)
                attended_ref[rows, columns_at(step * wide + head * head_size, head_size)] = dot(
                    probs, value_ref[seen, :]
                ).astype(BF16)

    @pl.when(step == 1)
    def _():
        relay(0, 3)
        pack(0, 3, slots_ref)

    @pl.when(step == 2)
    def _():
        relay(1, 2)
        pack(1, 2, far_slots)

    def project(owner, goal, added):
        rows = tokens_of(owner)

        @pl.loop(0, width // chunk)
        def _(part):
            here = pl.ds(pl.multiple_of(part * chunk, chunk), chunk)
            value = dot(attended_ref[rows, :], wo_ref[:, here])
            if added is not None:
                value += hidden[added, here].astype(F32)
            goal[:, here] = value.astype(goal.dtype)

    def pair_copy(kind):
        at = pl.ds(kind * tokens, tokens)
        return remote(pair_out.at[kind], hidden.at[at], pair_send.at[kind], pair_recv.at[kind], (z, x, sibling))

    far_at = pl.ds(2 * tokens, tokens)
    far_copy = remote(far_out, hidden.at[far_at], pair_send.at[2], pair_recv.at[2], (z, x, opposite))

    @pl.when(step == last)
    def _():
        store = pltpu.make_async_copy(weights, weights_hbm, store_sem)
        store.start()
        small_store = pltpu.make_async_copy(small_in, small_hbm, small_sem)
        small_store.start()
        project(other, pair_out.at[0], None)
        pair_copy(0).start()
        project(sibling, pair_out.at[1], None)
        pair_copy(1).start()
        wait_bytes(hidden.at[pl.ds(0, tokens)], pair_recv.at[0])
        project(opposite, far_out, pl.ds(0, tokens))
        far_copy.start()
        wait_bytes(hidden.at[pl.ds(tokens, tokens)], pair_recv.at[1])
        project(w, middle_ref, pl.ds(tokens, tokens))
        @pl.loop(1, in_plane)
        def _(offset):
            index = (me + offset) % in_plane

            @pl.when(index != opposite_me)
            def _():
                wait_bytes(routes_in.at[index], plane_route_recv.at[index])

        fill_my_slots()
        relay(1, 3)
        pack(1, 3, far_slots)
        wait_bytes(hidden.at[far_at], pair_recv.at[2])
        wait_bytes(far_out, pair_send.at[2])
        ffn_row = jnp.concatenate([small_in[part, experts : experts + 1, :] for part in range(shards)], axis=1)

        def finish_rows(piece, carry):
            at = pl.ds(pl.multiple_of(piece * 64, 64), 64)
            far = pl.ds(pl.multiple_of(2 * tokens + piece * 64, 64), 64)
            branch = middle_ref[at, :] + hidden[far, :].astype(F32)
            source = own_ref[at, :].astype(F32)
            middle = source + branch
            middle_ref[at, :] = middle
            normed, _ = norm_forward(middle)
            far_out[at, :] = (normed * ffn_row).astype(BF16)
            return (
                carry[0] + jnp.sum(jnp.sum(source * source, axis=1, keepdims=True), axis=0, keepdims=True),
                carry[1] + jnp.sum(jnp.sum(branch * branch, axis=1, keepdims=True), axis=0, keepdims=True),
            )

        zero = jnp.zeros((1, 1), F32)
        source_square, branch_square = lax.fori_loop(0, tokens // 64, finish_rows, (zero, zero))
        second_store = pltpu.make_async_copy(far_out, second_hbm, second_sem)
        second_store.start()
        lane = lax.broadcasted_iota(jnp.int32, (8, 128), 1)
        row = lax.broadcasted_iota(jnp.int32, (8, 128), 0)
        values = jnp.where(lane == 0, source_square, 0.0) + jnp.where(lane == 1, branch_square, 0.0)
        squares_ref[...] = jnp.where(row == 2, values, 0.0)
        logits = jnp.zeros((experts, tokens), F32)
        for part in range(shards):
            logits += dot_nt(small_in[part, :experts, :].astype(BF16), far_out[:, part * depth : (part + 1) * depth])
        expert_ids = lax.broadcasted_iota(jnp.int32, (experts, tokens), 0)
        hits = jnp.zeros((experts, tokens), F32)
        for k in range(routes_ref.shape[0]):
            hits += (routes_ref[k : k + 1, :] == expert_ids).astype(F32)
        routed = hits > 0.0
        peaks = jnp.max(jnp.where(routed, logits, -jnp.inf), axis=0, keepdims=True)
        shifted = jnp.where(routed, jnp.exp(jnp.where(routed, logits - peaks, 0.0)), 0.0)
        shares = shifted / jnp.sum(shifted, axis=0, keepdims=True)
        for expert in range(experts):
            shares_ref[expert] = shares[expert : expert + 1, :]

        @pl.loop(0, planes)
        def _(block):
            wait_bytes(top_rows_hbm.at[block], top_recv.at[block])
            if targets > 1:
                for column in range(2):
                    wait_bytes(stage.at[column, 0, pl.ds(0, (targets - 1) * capacity)], top_send.at[column, block])

        for kind in range(2):
            wait_bytes(far_out, pair_send.at[kind])

        @pl.loop(1, shards)
        def _(offset):
            wait_bytes(small_in.at[w], small_send.at[offset])

        @pl.loop(1, planes)
        def _(offset):
            wait_bytes(routes_in.at[0, 0], route_send.at[offset])

        wait_bytes(routes_in.at[pl.ds(0, in_plane - 1)], plane_route_send)
        wait_bytes(plane_rows.at[1, 0], far_send)

        @pl.loop(0, last + 1)
        def _(piece):
            wait_bytes(weights.at[pl.ds(0, (shards - 1) * depth), pl.ds(0, wide)], weight_send.at[piece])

        for column in range(2):
            for hop in range(1, planes):

                @pl.when((z - (hop - 1) >= 0) & (z + 1 < planes))
                def _():
                    wait_bytes(plane_rows.at[0, 0], line_send.at[column, 0, hop])

                @pl.when((z + (hop - 1) < planes) & (z > 0))
                def _():
                    wait_bytes(plane_rows.at[0, 0], line_send.at[column, 1, hop])

        store.wait()
        small_store.wait()
        second_store.wait()


def attention_backward(
    planes, across, shards, capacity, heads_a_step,
    own_grad_ref, wo_ref, attended_ref, query_raw_ref, key_raw_ref, value_ref, input_ref, wq_ref,
    query_gain_ref, key_gain_ref, cosine_ref, sine_ref, slots_ref, weighted_hbm,
    wo_grad_ref, wq_grad_ref, first_grad_ref, query_gain_grad_ref, key_gain_grad_ref, returned_hbm, expert_sum_ref,
    total_ref, key_rot_ref, key_grad_ref, value_grad_ref, query_grad_ref, turned_ref, grad_ref,
    rows, chosen, partial_out, partial_in,
    gather_send, gather_recv, back_send, back_recv, sum_send, sum_recv, load_sem,
):
    step = pl.program_id(0)
    last = pl.num_programs(0) - 1
    head_size = cosine_ref.shape[1]
    seq_length = cosine_ref.shape[0]
    blocks = seq_length // BLOCK
    factor = head_size ** (-0.5)
    z, x, w = lax.axis_index("z"), lax.axis_index("x"), lax.axis_index("w")
    in_plane = across * shards
    me = x * shards + w
    tokens, width = own_grad_ref.shape
    count = in_plane * capacity
    chunk = 512
    pair, core = w // 2, w % 2
    sibling, opposite, other = pair * 2 + 1 - core, (1 - pair) * 2 + core, (1 - pair) * 2 + 1 - core

    def slice_of(index):
        return pl.ds(pl.multiple_of(index * capacity, 16), capacity)

    def tokens_of(index):
        return pl.ds(pl.multiple_of(index * tokens, tokens), tokens)

    def gather_copy(kind, owner, target):
        return remote(
            grad_ref.at[tokens_of(owner)], grad_ref.at[tokens_of(owner)], gather_send.at[kind], gather_recv.at[kind],
            (z, x, target),
        )

    def back_copy(block, index):
        return remote(
            weighted_hbm.at[block, slice_of(index)], returned_hbm.at[block, slice_of(me)],
            back_send.at[block], back_recv.at[block], (z, index // shards, index % shards),
        )

    pace = [(1, 1), (2, 2), (3, 3)]

    def start_back(turn, near, far):
        block, _, _ = line_order(z, planes, planes - 1 - turn)

        @pl.loop(1, in_plane)
        def _(offset):
            index = (me + offset) % in_plane
            beside = (index % shards) // 2 == pair

            @pl.when((beside & near) | (jnp.logical_not(beside) & far))
            def _():
                back_copy(block, index).start()

        @pl.when(near)
        def _():
            pltpu.make_async_copy(
                weighted_hbm.at[block, slice_of(me)], returned_hbm.at[block, slice_of(me)], back_recv.at[block]
            ).start()

    def sum_copy(block):
        return remote(partial_out.at[block], partial_in.at[z], sum_send.at[block], sum_recv.at[z], (block, x, w))

    def combine(turn):
        place = planes - 1 - turn
        block, _, _ = line_order(z, planes, place)
        wait_bytes(returned_hbm.at[block], back_recv.at[block])
        load = pltpu.make_async_copy(returned_hbm.at[block], rows, load_sem)
        load.start()
        if place > 0:
            start_back(turn + 1, step >= 0, step >= 0)
        slot_ids = lax.broadcasted_iota(jnp.int32, (capacity, tokens), 0)

        @pl.loop(0, in_plane)
        def _(index):
            slots = slots_ref[block * in_plane + index]
            chosen[slice_of(index), :] = (slot_ids == slots).astype(F32).astype(BF16)

        load.wait()

        @pl.loop(0, width // chunk)
        def _(part):
            wide = pl.ds(pl.multiple_of(part * chunk, chunk), chunk)
            summed = dot_tn(chosen[...], rows[:, wide])
            if place > 0:
                partial_out[block, :, wide] = summed.astype(BF16)
            else:
                expert_sum_ref[:, wide] = summed

        if place > 0:
            sum_copy(block).start()

    @pl.when(step == 0)
    def _():
        greet_plane_and_line(planes, across, shards)
        grad_ref[tokens_of(w), :] = own_grad_ref[...]
        gather_copy(1, w, opposite).start()
        gather_copy(0, w, sibling).start()
        start_back(0, step == 0, step != 0)
        key_normed, _ = norm_forward(key_raw_ref[...])
        key_rot_ref[...] = rotate(key_normed * key_gain_ref[...], cosine_ref[...], sine_ref[...]).astype(BF16)
        key_grad_ref[...] = jnp.zeros_like(key_grad_ref)
        value_grad_ref[...] = jnp.zeros_like(value_grad_ref)
        query_gain_grad_ref[...] = jnp.zeros_like(query_gain_grad_ref)
        for block in range(blocks):
            rows_here = pl.ds(block * BLOCK, BLOCK)
            turned_ref[:, rows_here] = input_ref[rows_here, :].T
        wait_bytes(grad_ref.at[tokens_of(opposite)], gather_recv.at[1])
        gather_copy(2, opposite, sibling).start()
        start_back(0, step != 0, step == 0)
        wait_bytes(grad_ref.at[tokens_of(sibling)], gather_recv.at[0])
        wait_bytes(grad_ref.at[tokens_of(other)], gather_recv.at[2])

    @pl.when(step < last)
    def _():
        wo_grad_ref[...] = dot_tn(attended_ref[...], grad_ref[...]).astype(BF16)
        for block in range(blocks):
            rows_here = pl.ds(block * BLOCK, BLOCK)
            seen = pl.ds(0, (block + 1) * BLOCK)
            query_grad_ref[rows_here, :] = dot_nt(grad_ref[rows_here, :], wo_ref[...]).astype(BF16)

            @pl.loop(0, heads_a_step)
            def _(head):
                columns = pl.ds(pl.multiple_of(head * head_size, head_size), head_size)
                query_normed, query_scale = norm_forward(query_raw_ref[rows_here, columns])
                cosine, sine = cosine_ref[rows_here, :], sine_ref[rows_here, :]
                query_rot = rotate(query_normed * query_gain_ref[...], cosine, sine).astype(BF16)
                head_grad = query_grad_ref[rows_here, columns]
                keys, values = key_rot_ref[seen, :], value_ref[seen, :]
                scores = dot_nt(query_rot, keys) * factor
                exponent = jnp.exp(scores - jnp.max(scores, axis=-1, keepdims=True))
                probs = exponent / jnp.sum(exponent, axis=-1, keepdims=True)
                prob_grad = dot_nt(head_grad, values)
                value_grad_ref[seen, :] += dot_tn(probs.astype(BF16), head_grad)
                center = jnp.sum(probs * prob_grad, axis=-1, keepdims=True)
                score_grad = (probs * (prob_grad - center)).astype(BF16)
                key_grad_ref[seen, :] += dot_tn(score_grad, query_rot) * factor
                query_rot_grad = dot(score_grad, keys) * factor
                unrotated = unrotate(query_rot_grad, cosine, sine)
                query_gain_grad_ref[0:1, :] += jnp.sum(unrotated * query_normed, axis=0, keepdims=True)
                query_grad_ref[rows_here, columns] = norm_backward(
                    unrotated * query_gain_ref[...], query_normed, query_scale
                ).astype(BF16)
            partial = dot_nt(query_grad_ref[rows_here, :], wq_ref[...])

            @pl.when(step == 0)
            def _():
                total_ref[rows_here, :] = partial

            @pl.when(step > 0)
            def _():
                total_ref[rows_here, :] += partial

            for turn, place in enumerate(pace):
                if place[1] == block:

                    @pl.when(step == place[0])
                    def _():
                        combine(turn)

    @pl.when(step == last)
    def _():
        key_normed, key_scale = norm_forward(key_raw_ref[...])
        unrotated = unrotate(key_grad_ref[...], cosine_ref[...], sine_ref[...])
        key_gain_grad_ref[...] = jnp.zeros_like(key_gain_grad_ref)
        key_gain_grad_ref[0:1, :] = jnp.sum(unrotated * key_normed, axis=0, keepdims=True)
        key_grad = norm_backward(unrotated * key_gain_ref[...], key_normed, key_scale)
        query_grad_ref[:, :head_size] = key_grad.astype(BF16)
        query_grad_ref[:, head_size : 2 * head_size] = value_grad_ref[...].astype(BF16)
        for block in range(blocks):
            rows_here = pl.ds(block * BLOCK, BLOCK)
            first_grad_ref[rows_here, :] = (
                total_ref[rows_here, :] + dot_nt(query_grad_ref[rows_here, :], wq_ref[...])
            ).astype(BF16)

    wq_grad_ref[...] = dot(turned_ref[...], query_grad_ref[...]).astype(BF16)

    @pl.when(step == last)
    def _():
        for turn in range(len(pace), planes):
            combine(turn)

        @pl.loop(1, planes)
        def _(offset):
            source = (z + offset) % planes
            wait_bytes(partial_in.at[source], sum_recv.at[source])

            @pl.loop(0, width // chunk)
            def _(part):
                wide = pl.ds(pl.multiple_of(part * chunk, chunk), chunk)
                expert_sum_ref[:, wide] += partial_in[source, :, wide].astype(F32)

            wait_bytes(partial_out.at[source], sum_send.at[source])

        @pl.loop(0, planes)
        def _(block):
            wait_bytes(weighted_hbm.at[block, pl.ds(0, count - capacity)], back_send.at[block])

        wait_bytes(grad_ref.at[tokens_of(w)], gather_send.at[0])
        wait_bytes(grad_ref.at[tokens_of(w)], gather_send.at[1])
        wait_bytes(grad_ref.at[tokens_of(w)], gather_send.at[2])


def whole(shape):
    return pl.BlockSpec(shape, lambda step: (0,) * len(shape), pipeline_mode=pl.Buffered(1))


def run_forward(
    planes, across, shards, capacity, own, small, routes, top, w_query, w_key, w_value, query_gain, key_gain, cosine, sine, wo
):
    tokens, width = own.shape
    seq_length = tokens * shards
    head_size = query_gain.shape[1]
    heads_here = wo.shape[0] // head_size
    pair = 2
    wide = pair * head_size
    steps = heads_here // pair
    in_plane = across * shards
    count = in_plane * capacity
    hbm = pl.BlockSpec(memory_space=pl.ANY)
    dma = pltpu.SemaphoreType.DMA
    slots_shape = (planes * in_plane, 1, tokens)
    return pl.pallas_call(
        functools.partial(attention_forward, planes, across, shards, capacity, pair),
        grid=(steps + 1,),
        in_specs=[
            whole((tokens, width)),
            whole(small.shape),
            whole(routes.shape),
            whole((tokens, width)),
            hbm,
            hbm,
            hbm,
            whole((1, head_size)),
            whole((1, head_size)),
            whole((seq_length, head_size)),
            whole((seq_length, head_size)),
            whole(wo.shape),
        ],
        out_specs=[
            whole((seq_length, width)),
            pl.BlockSpec((seq_length, wide), lambda step: (0, jnp.minimum(step, steps - 1))),
            whole((seq_length, head_size)),
            whole((seq_length, head_size)),
            whole((seq_length, heads_here * head_size)),
            whole((tokens, width)),
            whole(slots_shape),
            whole(slots_shape),
            whole(slots_shape),
            whole((8, 128)),
            hbm,
            hbm,
            hbm,
            hbm,
        ],
        out_shape=[
            jax.ShapeDtypeStruct((seq_length, width), BF16),
            jax.ShapeDtypeStruct((seq_length, heads_here * head_size), F32),
            jax.ShapeDtypeStruct((seq_length, head_size), F32),
            jax.ShapeDtypeStruct((seq_length, head_size), BF16),
            jax.ShapeDtypeStruct((seq_length, heads_here * head_size), BF16),
            jax.ShapeDtypeStruct((tokens, width), F32),
            jax.ShapeDtypeStruct(slots_shape, jnp.int32),
            jax.ShapeDtypeStruct(slots_shape, jnp.int32),
            jax.ShapeDtypeStruct(slots_shape, F32),
            jax.ShapeDtypeStruct((8, 128), F32),
            jax.ShapeDtypeStruct((tokens, width), BF16),
            jax.ShapeDtypeStruct((shards,) + small.shape, F32),
            jax.ShapeDtypeStruct((width, (steps + 1) * wide), BF16),
            jax.ShapeDtypeStruct((planes, count, width), BF16),
        ],
        scratch_shapes=[
            pltpu.VMEM((seq_length, width), BF16),
            pltpu.VMEM((shards,) + small.shape, F32),
            pltpu.VMEM((width, (steps + 1) * wide), BF16),
            pltpu.VMEM((seq_length, head_size), BF16),
            pltpu.VMEM((in_plane, planes) + routes.shape, jnp.int32),
            pltpu.VMEM(slots_shape, jnp.int32),
            pltpu.VMEM((2, planes, tokens, width), BF16),
            pltpu.VMEM((2, planes, count // 2, width), BF16),
            pltpu.VMEM((count // 2, tokens), BF16),
            pltpu.VMEM((2, tokens, width), BF16),
            pltpu.VMEM((tokens, width), BF16),
            dma((3,)), dma((3,)), dma((shards,)), dma((shards,)), dma((steps + 1,)), dma((steps + 1,)),
            dma((planes,)), dma((planes,)), dma, dma((in_plane,)), dma, dma,
            dma((2, 2, planes + 1)), dma((2, 2, planes + 1)), dma((2, planes)), dma((planes,)), dma((3,)), dma((3,)), dma, dma, dma,
        ],
        compiler_params=pltpu.CompilerParams(vmem_limit_bytes=VMEM_LIMIT, collective_id=5, has_side_effects=True),
        cost_estimate=pl.CostEstimate(flops=70 * 10**9, bytes_accessed=40 * 10**6, transcendentals=6 * 10**6),
    )(own, small, routes, top, w_query, w_key, w_value, query_gain, key_gain, cosine, sine, wo)


def run_backward(
    planes, across, shards, capacity, own_grad, wo, attended, query_raw, key_raw, value, first_input, weights, query_gain,
    key_gain, cosine, sine, slots, weighted,
):
    tokens, width = own_grad.shape
    seq_length = attended.shape[0]
    head_size = query_gain.shape[1]
    heads_here = wo.shape[0] // head_size
    pair = 2
    wide = pair * head_size
    steps = heads_here // pair
    count = across * shards * capacity
    hbm = pl.BlockSpec(memory_space=pl.ANY)
    dma = pltpu.SemaphoreType.DMA

    def held(step):
        return jnp.minimum(step, steps - 1)

    return pl.pallas_call(
        functools.partial(attention_backward, planes, across, shards, capacity, pair),
        grid=(steps + 1,),
        in_specs=[
            whole((tokens, width)),
            pl.BlockSpec((wide, width), lambda step: (held(step), 0)),
            pl.BlockSpec((seq_length, wide), lambda step: (0, held(step))),
            pl.BlockSpec((seq_length, wide), lambda step: (0, held(step))),
            whole((seq_length, head_size)),
            whole((seq_length, head_size)),
            whole((seq_length, width)),
            pl.BlockSpec((width, wide), lambda step: (0, step)),
            whole((1, head_size)),
            whole((1, head_size)),
            whole((seq_length, head_size)),
            whole((seq_length, head_size)),
            whole(slots.shape),
            hbm,
        ],
        out_specs=[
            pl.BlockSpec((wide, width), lambda step: (held(step), 0)),
            pl.BlockSpec((width, wide), lambda step: (0, step)),
            whole((seq_length, width)),
            whole((8, head_size)),
            whole((8, head_size)),
            hbm,
            whole((tokens, width)),
        ],
        out_shape=[
            jax.ShapeDtypeStruct((heads_here * head_size, width), BF16),
            jax.ShapeDtypeStruct((width, (steps + 1) * wide), BF16),
            jax.ShapeDtypeStruct((seq_length, width), BF16),
            jax.ShapeDtypeStruct((8, head_size), F32),
            jax.ShapeDtypeStruct((8, head_size), F32),
            jax.ShapeDtypeStruct(weighted.shape, BF16),
            jax.ShapeDtypeStruct((tokens, width), F32),
        ],
        scratch_shapes=[
            pltpu.VMEM((seq_length, width), F32),
            pltpu.VMEM((seq_length, head_size), BF16),
            pltpu.VMEM((seq_length, head_size), F32),
            pltpu.VMEM((seq_length, head_size), F32),
            pltpu.VMEM((seq_length, wide), BF16),
            pltpu.VMEM((width, seq_length), BF16),
            pltpu.VMEM((seq_length, width), BF16),
            pltpu.VMEM((count, width), BF16),
            pltpu.VMEM((count, tokens), BF16),
            pltpu.VMEM((planes, tokens, width), BF16),
            pltpu.VMEM((planes, tokens, width), BF16),
            dma((3,)), dma((3,)), dma((planes,)), dma((planes,)), dma((planes,)), dma((planes,)), dma,
        ],
        compiler_params=pltpu.CompilerParams(vmem_limit_bytes=VMEM_LIMIT, collective_id=2, has_side_effects=True),
        cost_estimate=pl.CostEstimate(flops=70 * 10**9, bytes_accessed=60 * 10**6, transcendentals=6 * 10**6),
    )(
        own_grad, wo, attended, query_raw, key_raw, value, first_input, weights, query_gain, key_gain, cosine, sine, slots,
        weighted,
    )


def reduce_kernel(
    planes, across, shards,
    wq_hbm, wo_hbm, first_hbm, hidden_ref, middle_hbm, expert_sum_hbm, middle_grad_hbm, scale_ref, early_ref, shared_ref,
    rows_hbm, gate_grad_hbm, up_grad_hbm, units_hbm, pair_grad_hbm,
    query_ref, key_ref, value_ref, output_ref, hidden_out_ref, grad_in_ref, early_total_ref, late_total_ref,
    gate_out_hbm, up_out_hbm, down_out_hbm,
    wq_parts, wo_parts, wq_out, wo_out, wq_in, wo_in, wq_total, wo_total, wq_final, wo_final, wq_home, wo_home, first_in,
    early_in, late, late_in, held_a, held_b, side, turned, tiles, tall, flat,
    across_send, across_recv, line_send, line_recv, home_send, home_recv, swap_send, swap_recv, first_send, first_recv,
    early_send, early_recv, late_send, late_recv, held_sem, side_sem, tile_sem, result_sem,
):
    z, x, w = lax.axis_index("z"), lax.axis_index("x"), lax.axis_index("w")
    rings = planes * across
    ring = z * across + x
    everyone = rings * shards
    wq_rows, wo_rows = wq_total.shape[0], wo_total.shape[0]
    mine = wq_rows // shards
    tokens, width = grad_in_ref.shape
    query_columns = query_ref.shape[1] // shards
    key_columns = key_ref.shape[1] // shards
    linear = ring * shards + w
    barrier = pltpu.get_barrier_semaphore()

    def place(index):
        return (index // shards // across, index // shards % across, index % shards)

    @pl.loop(1, everyone)
    def _(offset):
        pl.semaphore_signal(barrier, inc=1, device_id=place((linear + offset) % everyone), device_id_type=MESH)

    pl.semaphore_wait(barrier, everyone - 1)

    def rows_of(index, size):
        return pl.ds(pl.multiple_of(index * size, 16), size)

    sources = [(wq_hbm, wq_rows, wq_parts), (wo_hbm, wo_rows, wo_parts)]

    def across_copy(kind, plane, column):
        source, rows, goal = sources[kind]
        return remote(
            source.at[rows_of(plane * across + column, rows)], goal.at[plane, x],
            across_send.at[kind, plane], across_recv.at[kind, plane], (z, column, w),
        )

    def first_copy(offset):
        target = (w + offset) % shards
        return remote(
            first_hbm.at[rows_of(target, tokens)], first_in.at[offset], first_send.at[offset], first_recv.at[offset],
            (z, x, target),
        )

    @pl.loop(1, shards)
    def _(offset):
        first_copy(offset).start()

    pltpu.make_async_copy(first_hbm.at[rows_of(w, tokens)], first_in.at[0], first_recv.at[0]).start()
    hold_a = pltpu.make_async_copy(middle_hbm, held_a, held_sem.at[0])
    hold_b = pltpu.make_async_copy(expert_sum_hbm, held_b, held_sem.at[1])
    hold_a.start()
    hold_b.start()

    def start_across(kind, turn):
        plane, _, _ = line_order(z, planes, planes - 1 - turn)

        @pl.loop(1, across)
        def _(offset):
            across_copy(kind, plane, (x + offset) % across).start()

        source, rows, goal = sources[kind]
        pltpu.make_async_copy(
            source.at[rows_of(plane * across + x, rows)], goal.at[plane, x], across_recv.at[kind, plane]
        ).start()

    start_across(1, 0)
    start_across(1, 1)

    @pl.loop(1, everyone)
    def _(offset):
        other = (linear + offset) % everyone
        remote(early_ref.at[other], early_in.at[linear], early_send, early_recv, place(other)).start()

    early_in[linear] = early_ref[linear]
    lanes = tiles.shape[2]
    per_kind = width // lanes
    depth = side.shape[0]
    late_rows = width // 128
    pick = (lax.broadcasted_iota(jnp.int32, (8, 128), 0) == 2).astype(F32)
    lane = lax.broadcasted_iota(jnp.int32, (8, 128), 1)

    def tile_copy(unit):
        slot = unit % 2
        here = pl.ds(pl.multiple_of((unit % per_kind) * lanes, lanes), lanes)

        @pl.when(unit < 2 * per_kind)
        def _():
            pltpu.make_async_copy(rows_hbm.at[:, here], tiles.at[slot], tile_sem.at[slot]).start()

        @pl.when(unit >= 2 * per_kind)
        def _():
            pltpu.make_async_copy(pair_grad_hbm.at[:, here], tiles.at[slot], tile_sem.at[slot]).start()

    tile_copy(0)

    def multiply(unit):
        slot = unit % 2
        here = pl.ds(pl.multiple_of((unit % per_kind) * lanes, lanes), lanes)
        for kind, source in enumerate([gate_grad_hbm, up_grad_hbm, units_hbm]):

            @pl.when(unit == kind * per_kind)
            def _():
                load = pltpu.make_async_copy(source, side, side_sem)
                load.start()
                load.wait()
                if kind == 2:

                    @pl.loop(0, depth // 128)
                    def _(part):
                        at = pl.ds(pl.multiple_of(part * 128, 128), 128)
                        turned[:, at] = side[at, :].T

        @pl.when(unit + 1 < 3 * per_kind)
        def _():
            tile_copy(unit + 1)

        wait_bytes(tiles.at[slot], tile_sem.at[slot])

        @pl.when(unit >= 2)
        def _():
            wait_bytes(tall.at[slot], result_sem.at[slot])

        @pl.when(unit < 2 * per_kind)
        def _():
            tall[slot] = dot_tn(tiles[slot], side[...])

        @pl.when(unit < per_kind)
        def _():
            pltpu.make_async_copy(tall.at[slot], gate_out_hbm.at[here], result_sem.at[slot]).start()

        @pl.when((unit >= per_kind) & (unit < 2 * per_kind))
        def _():
            pltpu.make_async_copy(tall.at[slot], up_out_hbm.at[here], result_sem.at[slot]).start()

        @pl.when(unit >= 2 * per_kind)
        def _():
            flat[slot] = dot(turned[...], tiles[slot])
            pltpu.make_async_copy(flat.at[slot], down_out_hbm.at[:, here], result_sem.at[slot]).start()

    def late_copy(other):
        return remote(late, late_in.at[linear], late_send, late_recv, place(other))

    def finish_rows():
        hold_a.wait()
        hold_b.wait()
        pieces = tokens // 64

        def add_rows(piece, carry):
            at = pl.ds(pl.multiple_of(piece * 64, 64), 64)
            extra = held_b[at, :]
            hidden_out_ref[at, :] = (held_a[at, :] + extra).astype(BF16)
            return carry + jnp.sum(jnp.sum(extra * extra, axis=1, keepdims=True), axis=0, keepdims=True)

        expert_square = lax.fori_loop(0, pieces, add_rows, jnp.zeros((1, 1), F32))
        load = pltpu.make_async_copy(middle_grad_hbm, held_a, held_sem.at[0])
        load.start()

        @pl.loop(0, shards)
        def _(offset):
            wait_bytes(first_in.at[offset], first_recv.at[offset])

        load.wait()

        def grad_rows(piece, carry):
            square, gain_grad = carry
            at = pl.ds(pl.multiple_of(piece * 64, 64), 64)
            first = first_in[0, at, :].astype(F32)
            for offset in range(1, shards):
                first += first_in[offset, at, :].astype(F32)
            normed, scaling = norm_forward(hidden_ref[at, :].astype(F32))
            grad = held_a[at, :] + norm_backward(first * scale_ref[...], normed, scaling)
            grad_in_ref[at, :] = grad
            return (
                square + jnp.sum(jnp.sum(grad * grad, axis=1, keepdims=True), axis=0, keepdims=True),
                gain_grad + jnp.sum(first * normed, axis=0, keepdims=True),
            )

        square, gain_grad = lax.fori_loop(
            0, pieces, grad_rows, (jnp.zeros((1, 1), F32), jnp.zeros((1, width), F32))
        )
        for row in range(late_rows):
            late[row : row + 1, :] = gain_grad[:, row * 128 : (row + 1) * 128]
        late[late_rows:, :] = shared_ref[...] + pick * (
            jnp.where(lane == 2, expert_square, 0.0) + jnp.where(lane == 3, square, 0.0)
        )

        @pl.loop(1, everyone)
        def _(offset):
            late_copy((linear + offset) % everyone).start()

        late_in[linear] = late[...]

    outs, ins = [wq_out, wo_out], [wq_in, wo_in]
    totals, parts = [wq_total, wo_total], [wq_parts, wo_parts]

    def line_copy(kind, plane):
        up = (plane > z).astype(jnp.int32)
        ends = (plane == z + 2 * up - 1).astype(jnp.int32)
        slot = plane + ends * (1 - up) * (planes - plane)
        return remote(
            outs[kind].at[plane], ins[kind].at[slot], line_send.at[kind, plane], line_recv.at[kind, slot],
            (z + 2 * up - 1, x, w),
        )

    per_turn = 3 * per_kind // (2 * planes)

    def take(kind, slot):
        wait_bytes(ins[kind].at[slot], line_recv.at[kind, slot])
        totals[kind][...] += ins[kind][slot].astype(F32)

    def collect(kind):
        @pl.loop(0, planes)
        def _(turn):
            plane, _, _ = line_order(z, planes, planes - 1 - turn)

            @pl.loop(0, per_turn)
            def _(unit):
                multiply((turn + (1 - kind) * planes) * per_turn + unit)

            wait_bytes(parts[kind].at[plane], across_recv.at[kind, plane])

            @pl.when(turn < planes - 2)
            def _():
                start_across(kind, turn + 2)

            if kind == 1:

                @pl.when(turn >= planes - 2)
                def _():
                    start_across(0, turn + 2 - planes)

            totals[kind][...] = parts[kind][plane, 0].astype(F32)

            @pl.loop(1, across)
            def _(column):
                totals[kind][...] += parts[kind][plane, column].astype(F32)

            @pl.when(((plane > z) & (z > 0)) | ((plane < z) & (z < planes - 1)))
            def _():
                take(kind, plane)

            @pl.when(plane != z)
            def _():
                outs[kind][plane] = totals[kind][...].astype(BF16)
                line_copy(kind, plane).start()

    def finish(kind):
        @pl.when(z > 0)
        def _():
            take(kind, z)

        @pl.when(z < planes - 1)
        def _():
            take(kind, planes)

    collect(1)
    finish(1)
    wo_final[...] = wo_total[...].astype(BF16)
    goal = w * rings + ring
    stays = goal == linear
    swap = remote(
        wo_final, wo_home, swap_send, swap_recv, (goal // shards // across, goal // shards % across, goal % shards)
    )

    @pl.when(jnp.logical_not(stays))
    def _():
        swap.start()

    @pl.when(stays)
    def _():
        pltpu.make_async_copy(wo_final, wo_home, swap_recv).start()

    finish_rows()
    collect(0)
    finish(0)
    wq_final[...] = wq_total[...].astype(BF16)

    def home_copy(offset):
        target = (w + offset) % shards
        return remote(
            wq_final.at[rows_of(target, mine)], wq_home.at[w], home_send.at[offset], home_recv.at[w], (z, x, target)
        )

    @pl.loop(1, shards)
    def _(offset):
        home_copy(offset).start()

    pltpu.make_async_copy(wq_final.at[rows_of(w, mine)], wq_home.at[w], home_recv.at[w]).start()

    for part in range(shards):
        wait_bytes(wq_home.at[part], home_recv.at[part])
        rows = wq_home[part].astype(F32)
        query_ref[:, part * query_columns : (part + 1) * query_columns] = rows[:, :query_columns]
        key_ref[:, part * key_columns : (part + 1) * key_columns] = rows[:, query_columns : query_columns + key_columns]
        value_ref[:, part * key_columns : (part + 1) * key_columns] = rows[:, query_columns + key_columns :]

    wait_bytes(early_ref.at[pl.ds(0, everyone - 1)], early_recv)
    early_total_ref[...] = jnp.sum(early_in[...], axis=0)
    wait_bytes(late_in.at[pl.ds(0, everyone - 1)], late_recv)
    late_total_ref[...] = jnp.sum(late_in[...], axis=0)
    wait_bytes(early_ref.at[pl.ds(0, everyone - 1)], early_send)
    wait_bytes(late_in.at[pl.ds(0, everyone - 1)], late_send)
    for slot in range(2):
        wait_bytes(tall.at[slot], result_sem.at[slot])
    wait_bytes(wo_home, swap_recv)
    output_ref[...] = wo_home[...].astype(F32)

    @pl.when(jnp.logical_not(stays))
    def _():
        wait_bytes(wo_final, swap_send)

    @pl.loop(1, shards)
    def _(offset):
        wait_bytes(wq_home.at[0], home_send.at[offset])
        wait_bytes(first_in.at[0], first_send.at[offset])

    if across > 1:

        @pl.loop(0, planes)
        def _(plane):
            wait_bytes(wq_parts.at[plane, pl.ds(0, across - 1)], across_send.at[0, plane])
            wait_bytes(wo_parts.at[plane, pl.ds(0, across - 1)], across_send.at[1, plane])

    @pl.loop(1, planes)
    def _(offset):
        plane = (z + offset) % planes
        wait_bytes(wq_out.at[plane], line_send.at[0, plane])
        wait_bytes(wo_out.at[plane], line_send.at[1, plane])


def run_reduce(
    planes, across, shards, wq_grad, wo_grad, first_part, hidden, middle, expert_sum, middle_grad, scale, early, shared,
    rows_in, gate_grad, up_grad, units, pair_grad, query_columns, key_columns,
):
    rings = planes * across
    everyone = rings * shards
    width = wq_grad.shape[0]
    wq_wide = wq_grad.shape[1]
    wq_rows, wo_rows = width // rings, wo_grad.shape[0] // rings
    tokens = first_part.shape[0] // shards
    mine = wq_rows // shards
    depth, wide = units.shape
    late_rows = width // 128 + 8
    hbm = pl.BlockSpec(memory_space=pl.ANY)
    vmem = pl.BlockSpec(memory_space=pltpu.VMEM)
    dma = pltpu.SemaphoreType.DMA
    return pl.pallas_call(
        functools.partial(reduce_kernel, planes, across, shards),
        in_specs=[hbm] * 3 + [vmem] + [hbm] * 3 + [vmem] * 3 + [hbm] * 5,
        out_specs=[vmem] * 8 + [hbm] * 3,
        out_shape=[
            jax.ShapeDtypeStruct((mine, query_columns), F32),
            jax.ShapeDtypeStruct((mine, key_columns), F32),
            jax.ShapeDtypeStruct((mine, key_columns), F32),
            jax.ShapeDtypeStruct((wo_rows, width), F32),
            jax.ShapeDtypeStruct((tokens, width), BF16),
            jax.ShapeDtypeStruct((tokens, width), F32),
            jax.ShapeDtypeStruct(early.shape[1:], F32),
            jax.ShapeDtypeStruct((late_rows, 128), F32),
            jax.ShapeDtypeStruct((width, wide), F32),
            jax.ShapeDtypeStruct((width, wide), F32),
            jax.ShapeDtypeStruct((wide, width), F32),
        ],
        scratch_shapes=[
            pltpu.VMEM((planes, across, wq_rows, wq_wide), BF16),
            pltpu.VMEM((planes, across, wo_rows, width), BF16),
            pltpu.VMEM((planes, wq_rows, wq_wide), BF16),
            pltpu.VMEM((planes, wo_rows, width), BF16),
            pltpu.VMEM((planes + 1, wq_rows, wq_wide), BF16),
            pltpu.VMEM((planes + 1, wo_rows, width), BF16),
            pltpu.VMEM((wq_rows, wq_wide), F32),
            pltpu.VMEM((wo_rows, width), F32),
            pltpu.VMEM((wq_rows, wq_wide), BF16),
            pltpu.VMEM((wo_rows, width), BF16),
            pltpu.VMEM((shards, mine, wq_wide), BF16),
            pltpu.VMEM((wo_rows, width), BF16),
            pltpu.VMEM((shards, tokens, width), BF16),
            pltpu.VMEM(early.shape, F32),
            pltpu.VMEM((late_rows, 128), F32),
            pltpu.VMEM((everyone, late_rows, 128), F32),
            pltpu.VMEM((tokens, width), F32),
            pltpu.VMEM((tokens, width), F32),
            pltpu.VMEM((depth, wide), BF16),
            pltpu.VMEM((wide, depth), BF16),
            pltpu.VMEM((2, depth, 256), BF16),
            pltpu.VMEM((2, 256, wide), F32),
            pltpu.VMEM((2, wide, 256), F32),
            dma((2, planes)), dma((2, planes)), dma((2, planes)), dma((2, planes + 1)), dma((shards,)), dma((shards,)),
            dma, dma, dma((shards,)), dma((shards,)), dma, dma, dma, dma, dma((2,)), dma, dma((2,)), dma((2,)),
        ],
        compiler_params=pltpu.CompilerParams(vmem_limit_bytes=VMEM_LIMIT, collective_id=3, has_side_effects=True),
        cost_estimate=pl.CostEstimate(flops=70 * 10**9, bytes_accessed=40 * 10**6, transcendentals=0),
    )(
        wq_grad, wo_grad, first_part, hidden, middle, expert_sum, middle_grad, scale, early, shared, rows_in, gate_grad,
        up_grad, units, pair_grad,
    )


def expert_kernel(
    planes, across, shards, capacity,
    own_ref, share_ref, slots_ref, my_slots_ref, gate_ref, up_ref, down_ref, small_ref, top_hbm,
    middle_hbm, cotangent_hbm, rows_hbm, back_hbm, weighted_hbm, units_hbm, gate_grad_hbm, up_grad_hbm, pair_grad_hbm, row_grad_ref, low_grad_hbm, logit_grad_ref, gain_grad_ref,
    share_grad_ref, middle, plane_rows, plane_shares, share_in, share_back, share_home, stage, chosen, rows, top, units,
    gate_grad, up_grad, columns, partial_in,
    line_send, line_recv, plane_share_send, plane_share_recv, out_send, out_recv, out_share_send, out_share_recv,
    back_send, back_recv, back_share_send, back_share_recv, sum_send, sum_recv, sum_share_send, sum_share_recv,
    load_sem, top_sem, store_sem, middle_sem,
):
    z, x, w = lax.axis_index("z"), lax.axis_index("x"), lax.axis_index("w")
    in_plane = across * shards
    experts = planes * in_plane
    me = x * shards + w
    tokens, width = own_ref.shape
    count = in_plane * capacity
    half = count // 2
    per_half = in_plane // 2
    chunk = 512

    def place(index):
        return (z, index // shards, index % shards)

    def order(step):
        return line_order(z, planes, step)

    inner = ((z > 0) & (z < planes - 1)).astype(jnp.int32)
    first_back = 2 - (z == 1).astype(jnp.int32)
    second_back = 3 - inner * first_back
    third_back = 1 + 2 * inner
    greet_plane_and_line(planes, across, shards)

    def line_up(block, hop):
        return remote(
            plane_rows.at[block], plane_rows.at[block], line_send.at[0, hop], line_recv.at[0, hop], (z + 1, x, w)
        )

    def line_down(block, hop):
        return remote(
            plane_rows.at[block], plane_rows.at[block], line_send.at[1, hop], line_recv.at[1, hop], (z - 1, x, w)
        )

    middle_load = pltpu.make_async_copy(middle_hbm, middle, middle_sem)
    middle_load.start()
    plane_rows[z] = own_ref[...]

    @pl.when(z + 1 < planes)
    def _():
        line_up(z, 1).start()

    @pl.when(z > 0)
    def _():
        line_down(z, 1).start()

    def plane_share_copy(other):
        return remote(
            share_ref.at[pl.ds(other * in_plane, in_plane)], plane_shares.at[z],
            plane_share_send.at[other], plane_share_recv.at[z], (other, x, w),
        )

    @pl.loop(1, planes)
    def _(offset):
        plane_share_copy((z + offset) % planes).start()

    plane_shares[z] = share_ref[pl.ds(z * in_plane, in_plane)]

    def slice_of(index):
        return pl.ds(pl.multiple_of(index * capacity, 16), capacity)

    def out_copy(step, block, index):
        return remote(
            stage.at[step, slice_of(index)], rows_hbm.at[block, slice_of(me)],
            out_send.at[step], out_recv.at[step], place(index),
        )

    def out_share_copy(step, block, index):
        return remote(
            plane_shares.at[block, index], share_in.at[block, me],
            out_share_send.at[step], out_share_recv.at[step], place(index),
        )

    def back_copy(step, block, index):
        return remote(
            stage.at[step, slice_of(index)], back_hbm.at[block, slice_of(me)],
            back_send.at[step], back_recv.at[step], place(index),
        )

    def back_share_copy(step, block, index):
        return remote(
            share_back.at[block, index], share_home.at[block, me],
            back_share_send.at[step], back_share_recv.at[step], place(index),
        )

    def start_back(step, block):
        @pl.loop(1, in_plane)
        def _(offset):
            index = (me + offset) % in_plane
            back_copy(step, block, index).start()
            back_share_copy(step, block, index).start()

        pltpu.make_async_copy(stage.at[step, slice_of(me)], back_hbm.at[block, slice_of(me)], back_recv.at[step]).start()
        pltpu.make_async_copy(share_back.at[block, me], share_home.at[block, me], back_share_recv.at[step]).start()

    slot_ids = lax.broadcasted_iota(jnp.int32, (capacity, tokens), 0)

    def pack_step(step):
        block, _, _ = order(step)

        @pl.when(step > 0)
        def _():
            @pl.when(z - step >= 0)
            def _():
                wait_bytes(plane_rows.at[0], line_recv.at[0, step])

                @pl.when(z + 1 < planes)
                def _():
                    line_up(z - step, step + 1).start()

            @pl.when(z + step < planes)
            def _():
                wait_bytes(plane_rows.at[0], line_recv.at[1, step])

                @pl.when(z > 0)
                def _():
                    line_down(z + step, step + 1).start()

            wait_bytes(plane_shares.at[block], plane_share_recv.at[block])

        @pl.loop(0, in_plane)
        def _(index):
            slots = slots_ref[block * in_plane + index]
            chosen[step, slice_of(index), :] = (slot_ids == slots).astype(F32).astype(BF16)

        @pl.loop(0, width // chunk)
        def _(part):
            wide = pl.ds(pl.multiple_of(part * chunk, chunk), chunk)
            stage[step, :, wide] = dot(chosen[step], plane_rows[block, :, wide]).astype(BF16)

    def send_step(step):
        block, _, _ = order(step)

        @pl.loop(1, in_plane)
        def _(offset):
            index = (me + offset) % in_plane
            out_copy(step, block, index).start()
            out_share_copy(step, block, index).start()

        pltpu.make_async_copy(stage.at[step, slice_of(me)], rows_hbm.at[block, slice_of(me)], out_recv.at[step]).start()
        pltpu.make_async_copy(plane_shares.at[block, me], share_in.at[block, me], out_share_recv.at[step]).start()

    def expert_step(step):
        block, _, _ = order(step)

        pltpu.make_async_copy(top_hbm.at[block], top, top_sem).start()
        wait_bytes(rows_hbm.at[block], out_recv.at[step])
        load = pltpu.make_async_copy(rows_hbm.at[block], rows, load_sem)
        load.start()

        @pl.when(step + 1 < planes)
        def _():
            send_step(step + 1)

        wait_bytes(share_in.at[block], out_share_recv.at[step])
        wait_bytes(stage.at[step, pl.ds(0, count - capacity)], out_send.at[step])
        wait_bytes(plane_shares.at[block, pl.ds(0, in_plane - 1)], out_share_send.at[step])

        @pl.loop(0, in_plane)
        def _(index):
            mine = slot_ids == my_slots_ref[block * in_plane + index]
            columns[slice_of(index), :] = jnp.broadcast_to(
                jnp.sum(jnp.where(mine, share_in[block, index], 0.0), axis=1, keepdims=True), (capacity, 128)
            )

        load.wait()
        wait_bytes(top, top_sem)

        @pl.loop(0, 2)
        def _(part):
            here = pl.ds(pl.multiple_of(part * half, 16), half)
            gate = dot(rows[here, :], gate_ref[...])
            up = dot(rows[here, :], up_ref[...])
            sigmoid = 1.0 / (1.0 + jnp.exp(-gate))
            active = gate * sigmoid
            hidden = (active * up).astype(BF16)
            units[here, :] = hidden
            share = columns[here, 0:1]
            total = jnp.zeros((half, 1), F32)
            for piece in range(width // chunk):
                wide = pl.ds(piece * chunk, chunk)
                pair_out = dot(hidden, down_ref[:, wide]).astype(BF16).astype(F32)
                top_rows = top[here, wide].astype(F32)
                total += jnp.sum(pair_out * top_rows, axis=1, keepdims=True)
                rows[here, wide] = (share * pair_out).astype(BF16)
                top[here, wide] = (share * top_rows).astype(BF16)
            columns[here, :] = jnp.broadcast_to(total, (half, 128))
            hidden_grad = dot_nt(top[here, :], down_ref[...])
            gate_low = (hidden_grad * up * sigmoid * (1.0 + gate * (1.0 - sigmoid))).astype(BF16)
            up_low = (hidden_grad * active).astype(BF16)
            gate_grad[here, :] = gate_low
            up_grad[here, :] = up_low
            for piece in range(width // chunk):
                wide = pl.ds(piece * chunk, chunk)
                stage[step, here, wide] = (dot_nt(gate_low, gate_ref[wide, :]) + dot_nt(up_low, up_ref[wide, :])).astype(BF16)

        @pl.loop(0, in_plane)
        def _(index):
            mine = slot_ids == my_slots_ref[block * in_plane + index]
            values = columns[slice_of(index), 0:1]
            share_back[block, index] = jnp.sum(jnp.where(mine, values, 0.0), axis=0, keepdims=True)

        @pl.when((step == first_back) | (step == second_back))
        def _():
            start_back(step, block)

        stores = [
            pltpu.make_async_copy(units, units_hbm.at[block], store_sem.at[0]),
            pltpu.make_async_copy(gate_grad, gate_grad_hbm.at[block], store_sem.at[1]),
            pltpu.make_async_copy(up_grad, up_grad_hbm.at[block], store_sem.at[2]),
            pltpu.make_async_copy(top, pair_grad_hbm.at[block], store_sem.at[3]),
            pltpu.make_async_copy(rows, weighted_hbm.at[block], store_sem.at[4]),
        ]
        for store in stores:
            store.start()

        for store in stores:
            store.wait()

    @pl.loop(0, planes + 1)
    def _(step):
        @pl.when(step < planes)
        def _():
            pack_step(step)

        @pl.when(step == 0)
        def _():
            send_step(step)

        @pl.when(step > 0)
        def _():
            expert_step(step - 1)

    for hop in range(1, planes):

        @pl.when((z - (hop - 1) >= 0) & (z + 1 < planes))
        def _():
            wait_bytes(plane_rows.at[0], line_send.at[0, hop])

        @pl.when((z + (hop - 1) < planes) & (z > 0))
        def _():
            wait_bytes(plane_rows.at[0], line_send.at[1, hop])

    @pl.loop(1, planes)
    def _(offset):
        wait_bytes(plane_shares.at[0], plane_share_send.at[(z + offset) % planes])

    def wait_back(step):
        wait_bytes(stage.at[step, pl.ds(0, count - capacity)], back_send.at[step])
        wait_bytes(share_back.at[0, pl.ds(0, in_plane - 1)], back_share_send.at[step])

    def sum_copy(block):
        up = (block > z).astype(jnp.int32)
        relayed = (jnp.abs(block - z) == planes - 1).astype(jnp.int32)
        goal = block + relayed * (1 - 2 * up) * (planes - 2)
        slot = z + relayed * (goal - z)
        return remote(plane_rows.at[block], partial_in.at[slot], sum_send.at[block], sum_recv.at[slot], (goal, x, w))

    def sum_share_copy(block):
        return remote(
            share_home.at[block], share_grad_ref.at[pl.ds(z * in_plane, in_plane)],
            sum_share_send.at[block], sum_share_recv.at[z], (block, x, w),
        )

    @pl.loop(0, planes)
    def _(turn):
        step = jnp.where(turn == 0, first_back, jnp.where(turn == 1, second_back, jnp.where(turn == 2, third_back, 0)))
        block, _, _ = order(step)
        wait_bytes(back_hbm.at[block], back_recv.at[step])
        load = pltpu.make_async_copy(back_hbm.at[block], rows, load_sem)
        load.start()
        wait_bytes(share_home.at[block], back_share_recv.at[step])
        load.wait()

        @pl.when(step > 0)
        def _():
            sum_share_copy(block).start()

            merges = (inner == 1) & (jnp.abs(block - z) == 2)

            @pl.when(merges)
            def _():
                wait_bytes(partial_in.at[z], sum_recv.at[z])

            @pl.loop(0, width // chunk)
            def _(part):
                wide = pl.ds(pl.multiple_of(part * chunk, chunk), chunk)
                summed = dot_tn(chosen[step], rows[:, wide])

                @pl.when(merges)
                def _():
                    plane_rows[block, :, wide] = (summed + partial_in[z, :, wide].astype(F32)).astype(BF16)

                @pl.when(jnp.logical_not(merges))
                def _():
                    plane_rows[block, :, wide] = summed.astype(BF16)

            sum_copy(block).start()

        @pl.when(step == 0)
        def _():
            share_grad_ref[pl.ds(z * in_plane, in_plane)] = share_home[z]

            @pl.loop(0, width // chunk)
            def _(part):
                wide = pl.ds(pl.multiple_of(part * chunk, chunk), chunk)
                row_grad_ref[:, wide] = dot_tn(chosen[0], rows[:, wide])

        @pl.when(turn == 0)
        def _():
            wait_back(second_back)
            start_back(third_back, order(third_back)[0])

        @pl.when(turn == 1)
        def _():
            wait_back(third_back)
            start_back(0, z)

    cotangent_load = pltpu.make_async_copy(cotangent_hbm, rows.at[pl.ds(0, tokens)], load_sem)
    cotangent_load.start()

    @pl.loop(1, planes)
    def _(offset):
        other = (z + offset) % planes
        wait_bytes(share_home.at[other], sum_share_recv.at[other])

        @pl.when(jnp.abs(other - z) < planes - 1)
        def _():
            wait_bytes(partial_in.at[other], sum_recv.at[other])

            @pl.loop(0, width // chunk)
            def _(part):
                wide = pl.ds(pl.multiple_of(part * chunk, chunk), chunk)
                row_grad_ref[:, wide] += partial_in[other, :, wide].astype(F32)

    @pl.loop(1, planes)
    def _(offset):
        other = (z + offset) % planes
        wait_bytes(plane_rows.at[other], sum_send.at[other])
        wait_bytes(share_home.at[other], sum_share_send.at[other])

    cotangent_load.wait()
    middle_load.wait()
    depth = width // shards
    share_grad = jnp.concatenate([share_grad_ref[index] for index in range(experts)], axis=0)
    shares = jnp.concatenate([share_ref[index] for index in range(experts)], axis=0)
    center = jnp.sum(shares * share_grad, axis=0, keepdims=True)
    logit_grad_ref[...] = (shares * (share_grad - center)).astype(BF16)
    for part in range(shards):
        wide = slice(part * depth, (part + 1) * depth)
        row_grad_ref[:, wide] += dot_tn(logit_grad_ref[...], small_ref[part, :experts, :].astype(BF16))
    ffn_row = jnp.concatenate([small_ref[part, experts : experts + 1, :] for part in range(shards)], axis=1)

    def finish_rows(piece, gain_grad):
        at = pl.ds(pl.multiple_of(piece * 64, 64), 64)
        normed, scaling = norm_forward(middle[at, :])
        second_grad = row_grad_ref[at, :]
        grad = rows[at, :].astype(F32) + norm_backward(second_grad * ffn_row, normed, scaling)
        row_grad_ref[at, :] = grad
        rows[pl.ds(pl.multiple_of(tokens + piece * 64, 64), 64), :] = grad.astype(BF16)
        return gain_grad + jnp.sum(second_grad * normed, axis=0, keepdims=True)

    gain_grad_ref[...] = lax.fori_loop(0, tokens // 64, finish_rows, jnp.zeros((1, width), F32))
    low_store = pltpu.make_async_copy(rows.at[pl.ds(tokens, tokens)], low_grad_hbm, middle_sem)
    low_store.start()
    wait_back(0)
    wait_back(first_back)
    low_store.wait()


def run_experts(planes, across, shards, capacity, own, shares, slots, my_slots, w_gate, w_up, w_down, small_all, top_rows, middle, cotangent):
    tokens, width = own.shape
    in_plane = across * shards
    count = in_plane * capacity
    units = w_gate.shape[1]
    experts = planes * in_plane
    hbm = pl.BlockSpec(memory_space=pl.ANY)
    vmem = pl.BlockSpec(memory_space=pltpu.VMEM)
    dma = pltpu.SemaphoreType.DMA
    flops = 12 * planes * count * width * units
    return pl.pallas_call(
        functools.partial(expert_kernel, planes, across, shards, capacity),
        in_specs=[vmem] * 8 + [hbm] * 3,
        out_specs=[hbm] * 7 + [vmem, hbm, vmem, vmem],
        out_shape=[
            jax.ShapeDtypeStruct((planes, count, width), BF16),
            jax.ShapeDtypeStruct((planes, count, width), BF16),
            jax.ShapeDtypeStruct((planes, count, width), BF16),
            jax.ShapeDtypeStruct((planes, count, units), BF16),
            jax.ShapeDtypeStruct((planes, count, units), BF16),
            jax.ShapeDtypeStruct((planes, count, units), BF16),
            jax.ShapeDtypeStruct((planes, count, width), BF16),
            jax.ShapeDtypeStruct((tokens, width), F32),
            jax.ShapeDtypeStruct((tokens, width), BF16),
            jax.ShapeDtypeStruct((experts, tokens), BF16),
            jax.ShapeDtypeStruct((1, width), F32),
        ],
        scratch_shapes=[
            pltpu.VMEM((experts, 1, tokens), F32),
            pltpu.VMEM((tokens, width), F32),
            pltpu.VMEM((planes, tokens, width), BF16),
            pltpu.VMEM((planes, in_plane, 1, tokens), F32),
            pltpu.VMEM((planes, in_plane, 1, tokens), F32),
            pltpu.VMEM((planes, in_plane, 1, tokens), F32),
            pltpu.VMEM((planes, in_plane, 1, tokens), F32),
            pltpu.VMEM((planes, count, width), BF16),
            pltpu.VMEM((planes, count, tokens), BF16),
            pltpu.VMEM((count, width), BF16),
            pltpu.VMEM((count, width), BF16),
            pltpu.VMEM((count, units), BF16),
            pltpu.VMEM((count, units), BF16),
            pltpu.VMEM((count, units), BF16),
            pltpu.VMEM((count, 128), F32),
            pltpu.VMEM((planes, tokens, width), BF16),
            dma((2, planes + 1)), dma((2, planes + 1)), dma((planes,)), dma((planes,)),
            dma((planes,)), dma((planes,)), dma((planes,)), dma((planes,)),
            dma((planes,)), dma((planes,)), dma((planes,)), dma((planes,)),
            dma((planes,)), dma((planes,)), dma((planes,)), dma((planes,)),
            dma, dma, dma((5,)), dma,
        ],
        compiler_params=pltpu.CompilerParams(vmem_limit_bytes=VMEM_LIMIT, collective_id=1, has_side_effects=True),
        cost_estimate=pl.CostEstimate(flops=4 * flops, bytes_accessed=100 * 10**6, transcendentals=2 * 10**6),
    )(own, shares, slots, my_slots, w_gate, w_up, w_down, small_all, top_rows, middle, cotangent)


def local(
    hidden_in, attn_gain, w_query, key_projection, value_projection, query_gain, key_gain, w_output, ffn_gain, w_router,
    routes, w_gate, w_up, w_down, cotangent,
):
    tokens_here, width = hidden_in.shape
    head_size = query_gain.shape[0]
    top_count = routes.shape[1]
    planes, across, shards = lax.axis_size("z"), lax.axis_size("x"), lax.axis_size("w")
    rings = planes * across
    device_count = rings * shards
    in_plane = across * shards
    experts = device_count
    capacity = 5 * tokens_here * top_count // (4 * experts)
    seq_length = tokens_here * shards

    cosine, sine = rope_tables(seq_length, head_size)
    query_gain_row, key_gain_row = query_gain[None, :], key_gain[None, :]

    capacity = -(-capacity // 16) * 16
    small = jnp.concatenate([w_router.T, ffn_gain[None, :], attn_gain[None, :]], axis=0).astype(F32)
    small = jnp.pad(small, ((0, -small.shape[0] % 8), (0, 0)))
    (
        first_input, query_raw, key_raw, value, attended, middle, slots_flat, my_slots, shares, squares, second_input,
        small_all, weights, top_rows,
    ) = run_forward(
        planes, across, shards, capacity, hidden_in, small, routes.T, cotangent, w_query, key_projection,
        value_projection, query_gain_row, key_gain_row, cosine, sine, w_output,
    )
    (
        rows_in, _, weighted, hidden_units, gate_grad, up_grad, pair_grad, middle_grad, low_grad, logit_grad, ffn_gain_grad,
    ) = run_experts(
        planes, across, shards, capacity, second_input, shares, slots_flat, my_slots, w_gate[0], w_up[0], w_down[0],
        small_all, top_rows, middle, cotangent,
    )
    units = w_gate.shape[2]
    router_grad = dot_tn(second_input, logit_grad.T)
    attn_scale = small_all[:, experts + 1, :].reshape(1, width)
    wo_grad, wq_grad, first_part, query_gain_grad, key_gain_grad, _, expert_sum = run_backward(
        planes, across, shards, capacity, low_grad, w_output, attended, query_raw, key_raw, value,
        first_input, weights, query_gain_row, key_gain_row, cosine, sine, slots_flat, weighted,
    )
    mine = width // device_count
    early = jnp.concatenate(
        [router_grad.reshape(device_count, mine * experts), ffn_gain_grad.reshape(device_count, mine)], axis=1
    )
    early = jnp.pad(early, ((0, 0), (0, -early.shape[1] % 1024))).reshape(device_count, -1, 128)
    shared = squares + jnp.concatenate(
        [query_gain_grad[0:1], key_gain_grad[0:1], jnp.zeros((6, head_size), F32)], axis=0
    )
    (
        sum_query, sum_key, sum_value, sum_output, hidden_out, grad_in, early_total, late_total, grad_gate, grad_up, grad_down,
    ) = run_reduce(
        planes, across, shards, wq_grad, wo_grad, first_part, hidden_in, middle, expert_sum, middle_grad, attn_scale, early,
        shared, rows_in.reshape(-1, width), gate_grad.reshape(-1, units), up_grad.reshape(-1, units),
        hidden_units.reshape(-1, units), pair_grad.reshape(-1, width), w_query.shape[1], key_projection.shape[1],
    )
    early_total = early_total.reshape(-1)
    sum_router = early_total[: mine * experts].reshape(mine, experts)
    sum_ffn = early_total[mine * experts : mine * (experts + 1)]
    linear = (lax.axis_index("z") * across + lax.axis_index("x")) * shards + lax.axis_index("w")
    sum_attn = lax.dynamic_slice_in_dim(late_total[: width // 128].reshape(-1), linear * mine, mine)
    late_total = late_total[width // 128 :]
    totals = jnp.concatenate([late_total[0], late_total[1], late_total[2, :4]])
    root_mean_squares = jnp.sqrt(totals[2 * head_size :] / (tokens_here * device_count * width))
    return (
        hidden_out,
        grad_in,
        sum_attn,
        sum_query,
        sum_key,
        sum_value,
        totals[:head_size],
        totals[head_size : 2 * head_size],
        sum_output,
        sum_ffn,
        sum_router,
        grad_gate[None],
        grad_up[None],
        grad_down[None],
        root_mean_squares,
    )


def solution(mesh):
    rings, shards = mesh.shape["ep"], mesh.shape["ws"]
    planes = 4 if rings % 4 == 0 else 1
    fine = Mesh(mesh.devices.reshape(planes, rings // planes, shards), ("z", "x", "w"))
    every = ("z", "x", "w")
    rows, deep = P(every, None), P(every, None, None)
    return jax.shard_map(
        local,
        mesh=fine,
        in_specs=(
            rows, P("w"), P("w", None), P("w", None), P("w", None), P(), P(), P("w", None), P("w"), P("w", None),
            rows, deep, deep, deep, rows,
        ),
        out_specs=(
            rows, rows, P(every), rows, rows, rows, P(), P(), rows, P(every), rows, deep, deep, deep, P(),
        ),
        check_vma=False,
    )
```

```python
import functools

import jax
import jax.numpy as jnp
import numpy as np
from jax import lax
from jax.experimental import pallas as pl
from jax.experimental.pallas import tpu as pltpu
from jax.sharding import Mesh
from jax.sharding import PartitionSpec as P

BLOCK = 256
EPS = 1e-06
ROPE_BASE = 1000000.0
F32 = jnp.float32
BF16 = jnp.bfloat16
VMEM_LIMIT = 65024 * 1024


def dot(left, right):
    return jnp.dot(left, right, preferred_element_type=F32)


def dot_tn(left, right):
    return lax.dot_general(left, right, (((0,), (0,)), ((), ())), preferred_element_type=F32)


def dot_nt(left, right):
    return lax.dot_general(left, right, (((1,), (1,)), ((), ())), preferred_element_type=F32)


def rope_tables(seq_length, head_size):
    indices = np.arange(head_size // 2, dtype=np.float32)
    frequency = (np.float32(ROPE_BASE) ** (np.float32(-2.0) * indices / np.float32(head_size))).astype(np.float32)
    angles = np.arange(seq_length, dtype=np.float32)[:, None] * frequency[None, :]
    cosine, sine = np.cos(angles), np.sin(angles)
    return np.concatenate([cosine, cosine], axis=1), np.concatenate([-sine, sine], axis=1)


def norm_forward(values):
    scaling = lax.rsqrt(jnp.mean(values * values, axis=-1, keepdims=True) + EPS)
    return values * scaling, scaling


def norm_backward(grad_normed, normed, scaling):
    return scaling * (grad_normed - normed * jnp.mean(grad_normed * normed, axis=-1, keepdims=True))


def half_turn(values):
    return pltpu.roll(values, values.shape[-1] // 2, 1)


def rotate(values, cosine, signed_sine):
    return values * cosine + half_turn(values) * signed_sine


def unrotate(grads, cosine, signed_sine):
    return grads * cosine - half_turn(grads) * signed_sine


MESH = pl.DeviceIdType.MESH


def remote(source, target, send, recv, device):
    return pltpu.make_async_remote_copy(
        src_ref=source, dst_ref=target, send_sem=send, recv_sem=recv, device_id=device, device_id_type=MESH
    )


def wait_bytes(ref, sem):
    pltpu.make_async_copy(ref, ref, sem).wait()


def line_order(z, planes, step):
    low = jnp.minimum(z, planes - 1 - z)
    paired = (step <= 2 * low).astype(jnp.int32)
    hop = paired * ((step + 1) // 2) + (1 - paired) * (step - low)
    longer = (z > planes - 1 - z).astype(jnp.int32)
    below = paired * (step % 2) + (1 - paired) * longer
    return z + hop - 2 * below * hop, hop, below


def greet_plane_and_line(planes, across, shards):
    z, x, w = lax.axis_index("z"), lax.axis_index("x"), lax.axis_index("w")
    in_plane = across * shards
    me = x * shards + w
    barrier = pltpu.get_barrier_semaphore()

    @pl.loop(1, in_plane)
    def _(offset):
        index = (me + offset) % in_plane
        pl.semaphore_signal(barrier, inc=1, device_id=(z, index // shards, index % shards), device_id_type=MESH)

    @pl.loop(1, planes)
    def _(offset):
        pl.semaphore_signal(barrier, inc=1, device_id=((z + offset) % planes, x, w), device_id_type=MESH)

    pl.semaphore_wait(barrier, in_plane + planes - 2)


def attention_forward(
    planes, across, shards, capacity, heads_a_step,
    own_ref, small_ref, routes_ref, top_ref, wq_hbm, wk_hbm, wv_hbm, query_gain_ref, key_gain_ref, cosine_ref, sine_ref, wo_ref,
    input_ref, query_raw_ref, key_raw_ref, value_ref, attended_ref, middle_ref, slots_ref, my_slots_ref, shares_ref, squares_ref,
    second_hbm, small_hbm,
    weights_hbm, top_rows_hbm,
    hidden, small_in, weights, key_rot_ref, routes_in, far_slots, plane_rows, stage, chosen, pair_out, far_out,
    gather_send, gather_recv, small_send, small_recv, weight_send, weight_recv, route_send, route_recv, plane_route_send,
    plane_route_recv, far_send, far_recv,
    line_send, line_recv, top_send, top_recv, pair_send, pair_recv, store_sem, small_sem, second_sem,
):
    step = pl.program_id(0)
    head_size = cosine_ref.shape[1]
    last = wo_ref.shape[0] // (heads_a_step * head_size)
    seq_length = cosine_ref.shape[0]
    blocks = seq_length // BLOCK
    factor = head_size ** (-0.5)
    z, x, w = lax.axis_index("z"), lax.axis_index("x"), lax.axis_index("w")
    in_plane = across * shards
    tokens, width = own_ref.shape
    me = x * shards + w
    depth = width // shards
    experts = planes * in_plane
    wide = heads_a_step * head_size
    chunk = 512
    targets = in_plane // 2
    pair, core = w // 2, w % 2
    sibling, opposite, other = pair * 2 + 1 - core, (1 - pair) * 2 + core, (1 - pair) * 2 + 1 - core

    def slice_of(index):
        return pl.ds(pl.multiple_of(index * capacity, 16), capacity)

    def tokens_of(index):
        return pl.ds(pl.multiple_of(index * tokens, tokens), tokens)

    def gather_copy(kind, owner, target):
        return remote(
            hidden.at[tokens_of(owner)], hidden.at[tokens_of(owner)], gather_send.at[kind], gather_recv.at[kind],
            (z, x, target),
        )

    def small_copy(offset):
        return remote(small_ref, small_in.at[w], small_send.at[offset], small_recv.at[w], (z, x, (w + offset) % shards))

    def columns_at(start, size):
        return pl.ds(pl.multiple_of(start, 128), size)

    my_depth = pl.ds(pl.multiple_of(w * depth, 16), depth)
    query_wide = last * wide

    def weight_pieces(piece, target):
        if piece is None:
            key_at, value_at = columns_at(target * head_size, head_size), columns_at(target * head_size, head_size)
            return [
                (wk_hbm.at[:, key_at], weights.at[my_depth, columns_at(last * wide, head_size)], last),
                (wv_hbm.at[:, value_at], weights.at[my_depth, columns_at(last * wide + head_size, head_size)], last),
            ]
        return [
            (
                wq_hbm.at[:, columns_at(target * query_wide + piece * wide, wide)],
                weights.at[my_depth, columns_at(piece * wide, wide)], piece,
            )
        ]

    def start_weights(piece):
        @pl.loop(1, shards)
        def _(offset):
            for source, goal, sem in weight_pieces(piece, (w + offset) % shards):
                remote(source, goal, weight_send.at[sem], weight_recv.at[sem], (z, x, (w + offset) % shards)).start()

        for source, goal, sem in weight_pieces(piece, w):
            pltpu.make_async_copy(source, goal, weight_recv.at[sem]).start()

    def wait_weights(piece):
        whole_piece = weights.at[:, columns_at(piece * wide, wide)]
        wait_bytes(whole_piece, weight_recv.at[piece])

    def half_of(half):
        return pl.ds(half * (width // 2), width // 2)

    def line_copy(column, block, hop, direction, half):
        rows = plane_rows.at[column, block, :, half_of(half)]
        return remote(
            rows, rows, line_send.at[column, direction, hop, half], line_recv.at[column, direction, hop, half],
            (z + 1 - 2 * direction, x, w),
        )

    def start_line(column, block, hop, upward, downward):
        for half in range(2):

            @pl.when(upward & (z + 1 < planes))
            def _():
                line_copy(column, block, hop, 0, half).start()

            @pl.when(downward & (z > 0))
            def _():
                line_copy(column, block, hop, 1, half).start()

    def relay_half(column, hop, half):
        @pl.when(z - hop >= 0)
        def _():
            wait_bytes(plane_rows.at[column, 0, :, half_of(half)], line_recv.at[column, 0, hop, half])

            @pl.when(z + 1 < planes)
            def _():
                line_copy(column, z - hop, hop + 1, 0, half).start()

        @pl.when(z + hop < planes)
        def _():
            wait_bytes(plane_rows.at[column, 0, :, half_of(half)], line_recv.at[column, 1, hop, half])

            @pl.when(z > 0)
            def _():
                line_copy(column, z + hop, hop + 1, 1, half).start()

    def relay(column, hop):
        for half in range(2):
            relay_half(column, hop, half)

    expert_of = z * in_plane + lax.broadcasted_iota(jnp.int32, (in_plane, tokens), 0)
    earlier = (
        lax.broadcasted_iota(jnp.int32, (tokens, tokens), 0) < lax.broadcasted_iota(jnp.int32, (tokens, tokens), 1)
    ).astype(F32).astype(BF16)
    slot_ids = lax.broadcasted_iota(jnp.int32, (capacity, tokens), 0)

    def fill_slots(column, table):
        @pl.loop(0, planes)
        def _(block):
            hits = jnp.zeros((in_plane, tokens), F32)
            for k in range(routes_ref.shape[0]):
                hits += (routes_in[column, block, k : k + 1, :] == expert_of).astype(F32)
            ranks = dot(hits.astype(BF16), earlier).astype(jnp.int32)
            slots = jnp.where(hits > 0.0, ranks, -1)
            for index in range(in_plane):
                table[block * in_plane + index] = slots[index : index + 1, :]

    def pack(column, turn, table, halves=(0, 1)):
        block, _, _ = line_order(z, planes, turn)

        def index_of(target):
            return (target // 2) * shards + pair * 2 + target % 2

        for target in range(targets):
            slots = table[block * in_plane + index_of(target)]
            chosen[target * capacity : (target + 1) * capacity, :] = (slot_ids == slots).astype(F32).astype(BF16)

        wide_at = pl.ds(halves[0] * (width // 2), len(halves) * (width // 2))

        @pl.loop(halves[0] * (width // 2) // chunk, (halves[-1] + 1) * (width // 2) // chunk)
        def _(part):
            here = pl.ds(pl.multiple_of(part * chunk, chunk), chunk)
            stage[column, turn, :, here] = dot(chosen[...], plane_rows[column, block, :, here]).astype(BF16)

        source = x * shards + (w if column == 0 else opposite)
        mine = x * 2 + core

        @pl.loop(1, targets)
        def _(offset):
            target = (mine + offset) % targets
            remote(
                stage.at[column, turn, slice_of(target), wide_at], top_rows_hbm.at[block, slice_of(source), wide_at],
                top_send.at[column, turn], top_recv.at[block], (z, target // 2, pair * 2 + target % 2),
            ).start()

        pltpu.make_async_copy(
            stage.at[column, turn, slice_of(mine), wide_at], top_rows_hbm.at[block, slice_of(source), wide_at],
            top_recv.at[block],
        ).start()

    def route_copy(offset):
        return remote(
            routes_ref, routes_in.at[me, z], route_send.at[offset], route_recv.at[z], ((z + offset) % planes, x, w)
        )

    far_top = remote(top_ref, plane_rows.at[1, z], far_send, far_recv, (z, x, opposite))
    opposite_me = x * shards + opposite

    def plane_route_copy(index):
        return remote(
            routes_in.at[me], routes_in.at[me], plane_route_send, plane_route_recv.at[me],
            (z, index // shards, index % shards),
        )

    def fill_my_slots():
        my_expert = z * in_plane + me

        @pl.loop(0, planes)
        def _(block):
            hits = jnp.concatenate(
                [
                    jnp.max((routes_in[index, block] == my_expert).astype(F32), axis=0, keepdims=True)
                    for index in range(in_plane)
                ],
                axis=0,
            )
            ranks = dot(hits.astype(BF16), earlier).astype(jnp.int32)
            slots = jnp.where(hits > 0.0, ranks, -1)
            for index in range(in_plane):
                my_slots_ref[block * in_plane + index] = slots[index : index + 1, :]

    @pl.when(step == 0)
    def _():
        greet_plane_and_line(planes, across, shards)
        far_top.start()

        @pl.loop(1, planes)
        def _(offset):
            route_copy(offset).start()

        @pl.loop(1, shards)
        def _(offset):
            small_copy(offset).start()

        plane_rows[0, z] = top_ref[...]
        start_line(0, z, 1, True, True)
        hidden[tokens_of(w), :] = own_ref[...]
        gather_copy(0, w, sibling).start()
        small_in[w] = small_ref[...]
        routes_in[me, z] = routes_ref[...]

        @pl.loop(1, planes)
        def _(offset):
            source = (z + offset) % planes
            wait_bytes(routes_in.at[me, source], route_recv.at[source])

        @pl.loop(1, in_plane)
        def _(offset):
            plane_route_copy((me + offset) % in_plane).start()

        fill_slots(me, slots_ref)
        pack(0, 0, slots_ref)
        gather_copy(1, w, opposite).start()
        relay(0, 1)
        wait_bytes(plane_rows.at[1, z], far_recv)
        start_line(1, z, 1, True, True)
        start_weights(None)
        wait_bytes(routes_in.at[opposite_me], plane_route_recv.at[opposite_me])
        fill_slots(opposite_me, far_slots)
        pack(1, 0, far_slots)
        wait_bytes(hidden.at[tokens_of(opposite)], gather_recv.at[1])
        gather_copy(2, opposite, sibling).start()
        start_weights(0)
        pack(0, 1, slots_ref)

        @pl.loop(1, shards)
        def _(offset):
            source = (w + offset) % shards
            wait_bytes(small_in.at[source], small_recv.at[source])

        wait_bytes(hidden.at[tokens_of(sibling)], gather_recv.at[0])
        wait_bytes(hidden.at[tokens_of(other)], gather_recv.at[2])
        for block in range(blocks):
            rows = pl.ds(block * BLOCK, BLOCK)
            normed, _ = norm_forward(hidden[rows, :].astype(F32))
            for part in range(shards):
                here = slice(part * depth, (part + 1) * depth)
                input_ref[rows, here] = (normed[:, here] * small_in[part, experts + 1 : experts + 2, :]).astype(BF16)
        relay(0, 2)
        start_weights(1)
        pack(0, 2, slots_ref)
        wait_weights(last)
        for block in range(blocks):
            rows = pl.ds(block * BLOCK, BLOCK)
            key_value = dot(input_ref[rows, :], weights[:, columns_at(last * wide, wide)])
            key_raw = key_value[:, :head_size]
            key_raw_ref[rows, :] = key_raw
            value_ref[rows, :] = key_value[:, head_size:].astype(BF16)
            key_normed, _ = norm_forward(key_raw)
            key_rot_ref[rows, :] = rotate(
                key_normed * key_gain_ref[...], cosine_ref[rows, :], sine_ref[rows, :]
            ).astype(BF16)
        relay(1, 1)
        pack(1, 1, far_slots)

    for piece in range(2, last):

        @pl.when(step == piece - 2)
        def _():
            wait_weights(piece - 2)
            if piece == last - 1:
                for kind in range(3):
                    wait_bytes(hidden.at[tokens_of(w)], gather_send.at[kind])
            start_weights(piece)

    @pl.when((step >= last - 2) & (step < last))
    def _():
        wait_weights(step)

    @pl.when(step < last)
    def _():
        here = columns_at(step * wide, wide)
        for block in range(blocks):
            rows = pl.ds(block * BLOCK, BLOCK)
            seen = pl.ds(0, (block + 1) * BLOCK)
            query_raw = dot(input_ref[rows, :], weights[:, here])
            query_raw_ref[rows, :] = query_raw

            @pl.loop(0, heads_a_step)
            def _(head):
                query_normed, _ = norm_forward(query_raw_ref[rows, columns_at(head * head_size, head_size)])
                query_rot = rotate(
                    query_normed * query_gain_ref[...], cosine_ref[rows, :], sine_ref[rows, :]
                ).astype(BF16)
                scores = dot_nt(query_rot, key_rot_ref[seen, :]) * factor
                exponent = jnp.exp(scores - jnp.max(scores, axis=-1, keepdims=True))
                probs = (exponent / jnp.sum(exponent, axis=-1, keepdims=True)).astype(BF16)
                attended_ref[rows, columns_at(step * wide + head * head_size, head_size)] = dot(
                    probs, value_ref[seen, :]
                ).astype(BF16)

    @pl.when(step == 1)
    def _():
        relay(0, 3)
        pack(0, 3, slots_ref)

    @pl.when(step == 2)
    def _():
        relay(1, 2)
        pack(1, 2, far_slots)

    def project(owner, goal, added):
        rows = tokens_of(owner)

        @pl.loop(0, width // chunk)
        def _(part):
            here = pl.ds(pl.multiple_of(part * chunk, chunk), chunk)
            value = dot(attended_ref[rows, :], wo_ref[:, here])
            if added is not None:
                value += hidden[added, here].astype(F32)
            goal[:, here] = value.astype(goal.dtype)

    def pair_copy(kind):
        at = pl.ds(kind * tokens, tokens)
        return remote(pair_out.at[kind], hidden.at[at], pair_send.at[kind], pair_recv.at[kind], (z, x, sibling))

    far_at = pl.ds(2 * tokens, tokens)
    far_copy = remote(far_out, hidden.at[far_at], pair_send.at[2], pair_recv.at[2], (z, x, opposite))

    @pl.when(step == last)
    def _():
        store = pltpu.make_async_copy(weights, weights_hbm, store_sem)
        store.start()
        small_store = pltpu.make_async_copy(small_in, small_hbm, small_sem)
        small_store.start()
        project(other, pair_out.at[0], None)
        pair_copy(0).start()
        project(sibling, pair_out.at[1], None)
        pair_copy(1).start()
        wait_bytes(hidden.at[pl.ds(0, tokens)], pair_recv.at[0])
        project(opposite, far_out, pl.ds(0, tokens))
        far_copy.start()
        wait_bytes(hidden.at[pl.ds(tokens, tokens)], pair_recv.at[1])
        project(w, middle_ref, pl.ds(tokens, tokens))
        @pl.loop(1, in_plane)
        def _(offset):
            index = (me + offset) % in_plane

            @pl.when(index != opposite_me)
            def _():
                wait_bytes(routes_in.at[index], plane_route_recv.at[index])

        fill_my_slots()
        for half in range(2):
            relay_half(1, 3, half)
            pack(1, 3, far_slots, (half,))
        wait_bytes(hidden.at[far_at], pair_recv.at[2])
        wait_bytes(far_out, pair_send.at[2])
        ffn_row = jnp.concatenate([small_in[part, experts : experts + 1, :] for part in range(shards)], axis=1)

        def finish_rows(piece, carry):
            at = pl.ds(pl.multiple_of(piece * 64, 64), 64)
            far = pl.ds(pl.multiple_of(2 * tokens + piece * 64, 64), 64)
            branch = middle_ref[at, :] + hidden[far, :].astype(F32)
            source = own_ref[at, :].astype(F32)
            middle = source + branch
            middle_ref[at, :] = middle
            normed, _ = norm_forward(middle)
            far_out[at, :] = (normed * ffn_row).astype(BF16)
            return (
                carry[0] + jnp.sum(jnp.sum(source * source, axis=1, keepdims=True), axis=0, keepdims=True),
                carry[1] + jnp.sum(jnp.sum(branch * branch, axis=1, keepdims=True), axis=0, keepdims=True),
            )

        zero = jnp.zeros((1, 1), F32)
        source_square, branch_square = lax.fori_loop(0, tokens // 64, finish_rows, (zero, zero))
        second_store = pltpu.make_async_copy(far_out, second_hbm, second_sem)
        second_store.start()
        lane = lax.broadcasted_iota(jnp.int32, (8, 128), 1)
        row = lax.broadcasted_iota(jnp.int32, (8, 128), 0)
        values = jnp.where(lane == 0, source_square, 0.0) + jnp.where(lane == 1, branch_square, 0.0)
        squares_ref[...] = jnp.where(row == 2, values, 0.0)
        logits = jnp.zeros((experts, tokens), F32)
        for part in range(shards):
            logits += dot_nt(small_in[part, :experts, :].astype(BF16), far_out[:, part * depth : (part + 1) * depth])
        expert_ids = lax.broadcasted_iota(jnp.int32, (experts, tokens), 0)
        hits = jnp.zeros((experts, tokens), F32)
        for k in range(routes_ref.shape[0]):
            hits += (routes_ref[k : k + 1, :] == expert_ids).astype(F32)
        routed = hits > 0.0
        peaks = jnp.max(jnp.where(routed, logits, -jnp.inf), axis=0, keepdims=True)
        shifted = jnp.where(routed, jnp.exp(jnp.where(routed, logits - peaks, 0.0)), 0.0)
        shares = shifted / jnp.sum(shifted, axis=0, keepdims=True)
        for expert in range(experts):
            shares_ref[expert] = shares[expert : expert + 1, :]

        @pl.loop(0, planes)
        def _(block):
            wait_bytes(top_rows_hbm.at[block], top_recv.at[block])
            if targets > 1:
                for column in range(2):
                    wait_bytes(stage.at[column, 0, pl.ds(0, (targets - 1) * capacity)], top_send.at[column, block])

        for kind in range(2):
            wait_bytes(far_out, pair_send.at[kind])

        @pl.loop(1, shards)
        def _(offset):
            wait_bytes(small_in.at[w], small_send.at[offset])

        @pl.loop(1, planes)
        def _(offset):
            wait_bytes(routes_in.at[0, 0], route_send.at[offset])

        wait_bytes(routes_in.at[pl.ds(0, in_plane - 1)], plane_route_send)
        wait_bytes(plane_rows.at[1, 0], far_send)

        @pl.loop(0, last + 1)
        def _(piece):
            wait_bytes(weights.at[pl.ds(0, (shards - 1) * depth), pl.ds(0, wide)], weight_send.at[piece])

        for column in range(2):
            for hop in range(1, planes):

                @pl.when((z - (hop - 1) >= 0) & (z + 1 < planes))
                def _():
                    for half in range(2):
                        wait_bytes(plane_rows.at[0, 0, :, half_of(half)], line_send.at[column, 0, hop, half])

                @pl.when((z + (hop - 1) < planes) & (z > 0))
                def _():
                    for half in range(2):
                        wait_bytes(plane_rows.at[0, 0, :, half_of(half)], line_send.at[column, 1, hop, half])

        store.wait()
        small_store.wait()
        second_store.wait()


def attention_backward(
    planes, across, shards, capacity, heads_a_step,
    own_grad_ref, wo_ref, attended_ref, query_raw_ref, key_raw_ref, value_ref, input_ref, wq_ref,
    query_gain_ref, key_gain_ref, cosine_ref, sine_ref, slots_ref, weighted_hbm,
    wo_grad_ref, wq_grad_ref, first_grad_ref, query_gain_grad_ref, key_gain_grad_ref, returned_hbm, expert_sum_ref,
    total_ref, key_rot_ref, key_grad_ref, value_grad_ref, query_grad_ref, turned_ref, grad_ref,
    rows, chosen, partial_out, partial_in,
    gather_send, gather_recv, back_send, back_recv, sum_send, sum_recv, load_sem,
):
    step = pl.program_id(0)
    last = pl.num_programs(0) - 1
    head_size = cosine_ref.shape[1]
    seq_length = cosine_ref.shape[0]
    blocks = seq_length // BLOCK
    factor = head_size ** (-0.5)
    z, x, w = lax.axis_index("z"), lax.axis_index("x"), lax.axis_index("w")
    in_plane = across * shards
    me = x * shards + w
    tokens, width = own_grad_ref.shape
    count = in_plane * capacity
    chunk = 512
    pair, core = w // 2, w % 2
    sibling, opposite, other = pair * 2 + 1 - core, (1 - pair) * 2 + core, (1 - pair) * 2 + 1 - core

    def slice_of(index):
        return pl.ds(pl.multiple_of(index * capacity, 16), capacity)

    def tokens_of(index):
        return pl.ds(pl.multiple_of(index * tokens, tokens), tokens)

    def gather_copy(kind, owner, target):
        return remote(
            grad_ref.at[tokens_of(owner)], grad_ref.at[tokens_of(owner)], gather_send.at[kind], gather_recv.at[kind],
            (z, x, target),
        )

    def back_copy(block, index):
        return remote(
            weighted_hbm.at[block, slice_of(index)], returned_hbm.at[block, slice_of(me)],
            back_send.at[block], back_recv.at[block], (z, index // shards, index % shards),
        )

    pace = [(1, 0), (2, 1), (3, 2)]

    def start_back(turn, near, far):
        block, _, _ = line_order(z, planes, planes - 1 - turn)

        @pl.loop(1, in_plane)
        def _(offset):
            index = (me + offset) % in_plane
            beside = (index % shards) // 2 == pair

            @pl.when((beside & near) | (jnp.logical_not(beside) & far))
            def _():
                back_copy(block, index).start()

        @pl.when(near)
        def _():
            pltpu.make_async_copy(
                weighted_hbm.at[block, slice_of(me)], returned_hbm.at[block, slice_of(me)], back_recv.at[block]
            ).start()

    def sum_copy(block):
        return remote(partial_out.at[block], partial_in.at[z], sum_send.at[block], sum_recv.at[z], (block, x, w))

    def combine(turn):
        place = planes - 1 - turn
        block, _, _ = line_order(z, planes, place)
        wait_bytes(returned_hbm.at[block], back_recv.at[block])
        load = pltpu.make_async_copy(returned_hbm.at[block], rows, load_sem)
        load.start()
        if place > 0:
            start_back(turn + 1, step >= 0, step >= 0)
        slot_ids = lax.broadcasted_iota(jnp.int32, (capacity, tokens), 0)

        @pl.loop(0, in_plane)
        def _(index):
            slots = slots_ref[block * in_plane + index]
            chosen[slice_of(index), :] = (slot_ids == slots).astype(F32).astype(BF16)

        load.wait()

        @pl.loop(0, width // chunk)
        def _(part):
            wide = pl.ds(pl.multiple_of(part * chunk, chunk), chunk)
            summed = dot_tn(chosen[...], rows[:, wide])
            if place > 0:
                partial_out[block, :, wide] = summed.astype(BF16)
            else:
                expert_sum_ref[:, wide] = summed

        if place > 0:
            sum_copy(block).start()

    @pl.when(step == 0)
    def _():
        greet_plane_and_line(planes, across, shards)
        grad_ref[tokens_of(w), :] = own_grad_ref[...]
        gather_copy(1, w, opposite).start()
        gather_copy(0, w, sibling).start()
        start_back(0, step == 0, step != 0)
        key_normed, _ = norm_forward(key_raw_ref[...])
        key_rot_ref[...] = rotate(key_normed * key_gain_ref[...], cosine_ref[...], sine_ref[...]).astype(BF16)
        key_grad_ref[...] = jnp.zeros_like(key_grad_ref)
        value_grad_ref[...] = jnp.zeros_like(value_grad_ref)
        query_gain_grad_ref[...] = jnp.zeros_like(query_gain_grad_ref)
        for block in range(blocks):
            rows_here = pl.ds(block * BLOCK, BLOCK)
            turned_ref[:, rows_here] = input_ref[rows_here, :].T
        wait_bytes(grad_ref.at[tokens_of(opposite)], gather_recv.at[1])
        gather_copy(2, opposite, sibling).start()
        start_back(0, step != 0, step == 0)
        wait_bytes(grad_ref.at[tokens_of(sibling)], gather_recv.at[0])
        wait_bytes(grad_ref.at[tokens_of(other)], gather_recv.at[2])

    @pl.when(step < last)
    def _():
        wo_grad_ref[...] = dot_tn(attended_ref[...], grad_ref[...]).astype(BF16)
        for block in range(blocks):
            rows_here = pl.ds(block * BLOCK, BLOCK)
            seen = pl.ds(0, (block + 1) * BLOCK)
            query_grad_ref[rows_here, :] = dot_nt(grad_ref[rows_here, :], wo_ref[...]).astype(BF16)

            @pl.loop(0, heads_a_step)
            def _(head):
                columns = pl.ds(pl.multiple_of(head * head_size, head_size), head_size)
                query_normed, query_scale = norm_forward(query_raw_ref[rows_here, columns])
                cosine, sine = cosine_ref[rows_here, :], sine_ref[rows_here, :]
                query_rot = rotate(query_normed * query_gain_ref[...], cosine, sine).astype(BF16)
                head_grad = query_grad_ref[rows_here, columns]
                keys, values = key_rot_ref[seen, :], value_ref[seen, :]
                scores = dot_nt(query_rot, keys) * factor
                exponent = jnp.exp(scores - jnp.max(scores, axis=-1, keepdims=True))
                probs = exponent / jnp.sum(exponent, axis=-1, keepdims=True)
                prob_grad = dot_nt(head_grad, values)
                value_grad_ref[seen, :] += dot_tn(probs.astype(BF16), head_grad)
                center = jnp.sum(probs * prob_grad, axis=-1, keepdims=True)
                score_grad = (probs * (prob_grad - center)).astype(BF16)
                key_grad_ref[seen, :] += dot_tn(score_grad, query_rot) * factor
                query_rot_grad = dot(score_grad, keys) * factor
                unrotated = unrotate(query_rot_grad, cosine, sine)
                query_gain_grad_ref[0:1, :] += jnp.sum(unrotated * query_normed, axis=0, keepdims=True)
                query_grad_ref[rows_here, columns] = norm_backward(
                    unrotated * query_gain_ref[...], query_normed, query_scale
                ).astype(BF16)
            partial = dot_nt(query_grad_ref[rows_here, :], wq_ref[...])

            @pl.when(step == 0)
            def _():
                total_ref[rows_here, :] = partial

            @pl.when(step > 0)
            def _():
                total_ref[rows_here, :] += partial

            for turn, place in enumerate(pace):
                if place[1] == block:

                    @pl.when(step == place[0])
                    def _():
                        combine(turn)

    @pl.when(step == last)
    def _():
        key_normed, key_scale = norm_forward(key_raw_ref[...])
        unrotated = unrotate(key_grad_ref[...], cosine_ref[...], sine_ref[...])
        key_gain_grad_ref[...] = jnp.zeros_like(key_gain_grad_ref)
        key_gain_grad_ref[0:1, :] = jnp.sum(unrotated * key_normed, axis=0, keepdims=True)
        key_grad = norm_backward(unrotated * key_gain_ref[...], key_normed, key_scale)
        query_grad_ref[:, :head_size] = key_grad.astype(BF16)
        query_grad_ref[:, head_size : 2 * head_size] = value_grad_ref[...].astype(BF16)
        for block in range(blocks):
            rows_here = pl.ds(block * BLOCK, BLOCK)
            first_grad_ref[rows_here, :] = (
                total_ref[rows_here, :] + dot_nt(query_grad_ref[rows_here, :], wq_ref[...])
            ).astype(BF16)

    wq_grad_ref[...] = dot(turned_ref[...], query_grad_ref[...]).astype(BF16)

    @pl.when(step == last)
    def _():
        for turn in range(len(pace), planes):
            combine(turn)

        @pl.loop(1, planes)
        def _(offset):
            source = (z + offset) % planes
            wait_bytes(partial_in.at[source], sum_recv.at[source])

            @pl.loop(0, width // chunk)
            def _(part):
                wide = pl.ds(pl.multiple_of(part * chunk, chunk), chunk)
                expert_sum_ref[:, wide] += partial_in[source, :, wide].astype(F32)

            wait_bytes(partial_out.at[source], sum_send.at[source])

        @pl.loop(0, planes)
        def _(block):
            wait_bytes(weighted_hbm.at[block, pl.ds(0, count - capacity)], back_send.at[block])

        wait_bytes(grad_ref.at[tokens_of(w)], gather_send.at[0])
        wait_bytes(grad_ref.at[tokens_of(w)], gather_send.at[1])
        wait_bytes(grad_ref.at[tokens_of(w)], gather_send.at[2])


def whole(shape):
    return pl.BlockSpec(shape, lambda step: (0,) * len(shape), pipeline_mode=pl.Buffered(1))


def run_forward(
    planes, across, shards, capacity, own, small, routes, top, w_query, w_key, w_value, query_gain, key_gain, cosine, sine, wo
):
    tokens, width = own.shape
    seq_length = tokens * shards
    head_size = query_gain.shape[1]
    heads_here = wo.shape[0] // head_size
    pair = 2
    wide = pair * head_size
    steps = heads_here // pair
    in_plane = across * shards
    count = in_plane * capacity
    hbm = pl.BlockSpec(memory_space=pl.ANY)
    dma = pltpu.SemaphoreType.DMA
    slots_shape = (planes * in_plane, 1, tokens)
    return pl.pallas_call(
        functools.partial(attention_forward, planes, across, shards, capacity, pair),
        grid=(steps + 1,),
        in_specs=[
            whole((tokens, width)),
            whole(small.shape),
            whole(routes.shape),
            whole((tokens, width)),
            hbm,
            hbm,
            hbm,
            whole((1, head_size)),
            whole((1, head_size)),
            whole((seq_length, head_size)),
            whole((seq_length, head_size)),
            whole(wo.shape),
        ],
        out_specs=[
            whole((seq_length, width)),
            pl.BlockSpec((seq_length, wide), lambda step: (0, jnp.minimum(step, steps - 1))),
            whole((seq_length, head_size)),
            whole((seq_length, head_size)),
            whole((seq_length, heads_here * head_size)),
            whole((tokens, width)),
            whole(slots_shape),
            whole(slots_shape),
            whole(slots_shape),
            whole((8, 128)),
            hbm,
            hbm,
            hbm,
            hbm,
        ],
        out_shape=[
            jax.ShapeDtypeStruct((seq_length, width), BF16),
            jax.ShapeDtypeStruct((seq_length, heads_here * head_size), F32),
            jax.ShapeDtypeStruct((seq_length, head_size), F32),
            jax.ShapeDtypeStruct((seq_length, head_size), BF16),
            jax.ShapeDtypeStruct((seq_length, heads_here * head_size), BF16),
            jax.ShapeDtypeStruct((tokens, width), F32),
            jax.ShapeDtypeStruct(slots_shape, jnp.int32),
            jax.ShapeDtypeStruct(slots_shape, jnp.int32),
            jax.ShapeDtypeStruct(slots_shape, F32),
            jax.ShapeDtypeStruct((8, 128), F32),
            jax.ShapeDtypeStruct((tokens, width), BF16),
            jax.ShapeDtypeStruct((shards,) + small.shape, F32),
            jax.ShapeDtypeStruct((width, (steps + 1) * wide), BF16),
            jax.ShapeDtypeStruct((planes, count, width), BF16),
        ],
        scratch_shapes=[
            pltpu.VMEM((seq_length, width), BF16),
            pltpu.VMEM((shards,) + small.shape, F32),
            pltpu.VMEM((width, (steps + 1) * wide), BF16),
            pltpu.VMEM((seq_length, head_size), BF16),
            pltpu.VMEM((in_plane, planes) + routes.shape, jnp.int32),
            pltpu.VMEM(slots_shape, jnp.int32),
            pltpu.VMEM((2, planes, tokens, width), BF16),
            pltpu.VMEM((2, planes, count // 2, width), BF16),
            pltpu.VMEM((count // 2, tokens), BF16),
            pltpu.VMEM((2, tokens, width), BF16),
            pltpu.VMEM((tokens, width), BF16),
            dma((3,)), dma((3,)), dma((shards,)), dma((shards,)), dma((steps + 1,)), dma((steps + 1,)),
            dma((planes,)), dma((planes,)), dma, dma((in_plane,)), dma, dma,
            dma((2, 2, planes + 1, 2)), dma((2, 2, planes + 1, 2)), dma((2, planes)), dma((planes,)), dma((3,)), dma((3,)), dma, dma, dma,
        ],
        compiler_params=pltpu.CompilerParams(vmem_limit_bytes=VMEM_LIMIT, collective_id=5, has_side_effects=True),
        cost_estimate=pl.CostEstimate(flops=70 * 10**9, bytes_accessed=40 * 10**6, transcendentals=6 * 10**6),
    )(own, small, routes, top, w_query, w_key, w_value, query_gain, key_gain, cosine, sine, wo)


def run_backward(
    planes, across, shards, capacity, own_grad, wo, attended, query_raw, key_raw, value, first_input, weights, query_gain,
    key_gain, cosine, sine, slots, weighted,
):
    tokens, width = own_grad.shape
    seq_length = attended.shape[0]
    head_size = query_gain.shape[1]
    heads_here = wo.shape[0] // head_size
    pair = 2
    wide = pair * head_size
    steps = heads_here // pair
    count = across * shards * capacity
    hbm = pl.BlockSpec(memory_space=pl.ANY)
    dma = pltpu.SemaphoreType.DMA

    def held(step):
        return jnp.minimum(step, steps - 1)

    return pl.pallas_call(
        functools.partial(attention_backward, planes, across, shards, capacity, pair),
        grid=(steps + 1,),
        in_specs=[
            whole((tokens, width)),
            pl.BlockSpec((wide, width), lambda step: (held(step), 0)),
            pl.BlockSpec((seq_length, wide), lambda step: (0, held(step))),
            pl.BlockSpec((seq_length, wide), lambda step: (0, held(step))),
            whole((seq_length, head_size)),
            whole((seq_length, head_size)),
            whole((seq_length, width)),
            pl.BlockSpec((width, wide), lambda step: (0, step)),
            whole((1, head_size)),
            whole((1, head_size)),
            whole((seq_length, head_size)),
            whole((seq_length, head_size)),
            whole(slots.shape),
            hbm,
        ],
        out_specs=[
            pl.BlockSpec((wide, width), lambda step: (held(step), 0)),
            pl.BlockSpec((width, wide), lambda step: (0, step)),
            whole((seq_length, width)),
            whole((8, head_size)),
            whole((8, head_size)),
            hbm,
            whole((tokens, width)),
        ],
        out_shape=[
            jax.ShapeDtypeStruct((heads_here * head_size, width), BF16),
            jax.ShapeDtypeStruct((width, (steps + 1) * wide), BF16),
            jax.ShapeDtypeStruct((seq_length, width), BF16),
            jax.ShapeDtypeStruct((8, head_size), F32),
            jax.ShapeDtypeStruct((8, head_size), F32),
            jax.ShapeDtypeStruct(weighted.shape, BF16),
            jax.ShapeDtypeStruct((tokens, width), F32),
        ],
        scratch_shapes=[
            pltpu.VMEM((seq_length, width), F32),
            pltpu.VMEM((seq_length, head_size), BF16),
            pltpu.VMEM((seq_length, head_size), F32),
            pltpu.VMEM((seq_length, head_size), F32),
            pltpu.VMEM((seq_length, wide), BF16),
            pltpu.VMEM((width, seq_length), BF16),
            pltpu.VMEM((seq_length, width), BF16),
            pltpu.VMEM((count, width), BF16),
            pltpu.VMEM((count, tokens), BF16),
            pltpu.VMEM((planes, tokens, width), BF16),
            pltpu.VMEM((planes, tokens, width), BF16),
            dma((3,)), dma((3,)), dma((planes,)), dma((planes,)), dma((planes,)), dma((planes,)), dma,
        ],
        compiler_params=pltpu.CompilerParams(vmem_limit_bytes=VMEM_LIMIT, collective_id=2, has_side_effects=True),
        cost_estimate=pl.CostEstimate(flops=70 * 10**9, bytes_accessed=60 * 10**6, transcendentals=6 * 10**6),
    )(
        own_grad, wo, attended, query_raw, key_raw, value, first_input, weights, query_gain, key_gain, cosine, sine, slots,
        weighted,
    )


def reduce_kernel(
    planes, across, shards,
    wq_hbm, wo_hbm, first_hbm, hidden_ref, middle_hbm, expert_sum_hbm, middle_grad_hbm, small_ref, early_ref, query_gain_ref,
    key_gain_ref, squares_ref,
    rows_hbm, gate_grad_hbm, up_grad_hbm, units_hbm, pair_grad_hbm,
    query_ref, key_ref, value_ref, output_ref, hidden_out_ref, grad_in_ref, early_total_ref, late_total_ref,
    gate_out_hbm, up_out_hbm, down_out_hbm,
    wq_parts, wo_parts, wq_out, wo_out, wq_in, wo_in, wq_total, wo_total, wq_final, wo_final, wq_home, wo_home, first_in,
    early_in, late, late_in, held_a, held_b, side, turned, tiles, tall, flat,
    across_send, across_recv, line_send, line_recv, home_send, home_recv, swap_send, swap_recv, first_send, first_recv,
    early_send, early_recv, late_send, late_recv, held_sem, side_sem, tile_sem, result_sem,
):
    z, x, w = lax.axis_index("z"), lax.axis_index("x"), lax.axis_index("w")
    rings = planes * across
    ring = z * across + x
    everyone = rings * shards
    wq_rows, wo_rows = wq_total.shape[0], wo_total.shape[0]
    mine = wq_rows // shards
    tokens, width = grad_in_ref.shape
    query_columns = query_ref.shape[1] // shards
    key_columns = key_ref.shape[1] // shards
    linear = ring * shards + w
    barrier = pltpu.get_barrier_semaphore()

    def place(index):
        return (index // shards // across, index // shards % across, index % shards)

    @pl.loop(1, everyone)
    def _(offset):
        pl.semaphore_signal(barrier, inc=1, device_id=place((linear + offset) % everyone), device_id_type=MESH)

    pl.semaphore_wait(barrier, everyone - 1)

    def rows_of(index, size):
        return pl.ds(pl.multiple_of(index * size, 16), size)

    sources = [(wq_hbm, wq_rows, wq_parts), (wo_hbm, wo_rows, wo_parts)]

    def across_copy(kind, plane, column):
        source, rows, goal = sources[kind]
        return remote(
            source.at[rows_of(plane * across + column, rows)], goal.at[plane, x],
            across_send.at[kind, plane], across_recv.at[kind, plane], (z, column, w),
        )

    def first_copy(offset):
        target = (w + offset) % shards
        return remote(
            first_hbm.at[rows_of(target, tokens)], first_in.at[offset], first_send.at[offset], first_recv.at[offset],
            (z, x, target),
        )

    @pl.loop(1, shards)
    def _(offset):
        first_copy(offset).start()

    pltpu.make_async_copy(first_hbm.at[rows_of(w, tokens)], first_in.at[0], first_recv.at[0]).start()
    hold_a = pltpu.make_async_copy(middle_hbm, held_a, held_sem.at[0])
    hold_b = pltpu.make_async_copy(expert_sum_hbm, held_b, held_sem.at[1])
    hold_a.start()
    hold_b.start()

    def start_across(kind, turn):
        plane, _, _ = line_order(z, planes, planes - 1 - turn)

        @pl.loop(1, across)
        def _(offset):
            across_copy(kind, plane, (x + offset) % across).start()

        source, rows, goal = sources[kind]
        pltpu.make_async_copy(
            source.at[rows_of(plane * across + x, rows)], goal.at[plane, x], across_recv.at[kind, plane]
        ).start()

    start_across(1, 0)
    start_across(1, 1)

    @pl.loop(1, everyone)
    def _(offset):
        other = (linear + offset) % everyone
        remote(early_ref.at[other], early_in.at[linear], early_send, early_recv, place(other)).start()

    early_in[linear] = early_ref[linear]
    lanes = tiles.shape[2]
    per_kind = width // lanes
    depth = side.shape[0]
    late_rows = width // 128
    experts = everyone
    scale_row = jnp.concatenate([small_ref[part, experts + 1 : experts + 2, :] for part in range(shards)], axis=1)
    pick = (lax.broadcasted_iota(jnp.int32, (8, 128), 0) == 2).astype(F32)
    lane = lax.broadcasted_iota(jnp.int32, (8, 128), 1)

    def tile_copy(unit):
        slot = unit % 2
        here = pl.ds(pl.multiple_of((unit % per_kind) * lanes, lanes), lanes)

        @pl.when(unit < 2 * per_kind)
        def _():
            pltpu.make_async_copy(rows_hbm.at[:, here], tiles.at[slot], tile_sem.at[slot]).start()

        @pl.when(unit >= 2 * per_kind)
        def _():
            pltpu.make_async_copy(pair_grad_hbm.at[:, here], tiles.at[slot], tile_sem.at[slot]).start()

    tile_copy(0)

    def multiply(unit):
        slot = unit % 2
        here = pl.ds(pl.multiple_of((unit % per_kind) * lanes, lanes), lanes)
        for kind, source in enumerate([gate_grad_hbm, up_grad_hbm, units_hbm]):

            @pl.when(unit == kind * per_kind)
            def _():
                load = pltpu.make_async_copy(source, side, side_sem)
                load.start()
                load.wait()
                if kind == 2:

                    @pl.loop(0, depth // 128)
                    def _(part):
                        at = pl.ds(pl.multiple_of(part * 128, 128), 128)
                        turned[:, at] = side[at, :].T

        @pl.when(unit + 1 < 3 * per_kind)
        def _():
            tile_copy(unit + 1)

        wait_bytes(tiles.at[slot], tile_sem.at[slot])

        @pl.when(unit >= 2)
        def _():
            wait_bytes(tall.at[slot], result_sem.at[slot])

        @pl.when(unit < 2 * per_kind)
        def _():
            tall[slot] = dot_tn(tiles[slot], side[...])

        @pl.when(unit < per_kind)
        def _():
            pltpu.make_async_copy(tall.at[slot], gate_out_hbm.at[here], result_sem.at[slot]).start()

        @pl.when((unit >= per_kind) & (unit < 2 * per_kind))
        def _():
            pltpu.make_async_copy(tall.at[slot], up_out_hbm.at[here], result_sem.at[slot]).start()

        @pl.when(unit >= 2 * per_kind)
        def _():
            flat[slot] = dot(turned[...], tiles[slot])
            pltpu.make_async_copy(flat.at[slot], down_out_hbm.at[:, here], result_sem.at[slot]).start()

    def late_copy(other):
        return remote(late, late_in.at[linear], late_send, late_recv, place(other))

    def finish_rows():
        hold_a.wait()
        hold_b.wait()
        pieces = tokens // 64

        def add_rows(piece, carry):
            at = pl.ds(pl.multiple_of(piece * 64, 64), 64)
            extra = held_b[at, :]
            hidden_out_ref[at, :] = (held_a[at, :] + extra).astype(BF16)
            return carry + jnp.sum(jnp.sum(extra * extra, axis=1, keepdims=True), axis=0, keepdims=True)

        expert_square = lax.fori_loop(0, pieces, add_rows, jnp.zeros((1, 1), F32))
        load = pltpu.make_async_copy(middle_grad_hbm, held_a, held_sem.at[0])
        load.start()

        @pl.loop(0, shards)
        def _(offset):
            wait_bytes(first_in.at[offset], first_recv.at[offset])

        load.wait()

        def grad_rows(piece, carry):
            square, gain_grad = carry
            at = pl.ds(pl.multiple_of(piece * 64, 64), 64)
            first = first_in[0, at, :].astype(F32)
            for offset in range(1, shards):
                first += first_in[offset, at, :].astype(F32)
            normed, scaling = norm_forward(hidden_ref[at, :].astype(F32))
            grad = held_a[at, :] + norm_backward(first * scale_row, normed, scaling)
            grad_in_ref[at, :] = grad
            return (
                square + jnp.sum(jnp.sum(grad * grad, axis=1, keepdims=True), axis=0, keepdims=True),
                gain_grad + jnp.sum(first * normed, axis=0, keepdims=True),
            )

        square, gain_grad = lax.fori_loop(
            0, pieces, grad_rows, (jnp.zeros((1, 1), F32), jnp.zeros((1, width), F32))
        )
        for row in range(late_rows):
            late[row : row + 1, :] = gain_grad[:, row * 128 : (row + 1) * 128]
        late[late_rows:, :] = squares_ref[...] + pick * (
            jnp.where(lane == 2, expert_square, 0.0) + jnp.where(lane == 3, square, 0.0)
        )

        late[late_rows : late_rows + 1, :] = query_gain_ref[0:1, :]
        late[late_rows + 1 : late_rows + 2, :] = key_gain_ref[0:1, :]

        @pl.loop(1, everyone)
        def _(offset):
            late_copy((linear + offset) % everyone).start()

        late_in[linear] = late[...]

    outs, ins = [wq_out, wo_out], [wq_in, wo_in]
    totals, parts = [wq_total, wo_total], [wq_parts, wo_parts]

    def line_copy(kind, plane):
        up = (plane > z).astype(jnp.int32)
        ends = (plane == z + 2 * up - 1).astype(jnp.int32)
        slot = plane + ends * (1 - up) * (planes - plane)
        return remote(
            outs[kind].at[plane], ins[kind].at[slot], line_send.at[kind, plane], line_recv.at[kind, slot],
            (z + 2 * up - 1, x, w),
        )

    per_turn = 3 * per_kind // (2 * planes)

    def take(kind, slot):
        wait_bytes(ins[kind].at[slot], line_recv.at[kind, slot])
        totals[kind][...] += ins[kind][slot].astype(F32)

    def collect(kind):
        @pl.loop(0, planes)
        def _(turn):
            plane, _, _ = line_order(z, planes, planes - 1 - turn)

            @pl.loop(0, per_turn)
            def _(unit):
                multiply((turn + (1 - kind) * planes) * per_turn + unit)

            wait_bytes(parts[kind].at[plane], across_recv.at[kind, plane])

            @pl.when(turn < planes - 2)
            def _():
                start_across(kind, turn + 2)

            if kind == 1:

                @pl.when(turn >= planes - 2)
                def _():
                    start_across(0, turn + 2 - planes)

            totals[kind][...] = parts[kind][plane, 0].astype(F32)

            @pl.loop(1, across)
            def _(column):
                totals[kind][...] += parts[kind][plane, column].astype(F32)

            @pl.when(((plane > z) & (z > 0)) | ((plane < z) & (z < planes - 1)))
            def _():
                take(kind, plane)

            @pl.when(plane != z)
            def _():
                outs[kind][plane] = totals[kind][...].astype(BF16)
                line_copy(kind, plane).start()

    def finish(kind):
        @pl.when(z > 0)
        def _():
            take(kind, z)

        @pl.when(z < planes - 1)
        def _():
            take(kind, planes)

    collect(1)
    finish(1)
    wo_final[...] = wo_total[...].astype(BF16)
    goal = w * rings + ring
    stays = goal == linear
    swap = remote(
        wo_final, wo_home, swap_send, swap_recv, (goal // shards // across, goal // shards % across, goal % shards)
    )

    @pl.when(jnp.logical_not(stays))
    def _():
        swap.start()

    @pl.when(stays)
    def _():
        pltpu.make_async_copy(wo_final, wo_home, swap_recv).start()

    finish_rows()
    collect(0)
    finish(0)
    wq_final[...] = wq_total[...].astype(BF16)

    def home_copy(offset):
        target = (w + offset) % shards
        return remote(
            wq_final.at[rows_of(target, mine)], wq_home.at[w], home_send.at[offset], home_recv.at[w], (z, x, target)
        )

    @pl.loop(1, shards)
    def _(offset):
        home_copy(offset).start()

    pltpu.make_async_copy(wq_final.at[rows_of(w, mine)], wq_home.at[w], home_recv.at[w]).start()

    for part in range(shards):
        wait_bytes(wq_home.at[part], home_recv.at[part])
        rows = wq_home[part].astype(F32)
        query_ref[:, part * query_columns : (part + 1) * query_columns] = rows[:, :query_columns]
        key_ref[:, part * key_columns : (part + 1) * key_columns] = rows[:, query_columns : query_columns + key_columns]
        value_ref[:, part * key_columns : (part + 1) * key_columns] = rows[:, query_columns + key_columns :]

    wait_bytes(early_ref.at[pl.ds(0, everyone - 1)], early_recv)
    early_total_ref[...] = jnp.sum(early_in[...], axis=0)
    wait_bytes(late_in.at[pl.ds(0, everyone - 1)], late_recv)
    late_total_ref[...] = jnp.sum(late_in[...], axis=0)
    wait_bytes(early_ref.at[pl.ds(0, everyone - 1)], early_send)
    wait_bytes(late_in.at[pl.ds(0, everyone - 1)], late_send)
    for slot in range(2):
        wait_bytes(tall.at[slot], result_sem.at[slot])
    wait_bytes(wo_home, swap_recv)
    output_ref[...] = wo_home[...].astype(F32)

    @pl.when(jnp.logical_not(stays))
    def _():
        wait_bytes(wo_final, swap_send)

    @pl.loop(1, shards)
    def _(offset):
        wait_bytes(wq_home.at[0], home_send.at[offset])
        wait_bytes(first_in.at[0], first_send.at[offset])

    if across > 1:

        @pl.loop(0, planes)
        def _(plane):
            wait_bytes(wq_parts.at[plane, pl.ds(0, across - 1)], across_send.at[0, plane])
            wait_bytes(wo_parts.at[plane, pl.ds(0, across - 1)], across_send.at[1, plane])

    @pl.loop(1, planes)
    def _(offset):
        plane = (z + offset) % planes
        wait_bytes(wq_out.at[plane], line_send.at[0, plane])
        wait_bytes(wo_out.at[plane], line_send.at[1, plane])


def run_reduce(
    planes, across, shards, wq_grad, wo_grad, first_part, hidden, middle, expert_sum, middle_grad, small_all, early,
    query_gain_grad, key_gain_grad, squares, rows_in, gate_grad, up_grad, units, pair_grad, query_columns, key_columns,
):
    rings = planes * across
    everyone = rings * shards
    width = wq_grad.shape[0]
    wq_wide = wq_grad.shape[1]
    wq_rows, wo_rows = width // rings, wo_grad.shape[0] // rings
    tokens = first_part.shape[0] // shards
    mine = wq_rows // shards
    depth, wide = units.shape
    late_rows = width // 128 + 8
    hbm = pl.BlockSpec(memory_space=pl.ANY)
    vmem = pl.BlockSpec(memory_space=pltpu.VMEM)
    dma = pltpu.SemaphoreType.DMA
    return pl.pallas_call(
        functools.partial(reduce_kernel, planes, across, shards),
        in_specs=[hbm] * 3 + [vmem] + [hbm] * 3 + [vmem] * 5 + [hbm] * 5,
        out_specs=[vmem] * 8 + [hbm] * 3,
        out_shape=[
            jax.ShapeDtypeStruct((mine, query_columns), F32),
            jax.ShapeDtypeStruct((mine, key_columns), F32),
            jax.ShapeDtypeStruct((mine, key_columns), F32),
            jax.ShapeDtypeStruct((wo_rows, width), F32),
            jax.ShapeDtypeStruct((tokens, width), BF16),
            jax.ShapeDtypeStruct((tokens, width), F32),
            jax.ShapeDtypeStruct(early.shape[1:], F32),
            jax.ShapeDtypeStruct((late_rows, 128), F32),
            jax.ShapeDtypeStruct((width, wide), F32),
            jax.ShapeDtypeStruct((width, wide), F32),
            jax.ShapeDtypeStruct((wide, width), F32),
        ],
        scratch_shapes=[
            pltpu.VMEM((planes, across, wq_rows, wq_wide), BF16),
            pltpu.VMEM((planes, across, wo_rows, width), BF16),
            pltpu.VMEM((planes, wq_rows, wq_wide), BF16),
            pltpu.VMEM((planes, wo_rows, width), BF16),
            pltpu.VMEM((planes + 1, wq_rows, wq_wide), BF16),
            pltpu.VMEM((planes + 1, wo_rows, width), BF16),
            pltpu.VMEM((wq_rows, wq_wide), F32),
            pltpu.VMEM((wo_rows, width), F32),
            pltpu.VMEM((wq_rows, wq_wide), BF16),
            pltpu.VMEM((wo_rows, width), BF16),
            pltpu.VMEM((shards, mine, wq_wide), BF16),
            pltpu.VMEM((wo_rows, width), BF16),
            pltpu.VMEM((shards, tokens, width), BF16),
            pltpu.VMEM(early.shape, F32),
            pltpu.VMEM((late_rows, 128), F32),
            pltpu.VMEM((everyone, late_rows, 128), F32),
            pltpu.VMEM((tokens, width), F32),
            pltpu.VMEM((tokens, width), F32),
            pltpu.VMEM((depth, wide), BF16),
            pltpu.VMEM((wide, depth), BF16),
            pltpu.VMEM((2, depth, 256), BF16),
            pltpu.VMEM((2, 256, wide), F32),
            pltpu.VMEM((2, wide, 256), F32),
            dma((2, planes)), dma((2, planes)), dma((2, planes)), dma((2, planes + 1)), dma((shards,)), dma((shards,)),
            dma, dma, dma((shards,)), dma((shards,)), dma, dma, dma, dma, dma((2,)), dma, dma((2,)), dma((2,)),
        ],
        compiler_params=pltpu.CompilerParams(vmem_limit_bytes=VMEM_LIMIT, collective_id=3, has_side_effects=True),
        cost_estimate=pl.CostEstimate(flops=70 * 10**9, bytes_accessed=40 * 10**6, transcendentals=0),
    )(
        wq_grad, wo_grad, first_part, hidden, middle, expert_sum, middle_grad, small_all, early, query_gain_grad,
        key_gain_grad, squares, rows_in, gate_grad, up_grad, units, pair_grad,
    )


def expert_kernel(
    planes, across, shards, capacity,
    own_ref, share_ref, slots_ref, my_slots_ref, gate_ref, up_ref, down_ref, small_ref, top_hbm,
    middle_hbm, cotangent_hbm, rows_hbm, back_hbm, weighted_hbm, units_hbm, gate_grad_hbm, up_grad_hbm, pair_grad_hbm, row_grad_ref, low_grad_hbm, logit_grad_ref, gain_grad_ref,
    share_grad_ref, middle, plane_rows, plane_shares, share_in, share_back, share_home, stage, chosen, rows, top, units,
    gate_grad, up_grad, columns, partial_in,
    line_send, line_recv, plane_share_send, plane_share_recv, out_send, out_recv, out_share_send, out_share_recv,
    back_send, back_recv, back_share_send, back_share_recv, sum_send, sum_recv, sum_share_send, sum_share_recv,
    load_sem, top_sem, store_sem, middle_sem,
):
    z, x, w = lax.axis_index("z"), lax.axis_index("x"), lax.axis_index("w")
    in_plane = across * shards
    experts = planes * in_plane
    me = x * shards + w
    tokens, width = own_ref.shape
    count = in_plane * capacity
    half = count // 2
    per_half = in_plane // 2
    chunk = 512

    def place(index):
        return (z, index // shards, index % shards)

    def order(step):
        return line_order(z, planes, step)

    inner = ((z > 0) & (z < planes - 1)).astype(jnp.int32)
    first_back = 2 - (z == 1).astype(jnp.int32)
    second_back = 3 - inner * first_back
    third_back = 1 + 2 * inner
    greet_plane_and_line(planes, across, shards)

    def line_up(block, hop):
        return remote(
            plane_rows.at[block], plane_rows.at[block], line_send.at[0, hop], line_recv.at[0, hop], (z + 1, x, w)
        )

    def line_down(block, hop):
        return remote(
            plane_rows.at[block], plane_rows.at[block], line_send.at[1, hop], line_recv.at[1, hop], (z - 1, x, w)
        )

    middle_load = pltpu.make_async_copy(middle_hbm, middle, middle_sem)
    middle_load.start()
    plane_rows[z] = own_ref[...]

    @pl.when(z + 1 < planes)
    def _():
        line_up(z, 1).start()

    @pl.when(z > 0)
    def _():
        line_down(z, 1).start()

    def plane_share_copy(other):
        return remote(
            share_ref.at[pl.ds(other * in_plane, in_plane)], plane_shares.at[z],
            plane_share_send.at[other], plane_share_recv.at[z], (other, x, w),
        )

    @pl.loop(1, planes)
    def _(offset):
        plane_share_copy((z + offset) % planes).start()

    plane_shares[z] = share_ref[pl.ds(z * in_plane, in_plane)]

    def slice_of(index):
        return pl.ds(pl.multiple_of(index * capacity, 16), capacity)

    def out_copy(step, block, index):
        return remote(
            stage.at[step, slice_of(index)], rows_hbm.at[block, slice_of(me)],
            out_send.at[step], out_recv.at[step], place(index),
        )

    def out_share_copy(step, block, index):
        return remote(
            plane_shares.at[block, index], share_in.at[block, me],
            out_share_send.at[step], out_share_recv.at[step], place(index),
        )

    def back_copy(step, block, index):
        return remote(
            stage.at[step, slice_of(index)], back_hbm.at[block, slice_of(me)],
            back_send.at[step], back_recv.at[step], place(index),
        )

    def back_share_copy(step, block, index):
        return remote(
            share_back.at[block, index], share_home.at[block, me],
            back_share_send.at[step], back_share_recv.at[step], place(index),
        )

    def start_back(step, block):
        @pl.loop(1, in_plane)
        def _(offset):
            index = (me + offset) % in_plane
            back_copy(step, block, index).start()
            back_share_copy(step, block, index).start()

        pltpu.make_async_copy(stage.at[step, slice_of(me)], back_hbm.at[block, slice_of(me)], back_recv.at[step]).start()
        pltpu.make_async_copy(share_back.at[block, me], share_home.at[block, me], back_share_recv.at[step]).start()

    slot_ids = lax.broadcasted_iota(jnp.int32, (capacity, tokens), 0)

    def pack_step(step):
        block, _, _ = order(step)

        @pl.when(step > 0)
        def _():
            @pl.when(z - step >= 0)
            def _():
                wait_bytes(plane_rows.at[0], line_recv.at[0, step])

                @pl.when(z + 1 < planes)
                def _():
                    line_up(z - step, step + 1).start()

            @pl.when(z + step < planes)
            def _():
                wait_bytes(plane_rows.at[0], line_recv.at[1, step])

                @pl.when(z > 0)
                def _():
                    line_down(z + step, step + 1).start()

            wait_bytes(plane_shares.at[block], plane_share_recv.at[block])

        @pl.loop(0, in_plane)
        def _(index):
            slots = slots_ref[block * in_plane + index]
            chosen[step, slice_of(index), :] = (slot_ids == slots).astype(F32).astype(BF16)

        @pl.loop(0, width // chunk)
        def _(part):
            wide = pl.ds(pl.multiple_of(part * chunk, chunk), chunk)
            stage[step, :, wide] = dot(chosen[step], plane_rows[block, :, wide]).astype(BF16)

    def send_step(step):
        block, _, _ = order(step)

        @pl.loop(1, in_plane)
        def _(offset):
            index = (me + offset) % in_plane
            out_copy(step, block, index).start()
            out_share_copy(step, block, index).start()

        pltpu.make_async_copy(stage.at[step, slice_of(me)], rows_hbm.at[block, slice_of(me)], out_recv.at[step]).start()
        pltpu.make_async_copy(plane_shares.at[block, me], share_in.at[block, me], out_share_recv.at[step]).start()

    def expert_step(step):
        block, _, _ = order(step)

        pltpu.make_async_copy(top_hbm.at[block], top, top_sem).start()
        wait_bytes(rows_hbm.at[block], out_recv.at[step])
        load = pltpu.make_async_copy(rows_hbm.at[block], rows, load_sem)
        load.start()

        @pl.when(step + 1 < planes)
        def _():
            send_step(step + 1)

        wait_bytes(share_in.at[block], out_share_recv.at[step])
        wait_bytes(stage.at[step, pl.ds(0, count - capacity)], out_send.at[step])
        wait_bytes(plane_shares.at[block, pl.ds(0, in_plane - 1)], out_share_send.at[step])

        @pl.loop(0, in_plane)
        def _(index):
            mine = slot_ids == my_slots_ref[block * in_plane + index]
            columns[slice_of(index), :] = jnp.broadcast_to(
                jnp.sum(jnp.where(mine, share_in[block, index], 0.0), axis=1, keepdims=True), (capacity, 128)
            )

        load.wait()
        wait_bytes(top, top_sem)

        @pl.loop(0, 2)
        def _(part):
            here = pl.ds(pl.multiple_of(part * half, 16), half)
            gate = dot(rows[here, :], gate_ref[...])
            up = dot(rows[here, :], up_ref[...])
            sigmoid = 1.0 / (1.0 + jnp.exp(-gate))
            active = gate * sigmoid
            hidden = (active * up).astype(BF16)
            units[here, :] = hidden
            share = columns[here, 0:1]
            total = jnp.zeros((half, 1), F32)
            for piece in range(width // chunk):
                wide = pl.ds(piece * chunk, chunk)
                pair_out = dot(hidden, down_ref[:, wide]).astype(BF16).astype(F32)
                top_rows = top[here, wide].astype(F32)
                total += jnp.sum(pair_out * top_rows, axis=1, keepdims=True)
                rows[here, wide] = (share * pair_out).astype(BF16)
                top[here, wide] = (share * top_rows).astype(BF16)
            columns[here, :] = jnp.broadcast_to(total, (half, 128))
            hidden_grad = dot_nt(top[here, :], down_ref[...])
            gate_low = (hidden_grad * up * sigmoid * (1.0 + gate * (1.0 - sigmoid))).astype(BF16)
            up_low = (hidden_grad * active).astype(BF16)
            gate_grad[here, :] = gate_low
            up_grad[here, :] = up_low
            for piece in range(width // chunk):
                wide = pl.ds(piece * chunk, chunk)
                stage[step, here, wide] = (dot_nt(gate_low, gate_ref[wide, :]) + dot_nt(up_low, up_ref[wide, :])).astype(BF16)

        @pl.loop(0, in_plane)
        def _(index):
            mine = slot_ids == my_slots_ref[block * in_plane + index]
            values = columns[slice_of(index), 0:1]
            share_back[block, index] = jnp.sum(jnp.where(mine, values, 0.0), axis=0, keepdims=True)

        @pl.when((step == first_back) | (step == second_back))
        def _():
            start_back(step, block)

        stores = [
            pltpu.make_async_copy(units, units_hbm.at[block], store_sem.at[0]),
            pltpu.make_async_copy(gate_grad, gate_grad_hbm.at[block], store_sem.at[1]),
            pltpu.make_async_copy(up_grad, up_grad_hbm.at[block], store_sem.at[2]),
            pltpu.make_async_copy(top, pair_grad_hbm.at[block], store_sem.at[3]),
            pltpu.make_async_copy(rows, weighted_hbm.at[block], store_sem.at[4]),
        ]
        for store in stores:
            store.start()

        for store in stores:
            store.wait()

    @pl.loop(0, planes + 1)
    def _(step):
        @pl.when(step < planes)
        def _():
            pack_step(step)

        @pl.when(step == 0)
        def _():
            send_step(step)

        @pl.when(step > 0)
        def _():
            expert_step(step - 1)

    for hop in range(1, planes):

        @pl.when((z - (hop - 1) >= 0) & (z + 1 < planes))
        def _():
            wait_bytes(plane_rows.at[0], line_send.at[0, hop])

        @pl.when((z + (hop - 1) < planes) & (z > 0))
        def _():
            wait_bytes(plane_rows.at[0], line_send.at[1, hop])

    @pl.loop(1, planes)
    def _(offset):
        wait_bytes(plane_shares.at[0], plane_share_send.at[(z + offset) % planes])

    def wait_back(step):
        wait_bytes(stage.at[step, pl.ds(0, count - capacity)], back_send.at[step])
        wait_bytes(share_back.at[0, pl.ds(0, in_plane - 1)], back_share_send.at[step])

    def sum_copy(block):
        up = (block > z).astype(jnp.int32)
        relayed = (jnp.abs(block - z) == planes - 1).astype(jnp.int32)
        goal = block + relayed * (1 - 2 * up) * (planes - 2)
        slot = z + relayed * (goal - z)
        return remote(plane_rows.at[block], partial_in.at[slot], sum_send.at[block], sum_recv.at[slot], (goal, x, w))

    def sum_share_copy(block):
        return remote(
            share_home.at[block], share_grad_ref.at[pl.ds(z * in_plane, in_plane)],
            sum_share_send.at[block], sum_share_recv.at[z], (block, x, w),
        )

    @pl.loop(0, planes)
    def _(turn):
        step = jnp.where(turn == 0, first_back, jnp.where(turn == 1, second_back, jnp.where(turn == 2, third_back, 0)))
        block, _, _ = order(step)
        wait_bytes(back_hbm.at[block], back_recv.at[step])
        load = pltpu.make_async_copy(back_hbm.at[block], rows, load_sem)
        load.start()
        wait_bytes(share_home.at[block], back_share_recv.at[step])
        load.wait()

        @pl.when(step > 0)
        def _():
            sum_share_copy(block).start()

            merges = (inner == 1) & (jnp.abs(block - z) == 2)

            @pl.when(merges)
            def _():
                wait_bytes(partial_in.at[z], sum_recv.at[z])

            @pl.loop(0, width // chunk)
            def _(part):
                wide = pl.ds(pl.multiple_of(part * chunk, chunk), chunk)
                summed = dot_tn(chosen[step], rows[:, wide])

                @pl.when(merges)
                def _():
                    plane_rows[block, :, wide] = (summed + partial_in[z, :, wide].astype(F32)).astype(BF16)

                @pl.when(jnp.logical_not(merges))
                def _():
                    plane_rows[block, :, wide] = summed.astype(BF16)

            sum_copy(block).start()

        @pl.when(step == 0)
        def _():
            share_grad_ref[pl.ds(z * in_plane, in_plane)] = share_home[z]

            @pl.loop(0, width // chunk)
            def _(part):
                wide = pl.ds(pl.multiple_of(part * chunk, chunk), chunk)
                row_grad_ref[:, wide] = dot_tn(chosen[0], rows[:, wide])

        @pl.when(turn == 0)
        def _():
            wait_back(second_back)
            start_back(third_back, order(third_back)[0])

        @pl.when(turn == 1)
        def _():
            wait_back(third_back)
            start_back(0, z)

    cotangent_load = pltpu.make_async_copy(cotangent_hbm, rows.at[pl.ds(0, tokens)], load_sem)
    cotangent_load.start()

    @pl.loop(1, planes)
    def _(offset):
        other = (z + offset) % planes
        wait_bytes(share_home.at[other], sum_share_recv.at[other])

        @pl.when(jnp.abs(other - z) < planes - 1)
        def _():
            wait_bytes(partial_in.at[other], sum_recv.at[other])

            @pl.loop(0, width // chunk)
            def _(part):
                wide = pl.ds(pl.multiple_of(part * chunk, chunk), chunk)
                row_grad_ref[:, wide] += partial_in[other, :, wide].astype(F32)

    @pl.loop(1, planes)
    def _(offset):
        other = (z + offset) % planes
        wait_bytes(plane_rows.at[other], sum_send.at[other])
        wait_bytes(share_home.at[other], sum_share_send.at[other])

    cotangent_load.wait()
    middle_load.wait()
    depth = width // shards
    share_grad = jnp.concatenate([share_grad_ref[index] for index in range(experts)], axis=0)
    shares = jnp.concatenate([share_ref[index] for index in range(experts)], axis=0)
    center = jnp.sum(shares * share_grad, axis=0, keepdims=True)
    logit_grad_ref[...] = (shares * (share_grad - center)).astype(BF16)
    for part in range(shards):
        wide = slice(part * depth, (part + 1) * depth)
        row_grad_ref[:, wide] += dot_tn(logit_grad_ref[...], small_ref[part, :experts, :].astype(BF16))
    ffn_row = jnp.concatenate([small_ref[part, experts : experts + 1, :] for part in range(shards)], axis=1)

    def finish_rows(piece, gain_grad):
        at = pl.ds(pl.multiple_of(piece * 64, 64), 64)
        normed, scaling = norm_forward(middle[at, :])
        second_grad = row_grad_ref[at, :]
        grad = rows[at, :].astype(F32) + norm_backward(second_grad * ffn_row, normed, scaling)
        row_grad_ref[at, :] = grad
        rows[pl.ds(pl.multiple_of(tokens + piece * 64, 64), 64), :] = grad.astype(BF16)
        return gain_grad + jnp.sum(second_grad * normed, axis=0, keepdims=True)

    gain_grad_ref[...] = lax.fori_loop(0, tokens // 64, finish_rows, jnp.zeros((1, width), F32))
    low_store = pltpu.make_async_copy(rows.at[pl.ds(tokens, tokens)], low_grad_hbm, middle_sem)
    low_store.start()
    wait_back(0)
    wait_back(first_back)
    low_store.wait()


def run_experts(planes, across, shards, capacity, own, shares, slots, my_slots, w_gate, w_up, w_down, small_all, top_rows, middle, cotangent):
    tokens, width = own.shape
    in_plane = across * shards
    count = in_plane * capacity
    units = w_gate.shape[1]
    experts = planes * in_plane
    hbm = pl.BlockSpec(memory_space=pl.ANY)
    vmem = pl.BlockSpec(memory_space=pltpu.VMEM)
    dma = pltpu.SemaphoreType.DMA
    flops = 12 * planes * count * width * units
    return pl.pallas_call(
        functools.partial(expert_kernel, planes, across, shards, capacity),
        in_specs=[vmem] * 8 + [hbm] * 3,
        out_specs=[hbm] * 7 + [vmem, hbm, vmem, vmem],
        out_shape=[
            jax.ShapeDtypeStruct((planes, count, width), BF16),
            jax.ShapeDtypeStruct((planes, count, width), BF16),
            jax.ShapeDtypeStruct((planes, count, width), BF16),
            jax.ShapeDtypeStruct((planes, count, units), BF16),
            jax.ShapeDtypeStruct((planes, count, units), BF16),
            jax.ShapeDtypeStruct((planes, count, units), BF16),
            jax.ShapeDtypeStruct((planes, count, width), BF16),
            jax.ShapeDtypeStruct((tokens, width), F32),
            jax.ShapeDtypeStruct((tokens, width), BF16),
            jax.ShapeDtypeStruct((experts, tokens), BF16),
            jax.ShapeDtypeStruct((1, width), F32),
        ],
        scratch_shapes=[
            pltpu.VMEM((experts, 1, tokens), F32),
            pltpu.VMEM((tokens, width), F32),
            pltpu.VMEM((planes, tokens, width), BF16),
            pltpu.VMEM((planes, in_plane, 1, tokens), F32),
            pltpu.VMEM((planes, in_plane, 1, tokens), F32),
            pltpu.VMEM((planes, in_plane, 1, tokens), F32),
            pltpu.VMEM((planes, in_plane, 1, tokens), F32),
            pltpu.VMEM((planes, count, width), BF16),
            pltpu.VMEM((planes, count, tokens), BF16),
            pltpu.VMEM((count, width), BF16),
            pltpu.VMEM((count, width), BF16),
            pltpu.VMEM((count, units), BF16),
            pltpu.VMEM((count, units), BF16),
            pltpu.VMEM((count, units), BF16),
            pltpu.VMEM((count, 128), F32),
            pltpu.VMEM((planes, tokens, width), BF16),
            dma((2, planes + 1)), dma((2, planes + 1)), dma((planes,)), dma((planes,)),
            dma((planes,)), dma((planes,)), dma((planes,)), dma((planes,)),
            dma((planes,)), dma((planes,)), dma((planes,)), dma((planes,)),
            dma((planes,)), dma((planes,)), dma((planes,)), dma((planes,)),
            dma, dma, dma((5,)), dma,
        ],
        compiler_params=pltpu.CompilerParams(vmem_limit_bytes=VMEM_LIMIT, collective_id=1, has_side_effects=True),
        cost_estimate=pl.CostEstimate(flops=4 * flops, bytes_accessed=100 * 10**6, transcendentals=2 * 10**6),
    )(own, shares, slots, my_slots, w_gate, w_up, w_down, small_all, top_rows, middle, cotangent)


def local(
    hidden_in, attn_gain, w_query, key_projection, value_projection, query_gain, key_gain, w_output, ffn_gain, w_router,
    routes, w_gate, w_up, w_down, cotangent,
):
    tokens_here, width = hidden_in.shape
    head_size = query_gain.shape[0]
    top_count = routes.shape[1]
    planes, across, shards = lax.axis_size("z"), lax.axis_size("x"), lax.axis_size("w")
    rings = planes * across
    device_count = rings * shards
    in_plane = across * shards
    experts = device_count
    capacity = 5 * tokens_here * top_count // (4 * experts)
    seq_length = tokens_here * shards

    cosine, sine = rope_tables(seq_length, head_size)
    query_gain_row, key_gain_row = query_gain[None, :], key_gain[None, :]

    capacity = -(-capacity // 16) * 16
    small = jnp.concatenate([w_router.T, ffn_gain[None, :], attn_gain[None, :]], axis=0).astype(F32)
    small = jnp.pad(small, ((0, -small.shape[0] % 8), (0, 0)))
    (
        first_input, query_raw, key_raw, value, attended, middle, slots_flat, my_slots, shares, squares, second_input,
        small_all, weights, top_rows,
    ) = run_forward(
        planes, across, shards, capacity, hidden_in, small, routes.T, cotangent, w_query, key_projection,
        value_projection, query_gain_row, key_gain_row, cosine, sine, w_output,
    )
    (
        rows_in, _, weighted, hidden_units, gate_grad, up_grad, pair_grad, middle_grad, low_grad, logit_grad, ffn_gain_grad,
    ) = run_experts(
        planes, across, shards, capacity, second_input, shares, slots_flat, my_slots, w_gate[0], w_up[0], w_down[0],
        small_all, top_rows, middle, cotangent,
    )
    units = w_gate.shape[2]
    router_grad = dot_tn(second_input, logit_grad.T)
    wo_grad, wq_grad, first_part, query_gain_grad, key_gain_grad, _, expert_sum = run_backward(
        planes, across, shards, capacity, low_grad, w_output, attended, query_raw, key_raw, value,
        first_input, weights, query_gain_row, key_gain_row, cosine, sine, slots_flat, weighted,
    )
    mine = width // device_count
    early = jnp.concatenate(
        [router_grad.reshape(device_count, mine * experts), ffn_gain_grad.reshape(device_count, mine)], axis=1
    )
    early = jnp.pad(early, ((0, 0), (0, -early.shape[1] % 1024))).reshape(device_count, -1, 128)
    (
        sum_query, sum_key, sum_value, sum_output, hidden_out, grad_in, early_total, late_total, grad_gate, grad_up, grad_down,
    ) = run_reduce(
        planes, across, shards, wq_grad, wo_grad, first_part, hidden_in, middle, expert_sum, middle_grad, small_all, early,
        query_gain_grad, key_gain_grad, squares, rows_in.reshape(-1, width), gate_grad.reshape(-1, units), up_grad.reshape(-1, units),
        hidden_units.reshape(-1, units), pair_grad.reshape(-1, width), w_query.shape[1], key_projection.shape[1],
    )
    early_total = early_total.reshape(-1)
    sum_router = early_total[: mine * experts].reshape(mine, experts)
    sum_ffn = early_total[mine * experts : mine * (experts + 1)]
    linear = (lax.axis_index("z") * across + lax.axis_index("x")) * shards + lax.axis_index("w")
    sum_attn = lax.dynamic_slice_in_dim(late_total[: width // 128].reshape(-1), linear * mine, mine)
    late_total = late_total[width // 128 :]
    totals = jnp.concatenate([late_total[0], late_total[1], late_total[2, :4]])
    root_mean_squares = jnp.sqrt(totals[2 * head_size :] / (tokens_here * device_count * width))
    return (
        hidden_out,
        grad_in,
        sum_attn,
        sum_query,
        sum_key,
        sum_value,
        totals[:head_size],
        totals[head_size : 2 * head_size],
        sum_output,
        sum_ffn,
        sum_router,
        grad_gate[None],
        grad_up[None],
        grad_down[None],
        root_mean_squares,
    )


def solution(mesh):
    rings, shards = mesh.shape["ep"], mesh.shape["ws"]
    planes = 4 if rings % 4 == 0 else 1
    fine = Mesh(mesh.devices.reshape(planes, rings // planes, shards), ("z", "x", "w"))
    every = ("z", "x", "w")
    rows, deep = P(every, None), P(every, None, None)
    return jax.shard_map(
        local,
        mesh=fine,
        in_specs=(
            rows, P("w"), P("w", None), P("w", None), P("w", None), P(), P(), P("w", None), P("w"), P("w", None),
            rows, deep, deep, deep, rows,
        ),
        out_specs=(
            rows, rows, P(every), rows, rows, rows, P(), P(), rows, P(every), rows, deep, deep, deep, P(),
        ),
        check_vma=False,
    )
```

```python
import functools

import jax
import jax.numpy as jnp
import numpy as np
from jax import lax
from jax.experimental import pallas as pl
from jax.experimental.pallas import tpu as pltpu
from jax.sharding import Mesh
from jax.sharding import PartitionSpec as P

BLOCK = 256
EPS = 1e-06
ROPE_BASE = 1000000.0
F32 = jnp.float32
BF16 = jnp.bfloat16
VMEM_LIMIT = 65024 * 1024


def dot(left, right):
    return jnp.dot(left, right, preferred_element_type=F32)


def dot_tn(left, right):
    return lax.dot_general(left, right, (((0,), (0,)), ((), ())), preferred_element_type=F32)


def dot_nt(left, right):
    return lax.dot_general(left, right, (((1,), (1,)), ((), ())), preferred_element_type=F32)


def rope_tables(seq_length, head_size):
    indices = np.arange(head_size // 2, dtype=np.float32)
    frequency = (np.float32(ROPE_BASE) ** (np.float32(-2.0) * indices / np.float32(head_size))).astype(np.float32)
    angles = np.arange(seq_length, dtype=np.float32)[:, None] * frequency[None, :]
    cosine, sine = np.cos(angles), np.sin(angles)
    return np.concatenate([cosine, cosine], axis=1), np.concatenate([-sine, sine], axis=1)


def norm_forward(values):
    scaling = lax.rsqrt(jnp.mean(values * values, axis=-1, keepdims=True) + EPS)
    return values * scaling, scaling


def norm_backward(grad_normed, normed, scaling):
    return scaling * (grad_normed - normed * jnp.mean(grad_normed * normed, axis=-1, keepdims=True))


def half_turn(values):
    return pltpu.roll(values, values.shape[-1] // 2, 1)


def rotate(values, cosine, signed_sine):
    return values * cosine + half_turn(values) * signed_sine


def unrotate(grads, cosine, signed_sine):
    return grads * cosine - half_turn(grads) * signed_sine


MESH = pl.DeviceIdType.MESH


def remote(source, target, send, recv, device):
    return pltpu.make_async_remote_copy(
        src_ref=source, dst_ref=target, send_sem=send, recv_sem=recv, device_id=device, device_id_type=MESH
    )


def wait_bytes(ref, sem):
    pltpu.make_async_copy(ref, ref, sem).wait()


def line_order(z, planes, step):
    low = jnp.minimum(z, planes - 1 - z)
    paired = (step <= 2 * low).astype(jnp.int32)
    hop = paired * ((step + 1) // 2) + (1 - paired) * (step - low)
    longer = (z > planes - 1 - z).astype(jnp.int32)
    below = paired * (step % 2) + (1 - paired) * longer
    return z + hop - 2 * below * hop, hop, below


def greet_plane_and_line(planes, across, shards):
    z, x, w = lax.axis_index("z"), lax.axis_index("x"), lax.axis_index("w")
    in_plane = across * shards
    me = x * shards + w
    barrier = pltpu.get_barrier_semaphore()

    @pl.loop(1, in_plane)
    def _(offset):
        index = (me + offset) % in_plane
        pl.semaphore_signal(barrier, inc=1, device_id=(z, index // shards, index % shards), device_id_type=MESH)

    @pl.loop(1, planes)
    def _(offset):
        pl.semaphore_signal(barrier, inc=1, device_id=((z + offset) % planes, x, w), device_id_type=MESH)

    pl.semaphore_wait(barrier, in_plane + planes - 2)


def attention_forward(
    planes, across, shards, capacity, heads_a_step,
    own_ref, small_ref, routes_ref, top_ref, wq_hbm, wk_hbm, wv_hbm, query_gain_ref, key_gain_ref, cosine_ref, sine_ref, wo_ref,
    input_ref, query_raw_ref, key_raw_ref, value_ref, attended_ref, middle_ref, slots_ref, my_slots_ref, shares_ref, squares_ref,
    second_hbm, small_hbm,
    weights_hbm, top_rows_hbm,
    hidden, small_in, weights, key_rot_ref, routes_in, far_slots, plane_rows, stage, chosen, pair_out, far_out,
    gather_send, gather_recv, small_send, small_recv, weight_send, weight_recv, route_send, route_recv, plane_route_send,
    plane_route_recv, far_send, far_recv,
    line_send, line_recv, top_send, top_recv, pair_send, pair_recv, store_sem, small_sem, second_sem,
):
    step = pl.program_id(0)
    head_size = cosine_ref.shape[1]
    last = wo_ref.shape[0] // (heads_a_step * head_size)
    seq_length = cosine_ref.shape[0]
    blocks = seq_length // BLOCK
    factor = head_size ** (-0.5)
    z, x, w = lax.axis_index("z"), lax.axis_index("x"), lax.axis_index("w")
    in_plane = across * shards
    tokens, width = own_ref.shape
    me = x * shards + w
    depth = width // shards
    experts = planes * in_plane
    wide = heads_a_step * head_size
    chunk = 512
    targets = in_plane // 2
    pair, core = w // 2, w % 2
    sibling, opposite, other = pair * 2 + 1 - core, (1 - pair) * 2 + core, (1 - pair) * 2 + 1 - core

    def slice_of(index):
        return pl.ds(pl.multiple_of(index * capacity, 16), capacity)

    def tokens_of(index):
        return pl.ds(pl.multiple_of(index * tokens, tokens), tokens)

    def gather_copy(kind, owner, target):
        return remote(
            hidden.at[tokens_of(owner)], hidden.at[tokens_of(owner)], gather_send.at[kind], gather_recv.at[kind],
            (z, x, target),
        )

    def small_copy(offset):
        return remote(small_ref, small_in.at[w], small_send.at[offset], small_recv.at[w], (z, x, (w + offset) % shards))

    def columns_at(start, size):
        return pl.ds(pl.multiple_of(start, 128), size)

    my_depth = pl.ds(pl.multiple_of(w * depth, 16), depth)
    query_wide = last * wide

    def weight_pieces(piece, target):
        if piece is None:
            key_at, value_at = columns_at(target * head_size, head_size), columns_at(target * head_size, head_size)
            return [
                (wk_hbm.at[:, key_at], weights.at[my_depth, columns_at(last * wide, head_size)], last),
                (wv_hbm.at[:, value_at], weights.at[my_depth, columns_at(last * wide + head_size, head_size)], last),
            ]
        return [
            (
                wq_hbm.at[:, columns_at(target * query_wide + piece * wide, wide)],
                weights.at[my_depth, columns_at(piece * wide, wide)], piece,
            )
        ]

    def start_weights(piece):
        @pl.loop(1, shards)
        def _(offset):
            for source, goal, sem in weight_pieces(piece, (w + offset) % shards):
                remote(source, goal, weight_send.at[sem], weight_recv.at[sem], (z, x, (w + offset) % shards)).start()

        for source, goal, sem in weight_pieces(piece, w):
            pltpu.make_async_copy(source, goal, weight_recv.at[sem]).start()

    def wait_weights(piece):
        whole_piece = weights.at[:, columns_at(piece * wide, wide)]
        wait_bytes(whole_piece, weight_recv.at[piece])

    def half_of(half):
        return pl.ds(half * (width // 2), width // 2)

    def line_copy(column, block, hop, direction, half):
        rows = plane_rows.at[column, block, :, half_of(half)]
        return remote(
            rows, rows, line_send.at[column, direction, hop, half], line_recv.at[column, direction, hop, half],
            (z + 1 - 2 * direction, x, w),
        )

    def start_line(column, block, hop, upward, downward):
        for half in range(2):

            @pl.when(upward & (z + 1 < planes))
            def _():
                line_copy(column, block, hop, 0, half).start()

            @pl.when(downward & (z > 0))
            def _():
                line_copy(column, block, hop, 1, half).start()

    def relay_half(column, hop, half):
        @pl.when(z - hop >= 0)
        def _():
            wait_bytes(plane_rows.at[column, 0, :, half_of(half)], line_recv.at[column, 0, hop, half])

            @pl.when(z + 1 < planes)
            def _():
                line_copy(column, z - hop, hop + 1, 0, half).start()

        @pl.when(z + hop < planes)
        def _():
            wait_bytes(plane_rows.at[column, 0, :, half_of(half)], line_recv.at[column, 1, hop, half])

            @pl.when(z > 0)
            def _():
                line_copy(column, z + hop, hop + 1, 1, half).start()

    def relay(column, hop):
        for half in range(2):
            relay_half(column, hop, half)

    expert_of = z * in_plane + lax.broadcasted_iota(jnp.int32, (in_plane, tokens), 0)
    earlier = (
        lax.broadcasted_iota(jnp.int32, (tokens, tokens), 0) < lax.broadcasted_iota(jnp.int32, (tokens, tokens), 1)
    ).astype(F32).astype(BF16)
    slot_ids = lax.broadcasted_iota(jnp.int32, (capacity, tokens), 0)

    def fill_slots(column, table):
        @pl.loop(0, planes)
        def _(block):
            hits = jnp.zeros((in_plane, tokens), F32)
            for k in range(routes_ref.shape[0]):
                hits += (routes_in[column, block, k : k + 1, :] == expert_of).astype(F32)
            ranks = dot(hits.astype(BF16), earlier).astype(jnp.int32)
            slots = jnp.where(hits > 0.0, ranks, -1)
            for index in range(in_plane):
                table[block * in_plane + index] = slots[index : index + 1, :]

    def pack(column, turn, table, halves=(0, 1)):
        block, _, _ = line_order(z, planes, turn)

        def index_of(target):
            return (target // 2) * shards + pair * 2 + target % 2

        for target in range(targets):
            slots = table[block * in_plane + index_of(target)]
            chosen[target * capacity : (target + 1) * capacity, :] = (slot_ids == slots).astype(F32).astype(BF16)

        wide_at = pl.ds(halves[0] * (width // 2), len(halves) * (width // 2))

        @pl.loop(halves[0] * (width // 2) // chunk, (halves[-1] + 1) * (width // 2) // chunk)
        def _(part):
            here = pl.ds(pl.multiple_of(part * chunk, chunk), chunk)
            stage[column, turn, :, here] = dot(chosen[...], plane_rows[column, block, :, here]).astype(BF16)

        source = x * shards + (w if column == 0 else opposite)
        mine = x * 2 + core

        @pl.loop(1, targets)
        def _(offset):
            target = (mine + offset) % targets
            remote(
                stage.at[column, turn, slice_of(target), wide_at], top_rows_hbm.at[block, slice_of(source), wide_at],
                top_send.at[column, turn], top_recv.at[block], (z, target // 2, pair * 2 + target % 2),
            ).start()

        pltpu.make_async_copy(
            stage.at[column, turn, slice_of(mine), wide_at], top_rows_hbm.at[block, slice_of(source), wide_at],
            top_recv.at[block],
        ).start()

    def route_copy(offset):
        return remote(
            routes_ref, routes_in.at[me, z], route_send.at[offset], route_recv.at[z], ((z + offset) % planes, x, w)
        )

    far_top = remote(top_ref, plane_rows.at[1, z], far_send, far_recv, (z, x, opposite))
    opposite_me = x * shards + opposite

    def plane_route_copy(index):
        return remote(
            routes_in.at[me], routes_in.at[me], plane_route_send, plane_route_recv.at[me],
            (z, index // shards, index % shards),
        )

    def fill_my_slots():
        my_expert = z * in_plane + me

        @pl.loop(0, planes)
        def _(block):
            hits = jnp.concatenate(
                [
                    jnp.max((routes_in[index, block] == my_expert).astype(F32), axis=0, keepdims=True)
                    for index in range(in_plane)
                ],
                axis=0,
            )
            ranks = dot(hits.astype(BF16), earlier).astype(jnp.int32)
            slots = jnp.where(hits > 0.0, ranks, -1)
            for index in range(in_plane):
                my_slots_ref[block * in_plane + index] = slots[index : index + 1, :]

    @pl.when(step == 0)
    def _():
        greet_plane_and_line(planes, across, shards)
        far_top.start()

        @pl.loop(1, planes)
        def _(offset):
            route_copy(offset).start()

        @pl.loop(1, shards)
        def _(offset):
            small_copy(offset).start()

        plane_rows[0, z] = top_ref[...]
        start_line(0, z, 1, True, True)
        hidden[tokens_of(w), :] = own_ref[...]
        gather_copy(0, w, sibling).start()
        small_in[w] = small_ref[...]
        routes_in[me, z] = routes_ref[...]

        @pl.loop(1, planes)
        def _(offset):
            source = (z + offset) % planes
            wait_bytes(routes_in.at[me, source], route_recv.at[source])

        @pl.loop(1, in_plane)
        def _(offset):
            plane_route_copy((me + offset) % in_plane).start()

        fill_slots(me, slots_ref)
        pack(0, 0, slots_ref)
        gather_copy(1, w, opposite).start()
        relay(0, 1)
        wait_bytes(plane_rows.at[1, z], far_recv)
        start_line(1, z, 1, True, True)
        start_weights(None)
        wait_bytes(routes_in.at[opposite_me], plane_route_recv.at[opposite_me])
        fill_slots(opposite_me, far_slots)
        pack(1, 0, far_slots)
        wait_bytes(hidden.at[tokens_of(opposite)], gather_recv.at[1])
        gather_copy(2, opposite, sibling).start()
        start_weights(0)
        pack(0, 1, slots_ref)

        @pl.loop(1, shards)
        def _(offset):
            source = (w + offset) % shards
            wait_bytes(small_in.at[source], small_recv.at[source])

        wait_bytes(hidden.at[tokens_of(sibling)], gather_recv.at[0])
        wait_bytes(hidden.at[tokens_of(other)], gather_recv.at[2])
        for block in range(blocks):
            rows = pl.ds(block * BLOCK, BLOCK)
            normed, _ = norm_forward(hidden[rows, :].astype(F32))
            for part in range(shards):
                here = slice(part * depth, (part + 1) * depth)
                input_ref[rows, here] = (normed[:, here] * small_in[part, experts + 1 : experts + 2, :]).astype(BF16)
        relay(0, 2)
        start_weights(1)
        pack(0, 2, slots_ref)
        wait_weights(last)
        for block in range(blocks):
            rows = pl.ds(block * BLOCK, BLOCK)
            key_value = dot(input_ref[rows, :], weights[:, columns_at(last * wide, wide)])
            key_raw = key_value[:, :head_size]
            key_raw_ref[rows, :] = key_raw
            value_ref[rows, :] = key_value[:, head_size:].astype(BF16)
            key_normed, _ = norm_forward(key_raw)
            key_rot_ref[rows, :] = rotate(
                key_normed * key_gain_ref[...], cosine_ref[rows, :], sine_ref[rows, :]
            ).astype(BF16)
        relay(1, 1)
        pack(1, 1, far_slots)

    for piece in range(2, last):

        @pl.when(step == piece - 2)
        def _():
            wait_weights(piece - 2)
            if piece == last - 1:
                for kind in range(3):
                    wait_bytes(hidden.at[tokens_of(w)], gather_send.at[kind])
            start_weights(piece)

    @pl.when((step >= last - 2) & (step < last))
    def _():
        wait_weights(step)

    @pl.when(step < last)
    def _():
        here = columns_at(step * wide, wide)
        for block in range(blocks):
            rows = pl.ds(block * BLOCK, BLOCK)
            seen = pl.ds(0, (block + 1) * BLOCK)
            query_raw = dot(input_ref[rows, :], weights[:, here])
            query_raw_ref[rows, :] = query_raw

            @pl.loop(0, heads_a_step)
            def _(head):
                query_normed, _ = norm_forward(query_raw_ref[rows, columns_at(head * head_size, head_size)])
                query_rot = rotate(
                    query_normed * query_gain_ref[...], cosine_ref[rows, :], sine_ref[rows, :]
                ).astype(BF16)
                scores = dot_nt(query_rot, key_rot_ref[seen, :]) * factor
                exponent = jnp.exp(scores - jnp.max(scores, axis=-1, keepdims=True))
                probs = (exponent / jnp.sum(exponent, axis=-1, keepdims=True)).astype(BF16)
                attended_ref[rows, columns_at(step * wide + head * head_size, head_size)] = dot(
                    probs, value_ref[seen, :]
                ).astype(BF16)

    @pl.when(step == 1)
    def _():
        relay(0, 3)
        pack(0, 3, slots_ref)

    @pl.when(step == 3)
    def _():
        relay(1, 2)
        pack(1, 2, far_slots)

    def project(owner, goal, added):
        rows = tokens_of(owner)

        @pl.loop(0, width // chunk)
        def _(part):
            here = pl.ds(pl.multiple_of(part * chunk, chunk), chunk)
            value = dot(attended_ref[rows, :], wo_ref[:, here])
            if added is not None:
                value += hidden[added, here].astype(F32)
            goal[:, here] = value.astype(goal.dtype)

    def pair_copy(kind):
        at = pl.ds(kind * tokens, tokens)
        return remote(pair_out.at[kind], hidden.at[at], pair_send.at[kind], pair_recv.at[kind], (z, x, sibling))

    far_at = pl.ds(2 * tokens, tokens)
    far_copy = remote(far_out, hidden.at[far_at], pair_send.at[2], pair_recv.at[2], (z, x, opposite))

    @pl.when(step == last)
    def _():
        store = pltpu.make_async_copy(weights, weights_hbm, store_sem)
        store.start()
        small_store = pltpu.make_async_copy(small_in, small_hbm, small_sem)
        small_store.start()
        project(other, pair_out.at[0], None)
        pair_copy(0).start()
        project(sibling, pair_out.at[1], None)
        pair_copy(1).start()
        wait_bytes(hidden.at[pl.ds(0, tokens)], pair_recv.at[0])
        project(opposite, far_out, pl.ds(0, tokens))
        far_copy.start()
        wait_bytes(hidden.at[pl.ds(tokens, tokens)], pair_recv.at[1])
        project(w, middle_ref, pl.ds(tokens, tokens))
        @pl.loop(1, in_plane)
        def _(offset):
            index = (me + offset) % in_plane

            @pl.when(index != opposite_me)
            def _():
                wait_bytes(routes_in.at[index], plane_route_recv.at[index])

        fill_my_slots()
        for half in range(2):
            relay_half(1, 3, half)
            pack(1, 3, far_slots, (half,))
        wait_bytes(hidden.at[far_at], pair_recv.at[2])
        wait_bytes(far_out, pair_send.at[2])
        ffn_row = jnp.concatenate([small_in[part, experts : experts + 1, :] for part in range(shards)], axis=1)

        def finish_rows(piece, carry):
            at = pl.ds(pl.multiple_of(piece * 64, 64), 64)
            far = pl.ds(pl.multiple_of(2 * tokens + piece * 64, 64), 64)
            branch = middle_ref[at, :] + hidden[far, :].astype(F32)
            source = own_ref[at, :].astype(F32)
            middle = source + branch
            middle_ref[at, :] = middle
            normed, _ = norm_forward(middle)
            far_out[at, :] = (normed * ffn_row).astype(BF16)
            return (
                carry[0] + jnp.sum(jnp.sum(source * source, axis=1, keepdims=True), axis=0, keepdims=True),
                carry[1] + jnp.sum(jnp.sum(branch * branch, axis=1, keepdims=True), axis=0, keepdims=True),
            )

        zero = jnp.zeros((1, 1), F32)
        source_square, branch_square = lax.fori_loop(0, tokens // 64, finish_rows, (zero, zero))
        second_store = pltpu.make_async_copy(far_out, second_hbm, second_sem)
        second_store.start()
        lane = lax.broadcasted_iota(jnp.int32, (8, 128), 1)
        row = lax.broadcasted_iota(jnp.int32, (8, 128), 0)
        values = jnp.where(lane == 0, source_square, 0.0) + jnp.where(lane == 1, branch_square, 0.0)
        squares_ref[...] = jnp.where(row == 2, values, 0.0)
        logits = jnp.zeros((experts, tokens), F32)
        for part in range(shards):
            logits += dot_nt(small_in[part, :experts, :].astype(BF16), far_out[:, part * depth : (part + 1) * depth])
        expert_ids = lax.broadcasted_iota(jnp.int32, (experts, tokens), 0)
        hits = jnp.zeros((experts, tokens), F32)
        for k in range(routes_ref.shape[0]):
            hits += (routes_ref[k : k + 1, :] == expert_ids).astype(F32)
        routed = hits > 0.0
        peaks = jnp.max(jnp.where(routed, logits, -jnp.inf), axis=0, keepdims=True)
        shifted = jnp.where(routed, jnp.exp(jnp.where(routed, logits - peaks, 0.0)), 0.0)
        shares = shifted / jnp.sum(shifted, axis=0, keepdims=True)
        for expert in range(experts):
            shares_ref[expert] = shares[expert : expert + 1, :]

        @pl.loop(0, planes)
        def _(block):
            wait_bytes(top_rows_hbm.at[block], top_recv.at[block])
            if targets > 1:
                for column in range(2):
                    wait_bytes(stage.at[column, 0, pl.ds(0, (targets - 1) * capacity)], top_send.at[column, block])

        for kind in range(2):
            wait_bytes(far_out, pair_send.at[kind])

        @pl.loop(1, shards)
        def _(offset):
            wait_bytes(small_in.at[w], small_send.at[offset])

        @pl.loop(1, planes)
        def _(offset):
            wait_bytes(routes_in.at[0, 0], route_send.at[offset])

        wait_bytes(routes_in.at[pl.ds(0, in_plane - 1)], plane_route_send)
        wait_bytes(plane_rows.at[1, 0], far_send)

        @pl.loop(0, last + 1)
        def _(piece):
            wait_bytes(weights.at[pl.ds(0, (shards - 1) * depth), pl.ds(0, wide)], weight_send.at[piece])

        for column in range(2):
            for hop in range(1, planes):

                @pl.when((z - (hop - 1) >= 0) & (z + 1 < planes))
                def _():
                    for half in range(2):
                        wait_bytes(plane_rows.at[0, 0, :, half_of(half)], line_send.at[column, 0, hop, half])

                @pl.when((z + (hop - 1) < planes) & (z > 0))
                def _():
                    for half in range(2):
                        wait_bytes(plane_rows.at[0, 0, :, half_of(half)], line_send.at[column, 1, hop, half])

        store.wait()
        small_store.wait()
        second_store.wait()


def attention_backward(
    planes, across, shards, capacity, heads_a_step,
    own_grad_ref, wo_ref, attended_ref, query_raw_ref, key_raw_ref, value_ref, input_ref, wq_ref,
    query_gain_ref, key_gain_ref, cosine_ref, sine_ref, slots_ref, weighted_hbm,
    wo_grad_ref, wq_grad_ref, first_grad_ref, query_gain_grad_ref, key_gain_grad_ref, returned_hbm, expert_sum_ref,
    total_ref, key_rot_ref, key_grad_ref, value_grad_ref, query_grad_ref, turned_ref, grad_ref,
    rows, chosen, partial_out, partial_in,
    gather_send, gather_recv, back_send, back_recv, sum_send, sum_recv, load_sem,
):
    step = pl.program_id(0)
    last = pl.num_programs(0) - 1
    head_size = cosine_ref.shape[1]
    seq_length = cosine_ref.shape[0]
    blocks = seq_length // BLOCK
    factor = head_size ** (-0.5)
    z, x, w = lax.axis_index("z"), lax.axis_index("x"), lax.axis_index("w")
    in_plane = across * shards
    me = x * shards + w
    tokens, width = own_grad_ref.shape
    count = in_plane * capacity
    chunk = 512
    pair, core = w // 2, w % 2
    sibling, opposite, other = pair * 2 + 1 - core, (1 - pair) * 2 + core, (1 - pair) * 2 + 1 - core

    def slice_of(index):
        return pl.ds(pl.multiple_of(index * capacity, 16), capacity)

    def tokens_of(index):
        return pl.ds(pl.multiple_of(index * tokens, tokens), tokens)

    def gather_copy(kind, owner, target):
        return remote(
            grad_ref.at[tokens_of(owner)], grad_ref.at[tokens_of(owner)], gather_send.at[kind], gather_recv.at[kind],
            (z, x, target),
        )

    def back_copy(block, index):
        return remote(
            weighted_hbm.at[block, slice_of(index)], returned_hbm.at[block, slice_of(me)],
            back_send.at[block], back_recv.at[block], (z, index // shards, index % shards),
        )

    pace = [(1, 0), (2, 1), (3, 2)]

    def start_back(turn, near, far):
        block, _, _ = line_order(z, planes, planes - 1 - turn)

        @pl.loop(1, in_plane)
        def _(offset):
            index = (me + offset) % in_plane
            beside = (index % shards) // 2 == pair

            @pl.when((beside & near) | (jnp.logical_not(beside) & far))
            def _():
                back_copy(block, index).start()

        @pl.when(near)
        def _():
            pltpu.make_async_copy(
                weighted_hbm.at[block, slice_of(me)], returned_hbm.at[block, slice_of(me)], back_recv.at[block]
            ).start()

    def sum_copy(block):
        return remote(partial_out.at[block], partial_in.at[z], sum_send.at[block], sum_recv.at[z], (block, x, w))

    def combine(turn):
        place = planes - 1 - turn
        block, _, _ = line_order(z, planes, place)
        wait_bytes(returned_hbm.at[block], back_recv.at[block])
        load = pltpu.make_async_copy(returned_hbm.at[block], rows, load_sem)
        load.start()
        if place > 0:
            start_back(turn + 1, step >= 0, step >= 0)
        slot_ids = lax.broadcasted_iota(jnp.int32, (capacity, tokens), 0)

        @pl.loop(0, in_plane)
        def _(index):
            slots = slots_ref[block * in_plane + index]
            chosen[slice_of(index), :] = (slot_ids == slots).astype(F32).astype(BF16)

        load.wait()

        @pl.loop(0, width // chunk)
        def _(part):
            wide = pl.ds(pl.multiple_of(part * chunk, chunk), chunk)
            summed = dot_tn(chosen[...], rows[:, wide])
            if place > 0:
                partial_out[block, :, wide] = summed.astype(BF16)
            else:
                expert_sum_ref[:, wide] = summed

        if place > 0:
            sum_copy(block).start()

    @pl.when(step == 0)
    def _():
        greet_plane_and_line(planes, across, shards)
        grad_ref[tokens_of(w), :] = own_grad_ref[...]
        gather_copy(1, w, opposite).start()
        gather_copy(0, w, sibling).start()
        start_back(0, step == 0, step != 0)
        key_normed, _ = norm_forward(key_raw_ref[...])
        key_rot_ref[...] = rotate(key_normed * key_gain_ref[...], cosine_ref[...], sine_ref[...]).astype(BF16)
        key_grad_ref[...] = jnp.zeros_like(key_grad_ref)
        value_grad_ref[...] = jnp.zeros_like(value_grad_ref)
        query_gain_grad_ref[...] = jnp.zeros_like(query_gain_grad_ref)
        for block in range(blocks):
            rows_here = pl.ds(block * BLOCK, BLOCK)
            turned_ref[:, rows_here] = input_ref[rows_here, :].T
        wait_bytes(grad_ref.at[tokens_of(opposite)], gather_recv.at[1])
        gather_copy(2, opposite, sibling).start()
        start_back(0, step != 0, step == 0)
        wait_bytes(grad_ref.at[tokens_of(sibling)], gather_recv.at[0])
        wait_bytes(grad_ref.at[tokens_of(other)], gather_recv.at[2])

    @pl.when(step < last)
    def _():
        wo_grad_ref[...] = dot_tn(attended_ref[...], grad_ref[...]).astype(BF16)
        for block in range(blocks):
            rows_here = pl.ds(block * BLOCK, BLOCK)
            seen = pl.ds(0, (block + 1) * BLOCK)
            query_grad_ref[rows_here, :] = dot_nt(grad_ref[rows_here, :], wo_ref[...]).astype(BF16)

            @pl.loop(0, heads_a_step)
            def _(head):
                columns = pl.ds(pl.multiple_of(head * head_size, head_size), head_size)
                query_normed, query_scale = norm_forward(query_raw_ref[rows_here, columns])
                cosine, sine = cosine_ref[rows_here, :], sine_ref[rows_here, :]
                query_rot = rotate(query_normed * query_gain_ref[...], cosine, sine).astype(BF16)
                head_grad = query_grad_ref[rows_here, columns]
                keys, values = key_rot_ref[seen, :], value_ref[seen, :]
                scores = dot_nt(query_rot, keys) * factor
                exponent = jnp.exp(scores - jnp.max(scores, axis=-1, keepdims=True))
                probs = exponent / jnp.sum(exponent, axis=-1, keepdims=True)
                prob_grad = dot_nt(head_grad, values)
                value_grad_ref[seen, :] += dot_tn(probs.astype(BF16), head_grad)
                center = jnp.sum(probs * prob_grad, axis=-1, keepdims=True)
                score_grad = (probs * (prob_grad - center)).astype(BF16)
                key_grad_ref[seen, :] += dot_tn(score_grad, query_rot) * factor
                query_rot_grad = dot(score_grad, keys) * factor
                unrotated = unrotate(query_rot_grad, cosine, sine)
                query_gain_grad_ref[0:1, :] += jnp.sum(unrotated * query_normed, axis=0, keepdims=True)
                query_grad_ref[rows_here, columns] = norm_backward(
                    unrotated * query_gain_ref[...], query_normed, query_scale
                ).astype(BF16)
            partial = dot_nt(query_grad_ref[rows_here, :], wq_ref[...])

            @pl.when(step == 0)
            def _():
                total_ref[rows_here, :] = partial

            @pl.when(step > 0)
            def _():
                total_ref[rows_here, :] += partial

            for turn, place in enumerate(pace):
                if place[1] == block:

                    @pl.when(step == place[0])
                    def _():
                        combine(turn)

    @pl.when(step == last)
    def _():
        key_normed, key_scale = norm_forward(key_raw_ref[...])
        unrotated = unrotate(key_grad_ref[...], cosine_ref[...], sine_ref[...])
        key_gain_grad_ref[...] = jnp.zeros_like(key_gain_grad_ref)
        key_gain_grad_ref[0:1, :] = jnp.sum(unrotated * key_normed, axis=0, keepdims=True)
        key_grad = norm_backward(unrotated * key_gain_ref[...], key_normed, key_scale)
        query_grad_ref[:, :head_size] = key_grad.astype(BF16)
        query_grad_ref[:, head_size : 2 * head_size] = value_grad_ref[...].astype(BF16)
        for block in range(blocks):
            rows_here = pl.ds(block * BLOCK, BLOCK)
            first_grad_ref[rows_here, :] = (
                total_ref[rows_here, :] + dot_nt(query_grad_ref[rows_here, :], wq_ref[...])
            ).astype(BF16)

    wq_grad_ref[...] = dot(turned_ref[...], query_grad_ref[...]).astype(BF16)

    @pl.when(step == last)
    def _():
        for turn in range(len(pace), planes):
            combine(turn)

        @pl.loop(1, planes)
        def _(offset):
            source = (z + offset) % planes
            wait_bytes(partial_in.at[source], sum_recv.at[source])

            @pl.loop(0, width // chunk)
            def _(part):
                wide = pl.ds(pl.multiple_of(part * chunk, chunk), chunk)
                expert_sum_ref[:, wide] += partial_in[source, :, wide].astype(F32)

            wait_bytes(partial_out.at[source], sum_send.at[source])

        @pl.loop(0, planes)
        def _(block):
            wait_bytes(weighted_hbm.at[block, pl.ds(0, count - capacity)], back_send.at[block])

        wait_bytes(grad_ref.at[tokens_of(w)], gather_send.at[0])
        wait_bytes(grad_ref.at[tokens_of(w)], gather_send.at[1])
        wait_bytes(grad_ref.at[tokens_of(w)], gather_send.at[2])


def whole(shape):
    return pl.BlockSpec(shape, lambda step: (0,) * len(shape), pipeline_mode=pl.Buffered(1))


def run_forward(
    planes, across, shards, capacity, own, small, routes, top, w_query, w_key, w_value, query_gain, key_gain, cosine, sine, wo
):
    tokens, width = own.shape
    seq_length = tokens * shards
    head_size = query_gain.shape[1]
    heads_here = wo.shape[0] // head_size
    pair = 2
    wide = pair * head_size
    steps = heads_here // pair
    in_plane = across * shards
    count = in_plane * capacity
    hbm = pl.BlockSpec(memory_space=pl.ANY)
    dma = pltpu.SemaphoreType.DMA
    slots_shape = (planes * in_plane, 1, tokens)
    return pl.pallas_call(
        functools.partial(attention_forward, planes, across, shards, capacity, pair),
        grid=(steps + 1,),
        in_specs=[
            whole((tokens, width)),
            whole(small.shape),
            whole(routes.shape),
            whole((tokens, width)),
            hbm,
            hbm,
            hbm,
            whole((1, head_size)),
            whole((1, head_size)),
            whole((seq_length, head_size)),
            whole((seq_length, head_size)),
            whole(wo.shape),
        ],
        out_specs=[
            whole((seq_length, width)),
            pl.BlockSpec((seq_length, wide), lambda step: (0, jnp.minimum(step, steps - 1))),
            whole((seq_length, head_size)),
            whole((seq_length, head_size)),
            whole((seq_length, heads_here * head_size)),
            whole((tokens, width)),
            whole(slots_shape),
            whole(slots_shape),
            whole(slots_shape),
            whole((8, 128)),
            hbm,
            hbm,
            hbm,
            hbm,
        ],
        out_shape=[
            jax.ShapeDtypeStruct((seq_length, width), BF16),
            jax.ShapeDtypeStruct((seq_length, heads_here * head_size), F32),
            jax.ShapeDtypeStruct((seq_length, head_size), F32),
            jax.ShapeDtypeStruct((seq_length, head_size), BF16),
            jax.ShapeDtypeStruct((seq_length, heads_here * head_size), BF16),
            jax.ShapeDtypeStruct((tokens, width), F32),
            jax.ShapeDtypeStruct(slots_shape, jnp.int32),
            jax.ShapeDtypeStruct(slots_shape, jnp.int32),
            jax.ShapeDtypeStruct(slots_shape, F32),
            jax.ShapeDtypeStruct((8, 128), F32),
            jax.ShapeDtypeStruct((tokens, width), BF16),
            jax.ShapeDtypeStruct((shards,) + small.shape, F32),
            jax.ShapeDtypeStruct((width, (steps + 1) * wide), BF16),
            jax.ShapeDtypeStruct((planes, count, width), BF16),
        ],
        scratch_shapes=[
            pltpu.VMEM((seq_length, width), BF16),
            pltpu.VMEM((shards,) + small.shape, F32),
            pltpu.VMEM((width, (steps + 1) * wide), BF16),
            pltpu.VMEM((seq_length, head_size), BF16),
            pltpu.VMEM((in_plane, planes) + routes.shape, jnp.int32),
            pltpu.VMEM(slots_shape, jnp.int32),
            pltpu.VMEM((2, planes, tokens, width), BF16),
            pltpu.VMEM((2, planes, count // 2, width), BF16),
            pltpu.VMEM((count // 2, tokens), BF16),
            pltpu.VMEM((2, tokens, width), BF16),
            pltpu.VMEM((tokens, width), BF16),
            dma((3,)), dma((3,)), dma((shards,)), dma((shards,)), dma((steps + 1,)), dma((steps + 1,)),
            dma((planes,)), dma((planes,)), dma, dma((in_plane,)), dma, dma,
            dma((2, 2, planes + 1, 2)), dma((2, 2, planes + 1, 2)), dma((2, planes)), dma((planes,)), dma((3,)), dma((3,)), dma, dma, dma,
        ],
        compiler_params=pltpu.CompilerParams(vmem_limit_bytes=VMEM_LIMIT, collective_id=5, has_side_effects=True),
        cost_estimate=pl.CostEstimate(flops=70 * 10**9, bytes_accessed=40 * 10**6, transcendentals=6 * 10**6),
    )(own, small, routes, top, w_query, w_key, w_value, query_gain, key_gain, cosine, sine, wo)


def run_backward(
    planes, across, shards, capacity, own_grad, wo, attended, query_raw, key_raw, value, first_input, weights, query_gain,
    key_gain, cosine, sine, slots, weighted,
):
    tokens, width = own_grad.shape
    seq_length = attended.shape[0]
    head_size = query_gain.shape[1]
    heads_here = wo.shape[0] // head_size
    pair = 2
    wide = pair * head_size
    steps = heads_here // pair
    count = across * shards * capacity
    hbm = pl.BlockSpec(memory_space=pl.ANY)
    dma = pltpu.SemaphoreType.DMA

    def held(step):
        return jnp.minimum(step, steps - 1)

    return pl.pallas_call(
        functools.partial(attention_backward, planes, across, shards, capacity, pair),
        grid=(steps + 1,),
        in_specs=[
            whole((tokens, width)),
            pl.BlockSpec((wide, width), lambda step: (held(step), 0)),
            pl.BlockSpec((seq_length, wide), lambda step: (0, held(step))),
            pl.BlockSpec((seq_length, wide), lambda step: (0, held(step))),
            whole((seq_length, head_size)),
            whole((seq_length, head_size)),
            whole((seq_length, width)),
            pl.BlockSpec((width, wide), lambda step: (0, step)),
            whole((1, head_size)),
            whole((1, head_size)),
            whole((seq_length, head_size)),
            whole((seq_length, head_size)),
            whole(slots.shape),
            hbm,
        ],
        out_specs=[
            pl.BlockSpec((wide, width), lambda step: (held(step), 0)),
            pl.BlockSpec((width, wide), lambda step: (0, step)),
            whole((seq_length, width)),
            whole((8, head_size)),
            whole((8, head_size)),
            hbm,
            whole((tokens, width)),
        ],
        out_shape=[
            jax.ShapeDtypeStruct((heads_here * head_size, width), BF16),
            jax.ShapeDtypeStruct((width, (steps + 1) * wide), BF16),
            jax.ShapeDtypeStruct((seq_length, width), BF16),
            jax.ShapeDtypeStruct((8, head_size), F32),
            jax.ShapeDtypeStruct((8, head_size), F32),
            jax.ShapeDtypeStruct(weighted.shape, BF16),
            jax.ShapeDtypeStruct((tokens, width), F32),
        ],
        scratch_shapes=[
            pltpu.VMEM((seq_length, width), F32),
            pltpu.VMEM((seq_length, head_size), BF16),
            pltpu.VMEM((seq_length, head_size), F32),
            pltpu.VMEM((seq_length, head_size), F32),
            pltpu.VMEM((seq_length, wide), BF16),
            pltpu.VMEM((width, seq_length), BF16),
            pltpu.VMEM((seq_length, width), BF16),
            pltpu.VMEM((count, width), BF16),
            pltpu.VMEM((count, tokens), BF16),
            pltpu.VMEM((planes, tokens, width), BF16),
            pltpu.VMEM((planes, tokens, width), BF16),
            dma((3,)), dma((3,)), dma((planes,)), dma((planes,)), dma((planes,)), dma((planes,)), dma,
        ],
        compiler_params=pltpu.CompilerParams(vmem_limit_bytes=VMEM_LIMIT, collective_id=2, has_side_effects=True),
        cost_estimate=pl.CostEstimate(flops=70 * 10**9, bytes_accessed=60 * 10**6, transcendentals=6 * 10**6),
    )(
        own_grad, wo, attended, query_raw, key_raw, value, first_input, weights, query_gain, key_gain, cosine, sine, slots,
        weighted,
    )


def reduce_kernel(
    planes, across, shards,
    wq_hbm, wo_hbm, first_hbm, hidden_ref, middle_hbm, expert_sum_hbm, middle_grad_hbm, small_ref, early_ref, query_gain_ref,
    key_gain_ref, squares_ref,
    rows_hbm, gate_grad_hbm, up_grad_hbm, units_hbm, pair_grad_hbm,
    query_ref, key_ref, value_ref, output_ref, hidden_out_ref, grad_in_ref, early_total_ref, late_total_ref,
    gate_out_hbm, up_out_hbm, down_out_hbm,
    wq_parts, wo_parts, wq_out, wo_out, wq_in, wo_in, wq_total, wo_total, wq_final, wo_final, wq_home, wo_home, first_in,
    early_in, late, late_in, held_a, held_b, side, turned, tiles, tall, flat,
    across_send, across_recv, line_send, line_recv, home_send, home_recv, swap_send, swap_recv, first_send, first_recv,
    early_send, early_recv, late_send, late_recv, held_sem, side_sem, tile_sem, result_sem,
):
    z, x, w = lax.axis_index("z"), lax.axis_index("x"), lax.axis_index("w")
    rings = planes * across
    ring = z * across + x
    everyone = rings * shards
    wq_rows, wo_rows = wq_total.shape[0], wo_total.shape[0]
    mine = wq_rows // shards
    tokens, width = grad_in_ref.shape
    query_columns = query_ref.shape[1] // shards
    key_columns = key_ref.shape[1] // shards
    linear = ring * shards + w
    barrier = pltpu.get_barrier_semaphore()

    def place(index):
        return (index // shards // across, index // shards % across, index % shards)

    @pl.loop(1, everyone)
    def _(offset):
        pl.semaphore_signal(barrier, inc=1, device_id=place((linear + offset) % everyone), device_id_type=MESH)

    pl.semaphore_wait(barrier, everyone - 1)

    def rows_of(index, size):
        return pl.ds(pl.multiple_of(index * size, 16), size)

    sources = [(wq_hbm, wq_rows, wq_parts), (wo_hbm, wo_rows, wo_parts)]

    def across_copy(kind, plane, column):
        source, rows, goal = sources[kind]
        return remote(
            source.at[rows_of(plane * across + column, rows)], goal.at[plane, x],
            across_send.at[kind, plane], across_recv.at[kind, plane], (z, column, w),
        )

    def first_copy(offset):
        target = (w + offset) % shards
        return remote(
            first_hbm.at[rows_of(target, tokens)], first_in.at[offset], first_send.at[offset], first_recv.at[offset],
            (z, x, target),
        )

    @pl.loop(1, shards)
    def _(offset):
        first_copy(offset).start()

    pltpu.make_async_copy(first_hbm.at[rows_of(w, tokens)], first_in.at[0], first_recv.at[0]).start()
    hold_a = pltpu.make_async_copy(middle_hbm, held_a, held_sem.at[0])
    hold_b = pltpu.make_async_copy(expert_sum_hbm, held_b, held_sem.at[1])
    hold_a.start()
    hold_b.start()

    def start_across(kind, turn):
        plane, _, _ = line_order(z, planes, planes - 1 - turn)

        @pl.loop(1, across)
        def _(offset):
            across_copy(kind, plane, (x + offset) % across).start()

        source, rows, goal = sources[kind]
        pltpu.make_async_copy(
            source.at[rows_of(plane * across + x, rows)], goal.at[plane, x], across_recv.at[kind, plane]
        ).start()

    start_across(1, 0)
    start_across(1, 1)

    @pl.loop(1, everyone)
    def _(offset):
        other = (linear + offset) % everyone
        remote(early_ref.at[other], early_in.at[linear], early_send, early_recv, place(other)).start()

    early_in[linear] = early_ref[linear]
    lanes = tiles.shape[2]
    per_kind = width // lanes
    depth = side.shape[0]
    late_rows = width // 128
    experts = everyone
    scale_row = jnp.concatenate([small_ref[part, experts + 1 : experts + 2, :] for part in range(shards)], axis=1)
    pick = (lax.broadcasted_iota(jnp.int32, (8, 128), 0) == 2).astype(F32)
    lane = lax.broadcasted_iota(jnp.int32, (8, 128), 1)

    def tile_copy(unit):
        slot = unit % 2
        here = pl.ds(pl.multiple_of((unit % per_kind) * lanes, lanes), lanes)

        @pl.when(unit < 2 * per_kind)
        def _():
            pltpu.make_async_copy(rows_hbm.at[:, here], tiles.at[slot], tile_sem.at[slot]).start()

        @pl.when(unit >= 2 * per_kind)
        def _():
            pltpu.make_async_copy(pair_grad_hbm.at[:, here], tiles.at[slot], tile_sem.at[slot]).start()

    tile_copy(0)

    def multiply(unit):
        slot = unit % 2
        here = pl.ds(pl.multiple_of((unit % per_kind) * lanes, lanes), lanes)
        for kind, source in enumerate([gate_grad_hbm, up_grad_hbm, units_hbm]):

            @pl.when(unit == kind * per_kind)
            def _():
                load = pltpu.make_async_copy(source, side, side_sem)
                load.start()
                load.wait()
                if kind == 2:

                    @pl.loop(0, depth // 128)
                    def _(part):
                        at = pl.ds(pl.multiple_of(part * 128, 128), 128)
                        turned[:, at] = side[at, :].T

        @pl.when(unit + 1 < 3 * per_kind)
        def _():
            tile_copy(unit + 1)

        wait_bytes(tiles.at[slot], tile_sem.at[slot])

        @pl.when(unit >= 2)
        def _():
            wait_bytes(tall.at[slot], result_sem.at[slot])

        @pl.when(unit < 2 * per_kind)
        def _():
            tall[slot] = dot_tn(tiles[slot], side[...])

        @pl.when(unit < per_kind)
        def _():
            pltpu.make_async_copy(tall.at[slot], gate_out_hbm.at[here], result_sem.at[slot]).start()

        @pl.when((unit >= per_kind) & (unit < 2 * per_kind))
        def _():
            pltpu.make_async_copy(tall.at[slot], up_out_hbm.at[here], result_sem.at[slot]).start()

        @pl.when(unit >= 2 * per_kind)
        def _():
            flat[slot] = dot(turned[...], tiles[slot])
            pltpu.make_async_copy(flat.at[slot], down_out_hbm.at[:, here], result_sem.at[slot]).start()

    def late_copy(other):
        return remote(late, late_in.at[linear], late_send, late_recv, place(other))

    def finish_rows():
        hold_a.wait()
        hold_b.wait()
        pieces = tokens // 64

        def add_rows(piece, carry):
            at = pl.ds(pl.multiple_of(piece * 64, 64), 64)
            extra = held_b[at, :]
            hidden_out_ref[at, :] = (held_a[at, :] + extra).astype(BF16)
            return carry + jnp.sum(jnp.sum(extra * extra, axis=1, keepdims=True), axis=0, keepdims=True)

        expert_square = lax.fori_loop(0, pieces, add_rows, jnp.zeros((1, 1), F32))
        load = pltpu.make_async_copy(middle_grad_hbm, held_a, held_sem.at[0])
        load.start()

        @pl.loop(0, shards)
        def _(offset):
            wait_bytes(first_in.at[offset], first_recv.at[offset])

        load.wait()

        def grad_rows(piece, carry):
            square, gain_grad = carry
            at = pl.ds(pl.multiple_of(piece * 64, 64), 64)
            first = first_in[0, at, :].astype(F32)
            for offset in range(1, shards):
                first += first_in[offset, at, :].astype(F32)
            normed, scaling = norm_forward(hidden_ref[at, :].astype(F32))
            grad = held_a[at, :] + norm_backward(first * scale_row, normed, scaling)
            grad_in_ref[at, :] = grad
            return (
                square + jnp.sum(jnp.sum(grad * grad, axis=1, keepdims=True), axis=0, keepdims=True),
                gain_grad + jnp.sum(first * normed, axis=0, keepdims=True),
            )

        square, gain_grad = lax.fori_loop(
            0, pieces, grad_rows, (jnp.zeros((1, 1), F32), jnp.zeros((1, width), F32))
        )
        for row in range(late_rows):
            late[row : row + 1, :] = gain_grad[:, row * 128 : (row + 1) * 128]
        late[late_rows:, :] = squares_ref[...] + pick * (
            jnp.where(lane == 2, expert_square, 0.0) + jnp.where(lane == 3, square, 0.0)
        )

        late[late_rows : late_rows + 1, :] = query_gain_ref[0:1, :]
        late[late_rows + 1 : late_rows + 2, :] = key_gain_ref[0:1, :]

        @pl.loop(1, everyone)
        def _(offset):
            late_copy((linear + offset) % everyone).start()

        late_in[linear] = late[...]

    outs, ins = [wq_out, wo_out], [wq_in, wo_in]
    totals, parts = [wq_total, wo_total], [wq_parts, wo_parts]

    def line_copy(kind, plane):
        up = (plane > z).astype(jnp.int32)
        ends = (plane == z + 2 * up - 1).astype(jnp.int32)
        slot = plane + ends * (1 - up) * (planes - plane)
        return remote(
            outs[kind].at[plane], ins[kind].at[slot], line_send.at[kind, plane], line_recv.at[kind, slot],
            (z + 2 * up - 1, x, w),
        )

    per_turn = 3 * per_kind // (2 * planes)

    def take(kind, slot):
        wait_bytes(ins[kind].at[slot], line_recv.at[kind, slot])
        totals[kind][...] += ins[kind][slot].astype(F32)

    def collect(kind):
        @pl.loop(0, planes)
        def _(turn):
            plane, _, _ = line_order(z, planes, planes - 1 - turn)

            @pl.loop(0, per_turn)
            def _(unit):
                multiply((turn + (1 - kind) * planes) * per_turn + unit)

            wait_bytes(parts[kind].at[plane], across_recv.at[kind, plane])

            @pl.when(turn < planes - 2)
            def _():
                start_across(kind, turn + 2)

            if kind == 1:

                @pl.when(turn >= planes - 2)
                def _():
                    start_across(0, turn + 2 - planes)

            totals[kind][...] = parts[kind][plane, 0].astype(F32)

            @pl.loop(1, across)
            def _(column):
                totals[kind][...] += parts[kind][plane, column].astype(F32)

            @pl.when(((plane > z) & (z > 0)) | ((plane < z) & (z < planes - 1)))
            def _():
                take(kind, plane)

            @pl.when(plane != z)
            def _():
                outs[kind][plane] = totals[kind][...].astype(BF16)
                line_copy(kind, plane).start()

    def finish(kind):
        @pl.when(z > 0)
        def _():
            take(kind, z)

        @pl.when(z < planes - 1)
        def _():
            take(kind, planes)

    collect(1)
    finish(1)
    wo_final[...] = wo_total[...].astype(BF16)
    goal = w * rings + ring
    stays = goal == linear
    swap = remote(
        wo_final, wo_home, swap_send, swap_recv, (goal // shards // across, goal // shards % across, goal % shards)
    )

    @pl.when(jnp.logical_not(stays))
    def _():
        swap.start()

    @pl.when(stays)
    def _():
        pltpu.make_async_copy(wo_final, wo_home, swap_recv).start()

    finish_rows()
    collect(0)
    finish(0)
    wq_final[...] = wq_total[...].astype(BF16)

    def home_copy(offset):
        target = (w + offset) % shards
        return remote(
            wq_final.at[rows_of(target, mine)], wq_home.at[w], home_send.at[offset], home_recv.at[w], (z, x, target)
        )

    @pl.loop(1, shards)
    def _(offset):
        home_copy(offset).start()

    pltpu.make_async_copy(wq_final.at[rows_of(w, mine)], wq_home.at[w], home_recv.at[w]).start()

    for part in range(shards):
        wait_bytes(wq_home.at[part], home_recv.at[part])
        rows = wq_home[part].astype(F32)
        query_ref[:, part * query_columns : (part + 1) * query_columns] = rows[:, :query_columns]
        key_ref[:, part * key_columns : (part + 1) * key_columns] = rows[:, query_columns : query_columns + key_columns]
        value_ref[:, part * key_columns : (part + 1) * key_columns] = rows[:, query_columns + key_columns :]

    wait_bytes(early_ref.at[pl.ds(0, everyone - 1)], early_recv)
    early_total_ref[...] = jnp.sum(early_in[...], axis=0)
    wait_bytes(late_in.at[pl.ds(0, everyone - 1)], late_recv)
    late_total_ref[...] = jnp.sum(late_in[...], axis=0)
    wait_bytes(early_ref.at[pl.ds(0, everyone - 1)], early_send)
    wait_bytes(late_in.at[pl.ds(0, everyone - 1)], late_send)
    for slot in range(2):
        wait_bytes(tall.at[slot], result_sem.at[slot])
    wait_bytes(wo_home, swap_recv)
    output_ref[...] = wo_home[...].astype(F32)

    @pl.when(jnp.logical_not(stays))
    def _():
        wait_bytes(wo_final, swap_send)

    @pl.loop(1, shards)
    def _(offset):
        wait_bytes(wq_home.at[0], home_send.at[offset])
        wait_bytes(first_in.at[0], first_send.at[offset])

    if across > 1:

        @pl.loop(0, planes)
        def _(plane):
            wait_bytes(wq_parts.at[plane, pl.ds(0, across - 1)], across_send.at[0, plane])
            wait_bytes(wo_parts.at[plane, pl.ds(0, across - 1)], across_send.at[1, plane])

    @pl.loop(1, planes)
    def _(offset):
        plane = (z + offset) % planes
        wait_bytes(wq_out.at[plane], line_send.at[0, plane])
        wait_bytes(wo_out.at[plane], line_send.at[1, plane])


def run_reduce(
    planes, across, shards, wq_grad, wo_grad, first_part, hidden, middle, expert_sum, middle_grad, small_all, early,
    query_gain_grad, key_gain_grad, squares, rows_in, gate_grad, up_grad, units, pair_grad, query_columns, key_columns,
):
    rings = planes * across
    everyone = rings * shards
    width = wq_grad.shape[0]
    wq_wide = wq_grad.shape[1]
    wq_rows, wo_rows = width // rings, wo_grad.shape[0] // rings
    tokens = first_part.shape[0] // shards
    mine = wq_rows // shards
    depth, wide = units.shape
    late_rows = width // 128 + 8
    hbm = pl.BlockSpec(memory_space=pl.ANY)
    vmem = pl.BlockSpec(memory_space=pltpu.VMEM)
    dma = pltpu.SemaphoreType.DMA
    return pl.pallas_call(
        functools.partial(reduce_kernel, planes, across, shards),
        in_specs=[hbm] * 3 + [vmem] + [hbm] * 3 + [vmem] * 5 + [hbm] * 5,
        out_specs=[vmem] * 8 + [hbm] * 3,
        out_shape=[
            jax.ShapeDtypeStruct((mine, query_columns), F32),
            jax.ShapeDtypeStruct((mine, key_columns), F32),
            jax.ShapeDtypeStruct((mine, key_columns), F32),
            jax.ShapeDtypeStruct((wo_rows, width), F32),
            jax.ShapeDtypeStruct((tokens, width), BF16),
            jax.ShapeDtypeStruct((tokens, width), F32),
            jax.ShapeDtypeStruct(early.shape[1:], F32),
            jax.ShapeDtypeStruct((late_rows, 128), F32),
            jax.ShapeDtypeStruct((width, wide), F32),
            jax.ShapeDtypeStruct((width, wide), F32),
            jax.ShapeDtypeStruct((wide, width), F32),
        ],
        scratch_shapes=[
            pltpu.VMEM((planes, across, wq_rows, wq_wide), BF16),
            pltpu.VMEM((planes, across, wo_rows, width), BF16),
            pltpu.VMEM((planes, wq_rows, wq_wide), BF16),
            pltpu.VMEM((planes, wo_rows, width), BF16),
            pltpu.VMEM((planes + 1, wq_rows, wq_wide), BF16),
            pltpu.VMEM((planes + 1, wo_rows, width), BF16),
            pltpu.VMEM((wq_rows, wq_wide), F32),
            pltpu.VMEM((wo_rows, width), F32),
            pltpu.VMEM((wq_rows, wq_wide), BF16),
            pltpu.VMEM((wo_rows, width), BF16),
            pltpu.VMEM((shards, mine, wq_wide), BF16),
            pltpu.VMEM((wo_rows, width), BF16),
            pltpu.VMEM((shards, tokens, width), BF16),
            pltpu.VMEM(early.shape, F32),
            pltpu.VMEM((late_rows, 128), F32),
            pltpu.VMEM((everyone, late_rows, 128), F32),
            pltpu.VMEM((tokens, width), F32),
            pltpu.VMEM((tokens, width), F32),
            pltpu.VMEM((depth, wide), BF16),
            pltpu.VMEM((wide, depth), BF16),
            pltpu.VMEM((2, depth, 256), BF16),
            pltpu.VMEM((2, 256, wide), F32),
            pltpu.VMEM((2, wide, 256), F32),
            dma((2, planes)), dma((2, planes)), dma((2, planes)), dma((2, planes + 1)), dma((shards,)), dma((shards,)),
            dma, dma, dma((shards,)), dma((shards,)), dma, dma, dma, dma, dma((2,)), dma, dma((2,)), dma((2,)),
        ],
        compiler_params=pltpu.CompilerParams(vmem_limit_bytes=VMEM_LIMIT, collective_id=3, has_side_effects=True),
        cost_estimate=pl.CostEstimate(flops=70 * 10**9, bytes_accessed=40 * 10**6, transcendentals=0),
    )(
        wq_grad, wo_grad, first_part, hidden, middle, expert_sum, middle_grad, small_all, early, query_gain_grad,
        key_gain_grad, squares, rows_in, gate_grad, up_grad, units, pair_grad,
    )


def expert_kernel(
    planes, across, shards, capacity,
    own_ref, share_ref, slots_ref, my_slots_ref, gate_ref, up_ref, down_ref, small_ref, top_hbm,
    middle_hbm, cotangent_hbm, rows_hbm, back_hbm, weighted_hbm, units_hbm, gate_grad_hbm, up_grad_hbm, pair_grad_hbm, row_grad_ref, low_grad_hbm, logit_grad_ref, gain_grad_ref,
    share_grad_ref, middle, plane_rows, plane_shares, share_in, share_back, share_home, stage, chosen, rows, top, units,
    gate_grad, up_grad, columns, partial_in,
    line_send, line_recv, plane_share_send, plane_share_recv, out_send, out_recv, out_share_send, out_share_recv,
    back_send, back_recv, back_share_send, back_share_recv, sum_send, sum_recv, sum_share_send, sum_share_recv,
    load_sem, top_sem, store_sem, middle_sem,
):
    z, x, w = lax.axis_index("z"), lax.axis_index("x"), lax.axis_index("w")
    in_plane = across * shards
    experts = planes * in_plane
    me = x * shards + w
    tokens, width = own_ref.shape
    count = in_plane * capacity
    half = count // 2
    per_half = in_plane // 2
    chunk = 512

    def place(index):
        return (z, index // shards, index % shards)

    def order(step):
        return line_order(z, planes, step)

    inner = ((z > 0) & (z < planes - 1)).astype(jnp.int32)
    first_back = 2 - (z == 1).astype(jnp.int32)
    second_back = 3 - inner * first_back
    third_back = 1 + 2 * inner
    greet_plane_and_line(planes, across, shards)

    def line_up(block, hop):
        return remote(
            plane_rows.at[block], plane_rows.at[block], line_send.at[0, hop], line_recv.at[0, hop], (z + 1, x, w)
        )

    def line_down(block, hop):
        return remote(
            plane_rows.at[block], plane_rows.at[block], line_send.at[1, hop], line_recv.at[1, hop], (z - 1, x, w)
        )

    middle_load = pltpu.make_async_copy(middle_hbm, middle, middle_sem)
    middle_load.start()
    plane_rows[z] = own_ref[...]

    @pl.when(z + 1 < planes)
    def _():
        line_up(z, 1).start()

    @pl.when(z > 0)
    def _():
        line_down(z, 1).start()

    def plane_share_copy(other):
        return remote(
            share_ref.at[pl.ds(other * in_plane, in_plane)], plane_shares.at[z],
            plane_share_send.at[other], plane_share_recv.at[z], (other, x, w),
        )

    @pl.loop(1, planes)
    def _(offset):
        plane_share_copy((z + offset) % planes).start()

    plane_shares[z] = share_ref[pl.ds(z * in_plane, in_plane)]

    def slice_of(index):
        return pl.ds(pl.multiple_of(index * capacity, 16), capacity)

    def out_copy(step, block, index):
        return remote(
            stage.at[step, slice_of(index)], rows_hbm.at[block, slice_of(me)],
            out_send.at[step], out_recv.at[step], place(index),
        )

    def out_share_copy(step, block, index):
        return remote(
            plane_shares.at[block, index], share_in.at[block, me],
            out_share_send.at[step], out_share_recv.at[step], place(index),
        )

    def back_copy(step, block, index):
        return remote(
            stage.at[step, slice_of(index)], back_hbm.at[block, slice_of(me)],
            back_send.at[step], back_recv.at[step], place(index),
        )

    def back_share_copy(step, block, index):
        return remote(
            share_back.at[block, index], share_home.at[block, me],
            back_share_send.at[step], back_share_recv.at[step], place(index),
        )

    def start_back(step, block):
        @pl.loop(1, in_plane)
        def _(offset):
            index = (me + offset) % in_plane
            back_copy(step, block, index).start()
            back_share_copy(step, block, index).start()

        pltpu.make_async_copy(stage.at[step, slice_of(me)], back_hbm.at[block, slice_of(me)], back_recv.at[step]).start()
        pltpu.make_async_copy(share_back.at[block, me], share_home.at[block, me], back_share_recv.at[step]).start()

    slot_ids = lax.broadcasted_iota(jnp.int32, (capacity, tokens), 0)

    def pack_step(step):
        block, _, _ = order(step)

        @pl.when(step > 0)
        def _():
            @pl.when(z - step >= 0)
            def _():
                wait_bytes(plane_rows.at[0], line_recv.at[0, step])

                @pl.when(z + 1 < planes)
                def _():
                    line_up(z - step, step + 1).start()

            @pl.when(z + step < planes)
            def _():
                wait_bytes(plane_rows.at[0], line_recv.at[1, step])

                @pl.when(z > 0)
                def _():
                    line_down(z + step, step + 1).start()

            wait_bytes(plane_shares.at[block], plane_share_recv.at[block])

        @pl.loop(0, in_plane)
        def _(index):
            slots = slots_ref[block * in_plane + index]
            chosen[step, slice_of(index), :] = (slot_ids == slots).astype(F32).astype(BF16)

        @pl.loop(0, width // chunk)
        def _(part):
            wide = pl.ds(pl.multiple_of(part * chunk, chunk), chunk)
            stage[step, :, wide] = dot(chosen[step], plane_rows[block, :, wide]).astype(BF16)

    def send_step(step):
        block, _, _ = order(step)

        @pl.loop(1, in_plane)
        def _(offset):
            index = (me + offset) % in_plane
            out_copy(step, block, index).start()
            out_share_copy(step, block, index).start()

        pltpu.make_async_copy(stage.at[step, slice_of(me)], rows_hbm.at[block, slice_of(me)], out_recv.at[step]).start()
        pltpu.make_async_copy(plane_shares.at[block, me], share_in.at[block, me], out_share_recv.at[step]).start()

    def expert_step(step):
        block, _, _ = order(step)

        pltpu.make_async_copy(top_hbm.at[block], top, top_sem).start()
        wait_bytes(rows_hbm.at[block], out_recv.at[step])
        load = pltpu.make_async_copy(rows_hbm.at[block], rows, load_sem)
        load.start()

        @pl.when(step + 1 < planes)
        def _():
            send_step(step + 1)

        wait_bytes(share_in.at[block], out_share_recv.at[step])
        wait_bytes(stage.at[step, pl.ds(0, count - capacity)], out_send.at[step])
        wait_bytes(plane_shares.at[block, pl.ds(0, in_plane - 1)], out_share_send.at[step])

        @pl.loop(0, in_plane)
        def _(index):
            mine = slot_ids == my_slots_ref[block * in_plane + index]
            columns[slice_of(index), :] = jnp.broadcast_to(
                jnp.sum(jnp.where(mine, share_in[block, index], 0.0), axis=1, keepdims=True), (capacity, 128)
            )

        load.wait()
        wait_bytes(top, top_sem)

        @pl.loop(0, 2)
        def _(part):
            here = pl.ds(pl.multiple_of(part * half, 16), half)
            gate = dot(rows[here, :], gate_ref[...])
            up = dot(rows[here, :], up_ref[...])
            sigmoid = 1.0 / (1.0 + jnp.exp(-gate))
            active = gate * sigmoid
            hidden = (active * up).astype(BF16)
            units[here, :] = hidden
            share = columns[here, 0:1]
            total = jnp.zeros((half, 1), F32)
            for piece in range(width // chunk):
                wide = pl.ds(piece * chunk, chunk)
                pair_out = dot(hidden, down_ref[:, wide]).astype(BF16).astype(F32)
                top_rows = top[here, wide].astype(F32)
                total += jnp.sum(pair_out * top_rows, axis=1, keepdims=True)
                rows[here, wide] = (share * pair_out).astype(BF16)
                top[here, wide] = (share * top_rows).astype(BF16)
            columns[here, :] = jnp.broadcast_to(total, (half, 128))
            hidden_grad = dot_nt(top[here, :], down_ref[...])
            gate_low = (hidden_grad * up * sigmoid * (1.0 + gate * (1.0 - sigmoid))).astype(BF16)
            up_low = (hidden_grad * active).astype(BF16)
            gate_grad[here, :] = gate_low
            up_grad[here, :] = up_low
            for piece in range(width // chunk):
                wide = pl.ds(piece * chunk, chunk)
                stage[step, here, wide] = (dot_nt(gate_low, gate_ref[wide, :]) + dot_nt(up_low, up_ref[wide, :])).astype(BF16)

        @pl.loop(0, in_plane)
        def _(index):
            mine = slot_ids == my_slots_ref[block * in_plane + index]
            values = columns[slice_of(index), 0:1]
            share_back[block, index] = jnp.sum(jnp.where(mine, values, 0.0), axis=0, keepdims=True)

        @pl.when((step == first_back) | (step == second_back))
        def _():
            start_back(step, block)

        stores = [
            pltpu.make_async_copy(units, units_hbm.at[block], store_sem.at[0]),
            pltpu.make_async_copy(gate_grad, gate_grad_hbm.at[block], store_sem.at[1]),
            pltpu.make_async_copy(up_grad, up_grad_hbm.at[block], store_sem.at[2]),
            pltpu.make_async_copy(top, pair_grad_hbm.at[block], store_sem.at[3]),
            pltpu.make_async_copy(rows, weighted_hbm.at[block], store_sem.at[4]),
        ]
        for store in stores:
            store.start()

        for store in stores:
            store.wait()

    @pl.loop(0, planes + 1)
    def _(step):
        @pl.when(step < planes)
        def _():
            pack_step(step)

        @pl.when(step == 0)
        def _():
            send_step(step)

        @pl.when(step > 0)
        def _():
            expert_step(step - 1)

    for hop in range(1, planes):

        @pl.when((z - (hop - 1) >= 0) & (z + 1 < planes))
        def _():
            wait_bytes(plane_rows.at[0], line_send.at[0, hop])

        @pl.when((z + (hop - 1) < planes) & (z > 0))
        def _():
            wait_bytes(plane_rows.at[0], line_send.at[1, hop])

    @pl.loop(1, planes)
    def _(offset):
        wait_bytes(plane_shares.at[0], plane_share_send.at[(z + offset) % planes])

    def wait_back(step):
        wait_bytes(stage.at[step, pl.ds(0, count - capacity)], back_send.at[step])
        wait_bytes(share_back.at[0, pl.ds(0, in_plane - 1)], back_share_send.at[step])

    def sum_copy(block):
        up = (block > z).astype(jnp.int32)
        relayed = (jnp.abs(block - z) == planes - 1).astype(jnp.int32)
        goal = block + relayed * (1 - 2 * up) * (planes - 2)
        slot = z + relayed * (goal - z)
        return remote(plane_rows.at[block], partial_in.at[slot], sum_send.at[block], sum_recv.at[slot], (goal, x, w))

    def sum_share_copy(block):
        return remote(
            share_home.at[block], share_grad_ref.at[pl.ds(z * in_plane, in_plane)],
            sum_share_send.at[block], sum_share_recv.at[z], (block, x, w),
        )

    @pl.loop(0, planes)
    def _(turn):
        step = jnp.where(turn == 0, first_back, jnp.where(turn == 1, second_back, jnp.where(turn == 2, third_back, 0)))
        block, _, _ = order(step)
        wait_bytes(back_hbm.at[block], back_recv.at[step])
        load = pltpu.make_async_copy(back_hbm.at[block], rows, load_sem)
        load.start()
        wait_bytes(share_home.at[block], back_share_recv.at[step])
        load.wait()

        @pl.when(step > 0)
        def _():
            sum_share_copy(block).start()

            merges = (inner == 1) & (jnp.abs(block - z) == 2)

            @pl.when(merges)
            def _():
                wait_bytes(partial_in.at[z], sum_recv.at[z])

            @pl.loop(0, width // chunk)
            def _(part):
                wide = pl.ds(pl.multiple_of(part * chunk, chunk), chunk)
                summed = dot_tn(chosen[step], rows[:, wide])

                @pl.when(merges)
                def _():
                    plane_rows[block, :, wide] = (summed + partial_in[z, :, wide].astype(F32)).astype(BF16)

                @pl.when(jnp.logical_not(merges))
                def _():
                    plane_rows[block, :, wide] = summed.astype(BF16)

            sum_copy(block).start()

        @pl.when(step == 0)
        def _():
            share_grad_ref[pl.ds(z * in_plane, in_plane)] = share_home[z]

            @pl.loop(0, width // chunk)
            def _(part):
                wide = pl.ds(pl.multiple_of(part * chunk, chunk), chunk)
                row_grad_ref[:, wide] = dot_tn(chosen[0], rows[:, wide])

        @pl.when(turn == 0)
        def _():
            wait_back(second_back)
            start_back(third_back, order(third_back)[0])

        @pl.when(turn == 1)
        def _():
            wait_back(third_back)
            start_back(0, z)

    cotangent_load = pltpu.make_async_copy(cotangent_hbm, rows.at[pl.ds(0, tokens)], load_sem)
    cotangent_load.start()

    @pl.loop(1, planes)
    def _(offset):
        other = (z + offset) % planes
        wait_bytes(share_home.at[other], sum_share_recv.at[other])

        @pl.when(jnp.abs(other - z) < planes - 1)
        def _():
            wait_bytes(partial_in.at[other], sum_recv.at[other])

            @pl.loop(0, width // chunk)
            def _(part):
                wide = pl.ds(pl.multiple_of(part * chunk, chunk), chunk)
                row_grad_ref[:, wide] += partial_in[other, :, wide].astype(F32)

    @pl.loop(1, planes)
    def _(offset):
        other = (z + offset) % planes
        wait_bytes(plane_rows.at[other], sum_send.at[other])
        wait_bytes(share_home.at[other], sum_share_send.at[other])

    cotangent_load.wait()
    middle_load.wait()
    depth = width // shards
    share_grad = jnp.concatenate([share_grad_ref[index] for index in range(experts)], axis=0)
    shares = jnp.concatenate([share_ref[index] for index in range(experts)], axis=0)
    center = jnp.sum(shares * share_grad, axis=0, keepdims=True)
    logit_grad_ref[...] = (shares * (share_grad - center)).astype(BF16)
    for part in range(shards):
        wide = slice(part * depth, (part + 1) * depth)
        row_grad_ref[:, wide] += dot_tn(logit_grad_ref[...], small_ref[part, :experts, :].astype(BF16))
    ffn_row = jnp.concatenate([small_ref[part, experts : experts + 1, :] for part in range(shards)], axis=1)

    def finish_rows(piece, gain_grad):
        at = pl.ds(pl.multiple_of(piece * 64, 64), 64)
        normed, scaling = norm_forward(middle[at, :])
        second_grad = row_grad_ref[at, :]
        grad = rows[at, :].astype(F32) + norm_backward(second_grad * ffn_row, normed, scaling)
        row_grad_ref[at, :] = grad
        rows[pl.ds(pl.multiple_of(tokens + piece * 64, 64), 64), :] = grad.astype(BF16)
        return gain_grad + jnp.sum(second_grad * normed, axis=0, keepdims=True)

    gain_grad_ref[...] = lax.fori_loop(0, tokens // 64, finish_rows, jnp.zeros((1, width), F32))
    low_store = pltpu.make_async_copy(rows.at[pl.ds(tokens, tokens)], low_grad_hbm, middle_sem)
    low_store.start()
    wait_back(0)
    wait_back(first_back)
    low_store.wait()


def run_experts(planes, across, shards, capacity, own, shares, slots, my_slots, w_gate, w_up, w_down, small_all, top_rows, middle, cotangent):
    tokens, width = own.shape
    in_plane = across * shards
    count = in_plane * capacity
    units = w_gate.shape[1]
    experts = planes * in_plane
    hbm = pl.BlockSpec(memory_space=pl.ANY)
    vmem = pl.BlockSpec(memory_space=pltpu.VMEM)
    dma = pltpu.SemaphoreType.DMA
    flops = 12 * planes * count * width * units
    return pl.pallas_call(
        functools.partial(expert_kernel, planes, across, shards, capacity),
        in_specs=[vmem] * 8 + [hbm] * 3,
        out_specs=[hbm] * 7 + [vmem, hbm, vmem, vmem],
        out_shape=[
            jax.ShapeDtypeStruct((planes, count, width), BF16),
            jax.ShapeDtypeStruct((planes, count, width), BF16),
            jax.ShapeDtypeStruct((planes, count, width), BF16),
            jax.ShapeDtypeStruct((planes, count, units), BF16),
            jax.ShapeDtypeStruct((planes, count, units), BF16),
            jax.ShapeDtypeStruct((planes, count, units), BF16),
            jax.ShapeDtypeStruct((planes, count, width), BF16),
            jax.ShapeDtypeStruct((tokens, width), F32),
            jax.ShapeDtypeStruct((tokens, width), BF16),
            jax.ShapeDtypeStruct((experts, tokens), BF16),
            jax.ShapeDtypeStruct((1, width), F32),
        ],
        scratch_shapes=[
            pltpu.VMEM((experts, 1, tokens), F32),
            pltpu.VMEM((tokens, width), F32),
            pltpu.VMEM((planes, tokens, width), BF16),
            pltpu.VMEM((planes, in_plane, 1, tokens), F32),
            pltpu.VMEM((planes, in_plane, 1, tokens), F32),
            pltpu.VMEM((planes, in_plane, 1, tokens), F32),
            pltpu.VMEM((planes, in_plane, 1, tokens), F32),
            pltpu.VMEM((planes, count, width), BF16),
            pltpu.VMEM((planes, count, tokens), BF16),
            pltpu.VMEM((count, width), BF16),
            pltpu.VMEM((count, width), BF16),
            pltpu.VMEM((count, units), BF16),
            pltpu.VMEM((count, units), BF16),
            pltpu.VMEM((count, units), BF16),
            pltpu.VMEM((count, 128), F32),
            pltpu.VMEM((planes, tokens, width), BF16),
            dma((2, planes + 1)), dma((2, planes + 1)), dma((planes,)), dma((planes,)),
            dma((planes,)), dma((planes,)), dma((planes,)), dma((planes,)),
            dma((planes,)), dma((planes,)), dma((planes,)), dma((planes,)),
            dma((planes,)), dma((planes,)), dma((planes,)), dma((planes,)),
            dma, dma, dma((5,)), dma,
        ],
        compiler_params=pltpu.CompilerParams(vmem_limit_bytes=VMEM_LIMIT, collective_id=1, has_side_effects=True),
        cost_estimate=pl.CostEstimate(flops=4 * flops, bytes_accessed=100 * 10**6, transcendentals=2 * 10**6),
    )(own, shares, slots, my_slots, w_gate, w_up, w_down, small_all, top_rows, middle, cotangent)


def local(
    hidden_in, attn_gain, w_query, key_projection, value_projection, query_gain, key_gain, w_output, ffn_gain, w_router,
    routes, w_gate, w_up, w_down, cotangent,
):
    tokens_here, width = hidden_in.shape
    head_size = query_gain.shape[0]
    top_count = routes.shape[1]
    planes, across, shards = lax.axis_size("z"), lax.axis_size("x"), lax.axis_size("w")
    rings = planes * across
    device_count = rings * shards
    in_plane = across * shards
    experts = device_count
    capacity = 5 * tokens_here * top_count // (4 * experts)
    seq_length = tokens_here * shards

    cosine, sine = rope_tables(seq_length, head_size)
    query_gain_row, key_gain_row = query_gain[None, :], key_gain[None, :]

    capacity = -(-capacity // 16) * 16
    small = jnp.concatenate([w_router.T, ffn_gain[None, :], attn_gain[None, :]], axis=0).astype(F32)
    small = jnp.pad(small, ((0, -small.shape[0] % 8), (0, 0)))
    (
        first_input, query_raw, key_raw, value, attended, middle, slots_flat, my_slots, shares, squares, second_input,
        small_all, weights, top_rows,
    ) = run_forward(
        planes, across, shards, capacity, hidden_in, small, routes.T, cotangent, w_query, key_projection,
        value_projection, query_gain_row, key_gain_row, cosine, sine, w_output,
    )
    (
        rows_in, _, weighted, hidden_units, gate_grad, up_grad, pair_grad, middle_grad, low_grad, logit_grad, ffn_gain_grad,
    ) = run_experts(
        planes, across, shards, capacity, second_input, shares, slots_flat, my_slots, w_gate[0], w_up[0], w_down[0],
        small_all, top_rows, middle, cotangent,
    )
    units = w_gate.shape[2]
    router_grad = dot_tn(second_input, logit_grad.T)
    wo_grad, wq_grad, first_part, query_gain_grad, key_gain_grad, _, expert_sum = run_backward(
        planes, across, shards, capacity, low_grad, w_output, attended, query_raw, key_raw, value,
        first_input, weights, query_gain_row, key_gain_row, cosine, sine, slots_flat, weighted,
    )
    mine = width // device_count
    early = jnp.concatenate(
        [router_grad.reshape(device_count, mine * experts), ffn_gain_grad.reshape(device_count, mine)], axis=1
    )
    early = jnp.pad(early, ((0, 0), (0, -early.shape[1] % 1024))).reshape(device_count, -1, 128)
    (
        sum_query, sum_key, sum_value, sum_output, hidden_out, grad_in, early_total, late_total, grad_gate, grad_up, grad_down,
    ) = run_reduce(
        planes, across, shards, wq_grad, wo_grad, first_part, hidden_in, middle, expert_sum, middle_grad, small_all, early,
        query_gain_grad, key_gain_grad, squares, rows_in.reshape(-1, width), gate_grad.reshape(-1, units), up_grad.reshape(-1, units),
        hidden_units.reshape(-1, units), pair_grad.reshape(-1, width), w_query.shape[1], key_projection.shape[1],
    )
    early_total = early_total.reshape(-1)
    sum_router = early_total[: mine * experts].reshape(mine, experts)
    sum_ffn = early_total[mine * experts : mine * (experts + 1)]
    linear = (lax.axis_index("z") * across + lax.axis_index("x")) * shards + lax.axis_index("w")
    sum_attn = lax.dynamic_slice_in_dim(late_total[: width // 128].reshape(-1), linear * mine, mine)
    late_total = late_total[width // 128 :]
    totals = jnp.concatenate([late_total[0], late_total[1], late_total[2, :4]])
    root_mean_squares = jnp.sqrt(totals[2 * head_size :] / (tokens_here * device_count * width))
    return (
        hidden_out,
        grad_in,
        sum_attn,
        sum_query,
        sum_key,
        sum_value,
        totals[:head_size],
        totals[head_size : 2 * head_size],
        sum_output,
        sum_ffn,
        sum_router,
        grad_gate[None],
        grad_up[None],
        grad_down[None],
        root_mean_squares,
    )


def solution(mesh):
    rings, shards = mesh.shape["ep"], mesh.shape["ws"]
    planes = 4 if rings % 4 == 0 else 1
    fine = Mesh(mesh.devices.reshape(planes, rings // planes, shards), ("z", "x", "w"))
    every = ("z", "x", "w")
    rows, deep = P(every, None), P(every, None, None)
    return jax.shard_map(
        local,
        mesh=fine,
        in_specs=(
            rows, P("w"), P("w", None), P("w", None), P("w", None), P(), P(), P("w", None), P("w"), P("w", None),
            rows, deep, deep, deep, rows,
        ),
        out_specs=(
            rows, rows, P(every), rows, rows, rows, P(), P(), rows, P(every), rows, deep, deep, deep, P(),
        ),
        check_vma=False,
    )
```
